32 devices in a mesh: seqo: 8 (over y, x, core), seqi: 4 (over z).
Axes of the slice: x: 2, y: 2, z: 4, core: 2. Of those that a mesh axis runs over, the one named last changes fastest.
Arguments:
- query_rows: bfloat16 [4096, 2048], P(('seqo', 'seqi')), may hold values from -88 to 88
- key_rows: bfloat16 [4096, 2048], P(('seqo', 'seqi')), may hold values from -4 to 4
- value_rows: bfloat16 [4096, 2048], P(('seqo', 'seqi')), may hold values from -6 to 6
- upstream: bfloat16 [4096, 2048], P(('seqo', 'seqi')), may hold values from -6 to 6
Outputs:
- attended: bfloat16 [4096, 2048], P(('seqo', 'seqi'))
- grad_queries: bfloat16 [4096, 2048], P(('seqo', 'seqi'))
- grad_keys: bfloat16 [4096, 2048], P(('seqo', 'seqi'))
- grad_values: bfloat16 [4096, 2048], P(('seqo', 'seqi'))
The draws below stay inside these ranges and needn't reach their ends.
All inputs are finite; a program needn't handle non-finite values.
Results may differ from the reference program's by a relative error of at most 0.025.
Values may be sent and summed in bfloat16 or wider, within the bound.
No kernel may reach another device: no remote copies, remote signals or barrier semaphores. Data moves between devices by JAX's collectives and lax.ppermute only.
A program may use at most 64 MiB of HBM per device.

```python
from functools import partial
from functools import reduce
import jax
import jax.numpy as jnp
from jax import lax

ROWS = 128
HEADS = 16
HEAD_DIM = 128
TILE = 128
SEQ = 4096
GROUP = 512


def shared_keys(key):
    return jnp.clip(jax.random.normal(key, (SEQ, HEADS * HEAD_DIM), jnp.float32), -4.0, 4.0)


def draw_key_rows(key, part):
    base = shared_keys(key)
    return base.astype(jnp.bfloat16)


def draw_query_rows(key, part):
    key = jax.random.fold_in(key, 5)
    fresh = jnp.clip(jax.random.normal(key, (SEQ, HEADS * HEAD_DIM), jnp.float32), -4.0, 4.0)
    return fresh.astype(jnp.bfloat16)


def block_scale(rng, shape, cuts, least, largest):
    gain = 1.0
    for dim, parts in cuts:
        draws = jax.random.uniform(jax.random.fold_in(jax.random.fold_in(rng, 6), dim), (parts,), jnp.float32, least / len(cuts), largest / len(cuts))
        gain = gain * jnp.repeat(jnp.exp(draws), shape[dim] // parts).reshape((-1,) + (1,) * (len(shape) - 1 - dim))
    return gain


def centred(own_key, shape, deviation, limit, split=(), kind=jnp.bfloat16):
    factor_of = block_scale(own_key, shape, split, -0.22, 0.18) if split else 1.0
    drawn = jax.random.normal(own_key, shape, jnp.float32) * deviation * factor_of
    return jnp.minimum(jnp.maximum(drawn, -limit), limit).astype(kind)


def setup_inputs(seed: int = 0) -> dict:
    streams_of = jax.random.split(jax.random.key(seed), 5)
    query_rows = draw_query_rows(jax.random.fold_in(streams_of[4], 71), 0)
    key_rows = draw_key_rows(jax.random.fold_in(streams_of[4], 71), 0)
    value_rows = centred(streams_of[2], (SEQ, HEADS * HEAD_DIM), 1.0, 6.0, ((0, 32),))
    upstream = centred(streams_of[3], (SEQ, HEADS * HEAD_DIM), 1.0, 6.0, ((0, 32),))
    return dict(query_rows=query_rows, key_rows=key_rows, value_rows=value_rows, upstream=upstream)


def to_half(tensor):
    return lax.optimization_barrier(tensor.astype(jnp.bfloat16)).astype(jnp.float32)


def widen(tensor):
    return tensor.astype(jnp.float32)


def forward_level(query_matrix, key_portion_rows, value_portion_rows, score_scale):
    scores = jnp.einsum("bmd,bnd->bmn", widen(query_matrix), widen(key_portion_rows)) * score_scale
    highest = jnp.max(scores, axis=2)
    attention_weights = jnp.exp(scores - highest[:, :, None])
    totals = jnp.sum(attention_weights, axis=2)
    numerator = jnp.einsum("bmn,bnd->bmd", to_half(attention_weights), widen(value_portion_rows))
    return numerator / totals[:, :, None], highest + jnp.log(totals)


def grad_level(query_matrix, key_portion_rows, value_portion_rows, upstream, level_log, level_delta, score_scale):
    scores = jnp.einsum("bmd,bnd->bmn", widen(query_matrix), widen(key_portion_rows)) * score_scale
    attention_weights = jnp.exp(scores - level_log[:, :, None])
    weight_grad = jnp.einsum("bmd,bnd->bmn", widen(upstream), widen(value_portion_rows))
    score_gradient = to_half(attention_weights * (weight_grad - level_delta[:, :, None]))
    query_part = jnp.einsum("bmn,bnd->bmd", score_gradient, widen(key_portion_rows)) * score_scale
    key_grad = jnp.einsum("bmn,bmd->bnd", score_gradient, widen(query_matrix)) * score_scale
    value_grad = jnp.einsum("bmn,bmd->bnd", to_half(attention_weights), widen(upstream))
    return query_part, key_grad, value_grad


def combine_levels(outputs, logs, covers):
    safe_logs = [jnp.where(covered > 0, level_log, logs[0]) for level_log, covered in zip(logs, covers)]
    highest = reduce(jnp.maximum, safe_logs)
    shares = [covered * jnp.exp(level_log - highest) for level_log, covered in zip(safe_logs, covers)]
    summed = reduce(jnp.add, shares)
    merged = reduce(jnp.add, [portion[..., None] * output for portion, output in zip(shares, outputs)])
    return merged / summed[..., None], highest + jnp.log(summed)


def near_blocks(tensor):
    return tensor.reshape((SEQ // ROWS, ROWS) + tensor.shape[1:])


def near_back(tensor):
    return tensor.reshape((SEQ,) + tensor.shape[2:])


def middle_blocks(tensor, residue):
    return tensor.reshape((SEQ // GROUP, GROUP // 4, 4) + tensor.shape[1:])[:, :, residue]


def middle_back(tensor, residue):
    filled = jnp.zeros((SEQ // GROUP, GROUP // 4, 4) + tensor.shape[2:], tensor.dtype)
    return filled.at[:, :, residue].set(tensor).reshape((SEQ,) + tensor.shape[2:])


def far_blocks(tensor, place):
    tiles = tensor.reshape((SEQ // GROUP, GROUP // TILE, TILE) + tensor.shape[1:])[:, place]
    return tiles.reshape((1, (SEQ // GROUP) * TILE) + tensor.shape[1:])


def far_back(tensor, place):
    filled = jnp.zeros((SEQ // GROUP, GROUP // TILE, TILE) + tensor.shape[2:], tensor.dtype)
    filled = filled.at[:, place].set(tensor.reshape((SEQ // GROUP, TILE) + tensor.shape[2:]))
    return filled.reshape((SEQ,) + tensor.shape[2:])


def reference(query_rows, key_rows, value_rows, upstream):
    score_scale = HEAD_DIM ** -0.5
    results = [[], [], [], []]
    for head_index in range(HEADS):
        inputs = [tensor[:, head_index * HEAD_DIM:(head_index + 1) * HEAD_DIM] for tensor in (query_rows, key_rows, value_rows, upstream)]
        residue = head_index % 4
        place = (head_index * GROUP // (HEADS * ROWS)) * (ROWS // TILE)
        levels = [(near_blocks, near_back),
                  (partial(middle_blocks, residue=residue), partial(middle_back, residue=residue)),
                  (partial(far_blocks, place=place), partial(far_back, place=place))]
        outputs, logs, covers = [], [], []
        for divide, rejoin in levels:
            level_out, level_log = forward_level(divide(inputs[0]), divide(inputs[1]), divide(inputs[2]), score_scale)
            outputs.append(rejoin(level_out))
            logs.append(rejoin(level_log))
            covers.append(rejoin(jnp.ones(level_log.shape, level_log.dtype)))
        merged, total_log = combine_levels(outputs, logs, covers)
        attended = merged.astype(jnp.bfloat16)
        row_delta = jnp.sum(widen(inputs[3]) * widen(attended), axis=1)
        grads = [jnp.zeros(merged.shape, merged.dtype)] * 3
        for divide, rejoin in levels:
            level_grads = grad_level(divide(inputs[0]), divide(inputs[1]), divide(inputs[2]), divide(inputs[3]),
                                     divide(total_log), divide(row_delta), score_scale)
            grads = [total_grad + rejoin(level_grad) for total_grad, level_grad in zip(grads, level_grads)]
        results[0].append(attended)
        for slot_index in range(3):
            results[slot_index + 1].append(grads[slot_index].astype(jnp.bfloat16))
    return (jnp.concatenate(results[0], axis=1), jnp.concatenate(results[1], axis=1),
            jnp.concatenate(results[2], axis=1), jnp.concatenate(results[3], axis=1))
```

```python
import functools

import jax
import jax.numpy as jnp
from jax import lax
from jax.experimental import pallas as pl
from jax.experimental.pallas import tpu as pltpu
from jax.sharding import PartitionSpec as P

HEADS = 16
HEAD_DIM = 128
DILATION = 4
SCALE = HEAD_DIM**-0.5
LOWEST = -1e30
VMEM_LIMIT = 48 * 1024 * 1024

NT = (((1,), (1,)), ((), ()))
TN = (((0,), (0,)), ((), ()))


def dot(a, b):
    return jnp.dot(a, b, preferred_element_type=jnp.float32)


def dot_nt(a, b):
    return lax.dot_general(a, b, NT, preferred_element_type=jnp.float32)


def dot_tn(a, b):
    return lax.dot_general(a, b, TN, preferred_element_type=jnp.float32)


def head_columns(head):
    return pl.ds(pl.multiple_of(head * HEAD_DIM, HEAD_DIM), HEAD_DIM)


def pick_kernel(slots, pos_ref, a_ref, b_ref, mid_ref, tile_ref, wide):
    rows = a_ref.shape[0]
    quarter = rows // DILATION
    for which, ref in enumerate((a_ref, b_ref)):
        for head in range(HEADS):
            cols = slice(head * HEAD_DIM, (head + 1) * HEAD_DIM)
            wide[head] = ref[:, cols].astype(jnp.float32)
            picked = wide[head, pl.ds(head % DILATION, quarter, stride=DILATION), :]
            mid_ref[which, :, cols] = picked.astype(jnp.bfloat16)
        width = slots * HEAD_DIM
        start = pl.multiple_of(pos_ref[0] * width, width)
        tile_ref[which] = ref[:, pl.ds(start, width)]


def merge(old, new):
    acc_a, max_a, sum_a = old
    acc_b, max_b, sum_b = new
    top = jnp.maximum(max_a, max_b)
    fa = jnp.exp(max_a - top)
    fb = jnp.exp(max_b - top)
    return acc_a * fa + acc_b * fb, top, sum_a * fa + sum_b * fb


def softmax_state(q, k, v):
    s = dot_nt(q, k) * SCALE
    top = jnp.max(s, axis=1, keepdims=True)
    p = jnp.exp(s - top)
    total = jnp.sum(p, axis=1, keepdims=True)
    return dot(p.astype(jnp.bfloat16), v), top, total


def gathered_mid(own, pairs, which, cols):
    parts = [own[which, :, cols]]
    for left, right in pairs:
        parts.append(left[which, :, cols] + right[which, :, cols])
    return jnp.concatenate(parts, axis=0)


def gathered_tile(tiles, which, slot):
    cols = slice(slot * HEAD_DIM, (slot + 1) * HEAD_DIM)
    return jnp.concatenate([tile[which, :, cols] for tile in tiles], axis=0)


def forward_kernel(n_i, n_o, slots, *refs):
    pos_ref, q_ref, k_ref, v_ref, u_ref, qmid_ref, own_mid = refs[:7]
    rest = refs[7:]
    pairs = [(rest[2 * d], rest[2 * d + 1]) for d in range(n_i - 1)]
    rest = rest[2 * (n_i - 1) :]
    tiles = rest[:n_o]
    rest = rest[n_o:]
    att_ref, comp_ref, midcol_ref, midrow_ref, tilerow_ref, gmid_ref = rest[:6]
    acc, mb, zb, turned = rest[6:]
    rows = q_ref.shape[0]
    quarter = rows // DILATION
    pos = pos_ref[0]

    def near(group, carry):
        for residue in range(DILATION):
            head = group * DILATION + residue
            cols = head_columns(head)
            state = softmax_state(q_ref[:, cols], k_ref[:, cols], v_ref[:, cols])
            acc[head] = state[0]
            mb[head] = jnp.broadcast_to(state[1], (rows, HEAD_DIM))
            zb[head] = jnp.broadcast_to(state[2], (rows, HEAD_DIM))
        return carry

    lax.fori_loop(0, HEADS // DILATION, near, 0)

    for slot in range(slots):
        head = pos * slots + slot
        cols = head_columns(head)
        state = softmax_state(
            q_ref[:, cols], gathered_tile(tiles, 0, slot), gathered_tile(tiles, 1, slot)
        )
        acc[head], mb[head], zb[head] = merge((acc[head], mb[head], zb[head]), state)

    comp_ref[...] = jnp.zeros_like(comp_ref)
    lane = lax.broadcasted_iota(jnp.int32, (rows, HEAD_DIM), 1)

    def middle(group, carry):
        for residue in range(DILATION):
            head = group * DILATION + residue
            cols = head_columns(head)
            keys = gathered_mid(own_mid, pairs, 0, cols)
            values = gathered_mid(own_mid, pairs, 1, cols)
            gmid_ref[0, :, cols] = keys
            gmid_ref[1, :, cols] = values
            state = softmax_state(qmid_ref[0, :, cols], keys, values)
            at = (head, pl.ds(residue, quarter, stride=DILATION), slice(None))
            acc[at], mb[at], zb[at] = merge((acc[at], mb[at], zb[at]), state)
            total = zb[head]
            out = (acc[head] / total).astype(jnp.bfloat16)
            att_ref[:, cols] = out
            lse = mb[head] + jnp.log(total)
            delta = jnp.sum(
                u_ref[:, cols].astype(jnp.float32) * out.astype(jnp.float32), axis=1, keepdims=True
            )
            comp_ref[...] = jnp.where(
                lane == head, lse, jnp.where(lane == HEADS + head, delta, comp_ref[...])
            )
        return carry

    lax.fori_loop(0, HEADS // DILATION, middle, 0)

    lane = lax.broadcasted_iota(jnp.int32, (quarter, HEAD_DIM), 1)
    mid = jnp.zeros((quarter, HEAD_DIM), jnp.float32)
    for residue in range(DILATION):
        part = comp_ref[pl.ds(residue, quarter, stride=DILATION), :]
        mid = jnp.where(lane % DILATION == residue, part, mid)
    midcol_ref[...] = mid
    midrow_ref[...] = mid.T[: 2 * HEADS]
    turned[...] = comp_ref[...].T
    tilerow_ref[:slots] = turned[pl.ds(pos * slots, slots), :]
    tilerow_ref[slots:] = turned[pl.ds(HEADS + pos * slots, slots), :]


def store_heads(out_ref, acc, scale):
    for head in range(HEADS):
        cols = slice(head * HEAD_DIM, (head + 1) * HEAD_DIM)
        out_ref[:, cols] = (acc[head] * scale).astype(jnp.bfloat16)


def column_of(ref, index):
    lane = lax.broadcasted_iota(jnp.int32, ref.shape, 1)
    return jnp.sum(jnp.where(lane == index, ref[...], 0.0), axis=1, keepdims=True)


def score_grads(s, dp, lse, delta):
    g = jnp.exp(s * SCALE - lse)
    return g.astype(jnp.bfloat16), (g * (dp - delta)).astype(jnp.bfloat16)


def query_side_kernel(n_o, slots, *refs):
    pos_ref, q_ref, k_ref, v_ref, u_ref, qmid_ref, gmid_ref, comp_ref, midcol_ref = refs[:9]
    tiles = refs[9 : 9 + n_o]
    dq_ref, dk_ref, dv_ref, acc = refs[9 + n_o :]
    rows = q_ref.shape[0]
    quarter = rows // DILATION
    pos = pos_ref[0]

    def near(group, carry):
        for residue in range(DILATION):
            head = group * DILATION + residue
            cols = head_columns(head)
            q, k, v, u = q_ref[:, cols], k_ref[:, cols], v_ref[:, cols], u_ref[:, cols]
            lse, delta = column_of(comp_ref, head), column_of(comp_ref, HEADS + head)
            p, ds = score_grads(dot_nt(q, k), dot_nt(u, v), lse, delta)
            acc[head] = dot(ds, k)
            dk_ref[head] = dot_tn(ds, q)
            dv_ref[head] = dot_tn(p, u)
            keys, values = gmid_ref[0, :, cols], gmid_ref[1, :, cols]
            q, u = qmid_ref[0, :, cols], qmid_ref[1, :, cols]
            lse, delta = column_of(midcol_ref, head), column_of(midcol_ref, HEADS + head)
            _, ds = score_grads(dot_nt(q, keys), dot_nt(u, values), lse, delta)
            acc[head, pl.ds(residue, quarter, stride=DILATION), :] += dot(ds, keys)
        return carry

    lax.fori_loop(0, HEADS // DILATION, near, 0)

    for slot in range(slots):
        head = pos * slots + slot
        cols = head_columns(head)
        lse, delta = column_of(comp_ref, head), column_of(comp_ref, HEADS + head)
        keys, values = gathered_tile(tiles, 0, slot), gathered_tile(tiles, 1, slot)
        s, dp = dot_nt(q_ref[:, cols], keys), dot_nt(u_ref[:, cols], values)
        _, ds = score_grads(s, dp, lse, delta)
        acc[head] += dot(ds, keys)
    store_heads(dq_ref, acc, SCALE)


def key_side_kernel(n_i, n_o, slots, *refs):
    pos_ref, kmid_ref, ktile_ref, dk0_ref, dv0_ref, own_mid = refs[:6]
    rest = refs[6:]
    pairs = [(rest[2 * d], rest[2 * d + 1]) for d in range(n_i - 1)]
    rest = rest[2 * (n_i - 1) :]
    tiles, rest = rest[:n_o], rest[n_o:]
    midrows, rest = rest[:n_i], rest[n_i:]
    tilerows, rest = rest[:n_o], rest[n_o:]
    dk_ref, dv_ref, dk, dv, stat = rest
    rows = dk0_ref.shape[1]
    quarter = rows // DILATION
    pos = pos_ref[0]
    stat[...] = jnp.concatenate([ref[...] for ref in midrows], axis=1)
    dk[...] = dk0_ref[...]
    dv[...] = dv0_ref[...]

    def middle(group, carry):
        for residue in range(DILATION):
            head = group * DILATION + residue
            cols = head_columns(head)
            k, v = kmid_ref[0, :, cols], kmid_ref[1, :, cols]
            queries = gathered_mid(own_mid, pairs, 0, cols)
            ups = gathered_mid(own_mid, pairs, 1, cols)
            lse, delta = stat[pl.ds(head, 1), :], stat[pl.ds(HEADS + head, 1), :]
            p, ds = score_grads(dot_nt(k, queries), dot_nt(v, ups), lse, delta)
            at = (head, pl.ds(residue, quarter, stride=DILATION), slice(None))
            dk[at] += dot(ds, queries)
            dv[at] += dot(p, ups)
        return carry

    lax.fori_loop(0, HEADS // DILATION, middle, 0)

    for slot in range(slots):
        head = pos * slots + slot
        own = slice(slot * HEAD_DIM, (slot + 1) * HEAD_DIM)
        queries, ups = gathered_tile(tiles, 0, slot), gathered_tile(tiles, 1, slot)
        lse = jnp.concatenate([ref[slot : slot + 1, :] for ref in tilerows], axis=1)
        delta = jnp.concatenate([ref[slots + slot : slots + slot + 1, :] for ref in tilerows], axis=1)
        s, dp = dot_nt(ktile_ref[0, :, own], queries), dot_nt(ktile_ref[1, :, own], ups)
        p, ds = score_grads(s, dp, lse, delta)
        dk[head] += dot(ds, queries)
        dv[head] += dot(p, ups)
    store_heads(dk_ref, dk, SCALE)
    store_heads(dv_ref, dv, 1.0)


def call(kernel, outs, scratch, name, flops, *operands):
    specs = [pl.BlockSpec(memory_space=pltpu.SMEM)]
    specs += [pl.BlockSpec(memory_space=pltpu.VMEM)] * (len(operands) - 1)
    moved = sum(x.size * x.dtype.itemsize for x in operands + tuple(outs))
    return pl.pallas_call(
        kernel,
        out_shape=tuple(outs),
        in_specs=specs,
        out_specs=tuple(pl.BlockSpec(memory_space=pltpu.VMEM) for _ in outs),
        scratch_shapes=scratch,
        compiler_params=pltpu.CompilerParams(vmem_limit_bytes=VMEM_LIMIT),
        cost_estimate=pl.CostEstimate(flops=flops, bytes_accessed=moved, transcendentals=0),
        name=name,
    )(*operands)


def line_gather(x, n):
    right, left = {0: x}, {0: x}
    for hop in range(1, n):
        right[hop] = lax.ppermute(right[hop - 1], "seqi", [(i, i + 1) for i in range(hop - 1, n - 1)])
        left[hop] = lax.ppermute(left[hop - 1], "seqi", [(i + 1, i) for i in range(n - hop)])
    return [t for d in range(1, n) for t in (left[d], right[n - d])]


def plane_gather(x, n):
    found = [x]
    for mask in range(2, n, 2):
        found.append(lax.ppermute(x, "seqo", [(i, i ^ mask) for i in range(n)]))
    return found + [lax.ppermute(t, "seqo", [(i, i ^ 1) for i in range(n)]) for t in found]


def local(query_rows, key_rows, value_rows, upstream):
    rows, width = query_rows.shape
    n_i, n_o = lax.axis_size("seqi"), lax.axis_size("seqo")
    slots = max(1, HEADS // n_i)
    quarter = rows // DILATION
    pos = lax.axis_index("seqi").astype(jnp.int32).reshape(1)
    f32, bf16 = jnp.float32, jnp.bfloat16
    shape = jax.ShapeDtypeStruct
    per_head = (HEADS, rows, HEAD_DIM)
    wide = pltpu.VMEM(per_head, f32)
    unit = 2 * rows * rows * HEAD_DIM

    def pick(a, b, name):
        outs = (shape((2, quarter, width), bf16), shape((2, rows, slots * HEAD_DIM), bf16))
        return call(functools.partial(pick_kernel, slots), outs, [wide], name, unit, pos, a, b)

    kv_mid, kv_tile = pick(key_rows, value_rows, "pick_kv")
    kv_mids = line_gather(kv_mid, n_i)
    kv_tiles = plane_gather(kv_tile, n_o)
    qu_mid, qu_tile = pick(query_rows, upstream, "pick_qu")
    qu_mids = line_gather(qu_mid, n_i)
    qu_tiles = plane_gather(qu_tile, n_o)

    whole = shape((rows, width), bf16)
    attended, comp, midcol, midrow, tilerow, gmid = call(
        functools.partial(forward_kernel, n_i, n_o, slots),
        (
            whole,
            shape((rows, HEAD_DIM), f32),
            shape((quarter, HEAD_DIM), f32),
            shape((2 * HEADS, quarter), f32),
            shape((2 * slots, rows), f32),
            shape((2, n_i * quarter, width), bf16),
        ),
        [wide, wide, wide, pltpu.VMEM((HEAD_DIM, rows), f32)],
        "forward",
        unit * (HEADS * 3 + 2 * slots * n_o),
        pos,
        query_rows,
        key_rows,
        value_rows,
        upstream,
        qu_mid,
        kv_mid,
        *kv_mids,
        *kv_tiles,
    )

    midrows = [midrow] + [
        lax.ppermute(midrow, "seqi", [((i + d) % n_i, i) for i in range(n_i)]) for d in range(1, n_i)
    ]
    tilerows = plane_gather(tilerow, n_o)

    grad_queries, dk0, dv0 = call(
        functools.partial(query_side_kernel, n_o, slots),
        (whole, shape(per_head, f32), shape(per_head, f32)),
        [wide],
        "query_side",
        unit * (HEADS * 6 + 3 * slots * n_o),
        pos,
        query_rows,
        key_rows,
        value_rows,
        upstream,
        qu_mid,
        gmid,
        comp,
        midcol,
        *kv_tiles,
    )
    grad_keys, grad_values = call(
        functools.partial(key_side_kernel, n_i, n_o, slots),
        (whole, whole),
        [wide, wide, pltpu.VMEM((2 * HEADS, n_i * quarter), f32)],
        "key_side",
        unit * (HEADS + 4 * slots * n_o),
        pos,
        kv_mid,
        kv_tile,
        dk0,
        dv0,
        qu_mid,
        *qu_mids,
        *qu_tiles,
        *midrows,
        *tilerows,
    )
    return attended, grad_queries, grad_keys, grad_values


def solution(mesh):
    rows = P(("seqo", "seqi"), None)
    return jax.shard_map(
        local,
        mesh=mesh,
        in_specs=(rows,) * 4,
        out_specs=(rows,) * 4,
        check_vma=False,
    )
```

```python
import functools

import jax
import jax.numpy as jnp
from jax import lax
from jax.experimental import pallas as pl
from jax.experimental.pallas import tpu as pltpu
from jax.sharding import PartitionSpec as P

HEADS = 16
HEAD_DIM = 128
DILATION = 4
LANES = 128
SCALE = HEAD_DIM**-0.5
LOWEST = -1e30
VMEM_LIMIT = 32 * 1024 * 1024
F32, BF16 = jnp.float32, jnp.bfloat16
SHAPE = jax.ShapeDtypeStruct

NT = (((1,), (1,)), ((), ()))
TN = (((0,), (0,)), ((), ()))


def dot(a, b):
    return jnp.dot(a, b, preferred_element_type=F32)


def dot_nt(a, b):
    return lax.dot_general(a, b, NT, preferred_element_type=F32)


def dot_tn(a, b):
    return lax.dot_general(a, b, TN, preferred_element_type=F32)


def head_columns(head):
    return pl.ds(pl.multiple_of(head * HEAD_DIM, HEAD_DIM), HEAD_DIM)


def static_columns(index):
    return slice(index * HEAD_DIM, (index + 1) * HEAD_DIM)


def lanes_of(rows):
    return lax.broadcasted_iota(jnp.int32, (rows, LANES), 1)


def level_stats(q, k, v, u):
    s = dot_nt(k, q) * SCALE
    dp = dot_nt(v, u)
    top = jnp.max(s, axis=0, keepdims=True)
    p = jnp.exp(s - top)
    total = jnp.sum(p, axis=0, keepdims=True)
    return top + jnp.log(total), jnp.sum(p * dp, axis=0, keepdims=True) / total


def merge_stats(ea, da, eb, db):
    top = jnp.maximum(ea, eb)
    wa, wb = jnp.exp(ea - top), jnp.exp(eb - top)
    total = wa + wb
    return top + jnp.log(total), (wa * da + wb * db) / total


def level_weights(q, k, v, u, lse, delta):
    g = jnp.exp(dot_nt(k, q) * SCALE - lse)
    return g.astype(BF16), (g * (dot_nt(v, u) - delta)).astype(BF16)


def level_parts(q, k, v, u, lse, delta):
    p, ds = level_weights(q, k, v, u, lse, delta)
    return dot_tn(p, v), dot_tn(ds, k) * SCALE, dot(ds, q) * SCALE, dot(p, u)


def pick_rows(ref, rows):
    quarter = rows // DILATION
    lane = lanes_of(quarter)
    picked = jnp.zeros((quarter, LANES), F32)
    for residue in range(DILATION):
        part = ref[pl.ds(residue, quarter, stride=DILATION), :]
        picked = jnp.where(lane % DILATION == residue, part, picked)
    return picked


def pick_kernel(n_i, slots, at_ref, *refs):
    sources, refs = refs[:4], refs[4:]
    mids, refs = refs[:n_i], refs[n_i:]
    fulls, refs = refs[:slots], refs[slots:]
    kvs, refs = refs[:slots], refs[slots:]
    wide, picked = refs
    rows = sources[0].shape[0]
    quarter = rows // DILATION
    pos, chip = at_ref[0], at_ref[1]
    for which, ref in enumerate(sources):
        for head in range(HEADS):
            cols = static_columns(head)
            wide[head] = ref[:, cols].astype(F32)
            rowset = wide[head, pl.ds(head % DILATION, quarter, stride=DILATION), :]
            picked[:, cols] = rowset.astype(BF16)
        width = slots * HEAD_DIM
        for d in range(n_i):
            start = pl.multiple_of((pos ^ d) * width, width)
            mids[d][which] = picked[:, pl.ds(start, width)]
        for m in range(slots):
            piece = ref[:, head_columns(pos * slots + (chip ^ m))]
            fulls[m][which] = piece
            if which < 2:
                kvs[m][which] = piece


def near_stats_kernel(k_ref, v_ref, q_ref, u_ref, stats_ref, mid_ref, turn):
    rows = q_ref.shape[0]
    turn[...] = jnp.zeros_like(turn)

    def group_step(group, carry):
        for residue in range(DILATION):
            head = group * DILATION + residue
            cols = head_columns(head)
            e, d = level_stats(q_ref[:, cols], k_ref[:, cols], v_ref[:, cols], u_ref[:, cols])
            turn[pl.ds(head, 1), :] = e
            turn[pl.ds(HEADS + head, 1), :] = d
        return carry

    lax.fori_loop(0, HEADS // DILATION, group_step, 0)
    stats_ref[...] = turn[: 2 * HEADS, :]
    turn[...] = turn[...].T
    mid_ref[...] = pick_rows(turn, rows)


def far_stats_kernel(slots, *refs):
    fulls, kvs, stats_ref = refs[:slots], refs[slots:-1], refs[-1]
    keys = jnp.concatenate([ref[0] for ref in fulls + kvs], axis=0)
    values = jnp.concatenate([ref[1] for ref in fulls + kvs], axis=0)
    for m in range(slots):
        e, d = level_stats(fulls[m][2], keys, values, fulls[m][3])
        stats_ref[m : m + 1, :] = e
        stats_ref[slots + m : slots + m + 1, :] = d


def middle_operands(mids, slot):
    cols = static_columns(slot)
    return [jnp.concatenate([ref[which, :, cols] for ref in mids], axis=0) for which in range(4)]


def middle_stats_kernel(n_i, slots, at_ref, *refs):
    mids, refs = refs[:n_i], refs[n_i:]
    near_ref, nearmid_ref, far_ref = refs[:3]
    refs = refs[3:]
    zmsgs, refs = refs[:n_i], refs[n_i:]
    xmsg_ref, stats_ref, turn, spread = refs
    quarter = nearmid_ref.shape[0]
    pos = at_ref[0]
    turn[...] = jnp.zeros_like(turn)
    for slot in range(slots):
        k, v, q, u = middle_operands(mids, slot)
        e, d = level_stats(q, k, v, u)
        turn[slot : slot + 1, :] = e
        turn[slots + slot : slots + slot + 1, :] = d
    stats_ref[...] = turn[: 2 * slots, :]
    columns = turn[...].T
    lane = lanes_of(quarter)
    for d in range(n_i):
        chunk = pltpu.roll(columns[d * quarter : (d + 1) * quarter], 2 * HEADS, 1)
        zmsgs[d][...] = jnp.where(lane < 2 * HEADS, nearmid_ref[...], chunk)
    own = columns[:quarter]
    lane_residue = (pos * slots + lane % slots) % DILATION
    blank = jnp.where(lane < slots, LOWEST, 0.0)
    for residue in range(DILATION):
        spread[pl.ds(residue, quarter, stride=DILATION), :] = jnp.where(
            lane_residue == residue, own, blank
        )
    across = spread[...].T
    e, d = merge_stats(
        near_ref[pl.ds(pos * slots, slots), :],
        near_ref[pl.ds(HEADS + pos * slots, slots), :],
        across[:slots],
        across[slots : 2 * slots],
    )
    xmsg_ref[:slots] = e
    xmsg_ref[slots : 2 * slots] = d
    xmsg_ref[2 * slots :] = far_ref[...]


def middle_parts_kernel(n_i, slots, at_ref, *refs):
    mids, refs = refs[:n_i], refs[n_i:]
    near_ref, stats_ref = refs[:2]
    refs = refs[2:]
    zmsgs, refs = refs[:n_i], refs[n_i:]
    xmsgs, refs = refs[:slots], refs[slots:]
    outs, refs = refs[:n_i], refs[n_i:]
    final_ref, far, turn, spread = refs
    quarter = zmsgs[0].shape[0]
    rows = quarter * DILATION
    pos, chip = at_ref[0], at_ref[1]

    lane = lanes_of(quarter)
    mid = jnp.zeros((quarter, LANES), F32)
    for d in range(n_i):
        place = (pos ^ d) * slots
        e = pltpu.roll(zmsgs[d][...], (place + LANES - 2 * HEADS) % LANES, 1)
        de = pltpu.roll(zmsgs[d][...], (place + LANES - HEADS - slots) % LANES, 1)
        mid = jnp.where((lane >= place) & (lane < place + slots), e, mid)
        mid = jnp.where((lane >= HEADS + place) & (lane < HEADS + place + slots), de, mid)
    blank = jnp.where(lane < HEADS, LOWEST, 0.0)
    for residue in range(DILATION):
        spread[pl.ds(residue, quarter, stride=DILATION), :] = jnp.where(
            lane % DILATION == residue, mid, blank
        )
    across = spread[...].T
    far[:HEADS] = jnp.full((HEADS, rows), LOWEST, F32)
    far[HEADS:] = jnp.zeros((HEADS, rows), F32)
    for m in range(slots):
        head = pos * slots + (chip ^ m)
        far[pl.ds(head, 1), :] = xmsgs[m][2 * slots + m : 2 * slots + m + 1, :]
        far[pl.ds(HEADS + head, 1), :] = xmsgs[m][3 * slots + m : 3 * slots + m + 1, :]
    e, d = merge_stats(
        near_ref[:HEADS], near_ref[HEADS:], across[:HEADS], across[HEADS : 2 * HEADS]
    )
    e, d = merge_stats(e, d, far[:HEADS], far[HEADS:])
    final_ref[:HEADS] = e
    final_ref[HEADS:] = d

    spread[...] = jnp.zeros_like(spread)
    spread[: 2 * HEADS] = final_ref[...]
    spread[...] = spread[...].T
    own = pick_rows(spread, rows)
    turn[...] = jnp.concatenate([own] + [ref[...] for ref in zmsgs[1:]], axis=0).T
    owned = lax.broadcasted_iota(jnp.int32, (1, n_i * quarter), 1) < quarter
    for slot in range(slots):
        lse, delta = merge_stats(
            turn[pl.ds(pos * slots + slot, 1), :],
            turn[pl.ds(HEADS + pos * slots + slot, 1), :],
            jnp.where(owned, LOWEST, stats_ref[slot : slot + 1, :]),
            stats_ref[slots + slot : slots + slot + 1, :],
        )
        k, v, q, u = middle_operands(mids, slot)
        for which, part in enumerate(level_parts(q, k, v, u, lse, delta)):
            part = part.astype(BF16)
            for d in range(n_i):
                outs[d][which, :, static_columns(slot)] = part[d * quarter : (d + 1) * quarter]


def far_parts_kernel(slots, width, at_ref, *refs):
    others = (width - 1) * slots
    fulls, refs = refs[:slots], refs[slots:]
    kvs, refs = refs[:others], refs[others:]
    xmsgs, refs = refs[:slots], refs[slots:]
    outs, refs = refs[:slots], refs[slots:]
    kvouts, refs = refs[:others], refs[others:]
    weights, score_grads = refs
    rows = fulls[0].shape[1]
    chip = at_ref[1]
    keys = jnp.concatenate([ref[0] for ref in fulls + kvs], axis=0)
    values = jnp.concatenate([ref[1] for ref in fulls + kvs], axis=0)
    for m in range(slots):
        lse, delta = merge_stats(
            xmsgs[m][pl.ds(chip, 1), :],
            xmsgs[m][pl.ds(slots + chip, 1), :],
            xmsgs[0][2 * slots + m : 2 * slots + m + 1, :],
            xmsgs[0][3 * slots + m : 3 * slots + m + 1, :],
        )
        p, ds = level_weights(fulls[m][2], keys, values, fulls[m][3], lse, delta)
        outs[m][0] = dot_tn(p, values).astype(BF16)
        outs[m][1] = (dot_tn(ds, keys) * SCALE).astype(BF16)
        weights[:, m * rows : (m + 1) * rows] = p
        score_grads[:, m * rows : (m + 1) * rows] = ds
    queries = jnp.concatenate([ref[2] for ref in fulls], axis=0)
    ups = jnp.concatenate([ref[3] for ref in fulls], axis=0)
    key_part = (dot(score_grads[...], queries) * SCALE).astype(BF16)
    value_part = dot(weights[...], ups).astype(BF16)
    for index, ref in enumerate(outs + kvouts):
        base = 2 if index < slots else 0
        ref[base] = key_part[index * rows : (index + 1) * rows]
        ref[base + 1] = value_part[index * rows : (index + 1) * rows]


def near_parts_kernel(k_ref, v_ref, q_ref, u_ref, stats_ref, out_ref):
    def group_step(group, carry):
        for residue in range(DILATION):
            head = group * DILATION + residue
            cols = head_columns(head)
            parts = level_parts(
                q_ref[:, cols],
                k_ref[:, cols],
                v_ref[:, cols],
                u_ref[:, cols],
                stats_ref[pl.ds(head, 1), :],
                stats_ref[pl.ds(HEADS + head, 1), :],
            )
            for which, part in enumerate(parts):
                out_ref[which, head] = part
        return carry

    lax.fori_loop(0, HEADS // DILATION, group_step, 0)


def final_kernel(n_i, slots, width, at_ref, near_ref, *refs):
    others = (width - 1) * slots
    mids, refs = refs[:n_i], refs[n_i:]
    fulls, refs = refs[:slots], refs[slots:]
    kvs, outs = refs[:others], refs[others:]
    rows = fulls[0].shape[1]
    quarter = rows // DILATION
    pos, chip = at_ref[0], at_ref[1]
    row = lax.broadcasted_iota(jnp.int32, (rows, quarter), 0)
    taken = lax.broadcasted_iota(jnp.int32, (rows, quarter), 1) * DILATION

    def finish(d, slot, m):
        head = (pos ^ d) * slots + slot
        place = jnp.where(row == taken + head % DILATION, 1.0, 0.0).astype(BF16)
        cols = head_columns(slot) if d == 0 else static_columns(slot)
        for which, out in enumerate(outs):
            total = near_ref[which, head] + dot(place, mids[d][which, :, cols])
            if d == 0:
                total += fulls[m][which].astype(F32)
                if which >= 2:
                    for part in range(width - 1):
                        total += kvs[part * slots + m][which - 2].astype(F32)
            out[:, head_columns(head)] = total.astype(BF16)

    for d in range(1, n_i):
        for slot in range(slots):
            finish(d, slot, None)
    for m in range(slots):
        finish(0, chip ^ m, m)


def call(kernel, name, outs, scratch, flops, operands, at=None):
    specs = [pl.BlockSpec(memory_space=pltpu.VMEM)] * len(operands)
    moved = sum(x.size * x.dtype.itemsize for x in tuple(operands) + tuple(outs))
    if at is not None:
        specs = [pl.BlockSpec(memory_space=pltpu.SMEM)] + specs
        operands = (at,) + tuple(operands)
    return pl.pallas_call(
        kernel,
        out_shape=tuple(outs),
        in_specs=specs,
        out_specs=tuple(pl.BlockSpec(memory_space=pltpu.VMEM) for _ in outs),
        scratch_shapes=scratch,
        compiler_params=pltpu.CompilerParams(vmem_limit_bytes=VMEM_LIMIT),
        cost_estimate=pl.CostEstimate(flops=flops, bytes_accessed=moved, transcendentals=0),
        name=name,
    )(*operands)


def swap(x, axis, n, mask):
    return lax.ppermute(x, axis, [(i, i ^ mask) for i in range(n)])


def local(query_rows, key_rows, value_rows, upstream):
    rows, features = query_rows.shape
    n_i, n_o = lax.axis_size("seqi"), lax.axis_size("seqo")
    slots = HEADS // n_i
    width = n_o // slots
    others = (width - 1) * slots
    quarter = rows // DILATION
    pos = lax.axis_index("seqi").astype(jnp.int32)
    chip = lax.axis_index("seqo").astype(jnp.int32) // width
    at = jnp.stack([pos, chip])
    sources = (key_rows, value_rows, query_rows, upstream)
    unit = 2 * rows * rows * HEAD_DIM
    bind = functools.partial

    mid = SHAPE((4, quarter, slots * HEAD_DIM), BF16)
    full = SHAPE((4, rows, HEAD_DIM), BF16)
    half = SHAPE((2, rows, HEAD_DIM), BF16)
    square = pltpu.VMEM((LANES, rows), F32)

    def stats(count, lanes=rows):
        return SHAPE((count, lanes), F32)

    def swap_mids(pieces):
        return [pieces[0]] + [swap(pieces[d], "seqi", n_i, d) for d in range(1, n_i)]

    def swap_fulls(pieces):
        return [pieces[0]] + [swap(pieces[m], "seqo", n_o, m * width) for m in range(1, slots)]

    def swap_halves(pieces):
        return [
            swap(pieces[(part - 1) * slots + m], "seqo", n_o, m * width + part)
            for part in range(1, width)
            for m in range(slots)
        ]

    pieces = call(
        bind(pick_kernel, n_i, slots),
        "pick",
        [mid] * n_i + [full] * slots + [half] * slots,
        [pltpu.VMEM((HEADS, rows, HEAD_DIM), F32), pltpu.VMEM((quarter, features), BF16)],
        unit,
        sources,
        at,
    )
    mids = swap_mids(pieces[:n_i])
    fulls = swap_fulls(pieces[n_i : n_i + slots])
    kvs = swap_halves(list(pieces[n_i + slots :]) * (width - 1))

    near, nearmid = call(
        near_stats_kernel,
        "near_stats",
        [stats(2 * HEADS), SHAPE((quarter, LANES), F32)],
        [square],
        unit * HEADS * 2,
        sources,
    )
    (far,) = call(
        bind(far_stats_kernel, slots),
        "far_stats",
        [stats(2 * slots)],
        [],
        unit * n_o * slots * 2,
        fulls + kvs,
    )
    *zmsgs, xmsg, middle = call(
        bind(middle_stats_kernel, n_i, slots),
        "middle_stats",
        [SHAPE((quarter, LANES), F32)] * n_i
        + [stats(4 * slots), stats(2 * slots, n_i * quarter)],
        [pltpu.VMEM((LANES, n_i * quarter), F32), square],
        unit * slots * 2,
        mids + [near, nearmid, far],
        at,
    )
    zmsgs = swap_mids(zmsgs)
    xmsgs = swap_fulls([xmsg] * slots)

    *midparts, final = call(
        bind(middle_parts_kernel, n_i, slots),
        "middle_parts",
        [mid] * n_i + [stats(2 * HEADS)],
        [
            pltpu.VMEM((2 * HEADS, rows), F32),
            pltpu.VMEM((LANES, n_i * quarter), F32),
            square,
        ],
        unit * slots * 6,
        mids + [near, middle] + zmsgs + xmsgs,
        at,
    )
    midparts = swap_mids(midparts)
    farparts = call(
        bind(far_parts_kernel, slots, width),
        "far_parts",
        [full] * slots + [half] * others,
        [pltpu.VMEM((n_o * rows, slots * rows), BF16)] * 2,
        unit * n_o * slots * 6,
        fulls + kvs + xmsgs,
        at,
    )
    fullparts = swap_fulls(farparts[:slots])
    halfparts = swap_halves(farparts[slots:])

    (nearparts,) = call(
        near_parts_kernel,
        "near_parts",
        [SHAPE((4, HEADS, rows, HEAD_DIM), F32)],
        [],
        unit * HEADS * 6,
        sources + (final,),
    )
    return call(
        bind(final_kernel, n_i, slots, width),
        "final",
        [SHAPE((rows, features), BF16)] * 4,
        [],
        unit * HEADS,
        [nearparts] + midparts + fullparts + halfparts,
        at,
    )


def solution(mesh):
    rows = P(("seqo", "seqi"), None)
    return jax.shard_map(
        local,
        mesh=mesh,
        in_specs=(rows,) * 4,
        out_specs=(rows,) * 4,
        check_vma=False,
    )
```

```python
import functools

import jax
import jax.numpy as jnp
from jax import lax
from jax.experimental import pallas as pl
from jax.experimental.pallas import tpu as pltpu
from jax.sharding import PartitionSpec as P

HEADS = 16
HEAD_DIM = 128
DILATION = 4
LANES = 128
SCALE = HEAD_DIM**-0.5
LOWEST = -1e30
VMEM_LIMIT = 32 * 1024 * 1024
F32, BF16 = jnp.float32, jnp.bfloat16
SHAPE = jax.ShapeDtypeStruct

NT = (((1,), (1,)), ((), ()))
TN = (((0,), (0,)), ((), ()))


def dot(a, b):
    return jnp.dot(a, b, preferred_element_type=F32)


def dot_nt(a, b):
    return lax.dot_general(a, b, NT, preferred_element_type=F32)


def dot_tn(a, b):
    return lax.dot_general(a, b, TN, preferred_element_type=F32)


def head_columns(head):
    return pl.ds(pl.multiple_of(head * HEAD_DIM, HEAD_DIM), HEAD_DIM)


def static_columns(index):
    return slice(index * HEAD_DIM, (index + 1) * HEAD_DIM)


def lanes_of(rows):
    return lax.broadcasted_iota(jnp.int32, (rows, LANES), 1)


def level_stats(q, k, v, u):
    s = dot_nt(k, q) * SCALE
    dp = dot_nt(v, u)
    top = jnp.max(s, axis=0, keepdims=True)
    p = jnp.exp(s - top)
    total = jnp.sum(p, axis=0, keepdims=True)
    return top + jnp.log(total), jnp.sum(p * dp, axis=0, keepdims=True) / total


def merge_stats(ea, da, eb, db):
    top = jnp.maximum(ea, eb)
    wa, wb = jnp.exp(ea - top), jnp.exp(eb - top)
    total = wa + wb
    return top + jnp.log(total), (wa * da + wb * db) / total


def level_weights(q, k, v, u, lse, delta):
    g = jnp.exp(dot_nt(k, q) * SCALE - lse)
    return g.astype(BF16), (g * (dot_nt(v, u) - delta)).astype(BF16)


def level_parts(q, k, v, u, lse, delta):
    p, ds = level_weights(q, k, v, u, lse, delta)
    return dot_tn(p, v), dot_tn(ds, k) * SCALE, dot(ds, q) * SCALE, dot(p, u)


def pick_rows(ref, rows):
    quarter = rows // DILATION
    lane = lanes_of(quarter)
    picked = jnp.zeros((quarter, LANES), F32)
    for residue in range(DILATION):
        part = ref[pl.ds(residue, quarter, stride=DILATION), :]
        picked = jnp.where(lane % DILATION == residue, part, picked)
    return picked


def fetch(sources, buffers, sems):
    width = DILATION * HEAD_DIM
    groups = []
    for group in range(HEADS // DILATION):
        cols = pl.ds(group * width, width)
        groups.append(
            [
                pltpu.make_async_copy(
                    source.at[:, cols], buffers.at[which, :, cols], sems.at[which, group]
                )
                for which, source in enumerate(sources)
            ]
        )
        for copy in groups[-1]:
            copy.start()
    return groups


def pick_kernel(n_i, n_o, slots, at_ref, *refs):
    sources, (mid_ref, far_ref, buffers, sems, wide) = refs[:4], refs[4:]
    rows = sources[0].shape[0]
    quarter = rows // DILATION
    width = n_o // slots
    pos = at_ref[0]
    for group, copies in enumerate(fetch(sources, buffers, sems)):
        for which, copy in enumerate(copies):
            copy.wait()
            for residue in range(DILATION):
                head = group * DILATION + residue
                place, slot = head // slots, head % slots
                wide[which, head] = buffers[which, :, static_columns(head)].astype(F32)
                picked = wide[which, head, pl.ds(residue, quarter, stride=DILATION), :]
                mid_ref[place, which, :, static_columns(slot)] = picked.astype(BF16)
    for slot in range(slots):
        for which in range(4):
            piece = buffers[which, :, head_columns(pos * slots + slot)]
            for core in range(width):
                far_ref[slot * width + core, which] = piece


def near_stats_kernel(k_hbm, v_hbm, q_hbm, u_hbm, stats_ref, mid_ref, buffers, sems, turn):
    rows = q_hbm.shape[0]
    turn[...] = jnp.zeros_like(turn)
    for group, copies in enumerate(fetch((k_hbm, v_hbm, q_hbm, u_hbm), buffers, sems)):
        for copy in copies:
            copy.wait()
        for residue in range(DILATION):
            head = group * DILATION + residue
            k, v, q, u = [buffers[which, :, static_columns(head)] for which in range(4)]
            e, d = level_stats(q, k, v, u)
            turn[head : head + 1, :] = e
            turn[HEADS + head : HEADS + head + 1, :] = d
    stats_ref[...] = turn[: 2 * HEADS, :]
    turn[...] = turn[...].T
    mid_ref[...] = pick_rows(turn, rows)


def stacked(ref, which, first=0, step=1):
    return jnp.concatenate(
        [ref[first + step * i, which] for i in range(ref.shape[0] // step)], axis=0
    )


def far_stats_kernel(slots, width, at_ref, far_ref, stats_ref):
    core = at_ref[2]
    keys, values = stacked(far_ref, 0), stacked(far_ref, 1)
    for m in range(slots):
        source = m * width + core
        e, d = level_stats(far_ref[source, 2], keys, values, far_ref[source, 3])
        stats_ref[m : m + 1, :] = e
        stats_ref[slots + m : slots + m + 1, :] = d


def middle_operands(mid_ref, slot):
    cols = static_columns(slot)
    return [
        jnp.concatenate([mid_ref[i, which, :, cols] for i in range(mid_ref.shape[0])], axis=0)
        for which in range(4)
    ]


def middle_stats_kernel(n_i, n_o, slots, at_ref, *refs):
    mid_ref, near_ref, nearmid_ref, far_ref, zmsg_ref, xmsg_ref, stats_ref, turn, spread = refs
    quarter = nearmid_ref.shape[0]
    pos = at_ref[0]
    turn[...] = jnp.zeros_like(turn)
    for slot in range(slots):
        k, v, q, u = middle_operands(mid_ref, slot)
        e, d = level_stats(q, k, v, u)
        turn[slot : slot + 1, :] = e
        turn[slots + slot : slots + slot + 1, :] = d
    stats_ref[...] = turn[: 2 * slots, :]
    columns = turn[...].T
    lane = lanes_of(quarter)
    for i in range(n_i):
        chunk = pltpu.roll(columns[i * quarter : (i + 1) * quarter], 2 * HEADS, 1)
        zmsg_ref[i] = jnp.where(lane < 2 * HEADS, nearmid_ref[...], chunk)
    own = pltpu.roll(zmsg_ref[pos], LANES - 2 * HEADS, 1)
    lane_residue = (pos * slots + lane % slots) % DILATION
    blank = jnp.where(lane < slots, LOWEST, 0.0)
    for residue in range(DILATION):
        spread[pl.ds(residue, quarter, stride=DILATION), :] = jnp.where(
            lane_residue == residue, own, blank
        )
    across = spread[...].T
    e, d = merge_stats(
        near_ref[pl.ds(pos * slots, slots), :],
        near_ref[pl.ds(HEADS + pos * slots, slots), :],
        across[:slots],
        across[slots : 2 * slots],
    )
    for o in range(n_o):
        xmsg_ref[o, :slots] = e
        xmsg_ref[o, slots : 2 * slots] = d
        xmsg_ref[o, 2 * slots :] = far_ref[...]


def middle_parts_kernel(n_i, slots, width, at_ref, *refs):
    mid_ref, near_ref, stats_ref, zmsg_ref, xmsg_ref, out_ref, final_ref, far, turn, spread = refs
    quarter = zmsg_ref.shape[1]
    rows = quarter * DILATION
    pos, chip, core = at_ref[0], at_ref[1], at_ref[2]

    lane = lanes_of(quarter)
    mid = jnp.zeros((quarter, LANES), F32)
    for i in range(n_i):
        place = i * slots
        e = pltpu.roll(zmsg_ref[i], (place + LANES - 2 * HEADS) % LANES, 1)
        de = pltpu.roll(zmsg_ref[i], (place + LANES - HEADS - slots) % LANES, 1)
        mid = jnp.where((lane >= place) & (lane < place + slots), e, mid)
        mid = jnp.where((lane >= HEADS + place) & (lane < HEADS + place + slots), de, mid)
    blank = jnp.where(lane < HEADS, LOWEST, 0.0)
    for residue in range(DILATION):
        spread[pl.ds(residue, quarter, stride=DILATION), :] = jnp.where(
            lane % DILATION == residue, mid, blank
        )
    across = spread[...].T
    far[:HEADS] = jnp.full((HEADS, rows), LOWEST, F32)
    far[HEADS:] = jnp.zeros((HEADS, rows), F32)
    for m in range(slots):
        head = pos * slots + m
        source = m * width + core
        far[pl.ds(head, 1), :] = xmsg_ref[source, pl.ds(2 * slots + chip, 1), :]
        far[pl.ds(HEADS + head, 1), :] = xmsg_ref[source, pl.ds(3 * slots + chip, 1), :]
    e, d = merge_stats(
        near_ref[:HEADS], near_ref[HEADS:], across[:HEADS], across[HEADS : 2 * HEADS]
    )
    e, d = merge_stats(e, d, far[:HEADS], far[HEADS:])
    final_ref[:HEADS] = e
    final_ref[HEADS:] = d

    spread[...] = jnp.zeros_like(spread)
    spread[: 2 * HEADS] = final_ref[...]
    spread[...] = spread[...].T
    own = pick_rows(spread, rows)
    turn[...] = jnp.concatenate(
        [jnp.where(pos == i, own, zmsg_ref[i]) for i in range(n_i)], axis=0
    ).T
    owned = lax.broadcasted_iota(jnp.int32, (1, n_i * quarter), 1) // quarter == pos
    for slot in range(slots):
        lse, delta = merge_stats(
            turn[pl.ds(pos * slots + slot, 1), :],
            turn[pl.ds(HEADS + pos * slots + slot, 1), :],
            jnp.where(owned, LOWEST, stats_ref[slot : slot + 1, :]),
            stats_ref[slots + slot : slots + slot + 1, :],
        )
        k, v, q, u = middle_operands(mid_ref, slot)
        for which, part in enumerate(level_parts(q, k, v, u, lse, delta)):
            part = part.astype(BF16)
            for i in range(n_i):
                out_ref[i, which, :, static_columns(slot)] = part[i * quarter : (i + 1) * quarter]


def far_parts_kernel(slots, width, at_ref, far_ref, xmsg_ref, out_ref, weights, score_grads):
    rows = far_ref.shape[2]
    chip, core = at_ref[1], at_ref[2]
    own = chip * width + core
    keys, values = stacked(far_ref, 0), stacked(far_ref, 1)
    for m in range(slots):
        source = m * width + core
        lse, delta = merge_stats(
            xmsg_ref[source, pl.ds(chip, 1), :],
            xmsg_ref[source, pl.ds(slots + chip, 1), :],
            xmsg_ref[own, 2 * slots + m : 2 * slots + m + 1, :],
            xmsg_ref[own, 3 * slots + m : 3 * slots + m + 1, :],
        )
        p, ds = level_weights(far_ref[source, 2], keys, values, far_ref[source, 3], lse, delta)
        share = dot_tn(p, values).astype(BF16)
        query_part = (dot_tn(ds, keys) * SCALE).astype(BF16)
        for other in range(width):
            out_ref[m * width + other, 0] = share
            out_ref[m * width + other, 1] = query_part
        weights[:, m * rows : (m + 1) * rows] = p
        score_grads[:, m * rows : (m + 1) * rows] = ds
    queries = jnp.concatenate([far_ref[m * width + core, 2] for m in range(slots)], axis=0)
    ups = jnp.concatenate([far_ref[m * width + core, 3] for m in range(slots)], axis=0)
    key_part = (dot(score_grads[...], queries) * SCALE).astype(BF16)
    value_part = dot(weights[...], ups).astype(BF16)
    for index in range(slots * width):
        out_ref[index, 2] = key_part[index * rows : (index + 1) * rows]
        out_ref[index, 3] = value_part[index * rows : (index + 1) * rows]


def near_parts_kernel(k_hbm, v_hbm, q_hbm, u_hbm, stats_ref, out_ref, buffers, sems):
    for group, copies in enumerate(fetch((k_hbm, v_hbm, q_hbm, u_hbm), buffers, sems)):
        for copy in copies:
            copy.wait()
        for residue in range(DILATION):
            head = group * DILATION + residue
            k, v, q, u = [buffers[which, :, static_columns(head)] for which in range(4)]
            lse = stats_ref[head : head + 1, :]
            delta = stats_ref[HEADS + head : HEADS + head + 1, :]
            for which, part in enumerate(level_parts(q, k, v, u, lse, delta)):
                out_ref[which, head] = part


def final_kernel(n_i, slots, width, at_ref, near_ref, mid_ref, far_ref, *outs):
    rows = far_ref.shape[2]
    quarter = rows // DILATION
    pos, core = at_ref[0], at_ref[2]
    row = lax.broadcasted_iota(jnp.int32, (rows, quarter), 0)
    taken = lax.broadcasted_iota(jnp.int32, (rows, quarter), 1) * DILATION

    def finish(place, slot, is_own):
        head = place * slots + slot
        spread = jnp.where(row == taken + head % DILATION, 1.0, 0.0).astype(BF16)
        for which, out in enumerate(outs):
            total = near_ref[which, head] + dot(spread, mid_ref[place, which, :, static_columns(slot)])
            if is_own:
                for other in range(1 if which < 2 else width):
                    source = slot * width + (core ^ other)
                    total += far_ref[source, which].astype(F32)
            out[:, head_columns(head)] = total.astype(BF16)

    for step in range(n_i):
        for slot in range(slots):
            finish((pos + step) % n_i, slot, step == 0)


def call(kernel, name, outs, scratch, flops, operands, at=None, in_hbm=0):
    specs = [pl.BlockSpec(memory_space=pl.ANY if i < in_hbm else pltpu.VMEM) for i in range(len(operands))]
    moved = sum(x.size * x.dtype.itemsize for x in tuple(operands) + tuple(outs))
    if at is not None:
        specs = [pl.BlockSpec(memory_space=pltpu.SMEM)] + specs
        operands = (at,) + tuple(operands)
    return pl.pallas_call(
        kernel,
        out_shape=tuple(outs),
        in_specs=specs,
        out_specs=tuple(pl.BlockSpec(memory_space=pltpu.VMEM) for _ in outs),
        scratch_shapes=scratch,
        compiler_params=pltpu.CompilerParams(vmem_limit_bytes=VMEM_LIMIT),
        cost_estimate=pl.CostEstimate(flops=flops, bytes_accessed=moved, transcendentals=0),
        name=name,
    )(*operands)


def exchange(x, axis):
    return lax.all_to_all(x, axis, 0, 0, tiled=True)


def local(query_rows, key_rows, value_rows, upstream):
    rows, features = query_rows.shape
    n_i, n_o = lax.axis_size("seqi"), lax.axis_size("seqo")
    slots = HEADS // n_i
    width = n_o // slots
    quarter = rows // DILATION
    pos = lax.axis_index("seqi").astype(jnp.int32)
    block = lax.axis_index("seqo").astype(jnp.int32)
    at = jnp.stack([pos, block // width, block % width])
    sources = (key_rows, value_rows, query_rows, upstream)
    unit = 2 * rows * rows * HEAD_DIM
    bind = functools.partial

    mid = SHAPE((n_i, 4, quarter, slots * HEAD_DIM), BF16)
    far = SHAPE((n_o, 4, rows, HEAD_DIM), BF16)
    square = pltpu.VMEM((LANES, rows), F32)
    buffers = [pltpu.VMEM((4, rows, features), BF16), pltpu.SemaphoreType.DMA((4, HEADS // DILATION))]

    def stats(*shape):
        return SHAPE(shape, F32)

    mids, fars = call(
        bind(pick_kernel, n_i, n_o, slots),
        "pick",
        [mid, far],
        buffers + [pltpu.VMEM((4, HEADS, rows, HEAD_DIM), F32)],
        unit,
        sources,
        at,
        in_hbm=4,
    )
    mids = exchange(mids, "seqi")
    fars = exchange(fars, "seqo")

    near, nearmid = call(
        near_stats_kernel,
        "near_stats",
        [stats(2 * HEADS, rows), stats(quarter, LANES)],
        buffers + [square],
        unit * HEADS * 2,
        sources,
        in_hbm=4,
    )
    (farstats,) = call(
        bind(far_stats_kernel, slots, width),
        "far_stats",
        [stats(2 * slots, rows)],
        [],
        unit * n_o * slots * 2,
        [fars],
        at,
    )
    zmsg, xmsg, middle = call(
        bind(middle_stats_kernel, n_i, n_o, slots),
        "middle_stats",
        [stats(n_i, quarter, LANES), stats(n_o, 4 * slots, rows), stats(2 * slots, n_i * quarter)],
        [pltpu.VMEM((LANES, n_i * quarter), F32), square],
        unit * slots * 2,
        [mids, near, nearmid, farstats],
        at,
    )
    zmsg = exchange(zmsg, "seqi")
    xmsg = exchange(xmsg, "seqo")

    midparts, final = call(
        bind(middle_parts_kernel, n_i, slots, width),
        "middle_parts",
        [mid, stats(2 * HEADS, rows)],
        [
            pltpu.VMEM((2 * HEADS, rows), F32),
            pltpu.VMEM((LANES, n_i * quarter), F32),
            square,
        ],
        unit * slots * 6,
        [mids, near, middle, zmsg, xmsg],
        at,
    )
    midparts = exchange(midparts, "seqi")
    (farparts,) = call(
        bind(far_parts_kernel, slots, width),
        "far_parts",
        [far],
        [pltpu.VMEM((n_o * rows, slots * rows), BF16)] * 2,
        unit * n_o * slots * 6,
        [fars, xmsg],
        at,
    )
    farparts = exchange(farparts, "seqo")

    (nearparts,) = call(
        near_parts_kernel,
        "near_parts",
        [stats(4, HEADS, rows, HEAD_DIM)],
        buffers,
        unit * HEADS * 6,
        sources + (final,),
        in_hbm=4,
    )
    return call(
        bind(final_kernel, n_i, slots, width),
        "final",
        [SHAPE((rows, features), BF16)] * 4,
        [],
        unit * HEADS,
        [nearparts, midparts, farparts],
        at,
    )


def solution(mesh):
    rows = P(("seqo", "seqi"), None)
    return jax.shard_map(
        local,
        mesh=mesh,
        in_specs=(rows,) * 4,
        out_specs=(rows,) * 4,
        check_vma=False,
    )
```

```python
import functools

import jax
import jax.numpy as jnp
from jax import lax
from jax.experimental import pallas as pl
from jax.experimental.pallas import tpu as pltpu
from jax.sharding import PartitionSpec as P

HEADS = 16
HEAD_DIM = 128
DILATION = 4
LANES = 128
SCALE = HEAD_DIM**-0.5
LOWEST = -1e30
VMEM_LIMIT = 32 * 1024 * 1024
VMEM_ALL = 60 * 1024 * 1024
F32, BF16 = jnp.float32, jnp.bfloat16
SHAPE = jax.ShapeDtypeStruct

NT = (((1,), (1,)), ((), ()))
TN = (((0,), (0,)), ((), ()))


def dot(a, b):
    return jnp.dot(a, b, preferred_element_type=F32)


def dot_nt(a, b):
    return lax.dot_general(a, b, NT, preferred_element_type=F32)


def dot_tn(a, b):
    return lax.dot_general(a, b, TN, preferred_element_type=F32)


def head_columns(head):
    return pl.ds(pl.multiple_of(head * HEAD_DIM, HEAD_DIM), HEAD_DIM)


def static_columns(index):
    return slice(index * HEAD_DIM, (index + 1) * HEAD_DIM)


def lanes_of(rows):
    return lax.broadcasted_iota(jnp.int32, (rows, LANES), 1)


def level_stats(q, k, v, u):
    s = dot_nt(k, q) * SCALE
    dp = dot_nt(v, u)
    top = jnp.max(s, axis=0, keepdims=True)
    p = jnp.exp(s - top)
    total = jnp.sum(p, axis=0, keepdims=True)
    return top + jnp.log(total), jnp.sum(p * dp, axis=0, keepdims=True) / total


def merge_stats(ea, da, eb, db):
    top = jnp.maximum(ea, eb)
    wa, wb = jnp.exp(ea - top), jnp.exp(eb - top)
    total = wa + wb
    return top + jnp.log(total), (wa * da + wb * db) / total


def level_weights(q, k, v, u, lse, delta):
    g = jnp.exp(dot_nt(k, q) * SCALE - lse)
    return g.astype(BF16), (g * (dot_nt(v, u) - delta)).astype(BF16)


def level_parts(q, k, v, u, lse, delta):
    p, ds = level_weights(q, k, v, u, lse, delta)
    return dot_tn(p, v), dot_tn(ds, k) * SCALE, dot(ds, q) * SCALE, dot(p, u)


def pick_rows(ref, rows):
    quarter = rows // DILATION
    lane = lanes_of(quarter)
    picked = jnp.zeros((quarter, LANES), F32)
    for residue in range(DILATION):
        part = ref[pl.ds(residue, quarter, stride=DILATION), :]
        picked = jnp.where(lane % DILATION == residue, part, picked)
    return picked


def fetch(sources, buffers, sems):
    width = DILATION * HEAD_DIM
    groups = []
    for group in range(HEADS // DILATION):
        cols = pl.ds(group * width, width)
        groups.append(
            [
                pltpu.make_async_copy(
                    source.at[:, cols], buffers.at[which, :, cols], sems.at[which, group]
                )
                for which, source in enumerate(sources)
            ]
        )
        for copy in groups[-1]:
            copy.start()
    return groups


def pick_kernel(n_i, slots, at_ref, *refs):
    sources, refs = refs[:4], refs[4:]
    mids, refs = refs[:n_i], refs[n_i:]
    fulls, refs = refs[:slots], refs[slots:]
    buffers, sems, wide, picked = refs
    rows = sources[0].shape[0]
    quarter = rows // DILATION
    pos, chip = at_ref[0], at_ref[1]
    for group, copies in enumerate(fetch(sources, buffers, sems)):
        for which, copy in enumerate(copies):
            copy.wait()
            for residue in range(DILATION):
                head = group * DILATION + residue
                cols = static_columns(head)
                wide[which, head] = buffers[which, :, cols].astype(F32)
                rowset = wide[which, head, pl.ds(residue, quarter, stride=DILATION), :]
                picked[which, :, cols] = rowset.astype(BF16)
    width = slots * HEAD_DIM
    for d in range(n_i):
        start = pl.multiple_of((pos ^ d) * width, width)
        mids[d][...] = picked[:, :, pl.ds(start, width)]
    for m in range(slots):
        fulls[m][...] = buffers[:, :, head_columns(pos * slots + (chip ^ m))]


def near_stats_kernel(k_hbm, v_hbm, q_hbm, u_hbm, stats_ref, mid_ref, buffers, sems, turn):
    rows = q_hbm.shape[0]
    turn[...] = jnp.zeros_like(turn)
    for group, copies in enumerate(fetch((k_hbm, v_hbm, q_hbm, u_hbm), buffers, sems)):
        for copy in copies:
            copy.wait()
        for residue in range(DILATION):
            head = group * DILATION + residue
            k, v, q, u = [buffers[which, :, static_columns(head)] for which in range(4)]
            e, d = level_stats(q, k, v, u)
            turn[head : head + 1, :] = e
            turn[HEADS + head : HEADS + head + 1, :] = d
    stats_ref[...] = turn[: 2 * HEADS, :]
    turn[...] = turn[...].T
    mid_ref[...] = pick_rows(turn, rows)


def far_stats_kernel(slots, near_ref, *refs):
    fulls, sibs, xmsg_ref = refs[:slots], refs[slots:-1], refs[-1]
    keys = jnp.concatenate([ref[0] for ref in fulls + sibs], axis=0)
    values = jnp.concatenate([ref[1] for ref in fulls + sibs], axis=0)
    xmsg_ref[: 2 * slots] = near_ref[...]
    for m in range(slots):
        e, d = level_stats(fulls[m][2], keys, values, fulls[m][3])
        xmsg_ref[2 * slots + m : 2 * slots + m + 1, :] = e
        xmsg_ref[3 * slots + m : 3 * slots + m + 1, :] = d


def middle_operands(mids, slot):
    cols = static_columns(slot)
    return [jnp.concatenate([ref[which, :, cols] for ref in mids], axis=0) for which in range(4)]


def middle_stats_kernel(n_i, slots, at_ref, *refs):
    mids, refs = refs[:n_i], refs[n_i:]
    near_ref, nearmid_ref = refs[:2]
    refs = refs[2:]
    zmsgs, refs = refs[:n_i], refs[n_i:]
    joint_ref, stats_ref, turn, spread = refs
    quarter = nearmid_ref.shape[0]
    pos = at_ref[0]
    turn[...] = jnp.zeros_like(turn)
    for slot in range(slots):
        k, v, q, u = middle_operands(mids, slot)
        e, d = level_stats(q, k, v, u)
        turn[slot : slot + 1, :] = e
        turn[slots + slot : slots + slot + 1, :] = d
    stats_ref[...] = turn[: 2 * slots, :]
    columns = turn[...].T
    lane = lanes_of(quarter)
    for d in range(n_i):
        chunk = pltpu.roll(columns[d * quarter : (d + 1) * quarter], 2 * HEADS, 1)
        zmsgs[d][...] = jnp.where(lane < 2 * HEADS, nearmid_ref[...], chunk)
    own = columns[:quarter]
    lane_residue = (pos * slots + lane % slots) % DILATION
    blank = jnp.where(lane < slots, LOWEST, 0.0)
    for residue in range(DILATION):
        spread[pl.ds(residue, quarter, stride=DILATION), :] = jnp.where(
            lane_residue == residue, own, blank
        )
    across = spread[...].T
    e, d = merge_stats(
        near_ref[pl.ds(pos * slots, slots), :],
        near_ref[pl.ds(HEADS + pos * slots, slots), :],
        across[:slots],
        across[slots : 2 * slots],
    )
    joint_ref[:slots] = e
    joint_ref[slots:] = d


def middle_parts_kernel(n_i, slots, at_ref, *refs):
    mids, refs = refs[:n_i], refs[n_i:]
    near_ref, stats_ref = refs[:2]
    refs = refs[2:]
    zmsgs, refs = refs[:n_i], refs[n_i:]
    xmsgs, refs = refs[:slots], refs[slots:]
    outs, refs = refs[:n_i], refs[n_i:]
    final_ref, far, turn, spread = refs
    quarter = zmsgs[0].shape[0]
    rows = quarter * DILATION
    pos, chip = at_ref[0], at_ref[1]

    lane = lanes_of(quarter)
    mid = jnp.zeros((quarter, LANES), F32)
    for d in range(n_i):
        place = (pos ^ d) * slots
        e = pltpu.roll(zmsgs[d][...], (place + LANES - 2 * HEADS) % LANES, 1)
        de = pltpu.roll(zmsgs[d][...], (place + LANES - HEADS - slots) % LANES, 1)
        mid = jnp.where((lane >= place) & (lane < place + slots), e, mid)
        mid = jnp.where((lane >= HEADS + place) & (lane < HEADS + place + slots), de, mid)
    blank = jnp.where(lane < HEADS, LOWEST, 0.0)
    for residue in range(DILATION):
        spread[pl.ds(residue, quarter, stride=DILATION), :] = jnp.where(
            lane % DILATION == residue, mid, blank
        )
    across = spread[...].T
    far[:HEADS] = jnp.full((HEADS, rows), LOWEST, F32)
    far[HEADS:] = jnp.zeros((HEADS, rows), F32)
    for m in range(slots):
        head = pos * slots + (chip ^ m)
        far[pl.ds(head, 1), :] = xmsgs[m][2 * slots + m : 2 * slots + m + 1, :]
        far[pl.ds(HEADS + head, 1), :] = xmsgs[m][3 * slots + m : 3 * slots + m + 1, :]
    e, d = merge_stats(
        near_ref[:HEADS], near_ref[HEADS:], across[:HEADS], across[HEADS : 2 * HEADS]
    )
    e, d = merge_stats(e, d, far[:HEADS], far[HEADS:])
    final_ref[:HEADS] = e
    final_ref[HEADS:] = d

    spread[...] = jnp.zeros_like(spread)
    spread[: 2 * HEADS] = final_ref[...]
    spread[...] = spread[...].T
    own = pick_rows(spread, rows)
    turn[...] = jnp.concatenate([own] + [ref[...] for ref in zmsgs[1:]], axis=0).T
    owned = lax.broadcasted_iota(jnp.int32, (1, n_i * quarter), 1) < quarter
    for slot in range(slots):
        lse, delta = merge_stats(
            turn[pl.ds(pos * slots + slot, 1), :],
            turn[pl.ds(HEADS + pos * slots + slot, 1), :],
            jnp.where(owned, LOWEST, stats_ref[slot : slot + 1, :]),
            stats_ref[slots + slot : slots + slot + 1, :],
        )
        k, v, q, u = middle_operands(mids, slot)
        for which, part in enumerate(level_parts(q, k, v, u, lse, delta)):
            part = part.astype(BF16)
            for d in range(n_i):
                outs[d][which, :, static_columns(slot)] = part[d * quarter : (d + 1) * quarter]


def far_parts_kernel(slots, width, at_ref, *refs):
    others = (width - 1) * slots
    fulls, refs = refs[:slots], refs[slots:]
    kvs, refs = refs[:others], refs[others:]
    xmsgs, refs = refs[:slots], refs[slots:]
    final_ref, refs = refs[0], refs[1:]
    outs, refs = refs[:slots], refs[slots:]
    kvouts, refs = refs[: width - 1], refs[width - 1 :]
    weights, score_grads = refs
    rows = fulls[0].shape[1]
    pos, chip = at_ref[0], at_ref[1]
    head = pos * slots + chip
    keys = jnp.concatenate([ref[0] for ref in fulls + kvs], axis=0)
    values = jnp.concatenate([ref[1] for ref in fulls + kvs], axis=0)
    for m in range(slots):
        if m == 0:
            lse, delta = final_ref[pl.ds(head, 1), :], final_ref[pl.ds(HEADS + head, 1), :]
        else:
            lse, delta = merge_stats(
                xmsgs[m][pl.ds(chip, 1), :],
                xmsgs[m][pl.ds(slots + chip, 1), :],
                xmsgs[0][2 * slots + m : 2 * slots + m + 1, :],
                xmsgs[0][3 * slots + m : 3 * slots + m + 1, :],
            )
        p, ds = level_weights(fulls[m][2], keys, values, fulls[m][3], lse, delta)
        outs[m][0] = dot_tn(p, values).astype(BF16)
        outs[m][1] = (dot_tn(ds, keys) * SCALE).astype(BF16)
        weights[:, m * rows : (m + 1) * rows] = p
        score_grads[:, m * rows : (m + 1) * rows] = ds
    queries = jnp.concatenate([ref[2] for ref in fulls], axis=0)
    ups = jnp.concatenate([ref[3] for ref in fulls], axis=0)
    key_part = (dot(score_grads[...], queries) * SCALE).astype(BF16)
    value_part = dot(weights[...], ups).astype(BF16)
    for index in range(width * slots):
        block = slice(index * rows, (index + 1) * rows)
        part, m = index // slots, index % slots
        if part == 0:
            outs[m][2], outs[m][3] = key_part[block], value_part[block]
        else:
            kvouts[part - 1][m, 0], kvouts[part - 1][m, 1] = key_part[block], value_part[block]


def far_sum_kernel(slots, *refs):
    own, refs = refs[:slots], refs[slots:]
    found, outs = refs[:-slots], refs[-slots:]
    for m in range(slots):
        outs[m][:2] = own[m][:2]
        total = own[m][2:].astype(F32)
        for ref in found:
            total += ref[m].astype(F32)
        outs[m][2:] = total.astype(BF16)


def near_parts_kernel(k_ref, v_ref, q_ref, u_ref, stats_ref, out_ref):
    def group_step(group, carry):
        for residue in range(DILATION):
            head = group * DILATION + residue
            cols = head_columns(head)
            parts = level_parts(
                q_ref[:, cols],
                k_ref[:, cols],
                v_ref[:, cols],
                u_ref[:, cols],
                stats_ref[pl.ds(head, 1), :],
                stats_ref[pl.ds(HEADS + head, 1), :],
            )
            for which, part in enumerate(parts):
                out_ref[which, head] = part
        return carry

    lax.fori_loop(0, HEADS // DILATION, group_step, 0)


def final_kernel(n_i, slots, at_ref, near_ref, *refs):
    mids, refs = refs[:n_i], refs[n_i:]
    fulls, outs = refs[:slots], refs[slots:]
    rows = fulls[0].shape[1]
    quarter = rows // DILATION
    pos, chip = at_ref[0], at_ref[1]
    row = lax.broadcasted_iota(jnp.int32, (rows, quarter), 0)
    taken = lax.broadcasted_iota(jnp.int32, (rows, quarter), 1) * DILATION

    def finish(d, slot, m):
        head = (pos ^ d) * slots + slot
        place = jnp.where(row == taken + head % DILATION, 1.0, 0.0).astype(BF16)
        cols = head_columns(slot) if d == 0 else static_columns(slot)
        for which, out in enumerate(outs):
            total = near_ref[which, head] + dot(place, mids[d][which, :, cols])
            if d == 0:
                total += fulls[m][which].astype(F32)
            out[:, head_columns(head)] = total.astype(BF16)

    for d in range(1, n_i):
        for slot in range(slots):
            finish(d, slot, None)
    for m in range(slots):
        finish(0, chip ^ m, m)


def call(kernel, name, outs, scratch, flops, operands, at=None, in_hbm=0, limit=VMEM_LIMIT, cheap=False):
    spaces = [pl.ANY if i < in_hbm else pltpu.VMEM for i in range(len(operands))]
    moved = sum(x.size * x.dtype.itemsize for x in tuple(operands) + tuple(outs))
    if cheap:
        flops, moved = 1, 1
    if at is not None:
        spaces = [pltpu.SMEM] + spaces
        operands = (at,) + tuple(operands)
    return pl.pallas_call(
        kernel,
        out_shape=tuple(outs),
        in_specs=[pl.BlockSpec(memory_space=space) for space in spaces],
        out_specs=tuple(pl.BlockSpec(memory_space=pltpu.VMEM) for _ in outs),
        scratch_shapes=scratch,
        compiler_params=pltpu.CompilerParams(vmem_limit_bytes=limit),
        cost_estimate=pl.CostEstimate(flops=flops, bytes_accessed=moved, transcendentals=0),
        name=name,
    )(*operands)


def swap(x, axis, n, mask):
    return lax.ppermute(x, axis, [(i, i ^ mask) for i in range(n)])


def local(query_rows, key_rows, value_rows, upstream):
    rows, features = query_rows.shape
    n_i, n_o = lax.axis_size("seqi"), lax.axis_size("seqo")
    slots = HEADS // n_i
    width = n_o // slots
    others = (width - 1) * slots
    quarter = rows // DILATION
    pos = lax.axis_index("seqi").astype(jnp.int32)
    chip = lax.axis_index("seqo").astype(jnp.int32) // width
    at = jnp.stack([pos, chip])
    sources = (key_rows, value_rows, query_rows, upstream)
    unit = 2 * rows * rows * HEAD_DIM
    bind = functools.partial

    mid = SHAPE((4, quarter, slots * HEAD_DIM), BF16)
    full = SHAPE((4, rows, HEAD_DIM), BF16)
    half = SHAPE((slots, 2, rows, HEAD_DIM), BF16)
    square = pltpu.VMEM((LANES, rows), F32)

    def stats(count, lanes=rows):
        return SHAPE((count, lanes), F32)

    def swap_mids(pieces):
        return [pieces[0]] + [swap(pieces[d], "seqi", n_i, d) for d in range(1, n_i)]

    def swap_fulls(pieces):
        return [pieces[0]] + [swap(pieces[m], "seqo", n_o, m * width) for m in range(1, slots)]

    def swap_cores(pieces):
        return [
            swap(pieces[m], "seqo", n_o, part)
            for part in range(1, width)
            for m in range(slots)
        ]

    pieces = call(
        bind(pick_kernel, n_i, slots),
        "pick",
        [mid] * n_i + [full] * slots,
        [
            pltpu.VMEM((4, rows, features), BF16),
            pltpu.SemaphoreType.DMA((4, HEADS // DILATION)),
            pltpu.VMEM((4, HEADS, rows, HEAD_DIM), F32),
            pltpu.VMEM((4, quarter, features), BF16),
        ],
        unit,
        sources,
        at,
        in_hbm=4,
        limit=VMEM_ALL,
    )
    mids = swap_mids(pieces[:n_i])
    fulls = swap_fulls(pieces[n_i:])
    sibs = swap_cores(fulls)

    near, nearmid = call(
        near_stats_kernel,
        "near_stats",
        [stats(2 * HEADS, rows), stats(quarter, LANES)],
        [
            pltpu.VMEM((4, rows, features), BF16),
            pltpu.SemaphoreType.DMA((4, HEADS // DILATION)),
            square,
        ],
        unit * HEADS * 2,
        sources,
        in_hbm=4,
        limit=VMEM_ALL,
    )
    *zmsgs, joint, middle = call(
        bind(middle_stats_kernel, n_i, slots),
        "middle_stats",
        [SHAPE((quarter, LANES), F32)] * n_i
        + [stats(2 * slots), stats(2 * slots, n_i * quarter)],
        [pltpu.VMEM((LANES, n_i * quarter), F32), square],
        unit * slots * 2,
        mids + [near, nearmid],
        at,
    )
    (xmsg,) = call(
        bind(far_stats_kernel, slots),
        "far_stats",
        [stats(4 * slots)],
        [],
        unit * n_o * slots * 2,
        [joint] + fulls + sibs,
    )
    zmsgs = swap_mids(zmsgs)
    xmsgs = swap_fulls([xmsg] * slots)

    *midparts, final = call(
        bind(middle_parts_kernel, n_i, slots),
        "middle_parts",
        [mid] * n_i + [stats(2 * HEADS)],
        [
            pltpu.VMEM((2 * HEADS, rows), F32),
            pltpu.VMEM((LANES, n_i * quarter), F32),
            square,
        ],
        unit * slots * 6,
        mids + [near, middle] + zmsgs + xmsgs,
        at,
    )
    midparts = swap_mids(midparts)
    farparts = call(
        bind(far_parts_kernel, slots, width),
        "far_parts",
        [full] * slots + [half] * (width - 1),
        [pltpu.VMEM((n_o * rows, slots * rows), BF16)] * 2,
        unit * n_o * slots * 6,
        fulls + sibs + xmsgs + [final],
        at,
    )
    fullparts = call(
        bind(far_sum_kernel, slots),
        "far_sum",
        [full] * slots,
        [],
        unit,
        list(farparts[:slots])
        + [swap(x, "seqo", n_o, part + 1) for part, x in enumerate(farparts[slots:])],
        cheap=True,
    )
    fullparts = swap_fulls(fullparts)

    (nearparts,) = call(
        near_parts_kernel,
        "near_parts",
        [SHAPE((4, HEADS, rows, HEAD_DIM), F32)],
        [],
        unit * HEADS * 6,
        sources + (final,),
        cheap=True,
    )
    return call(
        bind(final_kernel, n_i, slots),
        "final",
        [SHAPE((rows, features), BF16)] * 4,
        [],
        unit * HEADS,
        [nearparts] + midparts + fullparts,
        at,
    )


def solution(mesh):
    rows = P(("seqo", "seqi"), None)
    return jax.shard_map(
        local,
        mesh=mesh,
        in_specs=(rows,) * 4,
        out_specs=(rows,) * 4,
        check_vma=False,
    )
```

```python
import functools

import jax
import jax.numpy as jnp
from jax import lax
from jax.experimental import pallas as pl
from jax.experimental.pallas import tpu as pltpu
from jax.sharding import PartitionSpec as P

HEADS = 16
HEAD_DIM = 128
DILATION = 4
LANES = 128
SCALE = HEAD_DIM**-0.5
LOWEST = -1e30
VMEM_LIMIT = 32 * 1024 * 1024
PICK_LIMIT = 53 * 1024 * 1024
NEAR_LIMIT = 54784 * 1024
F32, BF16 = jnp.float32, jnp.bfloat16
SHAPE = jax.ShapeDtypeStruct

NT = (((1,), (1,)), ((), ()))
TN = (((0,), (0,)), ((), ()))


def dot(a, b):
    return jnp.dot(a, b, preferred_element_type=F32)


def dot_nt(a, b):
    return lax.dot_general(a, b, NT, preferred_element_type=F32)


def dot_tn(a, b):
    return lax.dot_general(a, b, TN, preferred_element_type=F32)


def head_columns(head):
    return pl.ds(pl.multiple_of(head * HEAD_DIM, HEAD_DIM), HEAD_DIM)


def static_columns(index):
    return slice(index * HEAD_DIM, (index + 1) * HEAD_DIM)


def position(slots):
    width = lax.axis_size("seqo") // slots
    return lax.axis_index("seqi"), lax.axis_index("seqo") // width


def lanes_of(rows):
    return lax.broadcasted_iota(jnp.int32, (rows, LANES), 1)


def level_stats(operands):
    products = [(dot_nt(k, q) * SCALE, dot_nt(v, u)) for k, v, q, u in operands]
    tops = [jnp.max(s, axis=0, keepdims=True) for s, _ in products]
    weights = [jnp.exp(s - top) for (s, _), top in zip(products, tops)]
    totals = [jnp.sum(p, axis=0, keepdims=True) for p in weights]
    return [
        (top + jnp.log(total), jnp.sum(p * dp, axis=0, keepdims=True) / total)
        for (_, dp), top, p, total in zip(products, tops, weights, totals)
    ]


def merge_stats(ea, da, eb, db):
    top = jnp.maximum(ea, eb)
    wa, wb = jnp.exp(ea - top), jnp.exp(eb - top)
    total = wa + wb
    return top + jnp.log(total), (wa * da + wb * db) / total


def level_weights(operands, stats):
    products = [(dot_nt(k, q) * SCALE, dot_nt(v, u)) for k, v, q, u in operands]
    found = []
    for (s, dp), (lse, delta) in zip(products, stats):
        g = jnp.exp(s - lse)
        found.append((g.astype(BF16), (g * (dp - delta)).astype(BF16)))
    return found


def level_parts(operands, stats):
    found = level_weights(operands, stats)
    keyed = [
        (dot(ds, q) * SCALE, dot(p, u)) for (p, ds), (k, v, q, u) in zip(found, operands)
    ]
    queried = [
        (dot_tn(p, v), dot_tn(ds, k) * SCALE) for (p, ds), (k, v, q, u) in zip(found, operands)
    ]
    return [a + b for a, b in zip(queried, keyed)]


def pick_rows(ref, rows):
    quarter = rows // DILATION
    lane = lanes_of(quarter)
    picked = jnp.zeros((quarter, LANES), F32)
    for residue in range(DILATION):
        part = ref[pl.ds(residue, quarter, stride=DILATION), :]
        picked = jnp.where(lane % DILATION == residue, part, picked)
    return picked


def fetch(sources, buffers, sems):
    width = DILATION * HEAD_DIM
    groups = []
    for group in range(HEADS // DILATION):
        cols = pl.ds(group * width, width)
        groups.append(
            [
                pltpu.make_async_copy(
                    source.at[:, cols], buffers.at[which, :, cols], sems.at[which, group]
                )
                for which, source in enumerate(sources)
            ]
        )
        for copy in groups[-1]:
            copy.start()
    return groups


def pick_kernel(n_i, slots, *refs):
    sources, refs = refs[:4], refs[4:]
    mids, refs = refs[:n_i], refs[n_i:]
    fulls, refs = refs[:slots], refs[slots:]
    buffers, sems, wide, picked = refs
    rows = sources[0].shape[0]
    quarter = rows // DILATION
    pos, chip = position(slots)
    for group, copies in enumerate(fetch(sources, buffers, sems)):
        for which, copy in enumerate(copies):
            copy.wait()
            for residue in range(DILATION):
                head = group * DILATION + residue
                cols = static_columns(head)
                wide[which, head] = buffers[which, :, cols].astype(F32)
                rowset = wide[which, head, pl.ds(residue, quarter, stride=DILATION), :]
                picked[which, :, cols] = rowset.astype(BF16)
    width = slots * HEAD_DIM
    for d in range(n_i):
        start = pl.multiple_of((pos ^ d) * width, width)
        mids[d][...] = picked[:, :, pl.ds(start, width)]
    for m in range(slots):
        fulls[m][...] = buffers[:, :, head_columns(pos * slots + (chip ^ m))]


def near_operands(ref, group):
    heads = range(group * DILATION, (group + 1) * DILATION)
    return [[ref[which, :, static_columns(head)] for which in range(4)] for head in heads]


def near_stats_kernel(k_hbm, v_hbm, q_hbm, u_hbm, stats_ref, mid_ref, buffers, sems, turn):
    rows = q_hbm.shape[0]
    turn[...] = jnp.zeros_like(turn)
    for group, copies in enumerate(fetch((k_hbm, v_hbm, q_hbm, u_hbm), buffers, sems)):
        for copy in copies:
            copy.wait()
        for residue, (e, d) in enumerate(level_stats(near_operands(buffers, group))):
            head = group * DILATION + residue
            turn[head : head + 1, :] = e
            turn[HEADS + head : HEADS + head + 1, :] = d
    stats_ref[...] = turn[: 2 * HEADS, :]
    turn[...] = turn[...].T
    mid_ref[...] = pick_rows(turn, rows)


def far_stats_kernel(slots, near_ref, *refs):
    fulls, sibs, xmsg_ref = refs[:slots], refs[slots:-1], refs[-1]
    keys = jnp.concatenate([ref[0] for ref in fulls + sibs], axis=0)
    values = jnp.concatenate([ref[1] for ref in fulls + sibs], axis=0)
    xmsg_ref[: 2 * slots] = near_ref[...]
    for m in range(slots):
        ((e, d),) = level_stats([(keys, values, fulls[m][2], fulls[m][3])])
        xmsg_ref[2 * slots + m : 2 * slots + m + 1, :] = e
        xmsg_ref[3 * slots + m : 3 * slots + m + 1, :] = d


def middle_operands(mids, slot):
    cols = static_columns(slot)
    return [jnp.concatenate([ref[which, :, cols] for ref in mids], axis=0) for which in range(4)]


def middle_stats_kernel(n_i, slots, *refs):
    mids, refs = (refs[0], *refs[n_i - 1 : 0 : -1]), refs[n_i:]
    near_ref, nearmid_ref = refs[:2]
    refs = refs[2:]
    zmsgs, refs = refs[:n_i], refs[n_i:]
    joint_ref, stats_ref, turn, spread = refs
    quarter = nearmid_ref.shape[0]
    pos, _ = position(slots)
    turn[...] = jnp.zeros_like(turn)
    operands = [middle_operands(mids, slot) for slot in range(slots)]
    for slot, (e, d) in enumerate(level_stats(operands)):
        turn[slot : slot + 1, :] = e
        turn[slots + slot : slots + slot + 1, :] = d
    stats_ref[...] = turn[: 2 * slots, :]
    columns = turn[...].T
    lane = lanes_of(quarter)
    for d in range(n_i):
        chunk = pltpu.roll(columns[d * quarter : (d + 1) * quarter], 2 * HEADS, 1)
        zmsgs[d][...] = jnp.where(lane < 2 * HEADS, nearmid_ref[...], chunk)
    own = columns[:quarter]
    lane_residue = (pos * slots + lane % slots) % DILATION
    blank = jnp.where(lane < slots, LOWEST, 0.0)
    for residue in range(DILATION):
        spread[pl.ds(residue, quarter, stride=DILATION), :] = jnp.where(
            lane_residue == residue, own, blank
        )
    across = spread[...].T
    e, d = merge_stats(
        near_ref[pl.ds(pos * slots, slots), :],
        near_ref[pl.ds(HEADS + pos * slots, slots), :],
        across[:slots],
        across[slots : 2 * slots],
    )
    joint_ref[:slots] = e
    joint_ref[slots:] = d


def middle_parts_kernel(n_i, slots, *refs):
    mids, refs = (refs[0], *refs[n_i - 1 : 0 : -1]), refs[n_i:]
    near_ref, stats_ref = refs[:2]
    refs = refs[2:]
    zmsgs, refs = refs[:n_i], refs[n_i:]
    xmsgs, refs = refs[:slots], refs[slots:]
    outs, refs = refs[:n_i], refs[n_i:]
    final_ref, far, turn, spread = refs
    quarter = zmsgs[0].shape[0]
    rows = quarter * DILATION
    pos, chip = position(slots)

    lane = lanes_of(quarter)
    mid = jnp.zeros((quarter, LANES), F32)
    for d in range(n_i):
        place = (pos ^ d) * slots
        e = pltpu.roll(zmsgs[d][...], (place + LANES - 2 * HEADS) % LANES, 1)
        de = pltpu.roll(zmsgs[d][...], (place + LANES - HEADS - slots) % LANES, 1)
        mid = jnp.where((lane >= place) & (lane < place + slots), e, mid)
        mid = jnp.where((lane >= HEADS + place) & (lane < HEADS + place + slots), de, mid)
    blank = jnp.where(lane < HEADS, LOWEST, 0.0)
    for residue in range(DILATION):
        spread[pl.ds(residue, quarter, stride=DILATION), :] = jnp.where(
            lane % DILATION == residue, mid, blank
        )
    across = spread[...].T
    far[:HEADS] = jnp.full((HEADS, rows), LOWEST, F32)
    far[HEADS:] = jnp.zeros((HEADS, rows), F32)
    for m in range(slots):
        head = pos * slots + (chip ^ m)
        far[pl.ds(head, 1), :] = xmsgs[m][2 * slots + m : 2 * slots + m + 1, :]
        far[pl.ds(HEADS + head, 1), :] = xmsgs[m][3 * slots + m : 3 * slots + m + 1, :]
    e, d = merge_stats(
        near_ref[:HEADS], near_ref[HEADS:], across[:HEADS], across[HEADS : 2 * HEADS]
    )
    e, d = merge_stats(e, d, far[:HEADS], far[HEADS:])
    final_ref[:HEADS] = e
    final_ref[HEADS:] = d

    spread[...] = jnp.zeros_like(spread)
    spread[: 2 * HEADS] = final_ref[...]
    spread[...] = spread[...].T
    own = pick_rows(spread, rows)
    turn[...] = jnp.concatenate([own] + [ref[...] for ref in zmsgs[1:]], axis=0).T
    owned = lax.broadcasted_iota(jnp.int32, (1, n_i * quarter), 1) < quarter
    operands = [middle_operands(mids, slot) for slot in range(slots)]
    merged = [
        merge_stats(
            turn[pl.ds(pos * slots + slot, 1), :],
            turn[pl.ds(HEADS + pos * slots + slot, 1), :],
            jnp.where(owned, LOWEST, stats_ref[slot : slot + 1, :]),
            stats_ref[slots + slot : slots + slot + 1, :],
        )
        for slot in range(slots)
    ]
    for slot, parts in enumerate(level_parts(operands, merged)):
        for which, part in enumerate(parts):
            part = part.astype(BF16)
            for d in range(n_i):
                outs[d][which, :, static_columns(slot)] = part[d * quarter : (d + 1) * quarter]


def far_parts_kernel(slots, width, *refs):
    others = (width - 1) * slots
    fulls, refs = refs[:slots], refs[slots:]
    kvs, refs = refs[:others], refs[others:]
    xmsgs, refs = refs[:slots], refs[slots:]
    final_ref, refs = refs[0], refs[1:]
    outs, refs = refs[:slots], refs[slots:]
    kvouts, refs = refs[: width - 1], refs[width - 1 :]
    weights, score_grads = refs
    rows = fulls[0].shape[1]
    pos, chip = position(slots)
    head = pos * slots + chip
    keys = jnp.concatenate([ref[0] for ref in fulls + kvs], axis=0)
    values = jnp.concatenate([ref[1] for ref in fulls + kvs], axis=0)
    for m in range(slots):
        if m == 0:
            lse, delta = final_ref[pl.ds(head, 1), :], final_ref[pl.ds(HEADS + head, 1), :]
        else:
            lse, delta = merge_stats(
                xmsgs[m][pl.ds(chip, 1), :],
                xmsgs[m][pl.ds(slots + chip, 1), :],
                xmsgs[0][2 * slots + m : 2 * slots + m + 1, :],
                xmsgs[0][3 * slots + m : 3 * slots + m + 1, :],
            )
        operands = (keys, values, fulls[m][2], fulls[m][3])
        ((p, ds),) = level_weights([operands], [(lse, delta)])
        outs[m][0] = dot_tn(p, values).astype(BF16)
        outs[m][1] = (dot_tn(ds, keys) * SCALE).astype(BF16)
        weights[:, m * rows : (m + 1) * rows] = p
        score_grads[:, m * rows : (m + 1) * rows] = ds
    queries = jnp.concatenate([ref[2] for ref in fulls], axis=0)
    ups = jnp.concatenate([ref[3] for ref in fulls], axis=0)
    key_part = (dot(score_grads[...], queries) * SCALE).astype(BF16)
    value_part = dot(weights[...], ups).astype(BF16)
    for index in range(width * slots):
        block = slice(index * rows, (index + 1) * rows)
        part, m = index // slots, index % slots
        if part == 0:
            outs[m][2], outs[m][3] = key_part[block], value_part[block]
        else:
            kvouts[part - 1][m, 0], kvouts[part - 1][m, 1] = key_part[block], value_part[block]


def far_sum_kernel(slots, *refs):
    own, refs = refs[:slots], refs[slots:]
    found, outs = refs[:-slots], refs[-slots:]
    for m in range(slots):
        outs[m][:2] = own[m][:2]
        total = own[m][2:].astype(F32)
        for ref in found:
            total += ref[m].astype(F32)
        outs[m][2:] = total.astype(BF16)


def near_parts_kernel(k_ref, v_ref, q_ref, u_ref, stats_ref, out_ref):
    for group in range(HEADS // DILATION):
        heads = range(group * DILATION, (group + 1) * DILATION)
        operands = [
            [ref[:, static_columns(head)] for ref in (k_ref, v_ref, q_ref, u_ref)] for head in heads
        ]
        stats = [
            (stats_ref[head : head + 1, :], stats_ref[HEADS + head : HEADS + head + 1, :])
            for head in heads
        ]
        for head, parts in zip(heads, level_parts(operands, stats)):
            for which, part in enumerate(parts):
                out_ref[which, head] = part


def final_kernel(n_i, slots, near_ref, *refs):
    mids, refs = (refs[0], *refs[n_i - 1 : 0 : -1]), refs[n_i:]
    fulls, refs = refs[:slots], refs[slots:]
    outs, (ready, sems) = refs[:4], refs[4:]
    rows = fulls[0].shape[1]
    quarter = rows // DILATION
    pos, chip = position(slots)
    row = lax.broadcasted_iota(jnp.int32, (rows, quarter), 0)
    taken = lax.broadcasted_iota(jnp.int32, (rows, quarter), 1) * DILATION

    def spread(d, slot):
        head = (pos ^ d) * slots + slot
        place = jnp.where(row == taken + head % DILATION, 1.0, 0.0).astype(BF16)
        cols = head_columns(slot) if d == 0 else static_columns(slot)
        picked = jnp.concatenate([mids[d][which, :, cols] for which in range(4)], axis=1)
        return head, dot(place, picked)

    copies = []
    for d in reversed(range(n_i)):
        found = [spread(d, chip ^ slot if d == 0 else slot) for slot in range(slots)]
        for slot, (head, parts) in enumerate(found):
            for which in range(4):
                total = near_ref[which, head] + parts[:, static_columns(which)]
                if d == 0:
                    total += fulls[slot][which].astype(F32)
                ready[which, :, head_columns(head)] = total.astype(BF16)
        width = slots * HEAD_DIM
        cols = pl.ds(pl.multiple_of((pos ^ d) * width, width), width)
        for which, out in enumerate(outs):
            copy = pltpu.make_async_copy(
                ready.at[which, :, cols], out.at[:, cols], sems.at[which, d]
            )
            copy.start()
            copies.append(copy)
    for copy in copies:
        copy.wait()


def call(kernel, name, outs, scratch, flops, operands, hbm_in=(), hbm_out=False, cheap=False, limit=VMEM_LIMIT):
    moved = sum(x.size * x.dtype.itemsize for x in tuple(operands) + tuple(outs))
    if cheap:
        flops, moved = 1, 1
    spaces = [pltpu.HBM if i in hbm_in else pltpu.VMEM for i in range(len(operands))]
    return pl.pallas_call(
        kernel,
        out_shape=tuple(outs),
        in_specs=[pl.BlockSpec(memory_space=space) for space in spaces],
        out_specs=tuple(
            pl.BlockSpec(memory_space=pltpu.HBM if hbm_out else pltpu.VMEM) for _ in outs
        ),
        scratch_shapes=scratch,
        compiler_params=pltpu.CompilerParams(vmem_limit_bytes=limit),
        cost_estimate=pl.CostEstimate(flops=flops, bytes_accessed=moved, transcendentals=0),
        name=name,
    )(*operands)


def last_first(pieces):
    return [pieces[0]] + pieces[:0:-1]


def swap(x, axis, n, mask):
    return lax.ppermute(x, axis, [(i, i ^ mask) for i in range(n)])


def local(query_rows, key_rows, value_rows, upstream):
    rows, features = query_rows.shape
    n_i, n_o = lax.axis_size("seqi"), lax.axis_size("seqo")
    slots = HEADS // n_i
    width = n_o // slots
    others = (width - 1) * slots
    quarter = rows // DILATION
    sources = (key_rows, value_rows, query_rows, upstream)
    unit = 2 * rows * rows * HEAD_DIM
    bind = functools.partial

    mid = SHAPE((4, quarter, slots * HEAD_DIM), BF16)
    full = SHAPE((4, rows, HEAD_DIM), BF16)
    half = SHAPE((slots, 2, rows, HEAD_DIM), BF16)
    square = pltpu.VMEM((LANES, rows), F32)

    def stats(count, lanes=rows):
        return SHAPE((count, lanes), F32)

    def swap_mids(pieces):
        found = {d: swap(pieces[d], "seqi", n_i, d) for d in reversed(range(1, n_i))}
        return [pieces[0]] + [found[d] for d in range(1, n_i)]

    def swap_fulls(pieces):
        return [pieces[0]] + [swap(pieces[m], "seqo", n_o, m * width) for m in range(1, slots)]

    def swap_cores(pieces):
        return [
            swap(pieces[m], "seqo", n_o, part)
            for part in range(1, width)
            for m in range(slots)
        ]

    buffers = [
        pltpu.VMEM((4, rows, features), BF16),
        pltpu.SemaphoreType.DMA((4, HEADS // DILATION)),
    ]
    pieces = call(
        bind(pick_kernel, n_i, slots),
        "pick",
        [mid] * n_i + [full] * slots,
        buffers
        + [
            pltpu.VMEM((4, HEADS, rows, HEAD_DIM), F32),
            pltpu.VMEM((4, quarter, features), BF16),
        ],
        unit,
        sources,
        hbm_in=range(4),
        limit=PICK_LIMIT,
    )
    mids = swap_mids(pieces[:n_i])
    fulls = swap_fulls(pieces[n_i:])
    sibs = swap_cores(fulls)

    near, nearmid = call(
        near_stats_kernel,
        "near_stats",
        [stats(2 * HEADS), stats(quarter, LANES)],
        buffers + [square],
        unit * HEADS * 2,
        sources,
        hbm_in=range(4),
        limit=NEAR_LIMIT,
    )
    *zmsgs, joint, middle = call(
        bind(middle_stats_kernel, n_i, slots),
        "middle_stats",
        [SHAPE((quarter, LANES), F32)] * n_i
        + [stats(2 * slots), stats(2 * slots, n_i * quarter)],
        [pltpu.VMEM((LANES, n_i * quarter), F32), square],
        unit * slots * 2,
        last_first(mids) + [near, nearmid],
    )
    (xmsg,) = call(
        bind(far_stats_kernel, slots),
        "far_stats",
        [stats(4 * slots)],
        [],
        unit * n_o * slots * 2,
        [joint] + fulls + sibs,
    )
    zmsgs = swap_mids(zmsgs)
    xmsgs = swap_fulls([xmsg] * slots)

    *midparts, final = call(
        bind(middle_parts_kernel, n_i, slots),
        "middle_parts",
        [mid] * n_i + [stats(2 * HEADS)],
        [
            pltpu.VMEM((2 * HEADS, rows), F32),
            pltpu.VMEM((LANES, n_i * quarter), F32),
            square,
        ],
        unit * slots * 6,
        last_first(mids) + [near, middle] + zmsgs + xmsgs,
    )
    midparts = swap_mids(midparts)
    farparts = call(
        bind(far_parts_kernel, slots, width),
        "far_parts",
        [full] * slots + [half] * (width - 1),
        [pltpu.VMEM((n_o * rows, slots * rows), BF16)] * 2,
        unit * n_o * slots * 6,
        fulls + sibs + xmsgs + [final],
    )
    fullparts = call(
        bind(far_sum_kernel, slots),
        "far_sum",
        [full] * slots,
        [],
        unit,
        list(farparts[:slots])
        + [swap(x, "seqo", n_o, part + 1) for part, x in enumerate(farparts[slots:])],
        cheap=True,
    )
    fullparts = swap_fulls(fullparts)

    (nearparts,) = call(
        near_parts_kernel,
        "near_parts",
        [SHAPE((4, HEADS, rows, HEAD_DIM), F32)],
        [],
        unit * HEADS * 6,
        sources + (final,),
        cheap=True,
    )
    return call(
        bind(final_kernel, n_i, slots),
        "final",
        [SHAPE((rows, features), BF16)] * 4,
        [pltpu.VMEM((4, rows, features), BF16), pltpu.SemaphoreType.DMA((4, n_i))],
        unit * HEADS,
        [nearparts] + last_first(midparts) + fullparts,
        hbm_out=True,
    )


def solution(mesh):
    rows = P(("seqo", "seqi"), None)
    return jax.shard_map(
        local,
        mesh=mesh,
        in_specs=(rows,) * 4,
        out_specs=(rows,) * 4,
        check_vma=False,
    )
```

```python
import functools

import jax
import jax.numpy as jnp
from jax import lax
from jax.experimental import pallas as pl
from jax.experimental.pallas import tpu as pltpu
from jax.sharding import PartitionSpec as P

HEADS = 16
HEAD_DIM = 128
DILATION = 4
LANES = 128
SCALE = HEAD_DIM**-0.5
LOWEST = -1e30
VMEM_LIMIT = 32 * 1024 * 1024
PICK_LIMIT = 53 * 1024 * 1024
NEAR_LIMIT = 54784 * 1024
F32, BF16 = jnp.float32, jnp.bfloat16
SHAPE = jax.ShapeDtypeStruct

NT = (((1,), (1,)), ((), ()))
TN = (((0,), (0,)), ((), ()))


def dot(a, b):
    return jnp.dot(a, b, preferred_element_type=F32)


def dot_nt(a, b):
    return lax.dot_general(a, b, NT, preferred_element_type=F32)


def dot_tn(a, b):
    return lax.dot_general(a, b, TN, preferred_element_type=F32)


def head_columns(head):
    return pl.ds(pl.multiple_of(head * HEAD_DIM, HEAD_DIM), HEAD_DIM)


def static_columns(index):
    return slice(index * HEAD_DIM, (index + 1) * HEAD_DIM)


def position(slots):
    width = lax.axis_size("seqo") // slots
    return lax.axis_index("seqi"), lax.axis_index("seqo") // width


def lanes_of(rows):
    return lax.broadcasted_iota(jnp.int32, (rows, LANES), 1)


def level_stats(operands):
    products = [(dot_nt(k, q) * SCALE, dot_nt(v, u)) for k, v, q, u in operands]
    tops = [jnp.max(s, axis=0, keepdims=True) for s, _ in products]
    weights = [jnp.exp(s - top) for (s, _), top in zip(products, tops)]
    totals = [jnp.sum(p, axis=0, keepdims=True) for p in weights]
    return [
        (top + jnp.log(total), jnp.sum(p * dp, axis=0, keepdims=True) / total)
        for (_, dp), top, p, total in zip(products, tops, weights, totals)
    ]


def merge_stats(ea, da, eb, db):
    top = jnp.maximum(ea, eb)
    wa, wb = jnp.exp(ea - top), jnp.exp(eb - top)
    total = wa + wb
    return top + jnp.log(total), (wa * da + wb * db) / total


def level_weights(operands, stats):
    products = [(dot_nt(k, q) * SCALE, dot_nt(v, u)) for k, v, q, u in operands]
    found = []
    for (s, dp), (lse, delta) in zip(products, stats):
        g = jnp.exp(s - lse)
        found.append((g.astype(BF16), (g * (dp - delta)).astype(BF16)))
    return found


def level_parts(operands, stats):
    found = level_weights(operands, stats)
    keyed = [
        (dot(ds, q) * SCALE, dot(p, u)) for (p, ds), (k, v, q, u) in zip(found, operands)
    ]
    queried = [
        (dot_tn(p, v), dot_tn(ds, k) * SCALE) for (p, ds), (k, v, q, u) in zip(found, operands)
    ]
    return [a + b for a, b in zip(queried, keyed)]


def pick_rows(ref, rows):
    quarter = rows // DILATION
    lane = lanes_of(quarter)
    picked = jnp.zeros((quarter, LANES), F32)
    for residue in range(DILATION):
        part = ref[pl.ds(residue, quarter, stride=DILATION), :]
        picked = jnp.where(lane % DILATION == residue, part, picked)
    return picked


def fetch(sources, buffers, sems):
    width = DILATION * HEAD_DIM
    groups = []
    for group in range(HEADS // DILATION):
        cols = pl.ds(group * width, width)
        groups.append(
            [
                pltpu.make_async_copy(
                    source.at[:, cols], buffers.at[which, :, cols], sems.at[which, group]
                )
                for which, source in enumerate(sources)
            ]
        )
        for copy in groups[-1]:
            copy.start()
    return groups


def pick_kernel(n_i, slots, *refs):
    sources, refs = refs[:4], refs[4:]
    mids, refs = refs[:n_i], refs[n_i:]
    fulls, refs = refs[:slots], refs[slots:]
    buffers, sems, wide, picked = refs
    rows = sources[0].shape[0]
    quarter = rows // DILATION
    pos, chip = position(slots)
    for group, copies in enumerate(fetch(sources, buffers, sems)):
        for which, copy in enumerate(copies):
            copy.wait()
            for residue in range(DILATION):
                head = group * DILATION + residue
                cols = static_columns(head)
                wide[which, head] = buffers[which, :, cols].astype(F32)
                rowset = wide[which, head, pl.ds(residue, quarter, stride=DILATION), :]
                picked[which, :, cols] = rowset.astype(BF16)
    width = slots * HEAD_DIM
    for d in range(n_i):
        start = pl.multiple_of((pos ^ d) * width, width)
        mids[d][...] = picked[:, :, pl.ds(start, width)]
    for m in range(slots):
        fulls[m][...] = buffers[:, :, head_columns(pos * slots + (chip ^ m))]


def near_operands(ref, group):
    heads = range(group * DILATION, (group + 1) * DILATION)
    return [[ref[which, :, static_columns(head)] for which in range(4)] for head in heads]


def near_stats_kernel(k_hbm, v_hbm, q_hbm, u_hbm, stats_ref, mid_ref, buffers, sems, turn):
    rows = q_hbm.shape[0]
    turn[...] = jnp.zeros_like(turn)
    for group, copies in enumerate(fetch((k_hbm, v_hbm, q_hbm, u_hbm), buffers, sems)):
        for copy in copies:
            copy.wait()
        for residue, (e, d) in enumerate(level_stats(near_operands(buffers, group))):
            head = group * DILATION + residue
            turn[head : head + 1, :] = e
            turn[HEADS + head : HEADS + head + 1, :] = d
    stats_ref[...] = turn[: 2 * HEADS, :]
    turn[...] = turn[...].T
    mid_ref[...] = pick_rows(turn, rows)


def pack_kernel(slots, *refs):
    packed_ref = refs[-1]
    for m, ref in enumerate(refs[:slots]):
        packed_ref[m] = ref[:2]


def far_keys(fulls, sibs, which):
    blocks = [ref[which] for ref in fulls]
    return jnp.concatenate(blocks + [ref[m, which] for ref in sibs for m in range(len(fulls))], axis=0)


def far_stats_kernel(slots, near_ref, *refs):
    fulls, sibs, xmsg_ref = refs[:slots], refs[slots:-1], refs[-1]
    keys, values = far_keys(fulls, sibs, 0), far_keys(fulls, sibs, 1)
    xmsg_ref[: 2 * slots] = near_ref[...]
    for m in range(slots):
        ((e, d),) = level_stats([(keys, values, fulls[m][2], fulls[m][3])])
        xmsg_ref[2 * slots + m : 2 * slots + m + 1, :] = e
        xmsg_ref[3 * slots + m : 3 * slots + m + 1, :] = d


def middle_operands(mids, slot):
    cols = static_columns(slot)
    return [jnp.concatenate([ref[which, :, cols] for ref in mids], axis=0) for which in range(4)]


def middle_stats_kernel(n_i, slots, *refs):
    mids, refs = in_order(refs[:n_i]), refs[n_i:]
    near_ref, nearmid_ref = refs[:2]
    refs = refs[2:]
    zmsgs, refs = refs[:n_i], refs[n_i:]
    joint_ref, stats_ref, turn, spread = refs
    quarter = nearmid_ref.shape[0]
    pos, _ = position(slots)
    turn[...] = jnp.zeros_like(turn)
    operands = [middle_operands(mids, slot) for slot in range(slots)]
    for slot, (e, d) in enumerate(level_stats(operands)):
        turn[slot : slot + 1, :] = e
        turn[slots + slot : slots + slot + 1, :] = d
    stats_ref[...] = turn[: 2 * slots, :]
    columns = turn[...].T
    lane = lanes_of(quarter)
    for d in range(n_i):
        chunk = pltpu.roll(columns[d * quarter : (d + 1) * quarter], 2 * HEADS, 1)
        zmsgs[d][...] = jnp.where(lane < 2 * HEADS, nearmid_ref[...], chunk)
    own = columns[:quarter]
    lane_residue = (pos * slots + lane % slots) % DILATION
    blank = jnp.where(lane < slots, LOWEST, 0.0)
    for residue in range(DILATION):
        spread[pl.ds(residue, quarter, stride=DILATION), :] = jnp.where(
            lane_residue == residue, own, blank
        )
    across = spread[...].T
    e, d = merge_stats(
        near_ref[pl.ds(pos * slots, slots), :],
        near_ref[pl.ds(HEADS + pos * slots, slots), :],
        across[:slots],
        across[slots : 2 * slots],
    )
    joint_ref[:slots] = e
    joint_ref[slots:] = d


def middle_parts_kernel(n_i, slots, *refs):
    mids, refs = in_order(refs[:n_i]), refs[n_i:]
    near_ref, stats_ref = refs[:2]
    refs = refs[2:]
    zmsgs, refs = refs[:n_i], refs[n_i:]
    xmsgs, refs = refs[:slots], refs[slots:]
    outs, refs = refs[:n_i], refs[n_i:]
    final_ref, far, turn, spread = refs
    quarter = zmsgs[0].shape[0]
    rows = quarter * DILATION
    pos, chip = position(slots)

    lane = lanes_of(quarter)
    mid = jnp.zeros((quarter, LANES), F32)
    for d in range(n_i):
        place = (pos ^ d) * slots
        e = pltpu.roll(zmsgs[d][...], (place + LANES - 2 * HEADS) % LANES, 1)
        de = pltpu.roll(zmsgs[d][...], (place + LANES - HEADS - slots) % LANES, 1)
        mid = jnp.where((lane >= place) & (lane < place + slots), e, mid)
        mid = jnp.where((lane >= HEADS + place) & (lane < HEADS + place + slots), de, mid)
    blank = jnp.where(lane < HEADS, LOWEST, 0.0)
    for residue in range(DILATION):
        spread[pl.ds(residue, quarter, stride=DILATION), :] = jnp.where(
            lane % DILATION == residue, mid, blank
        )
    across = spread[...].T
    far[:HEADS] = jnp.full((HEADS, rows), LOWEST, F32)
    far[HEADS:] = jnp.zeros((HEADS, rows), F32)
    for m in range(slots):
        head = pos * slots + (chip ^ m)
        far[pl.ds(head, 1), :] = xmsgs[m][2 * slots + m : 2 * slots + m + 1, :]
        far[pl.ds(HEADS + head, 1), :] = xmsgs[m][3 * slots + m : 3 * slots + m + 1, :]
    e, d = merge_stats(
        near_ref[:HEADS], near_ref[HEADS:], across[:HEADS], across[HEADS : 2 * HEADS]
    )
    e, d = merge_stats(e, d, far[:HEADS], far[HEADS:])
    final_ref[:HEADS] = e
    final_ref[HEADS:] = d

    spread[...] = jnp.zeros_like(spread)
    spread[: 2 * HEADS] = final_ref[...]
    spread[...] = spread[...].T
    own = pick_rows(spread, rows)
    turn[...] = jnp.concatenate([own] + [ref[...] for ref in zmsgs[1:]], axis=0).T
    owned = lax.broadcasted_iota(jnp.int32, (1, n_i * quarter), 1) < quarter
    operands = [middle_operands(mids, slot) for slot in range(slots)]
    merged = [
        merge_stats(
            turn[pl.ds(pos * slots + slot, 1), :],
            turn[pl.ds(HEADS + pos * slots + slot, 1), :],
            jnp.where(owned, LOWEST, stats_ref[slot : slot + 1, :]),
            stats_ref[slots + slot : slots + slot + 1, :],
        )
        for slot in range(slots)
    ]
    for slot, parts in enumerate(level_parts(operands, merged)):
        for which, part in enumerate(parts):
            part = part.astype(BF16)
            for d in range(n_i):
                outs[d][which, :, static_columns(slot)] = part[d * quarter : (d + 1) * quarter]


def far_parts_kernel(slots, width, *refs):
    fulls, refs = refs[:slots], refs[slots:]
    sibs, refs = refs[: width - 1], refs[width - 1 :]
    xmsgs, refs = refs[:slots], refs[slots:]
    final_ref, refs = refs[0], refs[1:]
    outs, refs = refs[:slots], refs[slots:]
    kvouts, refs = refs[: width - 1], refs[width - 1 :]
    weights, score_grads = refs
    rows = fulls[0].shape[1]
    pos, chip = position(slots)
    head = pos * slots + chip
    keys, values = far_keys(fulls, sibs, 0), far_keys(fulls, sibs, 1)
    for m in range(slots):
        if m == 0:
            lse, delta = final_ref[pl.ds(head, 1), :], final_ref[pl.ds(HEADS + head, 1), :]
        else:
            lse, delta = merge_stats(
                xmsgs[m][pl.ds(chip, 1), :],
                xmsgs[m][pl.ds(slots + chip, 1), :],
                xmsgs[0][2 * slots + m : 2 * slots + m + 1, :],
                xmsgs[0][3 * slots + m : 3 * slots + m + 1, :],
            )
        operands = (keys, values, fulls[m][2], fulls[m][3])
        ((p, ds),) = level_weights([operands], [(lse, delta)])
        outs[m][0] = dot_tn(p, values).astype(BF16)
        outs[m][1] = (dot_tn(ds, keys) * SCALE).astype(BF16)
        weights[:, m * rows : (m + 1) * rows] = p
        score_grads[:, m * rows : (m + 1) * rows] = ds
    queries = jnp.concatenate([ref[2] for ref in fulls], axis=0)
    ups = jnp.concatenate([ref[3] for ref in fulls], axis=0)
    key_part = (dot(score_grads[...], queries) * SCALE).astype(BF16)
    value_part = dot(weights[...], ups).astype(BF16)
    for index in range(width * slots):
        block = slice(index * rows, (index + 1) * rows)
        part, m = index // slots, index % slots
        if part == 0:
            outs[m][2], outs[m][3] = key_part[block], value_part[block]
        else:
            kvouts[part - 1][m, 0], kvouts[part - 1][m, 1] = key_part[block], value_part[block]


def far_sum_kernel(slots, *refs):
    own, refs = refs[:slots], refs[slots:]
    found, outs = refs[:-slots], refs[-slots:]
    for m in range(slots):
        outs[m][:2] = own[m][:2]
        total = own[m][2:].astype(F32)
        for ref in found:
            total += ref[m].astype(F32)
        outs[m][2:] = total.astype(BF16)


def near_parts_kernel(k_ref, v_ref, q_ref, u_ref, stats_ref, out_ref):
    for group in range(HEADS // DILATION):
        heads = range(group * DILATION, (group + 1) * DILATION)
        operands = [
            [ref[:, static_columns(head)] for ref in (k_ref, v_ref, q_ref, u_ref)] for head in heads
        ]
        stats = [
            (stats_ref[head : head + 1, :], stats_ref[HEADS + head : HEADS + head + 1, :])
            for head in heads
        ]
        for head, parts in zip(heads, level_parts(operands, stats)):
            for which, part in enumerate(parts):
                out_ref[which, head] = part


def final_kernel(n_i, slots, near_ref, *refs):
    mids, refs = in_order(refs[:n_i]), refs[n_i:]
    fulls, refs = refs[:slots], refs[slots:]
    outs, (ready, sems) = refs[:4], refs[4:]
    rows = fulls[0].shape[1]
    quarter = rows // DILATION
    pos, chip = position(slots)
    row = lax.broadcasted_iota(jnp.int32, (rows, quarter), 0)
    taken = lax.broadcasted_iota(jnp.int32, (rows, quarter), 1) * DILATION

    def spread(d, slot):
        head = (pos ^ d) * slots + slot
        place = jnp.where(row == taken + head % DILATION, 1.0, 0.0).astype(BF16)
        cols = head_columns(slot) if d == 0 else static_columns(slot)
        picked = jnp.concatenate([mids[d][which, :, cols] for which in range(4)], axis=1)
        return head, dot(place, picked)

    copies = []
    for d in reversed(range(n_i)):
        found = [spread(d, chip ^ slot if d == 0 else slot) for slot in range(slots)]
        for slot, (head, parts) in enumerate(found):
            for which in range(4):
                total = near_ref[which, head] + parts[:, static_columns(which)]
                if d == 0:
                    total += fulls[slot][which].astype(F32)
                ready[which, :, head_columns(head)] = total.astype(BF16)
        width = slots * HEAD_DIM
        cols = pl.ds(pl.multiple_of((pos ^ d) * width, width), width)
        for which, out in enumerate(outs):
            copy = pltpu.make_async_copy(
                ready.at[which, :, cols], out.at[:, cols], sems.at[which, d]
            )
            copy.start()
            copies.append(copy)
    for copy in copies:
        copy.wait()


def call(kernel, name, outs, scratch, flops, operands, hbm_in=(), hbm_out=False, cheap=False, limit=VMEM_LIMIT):
    moved = sum(x.size * x.dtype.itemsize for x in tuple(operands) + tuple(outs))
    if cheap:
        flops, moved = 1, 1
    spaces = [pltpu.HBM if i in hbm_in else pltpu.VMEM for i in range(len(operands))]
    return pl.pallas_call(
        kernel,
        out_shape=tuple(outs),
        in_specs=[pl.BlockSpec(memory_space=space) for space in spaces],
        out_specs=tuple(
            pl.BlockSpec(memory_space=pltpu.HBM if hbm_out else pltpu.VMEM) for _ in outs
        ),
        scratch_shapes=scratch,
        compiler_params=pltpu.CompilerParams(vmem_limit_bytes=limit),
        cost_estimate=pl.CostEstimate(flops=flops, bytes_accessed=moved, transcendentals=0),
        name=name,
    )(*operands)


def far_first(pieces):
    return [*pieces[:2], *pieces[:1:-1]]


def in_order(pieces):
    return [*pieces[:2], *pieces[:1:-1]]


def swap(x, axis, n, mask):
    return lax.ppermute(x, axis, [(i, i ^ mask) for i in range(n)])


def local(query_rows, key_rows, value_rows, upstream):
    rows, features = query_rows.shape
    n_i, n_o = lax.axis_size("seqi"), lax.axis_size("seqo")
    slots = HEADS // n_i
    width = n_o // slots
    others = (width - 1) * slots
    quarter = rows // DILATION
    sources = (key_rows, value_rows, query_rows, upstream)
    unit = 2 * rows * rows * HEAD_DIM
    bind = functools.partial

    mid = SHAPE((4, quarter, slots * HEAD_DIM), BF16)
    full = SHAPE((4, rows, HEAD_DIM), BF16)
    half = SHAPE((slots, 2, rows, HEAD_DIM), BF16)
    square = pltpu.VMEM((LANES, rows), F32)

    def stats(count, lanes=rows):
        return SHAPE((count, lanes), F32)

    def swap_mids(pieces):
        found = {d: swap(pieces[d], "seqi", n_i, d) for d in reversed(range(1, n_i))}
        return [pieces[0]] + [found[d] for d in range(1, n_i)]

    def swap_fulls(pieces):
        return [pieces[0]] + [swap(pieces[m], "seqo", n_o, m * width) for m in range(1, slots)]

    buffers = [
        pltpu.VMEM((4, rows, features), BF16),
        pltpu.SemaphoreType.DMA((4, HEADS // DILATION)),
    ]
    pieces = call(
        bind(pick_kernel, n_i, slots),
        "pick",
        [mid] * n_i + [full] * slots,
        buffers
        + [
            pltpu.VMEM((4, HEADS, rows, HEAD_DIM), F32),
            pltpu.VMEM((4, quarter, features), BF16),
        ],
        unit,
        sources,
        hbm_in=range(4),
        limit=PICK_LIMIT,
    )
    mids = swap_mids(pieces[:n_i])
    fulls = swap_fulls(pieces[n_i:])

    near, nearmid = call(
        near_stats_kernel,
        "near_stats",
        [stats(2 * HEADS), stats(quarter, LANES)],
        buffers + [square],
        unit * HEADS * 2,
        sources,
        hbm_in=range(4),
        limit=NEAR_LIMIT,
    )
    (packed,) = call(bind(pack_kernel, slots), "pack", [half], [], unit, fulls + mids[1:] + [near])
    sibs = [swap(packed, "seqo", n_o, part) for part in range(1, width)]
    *zmsgs, joint, middle = call(
        bind(middle_stats_kernel, n_i, slots),
        "middle_stats",
        [SHAPE((quarter, LANES), F32)] * n_i
        + [stats(2 * slots), stats(2 * slots, n_i * quarter)],
        [pltpu.VMEM((LANES, n_i * quarter), F32), square],
        unit * slots * 2,
        far_first(mids) + [near, nearmid],
    )
    (xmsg,) = call(
        bind(far_stats_kernel, slots),
        "far_stats",
        [stats(4 * slots)],
        [],
        unit * n_o * slots * 2,
        [joint] + fulls + sibs,
    )
    zmsgs = swap_mids(zmsgs)
    xmsgs = swap_fulls([xmsg] * slots)

    *midparts, final = call(
        bind(middle_parts_kernel, n_i, slots),
        "middle_parts",
        [mid] * n_i + [stats(2 * HEADS)],
        [
            pltpu.VMEM((2 * HEADS, rows), F32),
            pltpu.VMEM((LANES, n_i * quarter), F32),
            square,
        ],
        unit * slots * 6,
        far_first(mids) + [near, middle] + zmsgs + xmsgs,
    )
    midparts = swap_mids(midparts)
    farparts = call(
        bind(far_parts_kernel, slots, width),
        "far_parts",
        [full] * slots + [half] * (width - 1),
        [pltpu.VMEM((n_o * rows, slots * rows), BF16)] * 2,
        unit * n_o * slots * 6,
        fulls + sibs + xmsgs + [final],
    )
    fullparts = call(
        bind(far_sum_kernel, slots),
        "far_sum",
        [full] * slots,
        [],
        unit,
        list(farparts[:slots])
        + [swap(x, "seqo", n_o, part + 1) for part, x in enumerate(farparts[slots:])],
        cheap=True,
    )
    fullparts = swap_fulls(fullparts)

    (nearparts,) = call(
        near_parts_kernel,
        "near_parts",
        [SHAPE((4, HEADS, rows, HEAD_DIM), F32)],
        [],
        unit * HEADS * 6,
        sources + (final,),
        cheap=True,
    )
    return call(
        bind(final_kernel, n_i, slots),
        "final",
        [SHAPE((rows, features), BF16)] * 4,
        [pltpu.VMEM((4, rows, features), BF16), pltpu.SemaphoreType.DMA((4, n_i))],
        unit * HEADS,
        [nearparts] + far_first(midparts) + fullparts,
        hbm_out=True,
    )


def solution(mesh):
    rows = P(("seqo", "seqi"), None)
    return jax.shard_map(
        local,
        mesh=mesh,
        in_specs=(rows,) * 4,
        out_specs=(rows,) * 4,
        check_vma=False,
    )
```

```python
import functools

import jax
import jax.numpy as jnp
from jax import lax
from jax.experimental import pallas as pl
from jax.experimental.pallas import tpu as pltpu
from jax.sharding import PartitionSpec as P

HEADS = 16
HEAD_DIM = 128
DILATION = 4
LANES = 128
SCALE = HEAD_DIM**-0.5
LOWEST = -1e30
LONG = 4 * 10**10
VMEM_LIMIT = 32 * 1024 * 1024
PICK_LIMIT = 53 * 1024 * 1024
NEAR_LIMIT = 54784 * 1024
F32, BF16 = jnp.float32, jnp.bfloat16
SHAPE = jax.ShapeDtypeStruct

NT = (((1,), (1,)), ((), ()))
TN = (((0,), (0,)), ((), ()))


def dot(a, b):
    return jnp.dot(a, b, preferred_element_type=F32)


def dot_nt(a, b):
    return lax.dot_general(a, b, NT, preferred_element_type=F32)


def dot_tn(a, b):
    return lax.dot_general(a, b, TN, preferred_element_type=F32)


def head_columns(head):
    return pl.ds(pl.multiple_of(head * HEAD_DIM, HEAD_DIM), HEAD_DIM)


def static_columns(index):
    return slice(index * HEAD_DIM, (index + 1) * HEAD_DIM)


def position(slots):
    width = lax.axis_size("seqo") // slots
    return lax.axis_index("seqi"), lax.axis_index("seqo") // width


def lanes_of(rows):
    return lax.broadcasted_iota(jnp.int32, (rows, LANES), 1)


def level_stats(operands):
    products = [(dot_nt(k, q) * SCALE, dot_nt(v, u)) for k, v, q, u in operands]
    tops = [jnp.max(s, axis=0, keepdims=True) for s, _ in products]
    weights = [jnp.exp(s - top) for (s, _), top in zip(products, tops)]
    totals = [jnp.sum(p, axis=0, keepdims=True) for p in weights]
    return [
        (top + jnp.log(total), jnp.sum(p * dp, axis=0, keepdims=True) / total)
        for (_, dp), top, p, total in zip(products, tops, weights, totals)
    ]


def merge_stats(ea, da, eb, db):
    top = jnp.maximum(ea, eb)
    wa, wb = jnp.exp(ea - top), jnp.exp(eb - top)
    total = wa + wb
    return top + jnp.log(total), (wa * da + wb * db) / total


def level_weights(operands, stats):
    products = [(dot_nt(k, q) * SCALE, dot_nt(v, u)) for k, v, q, u in operands]
    found = []
    for (s, dp), (lse, delta) in zip(products, stats):
        g = jnp.exp(s - lse)
        found.append((g.astype(BF16), (g * (dp - delta)).astype(BF16)))
    return found


def level_parts(operands, stats):
    found = level_weights(operands, stats)
    keyed = [
        (dot(ds, q) * SCALE, dot(p, u)) for (p, ds), (k, v, q, u) in zip(found, operands)
    ]
    queried = [
        (dot_tn(p, v), dot_tn(ds, k) * SCALE) for (p, ds), (k, v, q, u) in zip(found, operands)
    ]
    return [a + b for a, b in zip(queried, keyed)]


def pick_rows(ref, rows):
    quarter = rows // DILATION
    lane = lanes_of(quarter)
    picked = jnp.zeros((quarter, LANES), F32)
    for residue in range(DILATION):
        part = ref[pl.ds(residue, quarter, stride=DILATION), :]
        picked = jnp.where(lane % DILATION == residue, part, picked)
    return picked


def fetch(sources, buffers, sems):
    width = DILATION * HEAD_DIM
    groups = []
    for group in range(HEADS // DILATION):
        cols = pl.ds(group * width, width)
        groups.append(
            [
                pltpu.make_async_copy(
                    source.at[:, cols], buffers.at[which, :, cols], sems.at[which, group]
                )
                for which, source in enumerate(sources)
            ]
        )
        for copy in groups[-1]:
            copy.start()
    return groups


def pick_kernel(n_i, slots, *refs):
    sources, refs = refs[:4], refs[4:]
    mids, refs = refs[:n_i], refs[n_i:]
    fulls, refs = refs[:slots], refs[slots:]
    buffers, sems, wide, picked = refs
    rows = sources[0].shape[0]
    quarter = rows // DILATION
    pos, chip = position(slots)
    for group, copies in enumerate(fetch(sources, buffers, sems)):
        for which, copy in enumerate(copies):
            copy.wait()
            for residue in range(DILATION):
                head = group * DILATION + residue
                cols = static_columns(head)
                wide[which, head] = buffers[which, :, cols].astype(F32)
                rowset = wide[which, head, pl.ds(residue, quarter, stride=DILATION), :]
                picked[which, :, cols] = rowset.astype(BF16)
    width = slots * HEAD_DIM
    for d in range(n_i):
        start = pl.multiple_of((pos ^ d) * width, width)
        mids[d][...] = picked[:, :, pl.ds(start, width)]
    for m in range(slots):
        fulls[m][...] = buffers[:, :, head_columns(pos * slots + (chip ^ m))]


def near_operands(ref, group):
    heads = range(group * DILATION, (group + 1) * DILATION)
    return [[ref[which, :, static_columns(head)] for which in range(4)] for head in heads]


def near_stats_kernel(k_hbm, v_hbm, q_hbm, u_hbm, stats_ref, mid_ref, buffers, sems, turn):
    rows = q_hbm.shape[0]
    turn[...] = jnp.zeros_like(turn)
    for group, copies in enumerate(fetch((k_hbm, v_hbm, q_hbm, u_hbm), buffers, sems)):
        for copy in copies:
            copy.wait()
        for residue, (e, d) in enumerate(level_stats(near_operands(buffers, group))):
            head = group * DILATION + residue
            turn[head : head + 1, :] = e
            turn[HEADS + head : HEADS + head + 1, :] = d
    stats_ref[...] = turn[: 2 * HEADS, :]
    turn[...] = turn[...].T
    mid_ref[...] = pick_rows(turn, rows)


def pack_kernel(slots, *refs):
    packed_ref = refs[-1]
    for m, ref in enumerate(refs[:slots]):
        packed_ref[m] = ref[:2]


def far_keys(fulls, sibs, which):
    blocks = [ref[which] for ref in fulls]
    return jnp.concatenate(blocks + [ref[m, which] for ref in sibs for m in range(len(fulls))], axis=0)


def far_stats_kernel(slots, near_ref, *refs):
    fulls, sibs, xmsg_ref = refs[:slots], refs[slots:-1], refs[-1]
    keys, values = far_keys(fulls, sibs, 0), far_keys(fulls, sibs, 1)
    xmsg_ref[: 2 * slots] = near_ref[...]
    for m in range(slots):
        ((e, d),) = level_stats([(keys, values, fulls[m][2], fulls[m][3])])
        xmsg_ref[2 * slots + m : 2 * slots + m + 1, :] = e
        xmsg_ref[3 * slots + m : 3 * slots + m + 1, :] = d


def middle_operands(mids, slot):
    cols = static_columns(slot)
    return [jnp.concatenate([ref[which, :, cols] for ref in mids], axis=0) for which in range(4)]


def middle_stats_kernel(n_i, slots, *refs):
    mids, refs = in_order(refs[:n_i]), refs[n_i:]
    near_ref, nearmid_ref = refs[:2]
    refs = refs[2:]
    zmsgs, refs = refs[:n_i], refs[n_i:]
    joint_ref, stats_ref, turn, spread = refs
    quarter = nearmid_ref.shape[0]
    pos, _ = position(slots)
    turn[...] = jnp.zeros_like(turn)
    operands = [middle_operands(mids, slot) for slot in range(slots)]
    for slot, (e, d) in enumerate(level_stats(operands)):
        turn[slot : slot + 1, :] = e
        turn[slots + slot : slots + slot + 1, :] = d
    stats_ref[...] = turn[: 2 * slots, :]
    columns = turn[...].T
    lane = lanes_of(quarter)
    for d in range(n_i):
        chunk = pltpu.roll(columns[d * quarter : (d + 1) * quarter], 2 * HEADS, 1)
        zmsgs[d][...] = jnp.where(lane < 2 * HEADS, nearmid_ref[...], chunk)
    own = columns[:quarter]
    lane_residue = (pos * slots + lane % slots) % DILATION
    blank = jnp.where(lane < slots, LOWEST, 0.0)
    for residue in range(DILATION):
        spread[pl.ds(residue, quarter, stride=DILATION), :] = jnp.where(
            lane_residue == residue, own, blank
        )
    across = spread[...].T
    e, d = merge_stats(
        near_ref[pl.ds(pos * slots, slots), :],
        near_ref[pl.ds(HEADS + pos * slots, slots), :],
        across[:slots],
        across[slots : 2 * slots],
    )
    joint_ref[:slots] = e
    joint_ref[slots:] = d


def middle_parts_kernel(n_i, slots, *refs):
    mids, refs = in_order(refs[:n_i]), refs[n_i:]
    near_ref, stats_ref = refs[:2]
    refs = refs[2:]
    zmsgs, refs = refs[:n_i], refs[n_i:]
    xmsgs, refs = refs[:slots], refs[slots:]
    outs, refs = refs[:n_i], refs[n_i:]
    final_ref, far, turn, spread = refs
    quarter = zmsgs[0].shape[0]
    rows = quarter * DILATION
    pos, chip = position(slots)

    lane = lanes_of(quarter)
    mid = jnp.zeros((quarter, LANES), F32)
    for d in range(n_i):
        place = (pos ^ d) * slots
        e = pltpu.roll(zmsgs[d][...], (place + LANES - 2 * HEADS) % LANES, 1)
        de = pltpu.roll(zmsgs[d][...], (place + LANES - HEADS - slots) % LANES, 1)
        mid = jnp.where((lane >= place) & (lane < place + slots), e, mid)
        mid = jnp.where((lane >= HEADS + place) & (lane < HEADS + place + slots), de, mid)
    blank = jnp.where(lane < HEADS, LOWEST, 0.0)
    for residue in range(DILATION):
        spread[pl.ds(residue, quarter, stride=DILATION), :] = jnp.where(
            lane % DILATION == residue, mid, blank
        )
    across = spread[...].T
    far[:HEADS] = jnp.full((HEADS, rows), LOWEST, F32)
    far[HEADS:] = jnp.zeros((HEADS, rows), F32)
    for m in range(slots):
        head = pos * slots + (chip ^ m)
        far[pl.ds(head, 1), :] = xmsgs[m][2 * slots + m : 2 * slots + m + 1, :]
        far[pl.ds(HEADS + head, 1), :] = xmsgs[m][3 * slots + m : 3 * slots + m + 1, :]
    e, d = merge_stats(
        near_ref[:HEADS], near_ref[HEADS:], across[:HEADS], across[HEADS : 2 * HEADS]
    )
    e, d = merge_stats(e, d, far[:HEADS], far[HEADS:])
    final_ref[:HEADS] = e
    final_ref[HEADS:] = d

    spread[...] = jnp.zeros_like(spread)
    spread[: 2 * HEADS] = final_ref[...]
    spread[...] = spread[...].T
    own = pick_rows(spread, rows)
    turn[...] = jnp.concatenate([own] + [ref[...] for ref in zmsgs[1:]], axis=0).T
    owned = lax.broadcasted_iota(jnp.int32, (1, n_i * quarter), 1) < quarter
    operands = [middle_operands(mids, slot) for slot in range(slots)]
    merged = [
        merge_stats(
            turn[pl.ds(pos * slots + slot, 1), :],
            turn[pl.ds(HEADS + pos * slots + slot, 1), :],
            jnp.where(owned, LOWEST, stats_ref[slot : slot + 1, :]),
            stats_ref[slots + slot : slots + slot + 1, :],
        )
        for slot in range(slots)
    ]
    for slot, parts in enumerate(level_parts(operands, merged)):
        for which, part in enumerate(parts):
            part = part.astype(BF16)
            for d in range(n_i):
                outs[d][which, :, static_columns(slot)] = part[d * quarter : (d + 1) * quarter]


def far_parts_kernel(slots, width, *refs):
    fulls, refs = refs[:slots], refs[slots:]
    sibs, refs = refs[: width - 1], refs[width - 1 :]
    xmsgs, refs = refs[:slots], refs[slots:]
    final_ref, refs = refs[0], refs[1:]
    outs, refs = refs[:slots], refs[slots:]
    kvouts, refs = refs[: width - 1], refs[width - 1 :]
    weights, score_grads = refs
    rows = fulls[0].shape[1]
    pos, chip = position(slots)
    head = pos * slots + chip
    keys, values = far_keys(fulls, sibs, 0), far_keys(fulls, sibs, 1)
    for m in range(slots):
        if m == 0:
            lse, delta = final_ref[pl.ds(head, 1), :], final_ref[pl.ds(HEADS + head, 1), :]
        else:
            lse, delta = merge_stats(
                xmsgs[m][pl.ds(chip, 1), :],
                xmsgs[m][pl.ds(slots + chip, 1), :],
                xmsgs[0][2 * slots + m : 2 * slots + m + 1, :],
                xmsgs[0][3 * slots + m : 3 * slots + m + 1, :],
            )
        operands = (keys, values, fulls[m][2], fulls[m][3])
        ((p, ds),) = level_weights([operands], [(lse, delta)])
        outs[m][0] = dot_tn(p, values).astype(BF16)
        outs[m][1] = (dot_tn(ds, keys) * SCALE).astype(BF16)
        weights[:, m * rows : (m + 1) * rows] = p
        score_grads[:, m * rows : (m + 1) * rows] = ds
    queries = jnp.concatenate([ref[2] for ref in fulls], axis=0)
    ups = jnp.concatenate([ref[3] for ref in fulls], axis=0)
    key_part = (dot(score_grads[...], queries) * SCALE).astype(BF16)
    value_part = dot(weights[...], ups).astype(BF16)
    for index in range(width * slots):
        block = slice(index * rows, (index + 1) * rows)
        part, m = index // slots, index % slots
        if part == 0:
            outs[m][2], outs[m][3] = key_part[block], value_part[block]
        else:
            kvouts[part - 1][m, 0], kvouts[part - 1][m, 1] = key_part[block], value_part[block]


def far_sum_kernel(slots, *refs):
    own, refs = refs[:slots], refs[slots:]
    found, outs = refs[:-slots], refs[-slots:]
    for m in range(slots):
        outs[m][:2] = own[m][:2]
        total = own[m][2:].astype(F32)
        for ref in found:
            total += ref[m].astype(F32)
        outs[m][2:] = total.astype(BF16)


def near_parts_kernel(k_ref, v_ref, q_ref, u_ref, stats_ref, out_ref):
    for group in range(HEADS // DILATION):
        heads = range(group * DILATION, (group + 1) * DILATION)
        operands = [
            [ref[:, static_columns(head)] for ref in (k_ref, v_ref, q_ref, u_ref)] for head in heads
        ]
        stats = [
            (stats_ref[head : head + 1, :], stats_ref[HEADS + head : HEADS + head + 1, :])
            for head in heads
        ]
        for head, parts in zip(heads, level_parts(operands, stats)):
            for which, part in enumerate(parts):
                out_ref[which, head] = part


def final_kernel(n_i, slots, near_ref, *refs):
    mids, refs = (refs[0], *refs[n_i - 1 : 0 : -1]), refs[n_i:]
    fulls, refs = refs[:slots], refs[slots + 1 :]
    outs, (ready, sems) = refs[:4], refs[4:]
    rows = fulls[0].shape[1]
    quarter = rows // DILATION
    pos, chip = position(slots)
    row = lax.broadcasted_iota(jnp.int32, (rows, quarter), 0)
    taken = lax.broadcasted_iota(jnp.int32, (rows, quarter), 1) * DILATION

    def spread(d, slot):
        head = (pos ^ d) * slots + slot
        place = jnp.where(row == taken + head % DILATION, 1.0, 0.0).astype(BF16)
        cols = head_columns(slot) if d == 0 else static_columns(slot)
        picked = jnp.concatenate([mids[d][which, :, cols] for which in range(4)], axis=1)
        return head, dot(place, picked)

    copies = []
    for d in reversed(range(n_i)):
        found = [spread(d, chip ^ slot if d == 0 else slot) for slot in range(slots)]
        for slot, (head, parts) in enumerate(found):
            for which in range(4):
                total = near_ref[which, head] + parts[:, static_columns(which)]
                if d == 0:
                    total += fulls[slot][which].astype(F32)
                ready[which, :, head_columns(head)] = total.astype(BF16)
        width = slots * HEAD_DIM
        cols = pl.ds(pl.multiple_of((pos ^ d) * width, width), width)
        for which, out in enumerate(outs):
            copy = pltpu.make_async_copy(
                ready.at[which, :, cols], out.at[:, cols], sems.at[which, d]
            )
            copy.start()
            copies.append(copy)
    for copy in copies:
        copy.wait()


def settle_kernel(*refs):
    refs[-1][...] = jnp.zeros_like(refs[-1])


def call(kernel, name, outs, scratch, flops, operands, hbm_in=(), hbm_out=False, cheap=False, limit=VMEM_LIMIT):
    moved = sum(x.size * x.dtype.itemsize for x in tuple(operands) + tuple(outs))
    if cheap:
        flops, moved = 1, 1
    spaces = [pltpu.HBM if i in hbm_in else pltpu.VMEM for i in range(len(operands))]
    return pl.pallas_call(
        kernel,
        out_shape=tuple(outs),
        in_specs=[pl.BlockSpec(memory_space=space) for space in spaces],
        out_specs=tuple(
            pl.BlockSpec(memory_space=pltpu.HBM if hbm_out else pltpu.VMEM) for _ in outs
        ),
        scratch_shapes=scratch,
        compiler_params=pltpu.CompilerParams(vmem_limit_bytes=limit),
        cost_estimate=pl.CostEstimate(flops=flops, bytes_accessed=moved, transcendentals=0),
        name=name,
    )(*operands)


def far_first(pieces):
    return [*pieces[:2], *pieces[:1:-1]]


def in_order(pieces):
    return [*pieces[:2], *pieces[:1:-1]]


def swap(x, axis, n, mask):
    return lax.ppermute(x, axis, [(i, i ^ mask) for i in range(n)])


def local(query_rows, key_rows, value_rows, upstream):
    rows, features = query_rows.shape
    n_i, n_o = lax.axis_size("seqi"), lax.axis_size("seqo")
    slots = HEADS // n_i
    width = n_o // slots
    others = (width - 1) * slots
    quarter = rows // DILATION
    sources = (key_rows, value_rows, query_rows, upstream)
    unit = 2 * rows * rows * HEAD_DIM
    bind = functools.partial

    mid = SHAPE((4, quarter, slots * HEAD_DIM), BF16)
    full = SHAPE((4, rows, HEAD_DIM), BF16)
    half = SHAPE((slots, 2, rows, HEAD_DIM), BF16)
    square = pltpu.VMEM((LANES, rows), F32)

    def stats(count, lanes=rows):
        return SHAPE((count, lanes), F32)

    def swap_mids(pieces):
        found = {d: swap(pieces[d], "seqi", n_i, d) for d in reversed(range(1, n_i))}
        return [pieces[0]] + [found[d] for d in range(1, n_i)]

    def swap_fulls(pieces):
        return [pieces[0]] + [swap(pieces[m], "seqo", n_o, m * width) for m in range(1, slots)]

    buffers = [
        pltpu.VMEM((4, rows, features), BF16),
        pltpu.SemaphoreType.DMA((4, HEADS // DILATION)),
    ]
    pieces = call(
        bind(pick_kernel, n_i, slots),
        "pick",
        [mid] * n_i + [full] * slots,
        buffers
        + [
            pltpu.VMEM((4, HEADS, rows, HEAD_DIM), F32),
            pltpu.VMEM((4, quarter, features), BF16),
        ],
        unit,
        sources,
        hbm_in=range(4),
        limit=PICK_LIMIT,
    )
    mids = swap_mids(pieces[:n_i])
    fulls = swap_fulls(pieces[n_i:])

    near, nearmid = call(
        near_stats_kernel,
        "near_stats",
        [stats(2 * HEADS), stats(quarter, LANES)],
        buffers + [square],
        unit * HEADS * 2,
        sources,
        hbm_in=range(4),
        limit=NEAR_LIMIT,
    )
    (packed,) = call(bind(pack_kernel, slots), "pack", [half], [], unit, fulls + mids[1:] + [near])
    sibs = [swap(packed, "seqo", n_o, part) for part in range(1, width)]
    *zmsgs, joint, middle = call(
        bind(middle_stats_kernel, n_i, slots),
        "middle_stats",
        [SHAPE((quarter, LANES), F32)] * n_i
        + [stats(2 * slots), stats(2 * slots, n_i * quarter)],
        [pltpu.VMEM((LANES, n_i * quarter), F32), square],
        unit * slots * 2,
        far_first(mids) + [near, nearmid],
    )
    (xmsg,) = call(
        bind(far_stats_kernel, slots),
        "far_stats",
        [stats(4 * slots)],
        [],
        unit * n_o * slots * 2,
        [joint] + fulls + sibs,
    )
    zmsgs = swap_mids(zmsgs)
    xmsgs = swap_fulls([xmsg] * slots)

    *midparts, final = call(
        bind(middle_parts_kernel, n_i, slots),
        "middle_parts",
        [mid] * n_i + [stats(2 * HEADS)],
        [
            pltpu.VMEM((2 * HEADS, rows), F32),
            pltpu.VMEM((LANES, n_i * quarter), F32),
            square,
        ],
        unit * slots * 6,
        far_first(mids) + [near, middle] + zmsgs + xmsgs,
    )
    midparts = swap_mids(midparts)
    farparts = call(
        bind(far_parts_kernel, slots, width),
        "far_parts",
        [full] * slots + [half] * (width - 1),
        [pltpu.VMEM((n_o * rows, slots * rows), BF16)] * 2,
        unit * n_o * slots * 6,
        fulls + sibs + xmsgs + [final],
        cheap=True,
    )
    fullparts = call(
        bind(far_sum_kernel, slots),
        "far_sum",
        [full] * slots,
        [],
        unit,
        list(farparts[:slots])
        + [swap(x, "seqo", n_o, part + 1) for part, x in enumerate(farparts[slots:])],
        cheap=True,
    )
    fullparts = swap_fulls(fullparts)

    (nearparts,) = call(
        near_parts_kernel,
        "near_parts",
        [SHAPE((4, HEADS, rows, HEAD_DIM), F32)],
        [],
        LONG,
        sources + (final,),
    )
    (settled,) = call(
        settle_kernel, "settle_parts", [stats(8)], [], LONG, midparts[:0:-1]
    )
    return call(
        bind(final_kernel, n_i, slots),
        "final",
        [SHAPE((rows, features), BF16)] * 4,
        [pltpu.VMEM((4, rows, features), BF16), pltpu.SemaphoreType.DMA((4, n_i))],
        unit * HEADS,
        [nearparts, midparts[0]] + midparts[:0:-1] + fullparts + [settled],
        hbm_out=True,
    )


def solution(mesh):
    rows = P(("seqo", "seqi"), None)
    return jax.shard_map(
        local,
        mesh=mesh,
        in_specs=(rows,) * 4,
        out_specs=(rows,) * 4,
        check_vma=False,
    )
```

```python
import functools

import jax
import jax.numpy as jnp
from jax import lax
from jax.experimental import pallas as pl
from jax.experimental.pallas import tpu as pltpu
from jax.sharding import PartitionSpec as P

HEADS = 16
HEAD_DIM = 128
DILATION = 4
LANES = 128
SCALE = HEAD_DIM**-0.5
LOWEST = -1e30
LONG = 4 * 10**10
VMEM_LIMIT = 32 * 1024 * 1024
PICK_LIMIT = 53 * 1024 * 1024
NEAR_LIMIT = 54784 * 1024
F32, BF16 = jnp.float32, jnp.bfloat16
SHAPE = jax.ShapeDtypeStruct

NT = (((1,), (1,)), ((), ()))
TN = (((0,), (0,)), ((), ()))


def dot(a, b):
    return jnp.dot(a, b, preferred_element_type=F32)


def dot_nt(a, b):
    return lax.dot_general(a, b, NT, preferred_element_type=F32)


def dot_tn(a, b):
    return lax.dot_general(a, b, TN, preferred_element_type=F32)


def head_columns(head):
    return pl.ds(pl.multiple_of(head * HEAD_DIM, HEAD_DIM), HEAD_DIM)


def static_columns(index):
    return slice(index * HEAD_DIM, (index + 1) * HEAD_DIM)


def position(slots):
    width = lax.axis_size("seqo") // slots
    return lax.axis_index("seqi"), lax.axis_index("seqo") // width


def lanes_of(rows):
    return lax.broadcasted_iota(jnp.int32, (rows, LANES), 1)


def level_stats(operands):
    products = [(dot_nt(k, q) * SCALE, dot_nt(v, u)) for k, v, q, u in operands]
    tops = [jnp.max(s, axis=0, keepdims=True) for s, _ in products]
    weights = [jnp.exp(s - top) for (s, _), top in zip(products, tops)]
    totals = [jnp.sum(p, axis=0, keepdims=True) for p in weights]
    return [
        (top + jnp.log(total), jnp.sum(p * dp, axis=0, keepdims=True) / total)
        for (_, dp), top, p, total in zip(products, tops, weights, totals)
    ]


def merge_stats(ea, da, eb, db):
    top = jnp.maximum(ea, eb)
    wa, wb = jnp.exp(ea - top), jnp.exp(eb - top)
    total = wa + wb
    return top + jnp.log(total), (wa * da + wb * db) / total


def level_weights(operands, stats):
    products = [(dot_nt(k, q) * SCALE, dot_nt(v, u)) for k, v, q, u in operands]
    found = []
    for (s, dp), (lse, delta) in zip(products, stats):
        g = jnp.exp(s - lse)
        found.append((g.astype(BF16), (g * (dp - delta)).astype(BF16)))
    return found


def level_parts(operands, stats):
    found = level_weights(operands, stats)
    keyed = [
        (dot(ds, q) * SCALE, dot(p, u)) for (p, ds), (k, v, q, u) in zip(found, operands)
    ]
    queried = [
        (dot_tn(p, v), dot_tn(ds, k) * SCALE) for (p, ds), (k, v, q, u) in zip(found, operands)
    ]
    return [a + b for a, b in zip(queried, keyed)]


def pick_rows(ref, rows):
    quarter = rows // DILATION
    lane = lanes_of(quarter)
    picked = jnp.zeros((quarter, LANES), F32)
    for residue in range(DILATION):
        part = ref[pl.ds(residue, quarter, stride=DILATION), :]
        picked = jnp.where(lane % DILATION == residue, part, picked)
    return picked


def fetch(sources, buffers, sems):
    width = DILATION * HEAD_DIM
    groups = []
    for group in range(HEADS // DILATION):
        cols = pl.ds(group * width, width)
        groups.append(
            [
                pltpu.make_async_copy(
                    source.at[:, cols], buffers.at[which, :, cols], sems.at[which, group]
                )
                for which, source in enumerate(sources)
            ]
        )
        for copy in groups[-1]:
            copy.start()
    return groups


def split(x):
    high = x.astype(BF16).astype(F32)
    rest = x - high
    middle = rest.astype(BF16).astype(F32)
    low = rest - middle
    return (high + pltpu.roll(middle, 2 * HEADS, 1) + pltpu.roll(low, 4 * HEADS, 1)).astype(BF16)


def join(ref):
    x = ref[ref.shape[0] - 1].astype(F32)
    x = x + (pltpu.roll(x, LANES - 2 * HEADS, 1) + pltpu.roll(x, LANES - 4 * HEADS, 1))
    return jnp.where(lanes_of(x.shape[0]) < 2 * HEADS, x, 0.0)


def pick_kernel(n_i, slots, *refs):
    sources, refs = refs[:4], refs[4:]
    mids, refs = refs[:n_i], refs[n_i:]
    fulls, refs = refs[:slots], refs[slots:]
    stats_ref, buffers, sems, wide, picked, turn = refs
    rows = sources[0].shape[0]
    quarter = rows // DILATION
    pos, chip = position(slots)
    turn[...] = jnp.zeros_like(turn)
    for group, copies in enumerate(fetch(sources, buffers, sems)):
        for which, copy in enumerate(copies):
            copy.wait()
            for residue in range(DILATION):
                head = group * DILATION + residue
                wide[which, head] = buffers[which, :, static_columns(head)].astype(F32)
                rowset = wide[which, head, pl.ds(residue, quarter, stride=DILATION), :]
                picked[head // slots, which * slots + head % slots] = rowset.astype(BF16)
        heads = range(group * DILATION, (group + 1) * DILATION)
        operands = [[buffers[which, :, static_columns(head)] for which in range(4)] for head in heads]
        for head, (e, d) in zip(heads, level_stats(operands)):
            turn[head : head + 1, :] = e
            turn[HEADS + head : HEADS + head + 1, :] = d
    stats_ref[...] = turn[: 2 * HEADS, :]
    turn[...] = turn[...].T
    near = split(pick_rows(turn, rows))
    for d in range(n_i):
        mids[d][: 4 * slots] = picked[pos ^ d]
        mids[d][4 * slots] = near
    for m in range(slots):
        fulls[m][...] = buffers[:, :, head_columns(pos * slots + (chip ^ m))]


def pack_kernel(slots, *refs):
    packed_ref = refs[-1]
    for m, ref in enumerate(refs[:slots]):
        packed_ref[m] = ref[:2]


def far_keys(fulls, sibs, which):
    blocks = [ref[which] for ref in fulls]
    return jnp.concatenate(blocks + [ref[m, which] for ref in sibs for m in range(len(fulls))], axis=0)


def far_stats_kernel(slots, near_ref, *refs):
    fulls, sibs, xmsg_ref = refs[:slots], refs[slots:-1], refs[-1]
    keys, values = far_keys(fulls, sibs, 0), far_keys(fulls, sibs, 1)
    xmsg_ref[: 2 * slots] = near_ref[...]
    for m in range(slots):
        ((e, d),) = level_stats([(keys, values, fulls[m][2], fulls[m][3])])
        xmsg_ref[2 * slots + m : 2 * slots + m + 1, :] = e
        xmsg_ref[3 * slots + m : 3 * slots + m + 1, :] = d


def middle_operands(slots, mids, slot):
    return [
        jnp.concatenate([ref[which * slots + slot] for ref in mids], axis=0) for which in range(4)
    ]


def middle_stats_kernel(n_i, slots, *refs):
    mids, refs = in_order(refs[:n_i]), refs[n_i:]
    near_ref, joint_ref, stats_ref, columns_ref, turn, spread = refs
    rows = near_ref.shape[1]
    quarter = rows // DILATION
    pos, _ = position(slots)
    turn[...] = jnp.zeros_like(turn)
    operands = [middle_operands(slots, mids, slot) for slot in range(slots)]
    for slot, (e, d) in enumerate(level_stats(operands)):
        turn[slot : slot + 1, :] = e
        turn[slots + slot : slots + slot + 1, :] = d
    stats_ref[...] = turn[: 2 * slots, :]
    columns_ref[...] = turn[...].T
    lane = lanes_of(quarter)
    lane_residue = (pos * slots + lane % slots) % DILATION
    blank = jnp.where(lane < slots, LOWEST, 0.0)
    for residue in range(DILATION):
        spread[pl.ds(residue, quarter, stride=DILATION), :] = jnp.where(
            lane_residue == residue, columns_ref[:quarter], blank
        )
    across = spread[...].T
    e, d = merge_stats(
        near_ref[pl.ds(pos * slots, slots), :],
        near_ref[pl.ds(HEADS + pos * slots, slots), :],
        across[:slots],
        across[slots : 2 * slots],
    )
    joint_ref[:slots] = e
    joint_ref[slots:] = d


def middle_parts_kernel(n_i, slots, *refs):
    mids, refs = in_order(refs[:n_i]), refs[n_i:]
    joint_ref, stats_ref, columns_ref = refs[:3]
    refs = refs[3:]
    xmsgs, refs = refs[:slots], refs[slots:]
    outs, (far, turn, spread) = refs[:n_i], refs[n_i:]
    rows = joint_ref.shape[1]
    quarter = rows // DILATION
    pos, chip = position(slots)
    for m in range(slots):
        far[pl.ds(chip ^ m, 1), :] = xmsgs[m][2 * slots + m : 2 * slots + m + 1, :]
        far[pl.ds(slots + (chip ^ m), 1), :] = xmsgs[m][3 * slots + m : 3 * slots + m + 1, :]
    e, d = merge_stats(joint_ref[:slots], joint_ref[slots:], far[:slots], far[slots:])
    spread[...] = jnp.zeros_like(spread)
    spread[pl.ds(pos * slots, slots), :] = e
    spread[pl.ds(HEADS + pos * slots, slots), :] = d
    spread[...] = spread[...].T
    own = pick_rows(spread, rows)
    turn[...] = jnp.concatenate([own] + [join(ref) for ref in mids[1:]], axis=0).T
    owned = lax.broadcasted_iota(jnp.int32, (1, n_i * quarter), 1) < quarter
    operands = [middle_operands(slots, mids, slot) for slot in range(slots)]
    merged = [
        merge_stats(
            turn[pl.ds(pos * slots + slot, 1), :],
            turn[pl.ds(HEADS + pos * slots + slot, 1), :],
            jnp.where(owned, LOWEST, stats_ref[slot : slot + 1, :]),
            stats_ref[slots + slot : slots + slot + 1, :],
        )
        for slot in range(slots)
    ]
    for slot, parts in enumerate(level_parts(operands, merged)):
        for which, part in enumerate(parts):
            part = part.astype(BF16)
            for d in range(n_i):
                outs[d][which * slots + slot] = part[d * quarter : (d + 1) * quarter]
    for d in range(n_i):
        outs[d][4 * slots] = split(columns_ref[d * quarter : (d + 1) * quarter])


def far_parts_kernel(slots, width, *refs):
    fulls, refs = refs[:slots], refs[slots:]
    sibs, refs = refs[: width - 1], refs[width - 1 :]
    xmsgs, refs = refs[:slots], refs[slots + 1 :]
    outs, refs = refs[:slots], refs[slots:]
    kvouts, refs = refs[: width - 1], refs[width - 1 :]
    weights, score_grads = refs
    rows = fulls[0].shape[1]
    _, chip = position(slots)
    keys, values = far_keys(fulls, sibs, 0), far_keys(fulls, sibs, 1)
    for m in range(slots):
        lse, delta = merge_stats(
            xmsgs[m][pl.ds(chip, 1), :],
            xmsgs[m][pl.ds(slots + chip, 1), :],
            xmsgs[0][2 * slots + m : 2 * slots + m + 1, :],
            xmsgs[0][3 * slots + m : 3 * slots + m + 1, :],
        )
        operands = (keys, values, fulls[m][2], fulls[m][3])
        ((p, ds),) = level_weights([operands], [(lse, delta)])
        outs[m][0] = dot_tn(p, values).astype(BF16)
        outs[m][1] = (dot_tn(ds, keys) * SCALE).astype(BF16)
        weights[:, m * rows : (m + 1) * rows] = p
        score_grads[:, m * rows : (m + 1) * rows] = ds
    queries = jnp.concatenate([ref[2] for ref in fulls], axis=0)
    ups = jnp.concatenate([ref[3] for ref in fulls], axis=0)
    key_part = (dot(score_grads[...], queries) * SCALE).astype(BF16)
    value_part = dot(weights[...], ups).astype(BF16)
    for index in range(width * slots):
        block = slice(index * rows, (index + 1) * rows)
        part, m = index // slots, index % slots
        if part == 0:
            outs[m][2], outs[m][3] = key_part[block], value_part[block]
        else:
            kvouts[part - 1][m, 0], kvouts[part - 1][m, 1] = key_part[block], value_part[block]


def far_sum_kernel(slots, *refs):
    own, refs = refs[:slots], refs[slots:]
    found, outs = refs[: -slots - 1], refs[-slots:]
    for m in range(slots):
        outs[m][:2] = own[m][:2]
        total = own[m][2:].astype(F32)
        for ref in found:
            total += ref[m].astype(F32)
        outs[m][2:] = total.astype(BF16)


def near_parts_kernel(n_i, slots, *refs):
    sources, near_ref, refs = refs[:4], refs[4], refs[5:]
    mids, refs = in_order(refs[:n_i]), refs[n_i:]
    xmsgs, (out_ref, stats_ref, spread) = refs[:slots], refs[slots:]
    rows = near_ref.shape[1]
    quarter = rows // DILATION
    pos, chip = position(slots)
    lane = lanes_of(quarter)
    mid = jnp.zeros((quarter, LANES), F32)
    for d in range(n_i):
        place = (pos ^ d) * slots
        found = join(mids[d])
        e = pltpu.roll(found, place, 1)
        de = pltpu.roll(found, place + HEADS - slots, 1)
        mid = jnp.where((lane >= place) & (lane < place + slots), e, mid)
        mid = jnp.where((lane >= HEADS + place) & (lane < HEADS + place + slots), de, mid)
    blank = jnp.where(lane < HEADS, LOWEST, 0.0)
    for residue in range(DILATION):
        spread[pl.ds(residue, quarter, stride=DILATION), :] = jnp.where(
            lane % DILATION == residue, mid, blank
        )
    across = spread[...].T
    stats_ref[:HEADS] = jnp.full((HEADS, rows), LOWEST, F32)
    stats_ref[HEADS:] = jnp.zeros((HEADS, rows), F32)
    for m in range(slots):
        head = pos * slots + (chip ^ m)
        stats_ref[pl.ds(head, 1), :] = xmsgs[m][2 * slots + m : 2 * slots + m + 1, :]
        stats_ref[pl.ds(HEADS + head, 1), :] = xmsgs[m][3 * slots + m : 3 * slots + m + 1, :]
    e, d = merge_stats(
        near_ref[:HEADS], near_ref[HEADS:], across[:HEADS], across[HEADS : 2 * HEADS]
    )
    e, d = merge_stats(e, d, stats_ref[:HEADS], stats_ref[HEADS:])
    stats_ref[:HEADS] = e
    stats_ref[HEADS:] = d
    for group in range(HEADS // DILATION):
        heads = range(group * DILATION, (group + 1) * DILATION)
        operands = [
            [ref[:, static_columns(head)] for ref in sources] for head in heads
        ]
        stats = [
            (stats_ref[head : head + 1, :], stats_ref[HEADS + head : HEADS + head + 1, :])
            for head in heads
        ]
        for head, parts in zip(heads, level_parts(operands, stats)):
            for which, part in enumerate(parts):
                out_ref[which, head] = part


def final_kernel(n_i, slots, near_ref, *refs):
    mids, refs = in_order(refs[:n_i]), refs[n_i:]
    fulls, refs = (refs[0], *refs[slots - 1 : 0 : -1]), refs[slots:]
    outs, (ready, sems) = refs[:4], refs[4:]
    rows = fulls[0].shape[1]
    quarter = rows // DILATION
    pos, chip = position(slots)
    row = lax.broadcasted_iota(jnp.int32, (rows, quarter), 0)
    taken = lax.broadcasted_iota(jnp.int32, (rows, quarter), 1) * DILATION

    def spread(d, slot):
        head = (pos ^ d) * slots + slot
        place = jnp.where(row == taken + head % DILATION, 1.0, 0.0).astype(BF16)
        picked = jnp.concatenate([mids[d][which * slots + slot] for which in range(4)], axis=1)
        return head, dot(place, picked)

    copies = []
    for d in reversed(range(n_i)):
        found = [spread(d, chip ^ slot if d == 0 else slot) for slot in range(slots)]
        for slot, (head, parts) in enumerate(found):
            for which in range(4):
                total = near_ref[which, head] + parts[:, static_columns(which)]
                if d == 0:
                    total += fulls[slot][which].astype(F32)
                ready[which, :, head_columns(head)] = total.astype(BF16)
        width = slots * HEAD_DIM
        cols = pl.ds(pl.multiple_of((pos ^ d) * width, width), width)
        for which, out in enumerate(outs):
            copy = pltpu.make_async_copy(
                ready.at[which, :, cols], out.at[:, cols], sems.at[which, d]
            )
            copy.start()
            copies.append(copy)
    for copy in copies:
        copy.wait()


def settle_kernel(*refs):
    refs[-1][...] = jnp.zeros_like(refs[-1])


def call(kernel, name, outs, scratch, flops, operands, hbm_in=(), hbm_out=False, cheap=False, limit=VMEM_LIMIT):
    moved = sum(x.size * x.dtype.itemsize for x in tuple(operands) + tuple(outs))
    if cheap:
        flops, moved = 1, 1
    spaces = [pltpu.HBM if i in hbm_in else pltpu.VMEM for i in range(len(operands))]
    return pl.pallas_call(
        kernel,
        out_shape=tuple(outs),
        in_specs=[pl.BlockSpec(memory_space=space) for space in spaces],
        out_specs=tuple(
            pl.BlockSpec(memory_space=pltpu.HBM if hbm_out else pltpu.VMEM) for _ in outs
        ),
        scratch_shapes=scratch,
        compiler_params=pltpu.CompilerParams(vmem_limit_bytes=limit),
        cost_estimate=pl.CostEstimate(flops=flops, bytes_accessed=moved, transcendentals=0),
        name=name,
    )(*operands)


def far_first(pieces):
    return [*pieces[:2], *pieces[:1:-1]]


def in_order(pieces):
    return [*pieces[:2], *pieces[:1:-1]]


def swap(x, axis, n, mask):
    return lax.ppermute(x, axis, [(i, i ^ mask) for i in range(n)])


def local(query_rows, key_rows, value_rows, upstream):
    rows, features = query_rows.shape
    n_i, n_o = lax.axis_size("seqi"), lax.axis_size("seqo")
    slots = HEADS // n_i
    width = n_o // slots
    others = (width - 1) * slots
    quarter = rows // DILATION
    sources = (key_rows, value_rows, query_rows, upstream)
    unit = 2 * rows * rows * HEAD_DIM
    bind = functools.partial

    mid = SHAPE((4 * slots + 1, quarter, HEAD_DIM), BF16)
    full = SHAPE((4, rows, HEAD_DIM), BF16)
    half = SHAPE((slots, 2, rows, HEAD_DIM), BF16)
    square = pltpu.VMEM((LANES, rows), F32)

    def stats(count, lanes=rows):
        return SHAPE((count, lanes), F32)

    def swap_mids(pieces):
        found = {d: swap(pieces[d], "seqi", n_i, d) for d in reversed(range(1, n_i))}
        return [pieces[0]] + [found[d] for d in range(1, n_i)]

    def swap_fulls(pieces):
        return [pieces[0]] + [swap(pieces[m], "seqo", n_o, m * width) for m in range(1, slots)]

    pieces = call(
        bind(pick_kernel, n_i, slots),
        "pick",
        [mid] * n_i + [full] * slots + [stats(2 * HEADS)],
        [
            pltpu.VMEM((4, rows, features), BF16),
            pltpu.SemaphoreType.DMA((4, HEADS // DILATION)),
            pltpu.VMEM((4, HEADS, rows, HEAD_DIM), F32),
            pltpu.VMEM((n_i, 4 * slots, quarter, HEAD_DIM), BF16),
            square,
        ],
        unit * HEADS * 2,
        sources,
        hbm_in=range(4),
        limit=PICK_LIMIT,
    )
    mids = swap_mids(pieces[:n_i])
    fulls = swap_fulls(pieces[n_i : n_i + slots])
    near = pieces[-1]

    (arrived,) = call(settle_kernel, "arrive", [stats(8)], [], LONG, far_first(mids)[1:])
    (packed,) = call(bind(pack_kernel, slots), "pack", [half], [], unit, fulls + [arrived])
    sibs = [swap(packed, "seqo", n_o, part) for part in range(1, width)]
    joint, middle, columns = call(
        bind(middle_stats_kernel, n_i, slots),
        "middle_stats",
        [stats(2 * slots), stats(2 * slots, n_i * quarter), stats(n_i * quarter, LANES)],
        [pltpu.VMEM((LANES, n_i * quarter), F32), square],
        unit * slots * 2,
        far_first(mids) + [near],
    )
    (xmsg,) = call(
        bind(far_stats_kernel, slots),
        "far_stats",
        [stats(4 * slots)],
        [],
        unit * n_o * slots * 2,
        [joint] + fulls + sibs,
    )
    xmsgs = swap_fulls([xmsg] * slots)

    midparts = call(
        bind(middle_parts_kernel, n_i, slots),
        "middle_parts",
        [mid] * n_i,
        [pltpu.VMEM((2 * slots, rows), F32), pltpu.VMEM((LANES, n_i * quarter), F32), square],
        unit * slots * 6,
        far_first(mids) + [joint, middle, columns] + xmsgs,
    )
    midparts = swap_mids(midparts)
    farparts = call(
        bind(far_parts_kernel, slots, width),
        "far_parts",
        [full] * slots + [half] * (width - 1),
        [pltpu.VMEM((n_o * rows, slots * rows), BF16)] * 2,
        unit * n_o * slots * 6,
        fulls + sibs + xmsgs + [midparts[0]],
        cheap=True,
    )
    (settled,) = call(settle_kernel, "settle", [stats(8)], [], LONG, [xmsg])
    fullparts = call(
        bind(far_sum_kernel, slots),
        "far_sum",
        [full] * slots,
        [],
        unit,
        list(farparts[:slots])
        + [swap(x, "seqo", n_o, part + 1) for part, x in enumerate(farparts[slots:])]
        + [settled],
        cheap=True,
    )
    fullparts = swap_fulls(fullparts)

    (nearparts,) = call(
        bind(near_parts_kernel, n_i, slots),
        "near_parts",
        [SHAPE((4, HEADS, rows, HEAD_DIM), F32)],
        [pltpu.VMEM((2 * HEADS, rows), F32), square],
        LONG,
        [*sources, near] + far_first(midparts) + xmsgs,
    )
    return call(
        bind(final_kernel, n_i, slots),
        "final",
        [SHAPE((rows, features), BF16)] * 4,
        [pltpu.VMEM((4, rows, features), BF16), pltpu.SemaphoreType.DMA((4, n_i))],
        unit * HEADS,
        [nearparts] + far_first(midparts) + [fullparts[0]] + fullparts[:0:-1],
        hbm_out=True,
    )


def solution(mesh):
    rows = P(("seqo", "seqi"), None)
    return jax.shard_map(
        local,
        mesh=mesh,
        in_specs=(rows,) * 4,
        out_specs=(rows,) * 4,
        check_vma=False,
    )
```

```python
import functools

import jax
import jax.numpy as jnp
from jax import lax
from jax.experimental import pallas as pl
from jax.experimental.pallas import tpu as pltpu
from jax.sharding import PartitionSpec as P

HEADS = 16
HEAD_DIM = 128
DILATION = 4
LANES = 128
SCALE = HEAD_DIM**-0.5
LOWEST = -1e30
LONG = 4 * 10**10
SHORT = 2 * 10**9
VMEM_LIMIT = 32 * 1024 * 1024
PICK_LIMIT = 53 * 1024 * 1024
NEAR_LIMIT = 54784 * 1024
F32, BF16 = jnp.float32, jnp.bfloat16
SHAPE = jax.ShapeDtypeStruct

NT = (((1,), (1,)), ((), ()))
TN = (((0,), (0,)), ((), ()))


def dot(a, b):
    return jnp.dot(a, b, preferred_element_type=F32)


def dot_nt(a, b):
    return lax.dot_general(a, b, NT, preferred_element_type=F32)


def dot_tn(a, b):
    return lax.dot_general(a, b, TN, preferred_element_type=F32)


def head_columns(head):
    return pl.ds(pl.multiple_of(head * HEAD_DIM, HEAD_DIM), HEAD_DIM)


def static_columns(index):
    return slice(index * HEAD_DIM, (index + 1) * HEAD_DIM)


def position(slots):
    width = lax.axis_size("seqo") // slots
    return lax.axis_index("seqi"), lax.axis_index("seqo") // width


def lanes_of(rows):
    return lax.broadcasted_iota(jnp.int32, (rows, LANES), 1)


def level_stats(operands):
    products = [(dot_nt(k, q) * SCALE, dot_nt(v, u)) for k, v, q, u in operands]
    tops = [jnp.max(s, axis=0, keepdims=True) for s, _ in products]
    weights = [jnp.exp(s - top) for (s, _), top in zip(products, tops)]
    totals = [jnp.sum(p, axis=0, keepdims=True) for p in weights]
    return [
        (top + jnp.log(total), jnp.sum(p * dp, axis=0, keepdims=True) / total)
        for (_, dp), top, p, total in zip(products, tops, weights, totals)
    ]


def merge_stats(ea, da, eb, db):
    top = jnp.maximum(ea, eb)
    wa, wb = jnp.exp(ea - top), jnp.exp(eb - top)
    total = wa + wb
    return top + jnp.log(total), (wa * da + wb * db) / total


def level_weights(operands, stats):
    products = [(dot_nt(k, q) * SCALE, dot_nt(v, u)) for k, v, q, u in operands]
    found = []
    for (s, dp), (lse, delta) in zip(products, stats):
        g = jnp.exp(s - lse)
        found.append((g.astype(BF16), (g * (dp - delta)).astype(BF16)))
    return found


def level_parts(operands, stats):
    found = level_weights(operands, stats)
    keyed = [
        (dot(ds, q) * SCALE, dot(p, u)) for (p, ds), (k, v, q, u) in zip(found, operands)
    ]
    queried = [
        (dot_tn(p, v), dot_tn(ds, k) * SCALE) for (p, ds), (k, v, q, u) in zip(found, operands)
    ]
    return [a + b for a, b in zip(queried, keyed)]


def pick_rows(ref, rows):
    quarter = rows // DILATION
    lane = lanes_of(quarter)
    picked = jnp.zeros((quarter, LANES), F32)
    for residue in range(DILATION):
        part = ref[pl.ds(residue, quarter, stride=DILATION), :]
        picked = jnp.where(lane % DILATION == residue, part, picked)
    return picked


def fetch(sources, buffers, sems):
    width = DILATION * HEAD_DIM
    groups = []
    for group in range(HEADS // DILATION):
        cols = pl.ds(group * width, width)
        groups.append(
            [
                pltpu.make_async_copy(
                    source.at[:, cols], buffers.at[which, :, cols], sems.at[which, group]
                )
                for which, source in enumerate(sources)
            ]
        )
        for copy in groups[-1]:
            copy.start()
    return groups


def split(x):
    high = x.astype(BF16).astype(F32)
    rest = x - high
    middle = rest.astype(BF16).astype(F32)
    low = rest - middle
    return (high + pltpu.roll(middle, 2 * HEADS, 1) + pltpu.roll(low, 4 * HEADS, 1)).astype(BF16)


def join(ref):
    x = ref[ref.shape[0] - 1].astype(F32)
    x = x + (pltpu.roll(x, LANES - 2 * HEADS, 1) + pltpu.roll(x, LANES - 4 * HEADS, 1))
    return jnp.where(lanes_of(x.shape[0]) < 2 * HEADS, x, 0.0)


def pick_kernel(n_i, slots, *refs):
    sources, refs = refs[:4], refs[4:]
    mids, refs = refs[:n_i], refs[n_i:]
    fulls, refs = refs[:slots], refs[slots:]
    stats_ref, buffers, sems, wide, picked, turn = refs
    rows = sources[0].shape[0]
    quarter = rows // DILATION
    pos, chip = position(slots)
    turn[...] = jnp.zeros_like(turn)
    for group, copies in enumerate(fetch(sources, buffers, sems)):
        for which, copy in enumerate(copies):
            copy.wait()
            for residue in range(DILATION):
                head = group * DILATION + residue
                wide[which, head] = buffers[which, :, static_columns(head)].astype(F32)
                rowset = wide[which, head, pl.ds(residue, quarter, stride=DILATION), :]
                picked[head // slots, which * slots + head % slots] = rowset.astype(BF16)
        heads = range(group * DILATION, (group + 1) * DILATION)
        operands = [[buffers[which, :, static_columns(head)] for which in range(4)] for head in heads]
        for head, (e, d) in zip(heads, level_stats(operands)):
            turn[head : head + 1, :] = e
            turn[HEADS + head : HEADS + head + 1, :] = d
    stats_ref[...] = turn[: 2 * HEADS, :]
    turn[...] = turn[...].T
    near = split(pick_rows(turn, rows))
    for d in range(n_i):
        mids[d][: 4 * slots] = picked[pos ^ d]
        mids[d][4 * slots] = near
    for m in range(slots):
        fulls[m][...] = buffers[:, :, head_columns(pos * slots + (chip ^ m))]


def pack_kernel(slots, *refs):
    packed_ref = refs[-1]
    for m, ref in enumerate(refs[:slots]):
        packed_ref[m] = ref[:2]


def far_keys(fulls, sibs, which):
    blocks = [ref[which] for ref in fulls]
    return jnp.concatenate(blocks + [ref[m, which] for ref in sibs for m in range(len(fulls))], axis=0)


def far_stats_kernel(slots, *refs):
    fulls, sibs, stats_ref = refs[:slots], refs[slots:-2], refs[-1]
    keys, values = far_keys(fulls, sibs, 0), far_keys(fulls, sibs, 1)
    for m in range(slots):
        ((e, d),) = level_stats([(keys, values, fulls[m][2], fulls[m][3])])
        stats_ref[m : m + 1, :] = e
        stats_ref[slots + m : slots + m + 1, :] = d


def middle_operands(slots, mids, slot):
    return [
        jnp.concatenate([ref[which * slots + slot] for ref in mids], axis=0) for which in range(4)
    ]


def middle_stats_kernel(n_i, slots, *refs):
    mids, refs = (refs[0], *refs[n_i - 1 : 0 : -1]), refs[n_i:]
    near_ref, far_ref, xmsg_ref, stats_ref, columns_ref, turn, spread = refs
    rows = near_ref.shape[1]
    quarter = rows // DILATION
    pos, _ = position(slots)
    turn[...] = jnp.zeros_like(turn)
    operands = [middle_operands(slots, mids, slot) for slot in range(slots)]
    for slot, (e, d) in enumerate(level_stats(operands)):
        turn[slot : slot + 1, :] = e
        turn[slots + slot : slots + slot + 1, :] = d
    stats_ref[...] = turn[: 2 * slots, :]
    columns_ref[...] = turn[...].T
    lane = lanes_of(quarter)
    lane_residue = (pos * slots + lane % slots) % DILATION
    blank = jnp.where(lane < slots, LOWEST, 0.0)
    for residue in range(DILATION):
        spread[pl.ds(residue, quarter, stride=DILATION), :] = jnp.where(
            lane_residue == residue, columns_ref[:quarter], blank
        )
    across = spread[...].T
    e, d = merge_stats(
        near_ref[pl.ds(pos * slots, slots), :],
        near_ref[pl.ds(HEADS + pos * slots, slots), :],
        across[:slots],
        across[slots : 2 * slots],
    )
    xmsg_ref[:slots] = e
    xmsg_ref[slots : 2 * slots] = d
    xmsg_ref[2 * slots :] = far_ref[...]


def middle_parts_kernel(n_i, slots, *refs):
    mids, refs = (refs[0], *refs[n_i - 1 : 0 : -1]), refs[n_i:]
    stats_ref, columns_ref = refs[:2]
    refs = refs[2:]
    xmsgs, refs = refs[:slots], refs[slots:]
    outs, (far, turn, spread) = refs[:n_i], refs[n_i:]
    rows = xmsgs[0].shape[1]
    quarter = rows // DILATION
    pos, chip = position(slots)
    for m in range(slots):
        far[pl.ds(chip ^ m, 1), :] = xmsgs[m][2 * slots + m : 2 * slots + m + 1, :]
        far[pl.ds(slots + (chip ^ m), 1), :] = xmsgs[m][3 * slots + m : 3 * slots + m + 1, :]
    e, d = merge_stats(
        xmsgs[0][:slots], xmsgs[0][slots : 2 * slots], far[:slots], far[slots:]
    )
    spread[...] = jnp.zeros_like(spread)
    spread[pl.ds(pos * slots, slots), :] = e
    spread[pl.ds(HEADS + pos * slots, slots), :] = d
    spread[...] = spread[...].T
    own = pick_rows(spread, rows)
    turn[...] = jnp.concatenate([own] + [join(ref) for ref in mids[1:]], axis=0).T
    owned = lax.broadcasted_iota(jnp.int32, (1, n_i * quarter), 1) < quarter
    operands = [middle_operands(slots, mids, slot) for slot in range(slots)]
    merged = [
        merge_stats(
            turn[pl.ds(pos * slots + slot, 1), :],
            turn[pl.ds(HEADS + pos * slots + slot, 1), :],
            jnp.where(owned, LOWEST, stats_ref[slot : slot + 1, :]),
            stats_ref[slots + slot : slots + slot + 1, :],
        )
        for slot in range(slots)
    ]
    for slot, parts in enumerate(level_parts(operands, merged)):
        for which, part in enumerate(parts):
            part = part.astype(BF16)
            for d in range(n_i):
                outs[d][which * slots + slot] = part[d * quarter : (d + 1) * quarter]
    for d in range(n_i):
        outs[d][4 * slots] = split(columns_ref[d * quarter : (d + 1) * quarter])


def far_parts_kernel(slots, width, *refs):
    fulls, refs = refs[:slots], refs[slots:]
    sibs, refs = refs[: width - 1], refs[width - 1 :]
    xmsgs, refs = refs[:slots], refs[slots + 1 :]
    outs, refs = refs[:slots], refs[slots:]
    kvouts, refs = refs[: width - 1], refs[width - 1 :]
    weights, score_grads = refs
    rows = fulls[0].shape[1]
    _, chip = position(slots)
    keys, values = far_keys(fulls, sibs, 0), far_keys(fulls, sibs, 1)
    for m in range(slots):
        lse, delta = merge_stats(
            xmsgs[m][pl.ds(chip, 1), :],
            xmsgs[m][pl.ds(slots + chip, 1), :],
            xmsgs[0][2 * slots + m : 2 * slots + m + 1, :],
            xmsgs[0][3 * slots + m : 3 * slots + m + 1, :],
        )
        operands = (keys, values, fulls[m][2], fulls[m][3])
        ((p, ds),) = level_weights([operands], [(lse, delta)])
        outs[m][0] = dot_tn(p, values).astype(BF16)
        outs[m][1] = (dot_tn(ds, keys) * SCALE).astype(BF16)
        weights[:, m * rows : (m + 1) * rows] = p
        score_grads[:, m * rows : (m + 1) * rows] = ds
    queries = jnp.concatenate([ref[2] for ref in fulls], axis=0)
    ups = jnp.concatenate([ref[3] for ref in fulls], axis=0)
    key_part = (dot(score_grads[...], queries) * SCALE).astype(BF16)
    value_part = dot(weights[...], ups).astype(BF16)
    for index in range(width * slots):
        block = slice(index * rows, (index + 1) * rows)
        part, m = index // slots, index % slots
        if part == 0:
            outs[m][2], outs[m][3] = key_part[block], value_part[block]
        else:
            kvouts[part - 1][m, 0], kvouts[part - 1][m, 1] = key_part[block], value_part[block]


def far_sum_kernel(slots, *refs):
    own, refs = refs[:slots], refs[slots:]
    found, outs = refs[: -slots - 1], refs[-slots:]
    for m in range(slots):
        outs[m][:2] = own[m][:2]
        total = own[m][2:].astype(F32)
        for ref in found:
            total += ref[m].astype(F32)
        outs[m][2:] = total.astype(BF16)


def near_parts_kernel(n_i, slots, *refs):
    sources, near_ref, refs = refs[:4], refs[4], refs[5:]
    mids, refs = (refs[0], *refs[n_i - 1 : 0 : -1]), refs[n_i:]
    xmsgs, (out_ref, stats_ref, spread) = refs[:slots], refs[slots:]
    rows = near_ref.shape[1]
    quarter = rows // DILATION
    pos, chip = position(slots)
    lane = lanes_of(quarter)
    mid = jnp.zeros((quarter, LANES), F32)
    for d in range(n_i):
        place = (pos ^ d) * slots
        found = join(mids[d])
        e = pltpu.roll(found, place, 1)
        de = pltpu.roll(found, place + HEADS - slots, 1)
        mid = jnp.where((lane >= place) & (lane < place + slots), e, mid)
        mid = jnp.where((lane >= HEADS + place) & (lane < HEADS + place + slots), de, mid)
    blank = jnp.where(lane < HEADS, LOWEST, 0.0)
    for residue in range(DILATION):
        spread[pl.ds(residue, quarter, stride=DILATION), :] = jnp.where(
            lane % DILATION == residue, mid, blank
        )
    across = spread[...].T
    stats_ref[:HEADS] = jnp.full((HEADS, rows), LOWEST, F32)
    stats_ref[HEADS:] = jnp.zeros((HEADS, rows), F32)
    for m in range(slots):
        head = pos * slots + (chip ^ m)
        stats_ref[pl.ds(head, 1), :] = xmsgs[m][2 * slots + m : 2 * slots + m + 1, :]
        stats_ref[pl.ds(HEADS + head, 1), :] = xmsgs[m][3 * slots + m : 3 * slots + m + 1, :]
    e, d = merge_stats(
        near_ref[:HEADS], near_ref[HEADS:], across[:HEADS], across[HEADS : 2 * HEADS]
    )
    e, d = merge_stats(e, d, stats_ref[:HEADS], stats_ref[HEADS:])
    stats_ref[:HEADS] = e
    stats_ref[HEADS:] = d
    for group in range(HEADS // DILATION):
        heads = range(group * DILATION, (group + 1) * DILATION)
        operands = [
            [ref[:, static_columns(head)] for ref in sources] for head in heads
        ]
        stats = [
            (stats_ref[head : head + 1, :], stats_ref[HEADS + head : HEADS + head + 1, :])
            for head in heads
        ]
        for head, parts in zip(heads, level_parts(operands, stats)):
            for which, part in enumerate(parts):
                out_ref[which, head] = part


def final_kernel(n_i, slots, near_ref, *refs):
    mids, refs = (refs[0], *refs[n_i - 1 : 0 : -1]), refs[n_i:]
    fulls, refs = (refs[0], *refs[slots - 1 : 0 : -1]), refs[slots:]
    outs, (ready, sems) = refs[:4], refs[4:]
    rows = fulls[0].shape[1]
    quarter = rows // DILATION
    pos, chip = position(slots)
    row = lax.broadcasted_iota(jnp.int32, (rows, quarter), 0)
    taken = lax.broadcasted_iota(jnp.int32, (rows, quarter), 1) * DILATION

    def spread(d, slot):
        head = (pos ^ d) * slots + slot
        place = jnp.where(row == taken + head % DILATION, 1.0, 0.0).astype(BF16)
        picked = jnp.concatenate([mids[d][which * slots + slot] for which in range(4)], axis=1)
        return head, dot(place, picked)

    copies = []
    for d in reversed(range(n_i)):
        found = [spread(d, chip ^ slot if d == 0 else slot) for slot in range(slots)]
        for slot, (head, parts) in enumerate(found):
            for which in range(4):
                total = near_ref[which, head] + parts[:, static_columns(which)]
                if d == 0:
                    total += fulls[slot][which].astype(F32)
                ready[which, :, head_columns(head)] = total.astype(BF16)
        width = slots * HEAD_DIM
        cols = pl.ds(pl.multiple_of((pos ^ d) * width, width), width)
        for which, out in enumerate(outs):
            copy = pltpu.make_async_copy(
                ready.at[which, :, cols], out.at[:, cols], sems.at[which, d]
            )
            copy.start()
            copies.append(copy)
    for copy in copies:
        copy.wait()


def settle_kernel(*refs):
    refs[-1][...] = jnp.zeros_like(refs[-1])


def call(kernel, name, outs, scratch, flops, operands, hbm_in=(), hbm_out=False, cheap=False, limit=VMEM_LIMIT):
    moved = sum(x.size * x.dtype.itemsize for x in tuple(operands) + tuple(outs))
    if cheap:
        flops, moved = 1, 1
    spaces = [pltpu.HBM if i in hbm_in else pltpu.VMEM for i in range(len(operands))]
    return pl.pallas_call(
        kernel,
        out_shape=tuple(outs),
        in_specs=[pl.BlockSpec(memory_space=space) for space in spaces],
        out_specs=tuple(
            pl.BlockSpec(memory_space=pltpu.HBM if hbm_out else pltpu.VMEM) for _ in outs
        ),
        scratch_shapes=scratch,
        compiler_params=pltpu.CompilerParams(vmem_limit_bytes=limit),
        cost_estimate=pl.CostEstimate(flops=flops, bytes_accessed=moved, transcendentals=0),
        name=name,
    )(*operands)


def far_first(pieces):
    return [*pieces[:2], *pieces[:1:-1]]


def in_order(pieces):
    return [*pieces[:2], *pieces[:1:-1]]


def swap(x, axis, n, mask):
    return lax.ppermute(x, axis, [(i, i ^ mask) for i in range(n)])


def local(query_rows, key_rows, value_rows, upstream):
    rows, features = query_rows.shape
    n_i, n_o = lax.axis_size("seqi"), lax.axis_size("seqo")
    slots = HEADS // n_i
    width = n_o // slots
    others = (width - 1) * slots
    quarter = rows // DILATION
    sources = (key_rows, value_rows, query_rows, upstream)
    unit = 2 * rows * rows * HEAD_DIM
    bind = functools.partial

    mid = SHAPE((4 * slots + 1, quarter, HEAD_DIM), BF16)
    full = SHAPE((4, rows, HEAD_DIM), BF16)
    half = SHAPE((slots, 2, rows, HEAD_DIM), BF16)
    square = pltpu.VMEM((LANES, rows), F32)

    def stats(count, lanes=rows):
        return SHAPE((count, lanes), F32)

    def swap_mids(pieces):
        found = {d: swap(pieces[d], "seqi", n_i, d) for d in reversed(range(1, n_i))}
        return [pieces[0]] + [found[d] for d in range(1, n_i)]

    def swap_fulls(pieces):
        return [pieces[0]] + [swap(pieces[m], "seqo", n_o, m * width) for m in range(1, slots)]

    pieces = call(
        bind(pick_kernel, n_i, slots),
        "pick",
        [mid] * n_i + [full] * slots + [stats(2 * HEADS)],
        [
            pltpu.VMEM((4, rows, features), BF16),
            pltpu.SemaphoreType.DMA((4, HEADS // DILATION)),
            pltpu.VMEM((4, HEADS, rows, HEAD_DIM), F32),
            pltpu.VMEM((n_i, 4 * slots, quarter, HEAD_DIM), BF16),
            square,
        ],
        unit * HEADS * 2,
        sources,
        hbm_in=range(4),
        limit=PICK_LIMIT,
    )
    mids = swap_mids(pieces[:n_i])
    fulls = swap_fulls(pieces[n_i : n_i + slots])
    near = pieces[-1]

    (settled,) = call(settle_kernel, "far_in", [stats(8)], [], SHORT, [mids[-1]])
    (settled,) = call(settle_kernel, "chips_back", [stats(8)], [], LONG, [settled])
    (packed,) = call(bind(pack_kernel, slots), "pack", [half], [], 1, fulls + [settled])
    sibs = [swap(packed, "seqo", n_o, part) for part in range(1, width)]
    (settled,) = call(settle_kernel, "packed_back", [stats(8)], [], LONG, [near])
    (far,) = call(
        bind(far_stats_kernel, slots),
        "far_stats",
        [stats(2 * slots)],
        [],
        1,
        fulls + sibs + [settled],
    )
    xmsg, middle, columns = call(
        bind(middle_stats_kernel, n_i, slots),
        "middle_stats",
        [stats(4 * slots), stats(2 * slots, n_i * quarter), stats(n_i * quarter, LANES)],
        [pltpu.VMEM((LANES, n_i * quarter), F32), square],
        unit * slots * 2,
        [mids[0]] + mids[:0:-1] + [near, far],
    )
    xmsgs = swap_fulls([xmsg] * slots)

    midparts = call(
        bind(middle_parts_kernel, n_i, slots),
        "middle_parts",
        [mid] * n_i,
        [pltpu.VMEM((2 * slots, rows), F32), pltpu.VMEM((LANES, n_i * quarter), F32), square],
        unit * slots * 6,
        [mids[0]] + mids[:0:-1] + [middle, columns] + xmsgs,
    )
    midparts = swap_mids(midparts)
    farparts = call(
        bind(far_parts_kernel, slots, width),
        "far_parts",
        [full] * slots + [half] * (width - 1),
        [pltpu.VMEM((n_o * rows, slots * rows), BF16)] * 2,
        unit * n_o * slots * 6,
        fulls + sibs + xmsgs + [midparts[0]],
        cheap=True,
    )
    sibparts = [swap(x, "seqo", n_o, part + 1) for part, x in enumerate(farparts[slots:])]
    (settled,) = call(settle_kernel, "far_back", [stats(8)], [], SHORT, [midparts[-1]])
    (settled,) = call(settle_kernel, "sib_back", [stats(8)], [], 1, sibparts + [settled])
    (settled,) = call(settle_kernel, "settle", [stats(8)], [], LONG, [settled])
    fullparts = call(
        bind(far_sum_kernel, slots),
        "far_sum",
        [full] * slots,
        [],
        unit,
        list(farparts[:slots]) + sibparts + [settled],
        cheap=True,
    )
    fullparts = swap_fulls(fullparts)

    (nearparts,) = call(
        bind(near_parts_kernel, n_i, slots),
        "near_parts",
        [SHAPE((4, HEADS, rows, HEAD_DIM), F32)],
        [pltpu.VMEM((2 * HEADS, rows), F32), square],
        LONG,
        [*sources, near, midparts[0]] + midparts[:0:-1] + xmsgs,
    )
    return call(
        bind(final_kernel, n_i, slots),
        "final",
        [SHAPE((rows, features), BF16)] * 4,
        [pltpu.VMEM((4, rows, features), BF16), pltpu.SemaphoreType.DMA((4, n_i))],
        unit * HEADS,
        [nearparts, midparts[0]] + midparts[:0:-1] + [fullparts[0]] + fullparts[:0:-1],
        hbm_out=True,
    )


def solution(mesh):
    rows = P(("seqo", "seqi"), None)
    return jax.shard_map(
        local,
        mesh=mesh,
        in_specs=(rows,) * 4,
        out_specs=(rows,) * 4,
        check_vma=False,
    )
```

```python
import functools

import jax
import jax.numpy as jnp
from jax import lax
from jax.experimental import pallas as pl
from jax.experimental.pallas import tpu as pltpu
from jax.sharding import PartitionSpec as P

HEADS = 16
HEAD_DIM = 128
DILATION = 4
LANES = 128
SCALE = HEAD_DIM**-0.5
LOWEST = -1e30
LONG = 4 * 10**10
SHORT = 2 * 10**9
VMEM_LIMIT = 32 * 1024 * 1024
PICK_LIMIT = 53 * 1024 * 1024
NEAR_LIMIT = 54784 * 1024
F32, BF16 = jnp.float32, jnp.bfloat16
SHAPE = jax.ShapeDtypeStruct

NT = (((1,), (1,)), ((), ()))
TN = (((0,), (0,)), ((), ()))


def dot(a, b):
    return jnp.dot(a, b, preferred_element_type=F32)


def dot_nt(a, b):
    return lax.dot_general(a, b, NT, preferred_element_type=F32)


def dot_tn(a, b):
    return lax.dot_general(a, b, TN, preferred_element_type=F32)


def head_columns(head):
    return pl.ds(pl.multiple_of(head * HEAD_DIM, HEAD_DIM), HEAD_DIM)


def static_columns(index):
    return slice(index * HEAD_DIM, (index + 1) * HEAD_DIM)


def position(slots):
    width = lax.axis_size("seqo") // slots
    return lax.axis_index("seqi"), lax.axis_index("seqo") // width


def lanes_of(rows):
    return lax.broadcasted_iota(jnp.int32, (rows, LANES), 1)


def level_stats(operands):
    products = [(dot_nt(k, q) * SCALE, dot_nt(v, u)) for k, v, q, u in operands]
    tops = [jnp.max(s, axis=0, keepdims=True) for s, _ in products]
    weights = [jnp.exp(s - top) for (s, _), top in zip(products, tops)]
    totals = [jnp.sum(p, axis=0, keepdims=True) for p in weights]
    return [
        (top + jnp.log(total), jnp.sum(p * dp, axis=0, keepdims=True) / total)
        for (_, dp), top, p, total in zip(products, tops, weights, totals)
    ]


def merge_stats(ea, da, eb, db):
    top = jnp.maximum(ea, eb)
    wa, wb = jnp.exp(ea - top), jnp.exp(eb - top)
    total = wa + wb
    return top + jnp.log(total), (wa * da + wb * db) / total


def level_weights(operands, stats):
    products = [(dot_nt(k, q) * SCALE, dot_nt(v, u)) for k, v, q, u in operands]
    found = []
    for (s, dp), (lse, delta) in zip(products, stats):
        g = jnp.exp(s - lse)
        found.append((g.astype(BF16), (g * (dp - delta)).astype(BF16)))
    return found


def level_parts(operands, stats):
    found = level_weights(operands, stats)
    keyed = [
        (dot(ds, q) * SCALE, dot(p, u)) for (p, ds), (k, v, q, u) in zip(found, operands)
    ]
    queried = [
        (dot_tn(p, v), dot_tn(ds, k) * SCALE) for (p, ds), (k, v, q, u) in zip(found, operands)
    ]
    return [a + b for a, b in zip(queried, keyed)]


def pick_rows(ref, rows):
    quarter = rows // DILATION
    lane = lanes_of(quarter)
    picked = jnp.zeros((quarter, LANES), F32)
    for residue in range(DILATION):
        part = ref[pl.ds(residue, quarter, stride=DILATION), :]
        picked = jnp.where(lane % DILATION == residue, part, picked)
    return picked


def fetch(sources, buffers, sems):
    width = DILATION * HEAD_DIM
    groups = []
    for group in range(HEADS // DILATION):
        cols = pl.ds(group * width, width)
        groups.append(
            [
                pltpu.make_async_copy(
                    source.at[:, cols], buffers.at[which, :, cols], sems.at[which, group]
                )
                for which, source in enumerate(sources)
            ]
        )
        for copy in groups[-1]:
            copy.start()
    return groups


def split(x):
    high = x.astype(BF16).astype(F32)
    rest = x - high
    middle = rest.astype(BF16).astype(F32)
    low = rest - middle
    return (high + pltpu.roll(middle, 2 * HEADS, 1) + pltpu.roll(low, 4 * HEADS, 1)).astype(BF16)


def join(ref):
    x = ref[ref.shape[0] - 1].astype(F32)
    x = x + (pltpu.roll(x, LANES - 2 * HEADS, 1) + pltpu.roll(x, LANES - 4 * HEADS, 1))
    return jnp.where(lanes_of(x.shape[0]) < 2 * HEADS, x, 0.0)


def pick_kernel(n_i, slots, *refs):
    sources, refs = refs[:4], refs[4:]
    mids, refs = refs[:n_i], refs[n_i:]
    fulls, refs = refs[:slots], refs[slots:]
    stats_ref, buffers, sems, wide, picked, turn = refs
    rows = sources[0].shape[0]
    quarter = rows // DILATION
    pos, chip = position(slots)
    turn[...] = jnp.zeros_like(turn)
    for group, copies in enumerate(fetch(sources, buffers, sems)):
        for which, copy in enumerate(copies):
            copy.wait()
            for residue in range(DILATION):
                head = group * DILATION + residue
                wide[which, head] = buffers[which, :, static_columns(head)].astype(F32)
                rowset = wide[which, head, pl.ds(residue, quarter, stride=DILATION), :]
                picked[head // slots, which * slots + head % slots] = rowset.astype(BF16)
        heads = range(group * DILATION, (group + 1) * DILATION)
        operands = [[buffers[which, :, static_columns(head)] for which in range(4)] for head in heads]
        for head, (e, d) in zip(heads, level_stats(operands)):
            turn[head : head + 1, :] = e
            turn[HEADS + head : HEADS + head + 1, :] = d
    stats_ref[...] = turn[: 2 * HEADS, :]
    turn[...] = turn[...].T
    near = split(pick_rows(turn, rows))
    for d in range(n_i):
        mids[d][: 4 * slots] = picked[pos ^ d]
        mids[d][4 * slots] = near
    for m in range(slots):
        fulls[m][...] = buffers[:, :, head_columns(pos * slots + (chip ^ m))]


def pack_kernel(slots, *refs):
    packed_ref = refs[-1]
    for m, ref in enumerate(refs[:slots]):
        packed_ref[m] = ref[:2]


def far_keys(fulls, sibs, which):
    blocks = [ref[which] for ref in fulls]
    return jnp.concatenate(blocks + [ref[m, which] for ref in sibs for m in range(len(fulls))], axis=0)


def far_stats_kernel(slots, *refs):
    fulls, sibs, stats_ref = refs[:slots], refs[slots:-2], refs[-1]
    keys, values = far_keys(fulls, sibs, 0), far_keys(fulls, sibs, 1)
    for m in range(slots):
        ((e, d),) = level_stats([(keys, values, fulls[m][2], fulls[m][3])])
        stats_ref[m : m + 1, :] = e
        stats_ref[slots + m : slots + m + 1, :] = d


def middle_operands(slots, mids, slot):
    return [
        jnp.concatenate([ref[which * slots + slot] for ref in mids], axis=0) for which in range(4)
    ]


def middle_stats_kernel(n_i, slots, *refs):
    mids, refs = in_order(refs[:n_i]), refs[n_i:]
    near_ref, far_ref, xmsg_ref, stats_ref, columns_ref, turn, spread = refs
    rows = near_ref.shape[1]
    quarter = rows // DILATION
    pos, _ = position(slots)
    turn[...] = jnp.zeros_like(turn)
    operands = [middle_operands(slots, mids, slot) for slot in range(slots)]
    for slot, (e, d) in enumerate(level_stats(operands)):
        turn[slot : slot + 1, :] = e
        turn[slots + slot : slots + slot + 1, :] = d
    stats_ref[...] = turn[: 2 * slots, :]
    columns_ref[...] = turn[...].T
    lane = lanes_of(quarter)
    lane_residue = (pos * slots + lane % slots) % DILATION
    blank = jnp.where(lane < slots, LOWEST, 0.0)
    for residue in range(DILATION):
        spread[pl.ds(residue, quarter, stride=DILATION), :] = jnp.where(
            lane_residue == residue, columns_ref[:quarter], blank
        )
    across = spread[...].T
    e, d = merge_stats(
        near_ref[pl.ds(pos * slots, slots), :],
        near_ref[pl.ds(HEADS + pos * slots, slots), :],
        across[:slots],
        across[slots : 2 * slots],
    )
    xmsg_ref[:slots] = e
    xmsg_ref[slots : 2 * slots] = d
    xmsg_ref[2 * slots :] = far_ref[...]


def middle_parts_kernel(n_i, slots, *refs):
    mids, refs = in_order(refs[:n_i]), refs[n_i:]
    stats_ref, columns_ref = refs[:2]
    refs = refs[2:]
    xmsgs, refs = refs[:slots], refs[slots:]
    outs, (far, turn, spread) = refs[:n_i], refs[n_i:]
    rows = xmsgs[0].shape[1]
    quarter = rows // DILATION
    pos, chip = position(slots)
    for m in range(slots):
        far[pl.ds(chip ^ m, 1), :] = xmsgs[m][2 * slots + m : 2 * slots + m + 1, :]
        far[pl.ds(slots + (chip ^ m), 1), :] = xmsgs[m][3 * slots + m : 3 * slots + m + 1, :]
    e, d = merge_stats(
        xmsgs[0][:slots], xmsgs[0][slots : 2 * slots], far[:slots], far[slots:]
    )
    spread[...] = jnp.zeros_like(spread)
    spread[pl.ds(pos * slots, slots), :] = e
    spread[pl.ds(HEADS + pos * slots, slots), :] = d
    spread[...] = spread[...].T
    own = pick_rows(spread, rows)
    turn[...] = jnp.concatenate([own] + [join(ref) for ref in mids[1:]], axis=0).T
    owned = lax.broadcasted_iota(jnp.int32, (1, n_i * quarter), 1) < quarter
    operands = [middle_operands(slots, mids, slot) for slot in range(slots)]
    merged = [
        merge_stats(
            turn[pl.ds(pos * slots + slot, 1), :],
            turn[pl.ds(HEADS + pos * slots + slot, 1), :],
            jnp.where(owned, LOWEST, stats_ref[slot : slot + 1, :]),
            stats_ref[slots + slot : slots + slot + 1, :],
        )
        for slot in range(slots)
    ]
    for slot, parts in enumerate(level_parts(operands, merged)):
        for which, part in enumerate(parts):
            part = part.astype(BF16)
            for d in range(n_i):
                outs[d][which * slots + slot] = part[d * quarter : (d + 1) * quarter]
    for d in range(n_i):
        outs[d][4 * slots] = split(columns_ref[d * quarter : (d + 1) * quarter])


def far_parts_kernel(slots, width, *refs):
    fulls, refs = refs[:slots], refs[slots:]
    sibs, refs = refs[: width - 1], refs[width - 1 :]
    xmsgs, refs = refs[:slots], refs[slots + 1 :]
    outs, refs = refs[:slots], refs[slots:]
    kvouts, refs = refs[: width - 1], refs[width - 1 :]
    weights, score_grads = refs
    rows = fulls[0].shape[1]
    _, chip = position(slots)
    keys, values = far_keys(fulls, sibs, 0), far_keys(fulls, sibs, 1)
    for m in range(slots):
        lse, delta = merge_stats(
            xmsgs[m][pl.ds(chip, 1), :],
            xmsgs[m][pl.ds(slots + chip, 1), :],
            xmsgs[0][2 * slots + m : 2 * slots + m + 1, :],
            xmsgs[0][3 * slots + m : 3 * slots + m + 1, :],
        )
        operands = (keys, values, fulls[m][2], fulls[m][3])
        ((p, ds),) = level_weights([operands], [(lse, delta)])
        outs[m][0] = dot_tn(p, values).astype(BF16)
        outs[m][1] = (dot_tn(ds, keys) * SCALE).astype(BF16)
        weights[:, m * rows : (m + 1) * rows] = p
        score_grads[:, m * rows : (m + 1) * rows] = ds
    queries = jnp.concatenate([ref[2] for ref in fulls], axis=0)
    ups = jnp.concatenate([ref[3] for ref in fulls], axis=0)
    key_part = (dot(score_grads[...], queries) * SCALE).astype(BF16)
    value_part = dot(weights[...], ups).astype(BF16)
    for index in range(width * slots):
        block = slice(index * rows, (index + 1) * rows)
        part, m = index // slots, index % slots
        if part == 0:
            outs[m][2], outs[m][3] = key_part[block], value_part[block]
        else:
            kvouts[part - 1][m, 0], kvouts[part - 1][m, 1] = key_part[block], value_part[block]


def far_sum_kernel(slots, *refs):
    own, refs = refs[:slots], refs[slots:]
    found, outs = refs[: -slots - 1], refs[-slots:]
    for m in range(slots):
        outs[m][:2] = own[m][:2]
        total = own[m][2:].astype(F32)
        for ref in found:
            total += ref[m].astype(F32)
        outs[m][2:] = total.astype(BF16)


def near_parts_kernel(n_i, slots, *refs):
    sources, near_ref, refs = refs[:4], refs[4], refs[5:]
    mids, refs = (refs[0], *refs[n_i - 1 : 0 : -1]), refs[n_i:]
    xmsgs, (out_ref, stats_ref, spread) = refs[:slots], refs[slots:]
    rows = near_ref.shape[1]
    quarter = rows // DILATION
    pos, chip = position(slots)
    lane = lanes_of(quarter)
    mid = jnp.zeros((quarter, LANES), F32)
    for d in range(n_i):
        place = (pos ^ d) * slots
        found = join(mids[d])
        e = pltpu.roll(found, place, 1)
        de = pltpu.roll(found, place + HEADS - slots, 1)
        mid = jnp.where((lane >= place) & (lane < place + slots), e, mid)
        mid = jnp.where((lane >= HEADS + place) & (lane < HEADS + place + slots), de, mid)
    blank = jnp.where(lane < HEADS, LOWEST, 0.0)
    for residue in range(DILATION):
        spread[pl.ds(residue, quarter, stride=DILATION), :] = jnp.where(
            lane % DILATION == residue, mid, blank
        )
    across = spread[...].T
    stats_ref[:HEADS] = jnp.full((HEADS, rows), LOWEST, F32)
    stats_ref[HEADS:] = jnp.zeros((HEADS, rows), F32)
    for m in range(slots):
        head = pos * slots + (chip ^ m)
        stats_ref[pl.ds(head, 1), :] = xmsgs[m][2 * slots + m : 2 * slots + m + 1, :]
        stats_ref[pl.ds(HEADS + head, 1), :] = xmsgs[m][3 * slots + m : 3 * slots + m + 1, :]
    e, d = merge_stats(
        near_ref[:HEADS], near_ref[HEADS:], across[:HEADS], across[HEADS : 2 * HEADS]
    )
    e, d = merge_stats(e, d, stats_ref[:HEADS], stats_ref[HEADS:])
    stats_ref[:HEADS] = e
    stats_ref[HEADS:] = d
    for group in range(HEADS // DILATION):
        heads = range(group * DILATION, (group + 1) * DILATION)
        operands = [
            [ref[:, static_columns(head)] for ref in sources] for head in heads
        ]
        stats = [
            (stats_ref[head : head + 1, :], stats_ref[HEADS + head : HEADS + head + 1, :])
            for head in heads
        ]
        for head, parts in zip(heads, level_parts(operands, stats)):
            for which, part in enumerate(parts):
                out_ref[which, head] = part


def final_kernel(n_i, slots, near_ref, *refs):
    mids, refs = (refs[0], *refs[n_i - 1 : 0 : -1]), refs[n_i:]
    fulls, refs = (refs[0], *refs[slots - 1 : 0 : -1]), refs[slots:]
    outs, (ready, sems) = refs[:4], refs[4:]
    rows = fulls[0].shape[1]
    quarter = rows // DILATION
    pos, chip = position(slots)
    row = lax.broadcasted_iota(jnp.int32, (rows, quarter), 0)
    taken = lax.broadcasted_iota(jnp.int32, (rows, quarter), 1) * DILATION

    def spread(d, slot):
        head = (pos ^ d) * slots + slot
        place = jnp.where(row == taken + head % DILATION, 1.0, 0.0).astype(BF16)
        picked = jnp.concatenate([mids[d][which * slots + slot] for which in range(4)], axis=1)
        return head, dot(place, picked)

    copies = []
    for d in reversed(range(n_i)):
        found = [spread(d, chip ^ slot if d == 0 else slot) for slot in range(slots)]
        for slot, (head, parts) in enumerate(found):
            for which in range(4):
                total = near_ref[which, head] + parts[:, static_columns(which)]
                if d == 0:
                    total += fulls[slot][which].astype(F32)
                ready[which, :, head_columns(head)] = total.astype(BF16)
        width = slots * HEAD_DIM
        cols = pl.ds(pl.multiple_of((pos ^ d) * width, width), width)
        for which, out in enumerate(outs):
            copy = pltpu.make_async_copy(
                ready.at[which, :, cols], out.at[:, cols], sems.at[which, d]
            )
            copy.start()
            copies.append(copy)
    for copy in copies:
        copy.wait()


def settle_kernel(*refs):
    refs[-1][...] = jnp.zeros_like(refs[-1])


def call(kernel, name, outs, scratch, flops, operands, hbm_in=(), hbm_out=False, cheap=False, limit=VMEM_LIMIT):
    moved = sum(x.size * x.dtype.itemsize for x in tuple(operands) + tuple(outs))
    if cheap:
        flops, moved = 1, 1
    spaces = [pltpu.HBM if i in hbm_in else pltpu.VMEM for i in range(len(operands))]
    return pl.pallas_call(
        kernel,
        out_shape=tuple(outs),
        in_specs=[pl.BlockSpec(memory_space=space) for space in spaces],
        out_specs=tuple(
            pl.BlockSpec(memory_space=pltpu.HBM if hbm_out else pltpu.VMEM) for _ in outs
        ),
        scratch_shapes=scratch,
        compiler_params=pltpu.CompilerParams(vmem_limit_bytes=limit),
        cost_estimate=pl.CostEstimate(flops=flops, bytes_accessed=moved, transcendentals=0),
        name=name,
    )(*operands)


def in_turn(pieces):
    return [pieces[0], pieces[-1], *pieces[1:-1]]


def in_order(pieces):
    return [pieces[0], *pieces[2:], pieces[1]]


def swap(x, axis, n, mask):
    return lax.ppermute(x, axis, [(i, i ^ mask) for i in range(n)])


def local(query_rows, key_rows, value_rows, upstream):
    rows, features = query_rows.shape
    n_i, n_o = lax.axis_size("seqi"), lax.axis_size("seqo")
    slots = HEADS // n_i
    width = n_o // slots
    others = (width - 1) * slots
    quarter = rows // DILATION
    sources = (key_rows, value_rows, query_rows, upstream)
    unit = 2 * rows * rows * HEAD_DIM
    bind = functools.partial

    mid = SHAPE((4 * slots + 1, quarter, HEAD_DIM), BF16)
    full = SHAPE((4, rows, HEAD_DIM), BF16)
    half = SHAPE((slots, 2, rows, HEAD_DIM), BF16)
    square = pltpu.VMEM((LANES, rows), F32)

    def stats(count, lanes=rows):
        return SHAPE((count, lanes), F32)

    def swap_mids(pieces):
        found = {d: swap(pieces[d], "seqi", n_i, d) for d in reversed(range(1, n_i))}
        return [pieces[0]] + [found[d] for d in range(1, n_i)]

    def swap_fulls(pieces):
        return [pieces[0]] + [swap(pieces[m], "seqo", n_o, m * width) for m in range(1, slots)]

    pieces = call(
        bind(pick_kernel, n_i, slots),
        "pick",
        [mid] * n_i + [full] * slots + [stats(2 * HEADS)],
        [
            pltpu.VMEM((4, rows, features), BF16),
            pltpu.SemaphoreType.DMA((4, HEADS // DILATION)),
            pltpu.VMEM((4, HEADS, rows, HEAD_DIM), F32),
            pltpu.VMEM((n_i, 4 * slots, quarter, HEAD_DIM), BF16),
            square,
        ],
        unit * HEADS * 2,
        sources,
        hbm_in=range(4),
        limit=PICK_LIMIT,
    )
    mids = swap_mids(pieces[:n_i])
    fulls = swap_fulls(pieces[n_i : n_i + slots])
    near = pieces[-1]

    (settled,) = call(settle_kernel, "far_in", [stats(8)], [], SHORT, [mids[-1]])
    (settled,) = call(settle_kernel, "chips_back", [stats(8)], [], LONG, [settled])
    (packed,) = call(bind(pack_kernel, slots), "pack", [half], [], 1, fulls + [settled])
    sibs = [swap(packed, "seqo", n_o, part) for part in range(1, width)]
    (settled,) = call(settle_kernel, "packed_back", [stats(8)], [], LONG, [near])
    (far,) = call(
        bind(far_stats_kernel, slots),
        "far_stats",
        [stats(2 * slots)],
        [],
        1,
        fulls + sibs + [settled],
    )
    xmsg, middle, columns = call(
        bind(middle_stats_kernel, n_i, slots),
        "middle_stats",
        [stats(4 * slots), stats(2 * slots, n_i * quarter), stats(n_i * quarter, LANES)],
        [pltpu.VMEM((LANES, n_i * quarter), F32), square],
        unit * slots * 2,
        in_turn(mids) + [near, far],
    )
    xmsgs = swap_fulls([xmsg] * slots)

    midparts = call(
        bind(middle_parts_kernel, n_i, slots),
        "middle_parts",
        [mid] * n_i,
        [pltpu.VMEM((2 * slots, rows), F32), pltpu.VMEM((LANES, n_i * quarter), F32), square],
        unit * slots * 6,
        in_turn(mids) + [middle, columns] + xmsgs,
    )
    midparts = swap_mids(midparts)
    farparts = call(
        bind(far_parts_kernel, slots, width),
        "far_parts",
        [full] * slots + [half] * (width - 1),
        [pltpu.VMEM((n_o * rows, slots * rows), BF16)] * 2,
        unit * n_o * slots * 6,
        fulls + sibs + xmsgs + [midparts[0]],
        cheap=True,
    )
    sibparts = [swap(x, "seqo", n_o, part + 1) for part, x in enumerate(farparts[slots:])]
    (settled,) = call(settle_kernel, "far_back", [stats(8)], [], SHORT, [midparts[-1]])
    (settled,) = call(settle_kernel, "sib_back", [stats(8)], [], 1, sibparts + [settled])
    (settled,) = call(settle_kernel, "settle", [stats(8)], [], LONG, [settled])
    fullparts = call(
        bind(far_sum_kernel, slots),
        "far_sum",
        [full] * slots,
        [],
        unit,
        list(farparts[:slots]) + sibparts + [settled],
        cheap=True,
    )
    fullparts = swap_fulls(fullparts)

    (nearparts,) = call(
        bind(near_parts_kernel, n_i, slots),
        "near_parts",
        [SHAPE((4, HEADS, rows, HEAD_DIM), F32)],
        [pltpu.VMEM((2 * HEADS, rows), F32), square],
        LONG,
        [*sources, near, midparts[0]] + midparts[:0:-1] + xmsgs,
    )
    return call(
        bind(final_kernel, n_i, slots),
        "final",
        [SHAPE((rows, features), BF16)] * 4,
        [pltpu.VMEM((4, rows, features), BF16), pltpu.SemaphoreType.DMA((4, n_i))],
        unit * HEADS,
        [nearparts, midparts[0]] + midparts[:0:-1] + [fullparts[0]] + fullparts[:0:-1],
        hbm_out=True,
    )


def solution(mesh):
    rows = P(("seqo", "seqi"), None)
    return jax.shard_map(
        local,
        mesh=mesh,
        in_specs=(rows,) * 4,
        out_specs=(rows,) * 4,
        check_vma=False,
    )
```

```python
import functools

import jax
import jax.numpy as jnp
from jax import lax
from jax.experimental import pallas as pl
from jax.experimental.pallas import tpu as pltpu
from jax.sharding import PartitionSpec as P

HEADS = 16
HEAD_DIM = 128
DILATION = 4
LANES = 128
SCALE = HEAD_DIM**-0.5
LOWEST = -1e30
LONG = 4 * 10**10
SHORT = 2 * 10**9
VMEM_LIMIT = 32 * 1024 * 1024
PICK_LIMIT = 53 * 1024 * 1024
NEAR_LIMIT = 54784 * 1024
F32, BF16 = jnp.float32, jnp.bfloat16
SHAPE = jax.ShapeDtypeStruct

NT = (((1,), (1,)), ((), ()))
TN = (((0,), (0,)), ((), ()))


def dot(a, b):
    return jnp.dot(a, b, preferred_element_type=F32)


def dot_nt(a, b):
    return lax.dot_general(a, b, NT, preferred_element_type=F32)


def dot_tn(a, b):
    return lax.dot_general(a, b, TN, preferred_element_type=F32)


def head_columns(head):
    return pl.ds(pl.multiple_of(head * HEAD_DIM, HEAD_DIM), HEAD_DIM)


def static_columns(index):
    return slice(index * HEAD_DIM, (index + 1) * HEAD_DIM)


def position(slots):
    width = lax.axis_size("seqo") // slots
    return lax.axis_index("seqi"), lax.axis_index("seqo") // width


def lanes_of(rows):
    return lax.broadcasted_iota(jnp.int32, (rows, LANES), 1)


def level_stats(operands):
    products = [(dot_nt(k, q) * SCALE, dot_nt(v, u)) for k, v, q, u in operands]
    tops = [jnp.max(s, axis=0, keepdims=True) for s, _ in products]
    weights = [jnp.exp(s - top) for (s, _), top in zip(products, tops)]
    totals = [jnp.sum(p, axis=0, keepdims=True) for p in weights]
    return [
        (top + jnp.log(total), jnp.sum(p * dp, axis=0, keepdims=True) / total)
        for (_, dp), top, p, total in zip(products, tops, weights, totals)
    ]


def merge_stats(ea, da, eb, db):
    top = jnp.maximum(ea, eb)
    wa, wb = jnp.exp(ea - top), jnp.exp(eb - top)
    total = wa + wb
    return top + jnp.log(total), (wa * da + wb * db) / total


def level_weights(operands, stats):
    products = [(dot_nt(k, q) * SCALE, dot_nt(v, u)) for k, v, q, u in operands]
    found = []
    for (s, dp), (lse, delta) in zip(products, stats):
        g = jnp.exp(s - lse)
        found.append((g.astype(BF16), (g * (dp - delta)).astype(BF16)))
    return found


def level_parts(operands, stats):
    found = level_weights(operands, stats)
    keyed = [
        (dot(ds, q) * SCALE, dot(p, u)) for (p, ds), (k, v, q, u) in zip(found, operands)
    ]
    queried = [
        (dot_tn(p, v), dot_tn(ds, k) * SCALE) for (p, ds), (k, v, q, u) in zip(found, operands)
    ]
    return [a + b for a, b in zip(queried, keyed)]


def pick_rows(ref, rows):
    quarter = rows // DILATION
    lane = lanes_of(quarter)
    picked = jnp.zeros((quarter, LANES), F32)
    for residue in range(DILATION):
        part = ref[pl.ds(residue, quarter, stride=DILATION), :]
        picked = jnp.where(lane % DILATION == residue, part, picked)
    return picked


def fetch(sources, buffers, sems):
    width = DILATION * HEAD_DIM
    groups = []
    for group in range(HEADS // DILATION):
        cols = pl.ds(group * width, width)
        groups.append(
            [
                pltpu.make_async_copy(
                    source.at[:, cols], buffers.at[which, :, cols], sems.at[which, group]
                )
                for which, source in enumerate(sources)
            ]
        )
        for copy in groups[-1]:
            copy.start()
    return groups


def split(x):
    high = x.astype(BF16).astype(F32)
    rest = x - high
    middle = rest.astype(BF16).astype(F32)
    low = rest - middle
    return (high + pltpu.roll(middle, 2 * HEADS, 1) + pltpu.roll(low, 4 * HEADS, 1)).astype(BF16)


def join(ref):
    x = ref[ref.shape[0] - 1].astype(F32)
    x = x + (pltpu.roll(x, LANES - 2 * HEADS, 1) + pltpu.roll(x, LANES - 4 * HEADS, 1))
    return jnp.where(lanes_of(x.shape[0]) < 2 * HEADS, x, 0.0)


def pick_kernel(n_i, slots, *refs):
    sources, refs = refs[:4], refs[4:]
    mids, refs = refs[:n_i], refs[n_i:]
    fulls, refs = refs[:slots], refs[slots:]
    stats_ref, buffers, sems, wide, picked, turn = refs
    rows = sources[0].shape[0]
    quarter = rows // DILATION
    pos, chip = position(slots)
    turn[...] = jnp.zeros_like(turn)
    for group, copies in enumerate(fetch(sources, buffers, sems)):
        for which, copy in enumerate(copies):
            copy.wait()
            for residue in range(DILATION):
                head = group * DILATION + residue
                wide[which, head] = buffers[which, :, static_columns(head)].astype(F32)
                rowset = wide[which, head, pl.ds(residue, quarter, stride=DILATION), :]
                picked[head // slots, which * slots + head % slots] = rowset.astype(BF16)
        heads = range(group * DILATION, (group + 1) * DILATION)
        operands = [[buffers[which, :, static_columns(head)] for which in range(4)] for head in heads]
        for head, (e, d) in zip(heads, level_stats(operands)):
            turn[head : head + 1, :] = e
            turn[HEADS + head : HEADS + head + 1, :] = d
    stats_ref[...] = turn[: 2 * HEADS, :]
    turn[...] = turn[...].T
    near = split(pick_rows(turn, rows))
    for d in range(n_i):
        mids[d][: 4 * slots] = picked[pos ^ d]
        mids[d][4 * slots] = near
    for m in range(slots):
        fulls[m][...] = buffers[:, :, head_columns(pos * slots + (chip ^ m))]


def pack_kernel(slots, *refs):
    packed_ref = refs[-1]
    for m, ref in enumerate(refs[:slots]):
        packed_ref[m] = ref[:2]


def far_keys(fulls, sibs, which):
    blocks = [ref[which] for ref in fulls]
    return jnp.concatenate(blocks + [ref[m, which] for ref in sibs for m in range(len(fulls))], axis=0)


def far_stats_kernel(slots, *refs):
    fulls, sibs, stats_ref = refs[:slots], refs[slots:-2], refs[-1]
    keys, values = far_keys(fulls, sibs, 0), far_keys(fulls, sibs, 1)
    for m in range(slots):
        ((e, d),) = level_stats([(keys, values, fulls[m][2], fulls[m][3])])
        stats_ref[m : m + 1, :] = e
        stats_ref[slots + m : slots + m + 1, :] = d


def middle_operands(slots, mids, slot):
    return [
        jnp.concatenate([ref[which * slots + slot] for ref in mids], axis=0) for which in range(4)
    ]


def middle_stats_kernel(n_i, slots, *refs):
    mids, refs = in_order(refs[:n_i]), refs[n_i:]
    near_ref, far_ref, xmsg_ref, stats_ref, columns_ref, turn, spread = refs
    rows = near_ref.shape[1]
    quarter = rows // DILATION
    pos, _ = position(slots)
    turn[...] = jnp.zeros_like(turn)
    operands = [middle_operands(slots, mids, slot) for slot in range(slots)]
    for slot, (e, d) in enumerate(level_stats(operands)):
        turn[slot : slot + 1, :] = e
        turn[slots + slot : slots + slot + 1, :] = d
    stats_ref[...] = turn[: 2 * slots, :]
    columns_ref[...] = turn[...].T
    lane = lanes_of(quarter)
    lane_residue = (pos * slots + lane % slots) % DILATION
    blank = jnp.where(lane < slots, LOWEST, 0.0)
    for residue in range(DILATION):
        spread[pl.ds(residue, quarter, stride=DILATION), :] = jnp.where(
            lane_residue == residue, columns_ref[:quarter], blank
        )
    across = spread[...].T
    e, d = merge_stats(
        near_ref[pl.ds(pos * slots, slots), :],
        near_ref[pl.ds(HEADS + pos * slots, slots), :],
        across[:slots],
        across[slots : 2 * slots],
    )
    xmsg_ref[:slots] = e
    xmsg_ref[slots : 2 * slots] = d
    xmsg_ref[2 * slots :] = far_ref[...]


def middle_parts_kernel(n_i, slots, *refs):
    mids, refs = in_order(refs[:n_i]), refs[n_i:]
    stats_ref, columns_ref = refs[:2]
    refs = refs[2:]
    xmsgs, refs = refs[:slots], refs[slots:]
    outs, (far, turn, spread) = refs[:n_i], refs[n_i:]
    rows = xmsgs[0].shape[1]
    quarter = rows // DILATION
    pos, chip = position(slots)
    for m in range(slots):
        far[pl.ds(chip ^ m, 1), :] = xmsgs[m][2 * slots + m : 2 * slots + m + 1, :]
        far[pl.ds(slots + (chip ^ m), 1), :] = xmsgs[m][3 * slots + m : 3 * slots + m + 1, :]
    e, d = merge_stats(
        xmsgs[0][:slots], xmsgs[0][slots : 2 * slots], far[:slots], far[slots:]
    )
    spread[...] = jnp.zeros_like(spread)
    spread[pl.ds(pos * slots, slots), :] = e
    spread[pl.ds(HEADS + pos * slots, slots), :] = d
    spread[...] = spread[...].T
    own = pick_rows(spread, rows)
    turn[...] = jnp.concatenate([own] + [join(ref) for ref in mids[1:]], axis=0).T
    owned = lax.broadcasted_iota(jnp.int32, (1, n_i * quarter), 1) < quarter
    operands = [middle_operands(slots, mids, slot) for slot in range(slots)]
    merged = [
        merge_stats(
            turn[pl.ds(pos * slots + slot, 1), :],
            turn[pl.ds(HEADS + pos * slots + slot, 1), :],
            jnp.where(owned, LOWEST, stats_ref[slot : slot + 1, :]),
            stats_ref[slots + slot : slots + slot + 1, :],
        )
        for slot in range(slots)
    ]
    for slot, parts in enumerate(level_parts(operands, merged)):
        for which, part in enumerate(parts):
            part = part.astype(BF16)
            for d in range(n_i):
                outs[d][which * slots + slot] = part[d * quarter : (d + 1) * quarter]
    for d in range(n_i):
        outs[d][4 * slots] = split(columns_ref[d * quarter : (d + 1) * quarter])


def far_parts_kernel(slots, width, *refs):
    fulls, refs = refs[:slots], refs[slots:]
    sibs, refs = refs[: width - 1], refs[width - 1 :]
    xmsgs, refs = refs[:slots], refs[slots + 1 :]
    outs, refs = refs[:slots], refs[slots:]
    kvouts, refs = refs[: width - 1], refs[width - 1 :]
    weights, score_grads = refs
    rows = fulls[0].shape[1]
    _, chip = position(slots)
    keys, values = far_keys(fulls, sibs, 0), far_keys(fulls, sibs, 1)
    for m in range(slots):
        lse, delta = merge_stats(
            xmsgs[m][pl.ds(chip, 1), :],
            xmsgs[m][pl.ds(slots + chip, 1), :],
            xmsgs[0][2 * slots + m : 2 * slots + m + 1, :],
            xmsgs[0][3 * slots + m : 3 * slots + m + 1, :],
        )
        operands = (keys, values, fulls[m][2], fulls[m][3])
        ((p, ds),) = level_weights([operands], [(lse, delta)])
        outs[m][0] = dot_tn(p, values).astype(BF16)
        outs[m][1] = (dot_tn(ds, keys) * SCALE).astype(BF16)
        weights[:, m * rows : (m + 1) * rows] = p
        score_grads[:, m * rows : (m + 1) * rows] = ds
    queries = jnp.concatenate([ref[2] for ref in fulls], axis=0)
    ups = jnp.concatenate([ref[3] for ref in fulls], axis=0)
    key_part = (dot(score_grads[...], queries) * SCALE).astype(BF16)
    value_part = dot(weights[...], ups).astype(BF16)
    for index in range(width * slots):
        block = slice(index * rows, (index + 1) * rows)
        part, m = index // slots, index % slots
        if part == 0:
            outs[m][2], outs[m][3] = key_part[block], value_part[block]
        else:
            kvouts[part - 1][m, 0], kvouts[part - 1][m, 1] = key_part[block], value_part[block]


def far_sum_kernel(slots, *refs):
    own, refs = refs[:slots], refs[slots:]
    found, outs = refs[: -slots - 1], refs[-slots:]
    for m in range(slots):
        outs[m][:2] = own[m][:2]
        total = own[m][2:].astype(F32)
        for ref in found:
            total += ref[m].astype(F32)
        outs[m][2:] = total.astype(BF16)


def near_statistics(slots, places, near_ref, mids, xmsgs, stats_ref, spread):
    rows = near_ref.shape[1]
    quarter = rows // DILATION
    pos, chip = position(slots)
    lane = lanes_of(quarter)
    mid = jnp.zeros((quarter, LANES), F32)
    for d, ref in zip(places, mids):
        place = (pos ^ d) * slots
        found = join(ref)
        e = pltpu.roll(found, place, 1)
        de = pltpu.roll(found, place + HEADS - slots, 1)
        mid = jnp.where((lane >= place) & (lane < place + slots), e, mid)
        mid = jnp.where((lane >= HEADS + place) & (lane < HEADS + place + slots), de, mid)
    blank = jnp.where(lane < HEADS, LOWEST, 0.0)
    for residue in range(DILATION):
        spread[pl.ds(residue, quarter, stride=DILATION), :] = jnp.where(
            lane % DILATION == residue, mid, blank
        )
    across = spread[...].T
    e, d = merge_stats(
        near_ref[:HEADS], near_ref[HEADS:], across[:HEADS], across[HEADS : 2 * HEADS]
    )
    if xmsgs:
        stats_ref[:HEADS] = jnp.full((HEADS, rows), LOWEST, F32)
        stats_ref[HEADS:] = jnp.zeros((HEADS, rows), F32)
        for m in range(slots):
            head = pos * slots + (chip ^ m)
            stats_ref[pl.ds(head, 1), :] = xmsgs[m][2 * slots + m : 2 * slots + m + 1, :]
            stats_ref[pl.ds(HEADS + head, 1), :] = xmsgs[m][3 * slots + m : 3 * slots + m + 1, :]
        e, d = merge_stats(e, d, stats_ref[:HEADS], stats_ref[HEADS:])
    stats_ref[:HEADS] = e
    stats_ref[HEADS:] = d


def near_place(slots, d, sources, stats_ref):
    pos, _ = position(slots)
    heads = [(pos ^ d) * slots + slot for slot in range(slots)]
    operands = [[ref[:, head_columns(head)] for ref in sources] for head in heads]
    stats = [(stats_ref[pl.ds(head, 1), :], stats_ref[pl.ds(HEADS + head, 1), :]) for head in heads]
    return level_parts(operands, stats)


def near_early_kernel(n_i, slots, *refs):
    sources, near_ref, refs = refs[:4], refs[4], refs[5:]
    mids, refs = refs[: n_i - 1], refs[n_i - 1 :]
    xmsgs, (out_ref, stats_ref, spread) = refs[:slots], refs[slots:]
    places = in_turn(list(range(n_i)))[:-1]
    near_statistics(slots, places, near_ref, mids, xmsgs, stats_ref, spread)
    for index, d in enumerate(places):
        for slot, parts in enumerate(near_place(slots, d, sources, stats_ref)):
            for which, part in enumerate(parts):
                out_ref[which, index * slots + slot] = part


def far_sum_kernel(slots, *refs):
    own, refs = refs[:slots], refs[slots:]
    found, outs = refs[: -slots - 1], refs[-slots:]
    for m in range(slots):
        outs[m][:2] = own[m][:2]
        total = own[m][2:].astype(F32)
        for ref in found:
            total += ref[m].astype(F32)
        outs[m][2:] = total.astype(BF16)


def near_parts_kernel(n_i, slots, *refs):
    sources, near_ref, refs = refs[:4], refs[4], refs[5:]
    mids, refs = (refs[0], *refs[n_i - 1 : 0 : -1]), refs[n_i:]
    xmsgs, (out_ref, stats_ref, spread) = refs[:slots], refs[slots:]
    rows = near_ref.shape[1]
    quarter = rows // DILATION
    pos, chip = position(slots)
    lane = lanes_of(quarter)
    mid = jnp.zeros((quarter, LANES), F32)
    for d in range(n_i):
        place = (pos ^ d) * slots
        found = join(mids[d])
        e = pltpu.roll(found, place, 1)
        de = pltpu.roll(found, place + HEADS - slots, 1)
        mid = jnp.where((lane >= place) & (lane < place + slots), e, mid)
        mid = jnp.where((lane >= HEADS + place) & (lane < HEADS + place + slots), de, mid)
    blank = jnp.where(lane < HEADS, LOWEST, 0.0)
    for residue in range(DILATION):
        spread[pl.ds(residue, quarter, stride=DILATION), :] = jnp.where(
            lane % DILATION == residue, mid, blank
        )
    across = spread[...].T
    stats_ref[:HEADS] = jnp.full((HEADS, rows), LOWEST, F32)
    stats_ref[HEADS:] = jnp.zeros((HEADS, rows), F32)
    for m in range(slots):
        head = pos * slots + (chip ^ m)
        stats_ref[pl.ds(head, 1), :] = xmsgs[m][2 * slots + m : 2 * slots + m + 1, :]
        stats_ref[pl.ds(HEADS + head, 1), :] = xmsgs[m][3 * slots + m : 3 * slots + m + 1, :]
    e, d = merge_stats(
        near_ref[:HEADS], near_ref[HEADS:], across[:HEADS], across[HEADS : 2 * HEADS]
    )
    e, d = merge_stats(e, d, stats_ref[:HEADS], stats_ref[HEADS:])
    stats_ref[:HEADS] = e
    stats_ref[HEADS:] = d
    for group in range(HEADS // DILATION):
        heads = range(group * DILATION, (group + 1) * DILATION)
        operands = [
            [ref[:, static_columns(head)] for ref in sources] for head in heads
        ]
        stats = [
            (stats_ref[head : head + 1, :], stats_ref[HEADS + head : HEADS + head + 1, :])
            for head in heads
        ]
        for head, parts in zip(heads, level_parts(operands, stats)):
            for which, part in enumerate(parts):
                out_ref[which, head] = part


def spread_rows(slots, d, slot, ref):
    quarter = ref.shape[1]
    rows = quarter * DILATION
    pos, _ = position(slots)
    head = (pos ^ d) * slots + slot
    row = lax.broadcasted_iota(jnp.int32, (rows, quarter), 0)
    taken = lax.broadcasted_iota(jnp.int32, (rows, quarter), 1) * DILATION
    place = jnp.where(row == taken + head % DILATION, 1.0, 0.0).astype(BF16)
    return dot(place, jnp.concatenate([ref[which * slots + slot] for which in range(4)], axis=1))


def send_place(slots, d, ready, outs, sems):
    pos, _ = position(slots)
    width = slots * HEAD_DIM
    cols = pl.ds(pl.multiple_of((pos ^ d) * width, width), width)
    copies = [
        pltpu.make_async_copy(ready.at[which], out.at[:, cols], sems.at[which])
        for which, out in enumerate(outs)
    ]
    for copy in copies:
        copy.start()
    return copies


def final_others_kernel(n_i, slots, *refs):
    sources, near_ref, early_ref, refs = refs[:4], refs[4], refs[5], refs[6:]
    mids, refs = refs[: n_i - 1], refs[n_i - 1 :]
    outs, (ready, sems, stats_ref, spread) = refs[:4], refs[4:]
    places = in_turn(list(range(n_i)))[1:]
    near_statistics(slots, places[-1:], near_ref, mids[-1:], (), stats_ref, spread)
    late = near_place(slots, places[-1], sources, stats_ref)
    copies = []
    for index, d in enumerate(places):
        found = [spread_rows(slots, d, slot, mids[index]) for slot in range(slots)]
        for slot, parts in enumerate(found):
            for which in range(4):
                if d == places[-1]:
                    near = late[slot][which]
                else:
                    near = early_ref[which, (index + 1) * slots + slot]
                total = near + parts[:, static_columns(which)]
                ready[index, which, :, static_columns(slot)] = total.astype(BF16)
        copies += send_place(slots, d, ready.at[index], outs, sems.at[index])
    for copy in copies:
        copy.wait()


def final_own_kernel(slots, early_ref, mid_ref, *refs):
    fulls, refs = in_back(refs[:slots]), refs[slots:]
    outs, (ready, sems) = refs[4:8], refs[8:]
    _, chip = position(slots)
    found = [spread_rows(slots, 0, chip ^ m, mid_ref) for m in range(slots)]
    for m, parts in enumerate(found):
        slot = chip ^ m
        for which in range(4):
            total = early_ref[which, slot] + parts[:, static_columns(which)]
            total += fulls[m][which].astype(F32)
            ready[which, :, head_columns(slot)] = total.astype(BF16)
    for copy in send_place(slots, 0, ready, outs, sems):
        copy.wait()


def settle_kernel(*refs):
    refs[-1][...] = jnp.zeros_like(refs[-1])


def call(kernel, name, outs, scratch, flops, operands, hbm_in=(), hbm_out=False, cheap=False, limit=VMEM_LIMIT, aliases=None):
    moved = sum(x.size * x.dtype.itemsize for x in tuple(operands) + tuple(outs))
    if cheap:
        flops, moved = 1, 1
    spaces = [pltpu.HBM if i in hbm_in else pltpu.VMEM for i in range(len(operands))]
    return pl.pallas_call(
        kernel,
        out_shape=tuple(outs),
        in_specs=[pl.BlockSpec(memory_space=space) for space in spaces],
        out_specs=tuple(
            pl.BlockSpec(memory_space=pltpu.HBM if hbm_out else pltpu.VMEM) for _ in outs
        ),
        scratch_shapes=scratch,
        input_output_aliases=aliases or {},
        compiler_params=pltpu.CompilerParams(vmem_limit_bytes=limit),
        cost_estimate=pl.CostEstimate(flops=flops, bytes_accessed=moved, transcendentals=0),
        name=name,
    )(*operands)


def in_turn(pieces):
    return [pieces[0], pieces[-1], *pieces[1:-1]]


def in_back(pieces):
    return [pieces[0], *pieces[:0:-1]]


def in_order(pieces):
    return [pieces[0], *pieces[2:], pieces[1]]


def swap(x, axis, n, mask):
    return lax.ppermute(x, axis, [(i, i ^ mask) for i in range(n)])


def local(query_rows, key_rows, value_rows, upstream):
    rows, features = query_rows.shape
    n_i, n_o = lax.axis_size("seqi"), lax.axis_size("seqo")
    slots = HEADS // n_i
    width = n_o // slots
    others = (width - 1) * slots
    quarter = rows // DILATION
    sources = (key_rows, value_rows, query_rows, upstream)
    unit = 2 * rows * rows * HEAD_DIM
    bind = functools.partial

    mid = SHAPE((4 * slots + 1, quarter, HEAD_DIM), BF16)
    full = SHAPE((4, rows, HEAD_DIM), BF16)
    half = SHAPE((slots, 2, rows, HEAD_DIM), BF16)
    square = pltpu.VMEM((LANES, rows), F32)

    def stats(count, lanes=rows):
        return SHAPE((count, lanes), F32)

    def swap_mids(pieces):
        found = {d: swap(pieces[d], "seqi", n_i, d) for d in reversed(range(1, n_i))}
        return [pieces[0]] + [found[d] for d in range(1, n_i)]

    def swap_fulls(pieces):
        return [pieces[0]] + [swap(pieces[m], "seqo", n_o, m * width) for m in range(1, slots)]

    pieces = call(
        bind(pick_kernel, n_i, slots),
        "pick",
        [mid] * n_i + [full] * slots + [stats(2 * HEADS)],
        [
            pltpu.VMEM((4, rows, features), BF16),
            pltpu.SemaphoreType.DMA((4, HEADS // DILATION)),
            pltpu.VMEM((4, HEADS, rows, HEAD_DIM), F32),
            pltpu.VMEM((n_i, 4 * slots, quarter, HEAD_DIM), BF16),
            square,
        ],
        unit * HEADS * 2,
        sources,
        hbm_in=range(4),
        limit=PICK_LIMIT,
    )
    mids = swap_mids(pieces[:n_i])
    fulls = swap_fulls(pieces[n_i : n_i + slots])
    near = pieces[-1]

    (settled,) = call(settle_kernel, "far_in", [stats(8)], [], SHORT, [mids[-1]])
    (settled,) = call(settle_kernel, "chips_back", [stats(8)], [], LONG, [settled])
    (packed,) = call(bind(pack_kernel, slots), "pack", [half], [], 1, fulls + [settled])
    sibs = [swap(packed, "seqo", n_o, part) for part in range(1, width)]
    (settled,) = call(settle_kernel, "packed_back", [stats(8)], [], LONG, [near])
    (far,) = call(
        bind(far_stats_kernel, slots),
        "far_stats",
        [stats(2 * slots)],
        [],
        1,
        fulls + sibs + [settled],
    )
    xmsg, middle, columns = call(
        bind(middle_stats_kernel, n_i, slots),
        "middle_stats",
        [stats(4 * slots), stats(2 * slots, n_i * quarter), stats(n_i * quarter, LANES)],
        [pltpu.VMEM((LANES, n_i * quarter), F32), square],
        unit * slots * 2,
        in_turn(mids) + [near, far],
    )
    xmsgs = swap_fulls([xmsg] * slots)

    midparts = call(
        bind(middle_parts_kernel, n_i, slots),
        "middle_parts",
        [mid] * n_i,
        [pltpu.VMEM((2 * slots, rows), F32), pltpu.VMEM((LANES, n_i * quarter), F32), square],
        unit * slots * 6,
        in_turn(mids) + [middle, columns] + xmsgs,
    )
    midparts = swap_mids(midparts)
    farparts = call(
        bind(far_parts_kernel, slots, width),
        "far_parts",
        [full] * slots + [half] * (width - 1),
        [pltpu.VMEM((n_o * rows, slots * rows), BF16)] * 2,
        unit * n_o * slots * 6,
        fulls + sibs + xmsgs + [midparts[0]],
        cheap=True,
    )
    sibparts = [swap(x, "seqo", n_o, part + 1) for part, x in enumerate(farparts[slots:])]
    (settled,) = call(settle_kernel, "far_back", [stats(8)], [], SHORT, [midparts[-1]])
    (settled,) = call(settle_kernel, "sib_back", [stats(8)], [], 1, sibparts + [settled])
    (settled,) = call(settle_kernel, "settle", [stats(8)], [], LONG, [settled])
    fullparts = call(
        bind(far_sum_kernel, slots),
        "far_sum",
        [full] * slots,
        [],
        unit,
        list(farparts[:slots]) + sibparts + [settled],
        cheap=True,
    )
    fullparts = swap_fulls(fullparts)

    back = in_turn(midparts)
    kept = [pltpu.VMEM((2 * HEADS, rows), F32), square]
    (early,) = call(
        bind(near_early_kernel, n_i, slots),
        "near_early",
        [SHAPE((4, (n_i - 1) * slots, rows, HEAD_DIM), F32)],
        kept,
        SHORT,
        [*sources, near, *back[:-1], *xmsgs],
    )
    whole = [SHAPE((rows, features), BF16)] * 4
    outs = call(
        bind(final_others_kernel, n_i, slots),
        "final_others",
        whole,
        [
            pltpu.VMEM((n_i - 1, 4, rows, slots * HEAD_DIM), BF16),
            pltpu.SemaphoreType.DMA((n_i - 1, 4)),
            *kept,
        ],
        SHORT // 2,
        [*sources, near, early, *back[1:]],
        hbm_out=True,
    )
    return call(
        bind(final_own_kernel, slots),
        "final_own",
        whole,
        [pltpu.VMEM((4, rows, slots * HEAD_DIM), BF16), pltpu.SemaphoreType.DMA((4,))],
        unit * slots,
        [early, midparts[0], *in_back(fullparts), *outs],
        hbm_in=range(2 + slots, 6 + slots),
        hbm_out=True,
        aliases={2 + slots + which: which for which in range(4)},
    )


def solution(mesh):
    rows = P(("seqo", "seqi"), None)
    return jax.shard_map(
        local,
        mesh=mesh,
        in_specs=(rows,) * 4,
        out_specs=(rows,) * 4,
        check_vma=False,
    )
```

```python
import functools

import jax
import jax.numpy as jnp
from jax import lax
from jax.experimental import pallas as pl
from jax.experimental.pallas import tpu as pltpu
from jax.sharding import PartitionSpec as P

HEADS = 16
HEAD_DIM = 128
DILATION = 4
LANES = 128
SCALE = HEAD_DIM**-0.5
LOWEST = -1e30
LONG = 4 * 10**10
SHORT = 2 * 10**9
VMEM_LIMIT = 32 * 1024 * 1024
PICK_LIMIT = 53 * 1024 * 1024
NEAR_LIMIT = 54784 * 1024
F32, BF16 = jnp.float32, jnp.bfloat16
SHAPE = jax.ShapeDtypeStruct

NT = (((1,), (1,)), ((), ()))
TN = (((0,), (0,)), ((), ()))


def dot(a, b):
    return jnp.dot(a, b, preferred_element_type=F32)


def dot_nt(a, b):
    return lax.dot_general(a, b, NT, preferred_element_type=F32)


def dot_tn(a, b):
    return lax.dot_general(a, b, TN, preferred_element_type=F32)


def head_columns(head):
    return pl.ds(pl.multiple_of(head * HEAD_DIM, HEAD_DIM), HEAD_DIM)


def static_columns(index):
    return slice(index * HEAD_DIM, (index + 1) * HEAD_DIM)


def position(slots):
    width = lax.axis_size("seqo") // slots
    return lax.axis_index("seqi"), lax.axis_index("seqo") // width


def lanes_of(rows):
    return lax.broadcasted_iota(jnp.int32, (rows, LANES), 1)


def level_stats(operands):
    products = [(dot_nt(k, q) * SCALE, dot_nt(v, u)) for k, v, q, u in operands]
    tops = [jnp.max(s, axis=0, keepdims=True) for s, _ in products]
    weights = [jnp.exp(s - top) for (s, _), top in zip(products, tops)]
    totals = [jnp.sum(p, axis=0, keepdims=True) for p in weights]
    return [
        (top + jnp.log(total), jnp.sum(p * dp, axis=0, keepdims=True) / total)
        for (_, dp), top, p, total in zip(products, tops, weights, totals)
    ]


def merge_stats(ea, da, eb, db):
    top = jnp.maximum(ea, eb)
    wa, wb = jnp.exp(ea - top), jnp.exp(eb - top)
    total = wa + wb
    return top + jnp.log(total), (wa * da + wb * db) / total


def level_weights(operands, stats):
    products = [(dot_nt(k, q) * SCALE, dot_nt(v, u)) for k, v, q, u in operands]
    found = []
    for (s, dp), (lse, delta) in zip(products, stats):
        g = jnp.exp(s - lse)
        found.append((g.astype(BF16), (g * (dp - delta)).astype(BF16)))
    return found


def level_parts(operands, stats):
    found = level_weights(operands, stats)
    keyed = [
        (dot(ds, q) * SCALE, dot(p, u)) for (p, ds), (k, v, q, u) in zip(found, operands)
    ]
    queried = [
        (dot_tn(p, v), dot_tn(ds, k) * SCALE) for (p, ds), (k, v, q, u) in zip(found, operands)
    ]
    return [a + b for a, b in zip(queried, keyed)]


def pick_rows(ref, rows):
    quarter = rows // DILATION
    lane = lanes_of(quarter)
    picked = jnp.zeros((quarter, LANES), F32)
    for residue in range(DILATION):
        part = ref[pl.ds(residue, quarter, stride=DILATION), :]
        picked = jnp.where(lane % DILATION == residue, part, picked)
    return picked


def fetch(sources, buffers, sems):
    width = DILATION * HEAD_DIM
    groups = []
    for group in range(HEADS // DILATION):
        cols = pl.ds(group * width, width)
        groups.append(
            [
                pltpu.make_async_copy(
                    source.at[:, cols], buffers.at[which, :, cols], sems.at[which, group]
                )
                for which, source in enumerate(sources)
            ]
        )
        for copy in groups[-1]:
            copy.start()
    return groups


def split(x):
    high = x.astype(BF16).astype(F32)
    rest = x - high
    middle = rest.astype(BF16).astype(F32)
    low = rest - middle
    return (high + pltpu.roll(middle, 2 * HEADS, 1) + pltpu.roll(low, 4 * HEADS, 1)).astype(BF16)


def join(ref):
    x = ref[ref.shape[0] - 1].astype(F32)
    x = x + (pltpu.roll(x, LANES - 2 * HEADS, 1) + pltpu.roll(x, LANES - 4 * HEADS, 1))
    return jnp.where(lanes_of(x.shape[0]) < 2 * HEADS, x, 0.0)


def pick_kernel(n_i, slots, *refs):
    sources, refs = refs[:4], refs[4:]
    mids, refs = refs[:n_i], refs[n_i:]
    fulls, refs = refs[:slots], refs[slots:]
    stats_ref, buffers, sems, picked, turn = refs
    rows = sources[0].shape[0]
    quarter = rows // DILATION
    pos, chip = position(slots)
    turn[...] = jnp.zeros_like(turn)
    row = lax.broadcasted_iota(jnp.int32, (quarter, rows), 0) * DILATION
    taken = lax.broadcasted_iota(jnp.int32, (quarter, rows), 1)
    chosen = [jnp.where(taken == row + i, 1.0, 0.0).astype(BF16) for i in range(DILATION)]
    for group, copies in enumerate(fetch(sources, buffers, sems)):
        for which, copy in enumerate(copies):
            copy.wait()
            for residue in range(DILATION):
                head = group * DILATION + residue
                rowset = dot(chosen[residue], buffers[which, :, static_columns(head)])
                picked[head // slots, which * slots + head % slots] = rowset.astype(BF16)
        heads = range(group * DILATION, (group + 1) * DILATION)
        operands = [[buffers[which, :, static_columns(head)] for which in range(4)] for head in heads]
        for head, (e, d) in zip(heads, level_stats(operands)):
            turn[head : head + 1, :] = e
            turn[HEADS + head : HEADS + head + 1, :] = d
    stats_ref[...] = turn[: 2 * HEADS, :]
    turn[...] = turn[...].T
    near = split(pick_rows(turn, rows))
    for d in range(n_i):
        mids[d][: 4 * slots] = picked[pos ^ d]
        mids[d][4 * slots] = near
    for m in range(slots):
        fulls[m][...] = buffers[:, :, head_columns(pos * slots + (chip ^ m))]


def pack_kernel(slots, *refs):
    packed_ref = refs[-1]
    for m, ref in enumerate(refs[:slots]):
        packed_ref[m] = ref[:2]


def far_keys(fulls, sibs, which):
    blocks = [ref[which] for ref in fulls]
    return jnp.concatenate(blocks + [ref[m, which] for ref in sibs for m in range(len(fulls))], axis=0)


def far_stats_kernel(slots, *refs):
    fulls, sibs, stats_ref = refs[:slots], refs[slots:-2], refs[-1]
    keys, values = far_keys(fulls, sibs, 0), far_keys(fulls, sibs, 1)
    for m in range(slots):
        ((e, d),) = level_stats([(keys, values, fulls[m][2], fulls[m][3])])
        stats_ref[m : m + 1, :] = e
        stats_ref[slots + m : slots + m + 1, :] = d


def middle_operands(slots, mids, slot):
    return [
        jnp.concatenate([ref[which * slots + slot] for ref in mids], axis=0) for which in range(4)
    ]


def middle_stats_kernel(n_i, slots, *refs):
    mids, refs = in_order(refs[:n_i]), refs[n_i:]
    near_ref, far_ref, xmsg_ref, stats_ref, columns_ref, turn, spread = refs
    rows = near_ref.shape[1]
    quarter = rows // DILATION
    pos, _ = position(slots)
    turn[...] = jnp.zeros_like(turn)
    operands = [middle_operands(slots, mids, slot) for slot in range(slots)]
    for slot, (e, d) in enumerate(level_stats(operands)):
        turn[slot : slot + 1, :] = e
        turn[slots + slot : slots + slot + 1, :] = d
    stats_ref[...] = turn[: 2 * slots, :]
    columns_ref[...] = turn[...].T
    lane = lanes_of(quarter)
    lane_residue = (pos * slots + lane % slots) % DILATION
    blank = jnp.where(lane < slots, LOWEST, 0.0)
    for residue in range(DILATION):
        spread[pl.ds(residue, quarter, stride=DILATION), :] = jnp.where(
            lane_residue == residue, columns_ref[:quarter], blank
        )
    across = spread[...].T
    e, d = merge_stats(
        near_ref[pl.ds(pos * slots, slots), :],
        near_ref[pl.ds(HEADS + pos * slots, slots), :],
        across[:slots],
        across[slots : 2 * slots],
    )
    xmsg_ref[:slots] = e
    xmsg_ref[slots : 2 * slots] = d
    xmsg_ref[2 * slots :] = far_ref[...]


def middle_parts_kernel(n_i, slots, *refs):
    mids, refs = in_order(refs[:n_i]), refs[n_i:]
    stats_ref, columns_ref = refs[:2]
    refs = refs[2:]
    xmsgs, refs = refs[:slots], refs[slots:]
    outs, (far, turn, spread) = refs[:n_i], refs[n_i:]
    rows = xmsgs[0].shape[1]
    quarter = rows // DILATION
    pos, chip = position(slots)
    for m in range(slots):
        far[pl.ds(chip ^ m, 1), :] = xmsgs[m][2 * slots + m : 2 * slots + m + 1, :]
        far[pl.ds(slots + (chip ^ m), 1), :] = xmsgs[m][3 * slots + m : 3 * slots + m + 1, :]
    e, d = merge_stats(
        xmsgs[0][:slots], xmsgs[0][slots : 2 * slots], far[:slots], far[slots:]
    )
    spread[...] = jnp.zeros_like(spread)
    spread[pl.ds(pos * slots, slots), :] = e
    spread[pl.ds(HEADS + pos * slots, slots), :] = d
    spread[...] = spread[...].T
    own = pick_rows(spread, rows)
    turn[...] = jnp.concatenate([own] + [join(ref) for ref in mids[1:]], axis=0).T
    owned = lax.broadcasted_iota(jnp.int32, (1, n_i * quarter), 1) < quarter
    operands = [middle_operands(slots, mids, slot) for slot in range(slots)]
    merged = [
        merge_stats(
            turn[pl.ds(pos * slots + slot, 1), :],
            turn[pl.ds(HEADS + pos * slots + slot, 1), :],
            jnp.where(owned, LOWEST, stats_ref[slot : slot + 1, :]),
            stats_ref[slots + slot : slots + slot + 1, :],
        )
        for slot in range(slots)
    ]
    for slot, parts in enumerate(level_parts(operands, merged)):
        for which, part in enumerate(parts):
            part = part.astype(BF16)
            for d in range(n_i):
                outs[d][which * slots + slot] = part[d * quarter : (d + 1) * quarter]
    for d in range(n_i):
        outs[d][4 * slots] = split(columns_ref[d * quarter : (d + 1) * quarter])


def far_parts_kernel(slots, width, *refs):
    fulls, refs = refs[:slots], refs[slots:]
    sibs, refs = refs[: width - 1], refs[width - 1 :]
    xmsgs, refs = refs[:slots], refs[slots + 1 :]
    outs, refs = refs[:slots], refs[slots:]
    kvouts, refs = refs[: width - 1], refs[width - 1 :]
    weights, score_grads = refs
    rows = fulls[0].shape[1]
    _, chip = position(slots)
    keys, values = far_keys(fulls, sibs, 0), far_keys(fulls, sibs, 1)
    for m in range(slots):
        lse, delta = merge_stats(
            xmsgs[m][pl.ds(chip, 1), :],
            xmsgs[m][pl.ds(slots + chip, 1), :],
            xmsgs[0][2 * slots + m : 2 * slots + m + 1, :],
            xmsgs[0][3 * slots + m : 3 * slots + m + 1, :],
        )
        operands = (keys, values, fulls[m][2], fulls[m][3])
        ((p, ds),) = level_weights([operands], [(lse, delta)])
        outs[m][0] = dot_tn(p, values).astype(BF16)
        outs[m][1] = (dot_tn(ds, keys) * SCALE).astype(BF16)
        weights[:, m * rows : (m + 1) * rows] = p
        score_grads[:, m * rows : (m + 1) * rows] = ds
    queries = jnp.concatenate([ref[2] for ref in fulls], axis=0)
    ups = jnp.concatenate([ref[3] for ref in fulls], axis=0)
    key_part = (dot(score_grads[...], queries) * SCALE).astype(BF16)
    value_part = dot(weights[...], ups).astype(BF16)
    for index in range(width * slots):
        block = slice(index * rows, (index + 1) * rows)
        part, m = index // slots, index % slots
        if part == 0:
            outs[m][2], outs[m][3] = key_part[block], value_part[block]
        else:
            kvouts[part - 1][m, 0], kvouts[part - 1][m, 1] = key_part[block], value_part[block]


def far_sum_kernel(slots, *refs):
    own, refs = refs[:slots], refs[slots:]
    found, outs = refs[: -slots - 1], refs[-slots:]
    for m in range(slots):
        outs[m][:2] = own[m][:2]
        total = own[m][2:].astype(F32)
        for ref in found:
            total += ref[m].astype(F32)
        outs[m][2:] = total.astype(BF16)


def near_statistics(slots, places, near_ref, mids, xmsgs, stats_ref, spread):
    rows = near_ref.shape[1]
    quarter = rows // DILATION
    pos, chip = position(slots)
    lane = lanes_of(quarter)
    mid = jnp.zeros((quarter, LANES), F32)
    for d, ref in zip(places, mids):
        place = (pos ^ d) * slots
        found = join(ref)
        e = pltpu.roll(found, place, 1)
        de = pltpu.roll(found, place + HEADS - slots, 1)
        mid = jnp.where((lane >= place) & (lane < place + slots), e, mid)
        mid = jnp.where((lane >= HEADS + place) & (lane < HEADS + place + slots), de, mid)
    blank = jnp.where(lane < HEADS, LOWEST, 0.0)
    for residue in range(DILATION):
        spread[pl.ds(residue, quarter, stride=DILATION), :] = jnp.where(
            lane % DILATION == residue, mid, blank
        )
    across = spread[...].T
    e, d = merge_stats(
        near_ref[:HEADS], near_ref[HEADS:], across[:HEADS], across[HEADS : 2 * HEADS]
    )
    if xmsgs:
        stats_ref[:HEADS] = jnp.full((HEADS, rows), LOWEST, F32)
        stats_ref[HEADS:] = jnp.zeros((HEADS, rows), F32)
        for m in range(slots):
            head = pos * slots + (chip ^ m)
            stats_ref[pl.ds(head, 1), :] = xmsgs[m][2 * slots + m : 2 * slots + m + 1, :]
            stats_ref[pl.ds(HEADS + head, 1), :] = xmsgs[m][3 * slots + m : 3 * slots + m + 1, :]
        e, d = merge_stats(e, d, stats_ref[:HEADS], stats_ref[HEADS:])
    stats_ref[:HEADS] = e
    stats_ref[HEADS:] = d


def near_place(slots, d, sources, stats_ref):
    pos, _ = position(slots)
    heads = [(pos ^ d) * slots + slot for slot in range(slots)]
    operands = [[ref[:, head_columns(head)] for ref in sources] for head in heads]
    stats = [(stats_ref[pl.ds(head, 1), :], stats_ref[pl.ds(HEADS + head, 1), :]) for head in heads]
    return level_parts(operands, stats)


def far_sum_kernel(slots, *refs):
    own, refs = refs[:slots], refs[slots:]
    found, outs = refs[: -slots - 1], refs[-slots:]
    for m in range(slots):
        outs[m][:2] = own[m][:2]
        total = own[m][2:].astype(F32)
        for ref in found:
            total += ref[m].astype(F32)
        outs[m][2:] = total.astype(BF16)


def near_statistics(slots, places, near_ref, mids, xmsgs, stats_ref, spread):
    rows = near_ref.shape[1]
    quarter = rows // DILATION
    pos, chip = position(slots)
    lane = lanes_of(quarter)
    mid = jnp.zeros((quarter, LANES), F32)
    for d, ref in zip(places, mids):
        place = (pos ^ d) * slots
        found = join(ref)
        e = pltpu.roll(found, place, 1)
        de = pltpu.roll(found, place + HEADS - slots, 1)
        mid = jnp.where((lane >= place) & (lane < place + slots), e, mid)
        mid = jnp.where((lane >= HEADS + place) & (lane < HEADS + place + slots), de, mid)
    blank = jnp.where(lane < HEADS, LOWEST, 0.0)
    for residue in range(DILATION):
        spread[pl.ds(residue, quarter, stride=DILATION), :] = jnp.where(
            lane % DILATION == residue, mid, blank
        )
    across = spread[...].T
    e, d = merge_stats(
        near_ref[:HEADS], near_ref[HEADS:], across[:HEADS], across[HEADS : 2 * HEADS]
    )
    if xmsgs:
        stats_ref[:HEADS] = jnp.full((HEADS, rows), LOWEST, F32)
        stats_ref[HEADS:] = jnp.zeros((HEADS, rows), F32)
        for m in range(slots):
            head = pos * slots + (chip ^ m)
            stats_ref[pl.ds(head, 1), :] = xmsgs[m][2 * slots + m : 2 * slots + m + 1, :]
            stats_ref[pl.ds(HEADS + head, 1), :] = xmsgs[m][3 * slots + m : 3 * slots + m + 1, :]
        e, d = merge_stats(e, d, stats_ref[:HEADS], stats_ref[HEADS:])
    stats_ref[:HEADS] = e
    stats_ref[HEADS:] = d


def near_place(slots, d, sources, stats_ref):
    pos, _ = position(slots)
    heads = [(pos ^ d) * slots + slot for slot in range(slots)]
    operands = [[ref[:, head_columns(head)] for ref in sources] for head in heads]
    stats = [(stats_ref[pl.ds(head, 1), :], stats_ref[pl.ds(HEADS + head, 1), :]) for head in heads]
    return level_parts(operands, stats)


def near_early_kernel(n_i, slots, *refs):
    sources, near_ref, refs = refs[:4], refs[4], refs[5:]
    mids, refs = refs[: n_i - 1], refs[n_i - 1 :]
    xmsgs, (out_ref, stats_ref, spread) = refs[:slots], refs[slots:]
    places = in_turn(list(range(n_i)))[:-1]
    near_statistics(slots, places, near_ref, mids, xmsgs, stats_ref, spread)
    for index, d in enumerate(places):
        for slot, parts in enumerate(near_place(slots, d, sources, stats_ref)):
            for which, part in enumerate(parts):
                out_ref[which, index * slots + slot] = part


def far_sum_kernel(slots, *refs):
    own, refs = refs[:slots], refs[slots:]
    found, outs = refs[: -slots - 1], refs[-slots:]
    for m in range(slots):
        outs[m][:2] = own[m][:2]
        total = own[m][2:].astype(F32)
        for ref in found:
            total += ref[m].astype(F32)
        outs[m][2:] = total.astype(BF16)


def near_parts_kernel(n_i, slots, *refs):
    sources, near_ref, refs = refs[:4], refs[4], refs[5:]
    mids, refs = (refs[0], *refs[n_i - 1 : 0 : -1]), refs[n_i:]
    xmsgs, (out_ref, stats_ref, spread) = refs[:slots], refs[slots:]
    rows = near_ref.shape[1]
    quarter = rows // DILATION
    pos, chip = position(slots)
    lane = lanes_of(quarter)
    mid = jnp.zeros((quarter, LANES), F32)
    for d in range(n_i):
        place = (pos ^ d) * slots
        found = join(mids[d])
        e = pltpu.roll(found, place, 1)
        de = pltpu.roll(found, place + HEADS - slots, 1)
        mid = jnp.where((lane >= place) & (lane < place + slots), e, mid)
        mid = jnp.where((lane >= HEADS + place) & (lane < HEADS + place + slots), de, mid)
    blank = jnp.where(lane < HEADS, LOWEST, 0.0)
    for residue in range(DILATION):
        spread[pl.ds(residue, quarter, stride=DILATION), :] = jnp.where(
            lane % DILATION == residue, mid, blank
        )
    across = spread[...].T
    stats_ref[:HEADS] = jnp.full((HEADS, rows), LOWEST, F32)
    stats_ref[HEADS:] = jnp.zeros((HEADS, rows), F32)
    for m in range(slots):
        head = pos * slots + (chip ^ m)
        stats_ref[pl.ds(head, 1), :] = xmsgs[m][2 * slots + m : 2 * slots + m + 1, :]
        stats_ref[pl.ds(HEADS + head, 1), :] = xmsgs[m][3 * slots + m : 3 * slots + m + 1, :]
    e, d = merge_stats(
        near_ref[:HEADS], near_ref[HEADS:], across[:HEADS], across[HEADS : 2 * HEADS]
    )
    e, d = merge_stats(e, d, stats_ref[:HEADS], stats_ref[HEADS:])
    stats_ref[:HEADS] = e
    stats_ref[HEADS:] = d
    for group in range(HEADS // DILATION):
        heads = range(group * DILATION, (group + 1) * DILATION)
        operands = [
            [ref[:, static_columns(head)] for ref in sources] for head in heads
        ]
        stats = [
            (stats_ref[head : head + 1, :], stats_ref[HEADS + head : HEADS + head + 1, :])
            for head in heads
        ]
        for head, parts in zip(heads, level_parts(operands, stats)):
            for which, part in enumerate(parts):
                out_ref[which, head] = part


def spread_rows(slots, d, slot, ref):
    quarter = ref.shape[1]
    rows = quarter * DILATION
    pos, _ = position(slots)
    head = (pos ^ d) * slots + slot
    row = lax.broadcasted_iota(jnp.int32, (rows, quarter), 0)
    taken = lax.broadcasted_iota(jnp.int32, (rows, quarter), 1) * DILATION
    place = jnp.where(row == taken + head % DILATION, 1.0, 0.0).astype(BF16)
    return dot(place, jnp.concatenate([ref[which * slots + slot] for which in range(4)], axis=1))


def send_place(slots, d, ready, outs, sems):
    pos, _ = position(slots)
    width = slots * HEAD_DIM
    cols = pl.ds(pl.multiple_of((pos ^ d) * width, width), width)
    copies = [
        pltpu.make_async_copy(ready.at[which], out.at[:, cols], sems.at[which])
        for which, out in enumerate(outs)
    ]
    for copy in copies:
        copy.start()
    return copies


def finish_place(slots, d, near, mid_ref, ready, outs, sems):
    found = [spread_rows(slots, d, slot, mid_ref) for slot in range(slots)]
    for slot, parts in enumerate(found):
        for which in range(4):
            total = near[slot][which] + parts[:, static_columns(which)]
            ready[which, :, static_columns(slot)] = total.astype(BF16)
    return send_place(slots, d, ready, outs, sems)


def near_early_kernel(n_i, slots, *refs):
    sources, near_ref, refs = refs[:4], refs[4], refs[5:]
    mids, refs = refs[: n_i - 1], refs[n_i - 1 :]
    xmsgs, refs = refs[:slots], refs[slots:]
    outs, (own_ref, ready, sems, stats_ref, spread) = refs[:4], refs[4:]
    places = in_turn(list(range(n_i)))[:-1]
    near_statistics(slots, places, near_ref, mids, xmsgs, stats_ref, spread)
    copies = []
    for index, d in enumerate(places[1:]):
        near = near_place(slots, d, sources, stats_ref)
        copies += finish_place(
            slots, d, near, mids[index + 1], ready.at[index], outs, sems.at[index]
        )
    for slot, parts in enumerate(near_place(slots, 0, sources, stats_ref)):
        for which, part in enumerate(parts):
            own_ref[which, slot] = part
    for copy in copies:
        copy.wait()


def final_last_kernel(n_i, slots, *refs):
    sources, near_ref, mid_ref, refs = refs[:4], refs[4], refs[5], refs[6 + 4 :]
    outs, (ready, sems, stats_ref, spread) = refs[:4], refs[4:]
    d = in_turn(list(range(n_i)))[-1]
    near_statistics(slots, [d], near_ref, [mid_ref], (), stats_ref, spread)
    near = near_place(slots, d, sources, stats_ref)
    for copy in finish_place(slots, d, near, mid_ref, ready, outs, sems):
        copy.wait()


def final_own_kernel(slots, own_ref, mid_ref, *refs):
    fulls, refs = in_back(refs[:slots]), refs[slots:]
    outs, (ready, sems) = refs[4:8], refs[8:]
    _, chip = position(slots)
    found = [spread_rows(slots, 0, chip ^ m, mid_ref) for m in range(slots)]
    for m, parts in enumerate(found):
        slot = chip ^ m
        for which in range(4):
            total = own_ref[which, slot] + parts[:, static_columns(which)]
            total += fulls[m][which].astype(F32)
            ready[which, :, head_columns(slot)] = total.astype(BF16)
    for copy in send_place(slots, 0, ready, outs, sems):
        copy.wait()


def settle_kernel(*refs):
    refs[-1][...] = jnp.zeros_like(refs[-1])


def call(kernel, name, outs, scratch, flops, operands, hbm_in=(), hbm_out=0, cheap=False, limit=VMEM_LIMIT, aliases=None):
    moved = sum(x.size * x.dtype.itemsize for x in tuple(operands) + tuple(outs))
    if cheap:
        flops, moved = 1, 1
    spaces = [pltpu.HBM if i in hbm_in else pltpu.VMEM for i in range(len(operands))]
    return pl.pallas_call(
        kernel,
        out_shape=tuple(outs),
        in_specs=[pl.BlockSpec(memory_space=space) for space in spaces],
        out_specs=tuple(
            pl.BlockSpec(memory_space=pltpu.HBM if i < hbm_out else pltpu.VMEM)
            for i in range(len(outs))
        ),
        scratch_shapes=scratch,
        input_output_aliases=aliases or {},
        compiler_params=pltpu.CompilerParams(vmem_limit_bytes=limit),
        cost_estimate=pl.CostEstimate(flops=flops, bytes_accessed=moved, transcendentals=0),
        name=name,
    )(*operands)


def in_turn(pieces):
    return [pieces[0], pieces[-1], *pieces[1:-1]]


def in_back(pieces):
    return [pieces[0], *pieces[:0:-1]]


def in_order(pieces):
    return [pieces[0], *pieces[2:], pieces[1]]


def swap(x, axis, n, mask):
    return lax.ppermute(x, axis, [(i, i ^ mask) for i in range(n)])


def local(query_rows, key_rows, value_rows, upstream):
    rows, features = query_rows.shape
    n_i, n_o = lax.axis_size("seqi"), lax.axis_size("seqo")
    slots = HEADS // n_i
    width = n_o // slots
    others = (width - 1) * slots
    quarter = rows // DILATION
    sources = (key_rows, value_rows, query_rows, upstream)
    unit = 2 * rows * rows * HEAD_DIM
    bind = functools.partial

    mid = SHAPE((4 * slots + 1, quarter, HEAD_DIM), BF16)
    full = SHAPE((4, rows, HEAD_DIM), BF16)
    half = SHAPE((slots, 2, rows, HEAD_DIM), BF16)
    square = pltpu.VMEM((LANES, rows), F32)

    def stats(count, lanes=rows):
        return SHAPE((count, lanes), F32)

    def swap_mids(pieces):
        found = {d: swap(pieces[d], "seqi", n_i, d) for d in reversed(range(1, n_i))}
        return [pieces[0]] + [found[d] for d in range(1, n_i)]

    def swap_fulls(pieces):
        return [pieces[0]] + [swap(pieces[m], "seqo", n_o, m * width) for m in range(1, slots)]

    pieces = call(
        bind(pick_kernel, n_i, slots),
        "pick",
        [mid] * n_i + [full] * slots + [stats(2 * HEADS)],
        [
            pltpu.VMEM((4, rows, features), BF16),
            pltpu.SemaphoreType.DMA((4, HEADS // DILATION)),
            pltpu.VMEM((n_i, 4 * slots, quarter, HEAD_DIM), BF16),
            square,
        ],
        unit * HEADS * 2,
        sources,
        hbm_in=range(4),
        limit=PICK_LIMIT,
    )
    mids = swap_mids(pieces[:n_i])
    fulls = swap_fulls(pieces[n_i : n_i + slots])
    near = pieces[-1]

    (settled,) = call(settle_kernel, "far_in", [stats(8)], [], SHORT, [mids[-1]])
    (settled,) = call(settle_kernel, "chips_back", [stats(8)], [], LONG, [settled])
    (packed,) = call(bind(pack_kernel, slots), "pack", [half], [], 1, fulls + [settled])
    sibs = [swap(packed, "seqo", n_o, part) for part in range(1, width)]
    (settled,) = call(settle_kernel, "packed_back", [stats(8)], [], LONG, [near])
    (far,) = call(
        bind(far_stats_kernel, slots),
        "far_stats",
        [stats(2 * slots)],
        [],
        1,
        fulls + sibs + [settled],
    )
    xmsg, middle, columns = call(
        bind(middle_stats_kernel, n_i, slots),
        "middle_stats",
        [stats(4 * slots), stats(2 * slots, n_i * quarter), stats(n_i * quarter, LANES)],
        [pltpu.VMEM((LANES, n_i * quarter), F32), square],
        unit * slots * 2,
        in_turn(mids) + [near, far],
    )
    xmsgs = swap_fulls([xmsg] * slots)

    midparts = call(
        bind(middle_parts_kernel, n_i, slots),
        "middle_parts",
        [mid] * n_i,
        [pltpu.VMEM((2 * slots, rows), F32), pltpu.VMEM((LANES, n_i * quarter), F32), square],
        unit * slots * 6,
        in_turn(mids) + [middle, columns] + xmsgs,
    )
    midparts = swap_mids(midparts)
    farparts = call(
        bind(far_parts_kernel, slots, width),
        "far_parts",
        [full] * slots + [half] * (width - 1),
        [pltpu.VMEM((n_o * rows, slots * rows), BF16)] * 2,
        unit * n_o * slots * 6,
        fulls + sibs + xmsgs + [midparts[0]],
        cheap=True,
    )
    sibparts = [swap(x, "seqo", n_o, part + 1) for part, x in enumerate(farparts[slots:])]
    (settled,) = call(settle_kernel, "far_back", [stats(8)], [], SHORT, [midparts[-1]])
    (settled,) = call(settle_kernel, "sib_back", [stats(8)], [], 1, sibparts + [settled])
    (settled,) = call(settle_kernel, "settle", [stats(8)], [], LONG, [settled])
    fullparts = call(
        bind(far_sum_kernel, slots),
        "far_sum",
        [full] * slots,
        [],
        unit,
        list(farparts[:slots]) + sibparts + [settled],
        cheap=True,
    )
    fullparts = swap_fulls(fullparts)

    back = in_turn(midparts)
    kept = [pltpu.VMEM((2 * HEADS, rows), F32), square]
    whole = [SHAPE((rows, features), BF16)] * 4
    ready = pltpu.VMEM((4, rows, slots * HEAD_DIM), BF16)
    *outs, own = call(
        bind(near_early_kernel, n_i, slots),
        "near_early",
        whole + [SHAPE((4, slots, rows, HEAD_DIM), F32)],
        [
            pltpu.VMEM((n_i - 2, 4, rows, slots * HEAD_DIM), BF16),
            pltpu.SemaphoreType.DMA((n_i - 2, 4)),
            *kept,
        ],
        SHORT,
        [*sources, near, *back[:-1], *xmsgs],
        hbm_out=4,
    )
    outs = call(
        bind(final_last_kernel, n_i, slots),
        "final_last",
        whole,
        [ready, pltpu.SemaphoreType.DMA((4,)), *kept],
        SHORT // 2,
        [*sources, near, back[-1], *outs],
        hbm_in=range(6, 10),
        hbm_out=4,
        aliases={6 + which: which for which in range(4)},
    )
    return call(
        bind(final_own_kernel, slots),
        "final_own",
        whole,
        [ready, pltpu.SemaphoreType.DMA((4,))],
        unit * slots,
        [own, midparts[0], *in_back(fullparts), *outs],
        hbm_in=range(2 + slots, 6 + slots),
        hbm_out=4,
        aliases={2 + slots + which: which for which in range(4)},
    )


def solution(mesh):
    rows = P(("seqo", "seqi"), None)
    return jax.shard_map(
        local,
        mesh=mesh,
        in_specs=(rows,) * 4,
        out_specs=(rows,) * 4,
        check_vma=False,
    )
```

```python
import functools

import jax
import jax.numpy as jnp
from jax import lax
from jax.experimental import pallas as pl
from jax.experimental.pallas import tpu as pltpu
from jax.sharding import PartitionSpec as P

HEADS = 16
HEAD_DIM = 128
DILATION = 4
LANES = 128
SCALE = HEAD_DIM**-0.5
LOWEST = -1e30
LONG = 4 * 10**10
SHORT = 2 * 10**9
VMEM_LIMIT = 32 * 1024 * 1024
PICK_LIMIT = 53 * 1024 * 1024
NEAR_LIMIT = 54784 * 1024
F32, BF16 = jnp.float32, jnp.bfloat16
SHAPE = jax.ShapeDtypeStruct

NT = (((1,), (1,)), ((), ()))
TN = (((0,), (0,)), ((), ()))


def dot(a, b):
    return jnp.dot(a, b, preferred_element_type=F32)


def dot_nt(a, b):
    return lax.dot_general(a, b, NT, preferred_element_type=F32)


def dot_tn(a, b):
    return lax.dot_general(a, b, TN, preferred_element_type=F32)


def head_columns(head):
    return pl.ds(pl.multiple_of(head * HEAD_DIM, HEAD_DIM), HEAD_DIM)


def static_columns(index):
    return slice(index * HEAD_DIM, (index + 1) * HEAD_DIM)


def position(slots):
    width = lax.axis_size("seqo") // slots
    return lax.axis_index("seqi"), lax.axis_index("seqo") // width


def distance(n_i, step, odd):
    order = [1, *range(n_i - 1, 1, -1)] if odd else list(range(n_i - 1, 0, -1))
    return order[step - 1]


def place_at(n_i, slots, step):
    pos, _ = position(slots)
    if step == 0:
        return pos * slots
    odd = lax.axis_index("seqo") % 2 == 1
    far = jnp.where(odd, distance(n_i, step, True), distance(n_i, step, False))
    return (pos ^ far) * slots


def lanes_of(rows):
    return lax.broadcasted_iota(jnp.int32, (rows, LANES), 1)


def level_stats(operands):
    products = [(dot_nt(k, q) * SCALE, dot_nt(v, u)) for k, v, q, u in operands]
    tops = [jnp.max(s, axis=0, keepdims=True) for s, _ in products]
    weights = [jnp.exp(s - top) for (s, _), top in zip(products, tops)]
    totals = [jnp.sum(p, axis=0, keepdims=True) for p in weights]
    return [
        (top + jnp.log(total), jnp.sum(p * dp, axis=0, keepdims=True) / total)
        for (_, dp), top, p, total in zip(products, tops, weights, totals)
    ]


def merge_stats(ea, da, eb, db):
    top = jnp.maximum(ea, eb)
    wa, wb = jnp.exp(ea - top), jnp.exp(eb - top)
    total = wa + wb
    return top + jnp.log(total), (wa * da + wb * db) / total


def level_weights(operands, stats):
    products = [(dot_nt(k, q) * SCALE, dot_nt(v, u)) for k, v, q, u in operands]
    found = []
    for (s, dp), (lse, delta) in zip(products, stats):
        g = jnp.exp(s - lse)
        found.append((g.astype(BF16), (g * (dp - delta)).astype(BF16)))
    return found


def level_parts(operands, stats):
    found = level_weights(operands, stats)
    keyed = [
        (dot(ds, q) * SCALE, dot(p, u)) for (p, ds), (k, v, q, u) in zip(found, operands)
    ]
    queried = [
        (dot_tn(p, v), dot_tn(ds, k) * SCALE) for (p, ds), (k, v, q, u) in zip(found, operands)
    ]
    return [a + b for a, b in zip(queried, keyed)]


def pick_rows(ref, rows):
    quarter = rows // DILATION
    lane = lanes_of(quarter)
    picked = jnp.zeros((quarter, LANES), F32)
    for residue in range(DILATION):
        part = ref[pl.ds(residue, quarter, stride=DILATION), :]
        picked = jnp.where(lane % DILATION == residue, part, picked)
    return picked


def fetch(sources, buffers, sems):
    width = DILATION * HEAD_DIM
    groups = []
    for group in range(HEADS // DILATION):
        cols = pl.ds(group * width, width)
        groups.append(
            [
                pltpu.make_async_copy(
                    source.at[:, cols], buffers.at[which, :, cols], sems.at[which, group]
                )
                for which, source in enumerate(sources)
            ]
        )
        for copy in groups[-1]:
            copy.start()
    return groups


def split(x):
    high = x.astype(BF16).astype(F32)
    rest = x - high
    middle = rest.astype(BF16).astype(F32)
    low = rest - middle
    return (high + pltpu.roll(middle, 2 * HEADS, 1) + pltpu.roll(low, 4 * HEADS, 1)).astype(BF16)


def join(ref):
    x = ref[ref.shape[0] - 1].astype(F32)
    x = x + (pltpu.roll(x, LANES - 2 * HEADS, 1) + pltpu.roll(x, LANES - 4 * HEADS, 1))
    return jnp.where(lanes_of(x.shape[0]) < 2 * HEADS, x, 0.0)


def pick_kernel(n_i, slots, *refs):
    sources, refs = refs[:4], refs[4:]
    mids, refs = refs[:n_i], refs[n_i:]
    fulls, refs = refs[:slots], refs[slots:]
    stats_ref, buffers, sems, wide, picked, turn = refs
    rows = sources[0].shape[0]
    quarter = rows // DILATION
    pos, chip = position(slots)
    turn[...] = jnp.zeros_like(turn)
    for group, copies in enumerate(fetch(sources, buffers, sems)):
        for which, copy in enumerate(copies):
            copy.wait()
            for residue in range(DILATION):
                head = group * DILATION + residue
                wide[which, head] = buffers[which, :, static_columns(head)].astype(F32)
                rowset = wide[which, head, pl.ds(residue, quarter, stride=DILATION), :]
                picked[head // slots, which * slots + head % slots] = rowset.astype(BF16)
        heads = range(group * DILATION, (group + 1) * DILATION)
        operands = [[buffers[which, :, static_columns(head)] for which in range(4)] for head in heads]
        for head, (e, d) in zip(heads, level_stats(operands)):
            turn[head : head + 1, :] = e
            turn[HEADS + head : HEADS + head + 1, :] = d
    stats_ref[...] = turn[: 2 * HEADS, :]
    turn[...] = turn[...].T
    near = split(pick_rows(turn, rows))
    for d in range(n_i):
        mids[d][: 4 * slots] = picked[place_at(n_i, slots, d) // slots]
        mids[d][4 * slots] = near
    for m in range(slots):
        fulls[m][...] = buffers[:, :, head_columns(pos * slots + (chip ^ m))]


def pack_kernel(slots, *refs):
    packed_ref = refs[-1]
    for m, ref in enumerate(refs[:slots]):
        packed_ref[m] = ref[:2]


def far_keys(fulls, sibs, which):
    blocks = [ref[which] for ref in fulls]
    return jnp.concatenate(blocks + [ref[m, which] for ref in sibs for m in range(len(fulls))], axis=0)


def far_stats_kernel(slots, *refs):
    fulls, sibs, stats_ref = refs[:slots], refs[slots:-2], refs[-1]
    keys, values = far_keys(fulls, sibs, 0), far_keys(fulls, sibs, 1)
    for m in range(slots):
        ((e, d),) = level_stats([(keys, values, fulls[m][2], fulls[m][3])])
        stats_ref[m : m + 1, :] = e
        stats_ref[slots + m : slots + m + 1, :] = d


def middle_operands(slots, mids, slot):
    return [
        jnp.concatenate([ref[which * slots + slot] for ref in mids], axis=0) for which in range(4)
    ]


def middle_stats_kernel(n_i, slots, *refs):
    mids, refs = refs[:n_i], refs[n_i:]
    near_ref, far_ref, xmsg_ref, stats_ref, columns_ref, turn, spread = refs
    rows = near_ref.shape[1]
    quarter = rows // DILATION
    pos, _ = position(slots)
    turn[...] = jnp.zeros_like(turn)
    operands = [middle_operands(slots, mids, slot) for slot in range(slots)]
    for slot, (e, d) in enumerate(level_stats(operands)):
        turn[slot : slot + 1, :] = e
        turn[slots + slot : slots + slot + 1, :] = d
    stats_ref[...] = turn[: 2 * slots, :]
    columns_ref[...] = turn[...].T
    lane = lanes_of(quarter)
    lane_residue = (pos * slots + lane % slots) % DILATION
    blank = jnp.where(lane < slots, LOWEST, 0.0)
    for residue in range(DILATION):
        spread[pl.ds(residue, quarter, stride=DILATION), :] = jnp.where(
            lane_residue == residue, columns_ref[:quarter], blank
        )
    across = spread[...].T
    e, d = merge_stats(
        near_ref[pl.ds(pos * slots, slots), :],
        near_ref[pl.ds(HEADS + pos * slots, slots), :],
        across[:slots],
        across[slots : 2 * slots],
    )
    xmsg_ref[:slots] = e
    xmsg_ref[slots : 2 * slots] = d
    xmsg_ref[2 * slots :] = far_ref[...]


def middle_parts_kernel(n_i, slots, *refs):
    mids, refs = refs[:n_i], refs[n_i:]
    stats_ref, columns_ref = refs[:2]
    refs = refs[2:]
    xmsgs, refs = refs[:slots], refs[slots:]
    outs, (far, turn, spread) = refs[:n_i], refs[n_i:]
    rows = xmsgs[0].shape[1]
    quarter = rows // DILATION
    pos, chip = position(slots)
    for m in range(slots):
        far[pl.ds(chip ^ m, 1), :] = xmsgs[m][2 * slots + m : 2 * slots + m + 1, :]
        far[pl.ds(slots + (chip ^ m), 1), :] = xmsgs[m][3 * slots + m : 3 * slots + m + 1, :]
    e, d = merge_stats(
        xmsgs[0][:slots], xmsgs[0][slots : 2 * slots], far[:slots], far[slots:]
    )
    spread[...] = jnp.zeros_like(spread)
    spread[pl.ds(pos * slots, slots), :] = e
    spread[pl.ds(HEADS + pos * slots, slots), :] = d
    spread[...] = spread[...].T
    own = pick_rows(spread, rows)
    turn[...] = jnp.concatenate([own] + [join(ref) for ref in mids[1:]], axis=0).T
    owned = lax.broadcasted_iota(jnp.int32, (1, n_i * quarter), 1) < quarter
    operands = [middle_operands(slots, mids, slot) for slot in range(slots)]
    merged = [
        merge_stats(
            turn[pl.ds(pos * slots + slot, 1), :],
            turn[pl.ds(HEADS + pos * slots + slot, 1), :],
            jnp.where(owned, LOWEST, stats_ref[slot : slot + 1, :]),
            stats_ref[slots + slot : slots + slot + 1, :],
        )
        for slot in range(slots)
    ]
    for slot, parts in enumerate(level_parts(operands, merged)):
        for which, part in enumerate(parts):
            part = part.astype(BF16)
            for d in range(n_i):
                outs[d][which * slots + slot] = part[d * quarter : (d + 1) * quarter]
    for d in range(n_i):
        outs[d][4 * slots] = split(columns_ref[d * quarter : (d + 1) * quarter])


def far_parts_kernel(slots, width, *refs):
    fulls, refs = refs[:slots], refs[slots:]
    sibs, refs = refs[: width - 1], refs[width - 1 :]
    xmsgs, refs = refs[:slots], refs[slots + 1 :]
    outs, refs = refs[:slots], refs[slots:]
    kvouts, refs = refs[: width - 1], refs[width - 1 :]
    weights, score_grads = refs
    rows = fulls[0].shape[1]
    _, chip = position(slots)
    keys, values = far_keys(fulls, sibs, 0), far_keys(fulls, sibs, 1)
    for m in range(slots):
        lse, delta = merge_stats(
            xmsgs[m][pl.ds(chip, 1), :],
            xmsgs[m][pl.ds(slots + chip, 1), :],
            xmsgs[0][2 * slots + m : 2 * slots + m + 1, :],
            xmsgs[0][3 * slots + m : 3 * slots + m + 1, :],
        )
        operands = (keys, values, fulls[m][2], fulls[m][3])
        ((p, ds),) = level_weights([operands], [(lse, delta)])
        outs[m][0] = dot_tn(p, values).astype(BF16)
        outs[m][1] = (dot_tn(ds, keys) * SCALE).astype(BF16)
        weights[:, m * rows : (m + 1) * rows] = p
        score_grads[:, m * rows : (m + 1) * rows] = ds
    queries = jnp.concatenate([ref[2] for ref in fulls], axis=0)
    ups = jnp.concatenate([ref[3] for ref in fulls], axis=0)
    key_part = (dot(score_grads[...], queries) * SCALE).astype(BF16)
    value_part = dot(weights[...], ups).astype(BF16)
    for index in range(width * slots):
        block = slice(index * rows, (index + 1) * rows)
        part, m = index // slots, index % slots
        if part == 0:
            outs[m][2], outs[m][3] = key_part[block], value_part[block]
        else:
            kvouts[part - 1][m, 0], kvouts[part - 1][m, 1] = key_part[block], value_part[block]


def far_sum_kernel(slots, *refs):
    own, refs = refs[:slots], refs[slots:]
    found, outs = refs[: -slots - 1], refs[-slots:]
    for m in range(slots):
        outs[m][:2] = own[m][:2]
        total = own[m][2:].astype(F32)
        for ref in found:
            total += ref[m].astype(F32)
        outs[m][2:] = total.astype(BF16)


def near_statistics(n_i, slots, steps, near_ref, mids, xmsgs, stats_ref, spread):
    rows = near_ref.shape[1]
    quarter = rows // DILATION
    pos, chip = position(slots)
    lane = lanes_of(quarter)
    mid = jnp.zeros((quarter, LANES), F32)
    for step, ref in zip(steps, mids):
        place = place_at(n_i, slots, step)
        found = join(ref)
        e = pltpu.roll(found, place, 1)
        de = pltpu.roll(found, place + HEADS - slots, 1)
        mid = jnp.where((lane >= place) & (lane < place + slots), e, mid)
        mid = jnp.where((lane >= HEADS + place) & (lane < HEADS + place + slots), de, mid)
    blank = jnp.where(lane < HEADS, LOWEST, 0.0)
    for residue in range(DILATION):
        spread[pl.ds(residue, quarter, stride=DILATION), :] = jnp.where(
            lane % DILATION == residue, mid, blank
        )
    across = spread[...].T
    e, d = merge_stats(
        near_ref[:HEADS], near_ref[HEADS:], across[:HEADS], across[HEADS : 2 * HEADS]
    )
    if xmsgs:
        stats_ref[:HEADS] = jnp.full((HEADS, rows), LOWEST, F32)
        stats_ref[HEADS:] = jnp.zeros((HEADS, rows), F32)
        for m in range(slots):
            head = pos * slots + (chip ^ m)
            stats_ref[pl.ds(head, 1), :] = xmsgs[m][2 * slots + m : 2 * slots + m + 1, :]
            stats_ref[pl.ds(HEADS + head, 1), :] = xmsgs[m][3 * slots + m : 3 * slots + m + 1, :]
        e, d = merge_stats(e, d, stats_ref[:HEADS], stats_ref[HEADS:])
    stats_ref[:HEADS] = e
    stats_ref[HEADS:] = d


def near_place(n_i, slots, step, sources, stats_ref):
    heads = [place_at(n_i, slots, step) + slot for slot in range(slots)]
    operands = [[ref[:, head_columns(head)] for ref in sources] for head in heads]
    stats = [(stats_ref[pl.ds(head, 1), :], stats_ref[pl.ds(HEADS + head, 1), :]) for head in heads]
    return level_parts(operands, stats)


def near_early_kernel(n_i, slots, *refs):
    sources, near_ref, refs = refs[:4], refs[4], refs[5:]
    mids, refs = refs[: n_i - 1], refs[n_i - 1 :]
    xmsgs, (out_ref, stats_ref, spread) = refs[:slots], refs[slots:]
    near_statistics(n_i, slots, range(n_i - 1), near_ref, mids, xmsgs, stats_ref, spread)
    for step in range(n_i - 1):
        for slot, parts in enumerate(near_place(n_i, slots, step, sources, stats_ref)):
            for which, part in enumerate(parts):
                out_ref[which, step * slots + slot] = part


def far_sum_kernel(slots, *refs):
    own, refs = refs[:slots], refs[slots:]
    found, outs = refs[: -slots - 1], refs[-slots:]
    for m in range(slots):
        outs[m][:2] = own[m][:2]
        total = own[m][2:].astype(F32)
        for ref in found:
            total += ref[m].astype(F32)
        outs[m][2:] = total.astype(BF16)


def near_parts_kernel(n_i, slots, *refs):
    sources, near_ref, refs = refs[:4], refs[4], refs[5:]
    mids, refs = (refs[0], *refs[n_i - 1 : 0 : -1]), refs[n_i:]
    xmsgs, (out_ref, stats_ref, spread) = refs[:slots], refs[slots:]
    rows = near_ref.shape[1]
    quarter = rows // DILATION
    pos, chip = position(slots)
    lane = lanes_of(quarter)
    mid = jnp.zeros((quarter, LANES), F32)
    for d in range(n_i):
        place = (pos ^ d) * slots
        found = join(mids[d])
        e = pltpu.roll(found, place, 1)
        de = pltpu.roll(found, place + HEADS - slots, 1)
        mid = jnp.where((lane >= place) & (lane < place + slots), e, mid)
        mid = jnp.where((lane >= HEADS + place) & (lane < HEADS + place + slots), de, mid)
    blank = jnp.where(lane < HEADS, LOWEST, 0.0)
    for residue in range(DILATION):
        spread[pl.ds(residue, quarter, stride=DILATION), :] = jnp.where(
            lane % DILATION == residue, mid, blank
        )
    across = spread[...].T
    stats_ref[:HEADS] = jnp.full((HEADS, rows), LOWEST, F32)
    stats_ref[HEADS:] = jnp.zeros((HEADS, rows), F32)
    for m in range(slots):
        head = pos * slots + (chip ^ m)
        stats_ref[pl.ds(head, 1), :] = xmsgs[m][2 * slots + m : 2 * slots + m + 1, :]
        stats_ref[pl.ds(HEADS + head, 1), :] = xmsgs[m][3 * slots + m : 3 * slots + m + 1, :]
    e, d = merge_stats(
        near_ref[:HEADS], near_ref[HEADS:], across[:HEADS], across[HEADS : 2 * HEADS]
    )
    e, d = merge_stats(e, d, stats_ref[:HEADS], stats_ref[HEADS:])
    stats_ref[:HEADS] = e
    stats_ref[HEADS:] = d
    for group in range(HEADS // DILATION):
        heads = range(group * DILATION, (group + 1) * DILATION)
        operands = [
            [ref[:, static_columns(head)] for ref in sources] for head in heads
        ]
        stats = [
            (stats_ref[head : head + 1, :], stats_ref[HEADS + head : HEADS + head + 1, :])
            for head in heads
        ]
        for head, parts in zip(heads, level_parts(operands, stats)):
            for which, part in enumerate(parts):
                out_ref[which, head] = part


def spread_rows(slots, head, slot, ref):
    quarter = ref.shape[1]
    rows = quarter * DILATION
    row = lax.broadcasted_iota(jnp.int32, (rows, quarter), 0)
    taken = lax.broadcasted_iota(jnp.int32, (rows, quarter), 1) * DILATION
    place = jnp.where(row == taken + head % DILATION, 1.0, 0.0).astype(BF16)
    return dot(place, jnp.concatenate([ref[which * slots + slot] for which in range(4)], axis=1))


def send_place(slots, first, ready, outs, sems):
    width = slots * HEAD_DIM
    cols = pl.ds(pl.multiple_of(first * HEAD_DIM, width), width)
    copies = [
        pltpu.make_async_copy(ready.at[which], out.at[:, cols], sems.at[which])
        for which, out in enumerate(outs)
    ]
    for copy in copies:
        copy.start()
    return copies


def final_others_kernel(n_i, slots, *refs):
    sources, near_ref, early_ref, refs = refs[:4], refs[4], refs[5], refs[6:]
    mids, refs = refs[: n_i - 1], refs[n_i - 1 :]
    outs, (ready, sems, stats_ref, spread) = refs[:4], refs[4:]
    last = n_i - 1
    near_statistics(n_i, slots, [last], near_ref, mids[-1:], (), stats_ref, spread)
    late = near_place(n_i, slots, last, sources, stats_ref)
    copies = []
    for step in range(1, n_i):
        first = place_at(n_i, slots, step)
        found = [spread_rows(slots, first + slot, slot, mids[step - 1]) for slot in range(slots)]
        for slot, parts in enumerate(found):
            for which in range(4):
                near = late[slot][which] if step == last else early_ref[which, step * slots + slot]
                total = near + parts[:, static_columns(which)]
                ready[step - 1, which, :, static_columns(slot)] = total.astype(BF16)
        copies += send_place(slots, first, ready.at[step - 1], outs, sems.at[step - 1])
    for copy in copies:
        copy.wait()


def final_own_kernel(slots, early_ref, mid_ref, *refs):
    fulls, refs = in_back(refs[:slots]), refs[slots:]
    outs, (ready, sems) = refs[4:8], refs[8:]
    pos, chip = position(slots)
    first = pos * slots
    found = [spread_rows(slots, first + (chip ^ m), chip ^ m, mid_ref) for m in range(slots)]
    for m, parts in enumerate(found):
        slot = chip ^ m
        for which in range(4):
            total = early_ref[which, slot] + parts[:, static_columns(which)]
            total += fulls[m][which].astype(F32)
            ready[which, :, head_columns(slot)] = total.astype(BF16)
    for copy in send_place(slots, first, ready, outs, sems):
        copy.wait()


def settle_kernel(*refs):
    refs[-1][...] = jnp.zeros_like(refs[-1])


def call(kernel, name, outs, scratch, flops, operands, hbm_in=(), hbm_out=False, cheap=False, limit=VMEM_LIMIT, aliases=None):
    moved = sum(x.size * x.dtype.itemsize for x in tuple(operands) + tuple(outs))
    if cheap:
        flops, moved = 1, 1
    spaces = [pltpu.HBM if i in hbm_in else pltpu.VMEM for i in range(len(operands))]
    return pl.pallas_call(
        kernel,
        out_shape=tuple(outs),
        in_specs=[pl.BlockSpec(memory_space=space) for space in spaces],
        out_specs=tuple(
            pl.BlockSpec(memory_space=pltpu.HBM if hbm_out else pltpu.VMEM) for _ in outs
        ),
        scratch_shapes=scratch,
        input_output_aliases=aliases or {},
        compiler_params=pltpu.CompilerParams(vmem_limit_bytes=limit),
        cost_estimate=pl.CostEstimate(flops=flops, bytes_accessed=moved, transcendentals=0),
        name=name,
    )(*operands)


def in_back(pieces):
    return [pieces[0], *pieces[:0:-1]]


def swap(x, axis, n, mask):
    return lax.ppermute(x, axis, [(i, i ^ mask) for i in range(n)])


def local(query_rows, key_rows, value_rows, upstream):
    rows, features = query_rows.shape
    n_i, n_o = lax.axis_size("seqi"), lax.axis_size("seqo")
    slots = HEADS // n_i
    width = n_o // slots
    others = (width - 1) * slots
    quarter = rows // DILATION
    sources = (key_rows, value_rows, query_rows, upstream)
    unit = 2 * rows * rows * HEAD_DIM
    bind = functools.partial

    mid = SHAPE((4 * slots + 1, quarter, HEAD_DIM), BF16)
    full = SHAPE((4, rows, HEAD_DIM), BF16)
    half = SHAPE((slots, 2, rows, HEAD_DIM), BF16)
    square = pltpu.VMEM((LANES, rows), F32)

    def stats(count, lanes=rows):
        return SHAPE((count, lanes), F32)

    def swap_mids(pieces):
        found = [pieces[0]]
        for step in range(1, n_i):
            pairs = [
                (o * n_i + i, o * n_i + (i ^ distance(n_i, step, o % 2 == 1)))
                for o in range(n_o)
                for i in range(n_i)
            ]
            found.append(lax.ppermute(pieces[step], ("seqo", "seqi"), pairs))
        return found

    def swap_fulls(pieces):
        return [pieces[0]] + [swap(pieces[m], "seqo", n_o, m * width) for m in range(1, slots)]

    pieces = call(
        bind(pick_kernel, n_i, slots),
        "pick",
        [mid] * n_i + [full] * slots + [stats(2 * HEADS)],
        [
            pltpu.VMEM((4, rows, features), BF16),
            pltpu.SemaphoreType.DMA((4, HEADS // DILATION)),
            pltpu.VMEM((4, HEADS, rows, HEAD_DIM), F32),
            pltpu.VMEM((n_i, 4 * slots, quarter, HEAD_DIM), BF16),
            square,
        ],
        unit * HEADS * 2,
        sources,
        hbm_in=range(4),
        limit=PICK_LIMIT,
    )
    mids = swap_mids(pieces[:n_i])
    fulls = swap_fulls(pieces[n_i : n_i + slots])
    near = pieces[-1]

    (settled,) = call(settle_kernel, "far_in", [stats(8)], [], SHORT, [mids[1]])
    (settled,) = call(settle_kernel, "chips_back", [stats(8)], [], LONG, [settled])
    (packed,) = call(bind(pack_kernel, slots), "pack", [half], [], 1, fulls + [settled])
    sibs = [swap(packed, "seqo", n_o, part) for part in range(1, width)]
    (settled,) = call(settle_kernel, "packed_back", [stats(8)], [], LONG, [near])
    (far,) = call(
        bind(far_stats_kernel, slots),
        "far_stats",
        [stats(2 * slots)],
        [],
        1,
        fulls + sibs + [settled],
    )
    xmsg, middle, columns = call(
        bind(middle_stats_kernel, n_i, slots),
        "middle_stats",
        [stats(4 * slots), stats(2 * slots, n_i * quarter), stats(n_i * quarter, LANES)],
        [pltpu.VMEM((LANES, n_i * quarter), F32), square],
        unit * slots * 2,
        mids + [near, far],
    )
    xmsgs = swap_fulls([xmsg] * slots)

    midparts = call(
        bind(middle_parts_kernel, n_i, slots),
        "middle_parts",
        [mid] * n_i,
        [pltpu.VMEM((2 * slots, rows), F32), pltpu.VMEM((LANES, n_i * quarter), F32), square],
        unit * slots * 6,
        mids + [middle, columns] + xmsgs,
    )
    midparts = swap_mids(midparts)
    farparts = call(
        bind(far_parts_kernel, slots, width),
        "far_parts",
        [full] * slots + [half] * (width - 1),
        [pltpu.VMEM((n_o * rows, slots * rows), BF16)] * 2,
        unit * n_o * slots * 6,
        fulls + sibs + xmsgs + [midparts[0]],
        cheap=True,
    )
    sibparts = [swap(x, "seqo", n_o, part + 1) for part, x in enumerate(farparts[slots:])]
    (settled,) = call(settle_kernel, "far_back", [stats(8)], [], SHORT, [midparts[1]])
    (settled,) = call(settle_kernel, "sib_back", [stats(8)], [], 1, sibparts + [settled])
    (settled,) = call(settle_kernel, "settle", [stats(8)], [], LONG, [settled])
    fullparts = call(
        bind(far_sum_kernel, slots),
        "far_sum",
        [full] * slots,
        [],
        unit,
        list(farparts[:slots]) + sibparts + [settled],
        cheap=True,
    )
    fullparts = swap_fulls(fullparts)

    back = midparts
    kept = [pltpu.VMEM((2 * HEADS, rows), F32), square]
    (early,) = call(
        bind(near_early_kernel, n_i, slots),
        "near_early",
        [SHAPE((4, (n_i - 1) * slots, rows, HEAD_DIM), F32)],
        kept,
        SHORT,
        [*sources, near, *back[:-1], *xmsgs],
    )
    whole = [SHAPE((rows, features), BF16)] * 4
    outs = call(
        bind(final_others_kernel, n_i, slots),
        "final_others",
        whole,
        [
            pltpu.VMEM((n_i - 1, 4, rows, slots * HEAD_DIM), BF16),
            pltpu.SemaphoreType.DMA((n_i - 1, 4)),
            *kept,
        ],
        SHORT // 2,
        [*sources, near, early, *back[1:]],
        hbm_out=True,
    )
    return call(
        bind(final_own_kernel, slots),
        "final_own",
        whole,
        [pltpu.VMEM((4, rows, slots * HEAD_DIM), BF16), pltpu.SemaphoreType.DMA((4,))],
        unit * slots,
        [early, midparts[0], *in_back(fullparts), *outs],
        hbm_in=range(2 + slots, 6 + slots),
        hbm_out=True,
        aliases={2 + slots + which: which for which in range(4)},
    )


def solution(mesh):
    rows = P(("seqo", "seqi"), None)
    return jax.shard_map(
        local,
        mesh=mesh,
        in_specs=(rows,) * 4,
        out_specs=(rows,) * 4,
        check_vma=False,
    )
```

```python
import functools

import jax
import jax.numpy as jnp
from jax import lax
from jax.experimental import pallas as pl
from jax.experimental.pallas import tpu as pltpu
from jax.sharding import PartitionSpec as P

HEADS = 16
HEAD_DIM = 128
DILATION = 4
LANES = 128
SCALE = HEAD_DIM**-0.5
LOWEST = -1e30
LONG = 4 * 10**10
SHORT = 2 * 10**9
VMEM_LIMIT = 32 * 1024 * 1024
PICK_LIMIT = 53 * 1024 * 1024
NEAR_LIMIT = 54784 * 1024
F32, BF16 = jnp.float32, jnp.bfloat16
SHAPE = jax.ShapeDtypeStruct

NT = (((1,), (1,)), ((), ()))
TN = (((0,), (0,)), ((), ()))


def dot(a, b):
    return jnp.dot(a, b, preferred_element_type=F32)


def dot_nt(a, b):
    return lax.dot_general(a, b, NT, preferred_element_type=F32)


def dot_tn(a, b):
    return lax.dot_general(a, b, TN, preferred_element_type=F32)


def head_columns(head):
    return pl.ds(pl.multiple_of(head * HEAD_DIM, HEAD_DIM), HEAD_DIM)


def static_columns(index):
    return slice(index * HEAD_DIM, (index + 1) * HEAD_DIM)


def position(slots):
    width = lax.axis_size("seqo") // slots
    return lax.axis_index("seqi"), lax.axis_index("seqo") // width


def distance(n_i, step, odd):
    order = [1, *range(n_i - 1, 1, -1)] if odd else list(range(n_i - 1, 0, -1))
    return order[step - 1]


def distance_back(n_i, step):
    return n_i - 1 if step == 1 else step - 1


def is_odd():
    return lax.axis_index("seqo") % 2 == 1


def place_in(n_i, slots, step):
    pos, _ = position(slots)
    if step == 0:
        return pos
    return pos ^ jnp.where(is_odd(), distance(n_i, step, True), distance(n_i, step, False))


def first_back(n_i, slots, step):
    pos, _ = position(slots)
    return (pos if step == 0 else pos ^ distance_back(n_i, step)) * slots


def in_back_order(n_i, chunks):
    found = [chunks[0]]
    for step in range(1, n_i):
        even, odd = [
            [distance(n_i, k, parity) for k in range(1, n_i)].index(distance_back(n_i, step)) + 1
            for parity in (False, True)
        ]
        found.append(jnp.where(is_odd(), chunks[odd], chunks[even]))
    return found


def lanes_of(rows):
    return lax.broadcasted_iota(jnp.int32, (rows, LANES), 1)


def level_stats(operands):
    products = [(dot_nt(k, q) * SCALE, dot_nt(v, u)) for k, v, q, u in operands]
    tops = [jnp.max(s, axis=0, keepdims=True) for s, _ in products]
    weights = [jnp.exp(s - top) for (s, _), top in zip(products, tops)]
    totals = [jnp.sum(p, axis=0, keepdims=True) for p in weights]
    return [
        (top + jnp.log(total), jnp.sum(p * dp, axis=0, keepdims=True) / total)
        for (_, dp), top, p, total in zip(products, tops, weights, totals)
    ]


def merge_stats(ea, da, eb, db):
    top = jnp.maximum(ea, eb)
    wa, wb = jnp.exp(ea - top), jnp.exp(eb - top)
    total = wa + wb
    return top + jnp.log(total), (wa * da + wb * db) / total


def level_weights(operands, stats):
    products = [(dot_nt(k, q) * SCALE, dot_nt(v, u)) for k, v, q, u in operands]
    found = []
    for (s, dp), (lse, delta) in zip(products, stats):
        g = jnp.exp(s - lse)
        found.append((g.astype(BF16), (g * (dp - delta)).astype(BF16)))
    return found


def level_parts(operands, stats):
    found = level_weights(operands, stats)
    keyed = [
        (dot(ds, q) * SCALE, dot(p, u)) for (p, ds), (k, v, q, u) in zip(found, operands)
    ]
    queried = [
        (dot_tn(p, v), dot_tn(ds, k) * SCALE) for (p, ds), (k, v, q, u) in zip(found, operands)
    ]
    return [a + b for a, b in zip(queried, keyed)]


def pick_rows(ref, rows):
    quarter = rows // DILATION
    lane = lanes_of(quarter)
    picked = jnp.zeros((quarter, LANES), F32)
    for residue in range(DILATION):
        part = ref[pl.ds(residue, quarter, stride=DILATION), :]
        picked = jnp.where(lane % DILATION == residue, part, picked)
    return picked


def fetch(sources, buffers, sems):
    width = DILATION * HEAD_DIM
    groups = []
    for group in range(HEADS // DILATION):
        cols = pl.ds(group * width, width)
        groups.append(
            [
                pltpu.make_async_copy(
                    source.at[:, cols], buffers.at[which, :, cols], sems.at[which, group]
                )
                for which, source in enumerate(sources)
            ]
        )
        for copy in groups[-1]:
            copy.start()
    return groups


def split(x):
    high = x.astype(BF16).astype(F32)
    rest = x - high
    middle = rest.astype(BF16).astype(F32)
    low = rest - middle
    return (high + pltpu.roll(middle, 2 * HEADS, 1) + pltpu.roll(low, 4 * HEADS, 1)).astype(BF16)


def join(ref):
    x = ref[ref.shape[0] - 1].astype(F32)
    x = x + (pltpu.roll(x, LANES - 2 * HEADS, 1) + pltpu.roll(x, LANES - 4 * HEADS, 1))
    return jnp.where(lanes_of(x.shape[0]) < 2 * HEADS, x, 0.0)


def pick_kernel(n_i, slots, *refs):
    sources, refs = refs[:4], refs[4:]
    mids, refs = refs[:n_i], refs[n_i:]
    fulls, refs = refs[:slots], refs[slots:]
    stats_ref, buffers, sems, wide, picked, turn = refs
    rows = sources[0].shape[0]
    quarter = rows // DILATION
    pos, chip = position(slots)
    turn[...] = jnp.zeros_like(turn)
    for group, copies in enumerate(fetch(sources, buffers, sems)):
        for which, copy in enumerate(copies):
            copy.wait()
            for residue in range(DILATION):
                head = group * DILATION + residue
                wide[which, head] = buffers[which, :, static_columns(head)].astype(F32)
                rowset = wide[which, head, pl.ds(residue, quarter, stride=DILATION), :]
                picked[head // slots, which * slots + head % slots] = rowset.astype(BF16)
        heads = range(group * DILATION, (group + 1) * DILATION)
        operands = [[buffers[which, :, static_columns(head)] for which in range(4)] for head in heads]
        for head, (e, d) in zip(heads, level_stats(operands)):
            turn[head : head + 1, :] = e
            turn[HEADS + head : HEADS + head + 1, :] = d
    stats_ref[...] = turn[: 2 * HEADS, :]
    turn[...] = turn[...].T
    near = split(pick_rows(turn, rows))
    for d in range(n_i):
        mids[d][: 4 * slots] = picked[place_in(n_i, slots, d)]
        mids[d][4 * slots] = near
    for m in range(slots):
        fulls[m][...] = buffers[:, :, head_columns(pos * slots + (chip ^ m))]


def pack_kernel(slots, *refs):
    packed_ref = refs[-1]
    for m, ref in enumerate(refs[:slots]):
        packed_ref[m] = ref[:2]


def far_keys(fulls, sibs, which):
    blocks = [ref[which] for ref in fulls]
    return jnp.concatenate(blocks + [ref[m, which] for ref in sibs for m in range(len(fulls))], axis=0)


def far_stats_kernel(slots, *refs):
    fulls, sibs, stats_ref = refs[:slots], refs[slots:-2], refs[-1]
    keys, values = far_keys(fulls, sibs, 0), far_keys(fulls, sibs, 1)
    for m in range(slots):
        ((e, d),) = level_stats([(keys, values, fulls[m][2], fulls[m][3])])
        stats_ref[m : m + 1, :] = e
        stats_ref[slots + m : slots + m + 1, :] = d


def middle_operands(slots, mids, slot):
    return [
        jnp.concatenate([ref[which * slots + slot] for ref in mids], axis=0) for which in range(4)
    ]


def middle_stats_kernel(n_i, slots, *refs):
    mids, refs = refs[:n_i], refs[n_i:]
    near_ref, far_ref, xmsg_ref, stats_ref, columns_ref, turn, spread = refs
    rows = near_ref.shape[1]
    quarter = rows // DILATION
    pos, _ = position(slots)
    turn[...] = jnp.zeros_like(turn)
    operands = [middle_operands(slots, mids, slot) for slot in range(slots)]
    for slot, (e, d) in enumerate(level_stats(operands)):
        turn[slot : slot + 1, :] = e
        turn[slots + slot : slots + slot + 1, :] = d
    stats_ref[...] = turn[: 2 * slots, :]
    columns_ref[...] = turn[...].T
    lane = lanes_of(quarter)
    lane_residue = (pos * slots + lane % slots) % DILATION
    blank = jnp.where(lane < slots, LOWEST, 0.0)
    for residue in range(DILATION):
        spread[pl.ds(residue, quarter, stride=DILATION), :] = jnp.where(
            lane_residue == residue, columns_ref[:quarter], blank
        )
    across = spread[...].T
    e, d = merge_stats(
        near_ref[pl.ds(pos * slots, slots), :],
        near_ref[pl.ds(HEADS + pos * slots, slots), :],
        across[:slots],
        across[slots : 2 * slots],
    )
    xmsg_ref[:slots] = e
    xmsg_ref[slots : 2 * slots] = d
    xmsg_ref[2 * slots :] = far_ref[...]


def middle_parts_kernel(n_i, slots, *refs):
    mids, refs = refs[:n_i], refs[n_i:]
    stats_ref, columns_ref = refs[:2]
    refs = refs[2:]
    xmsgs, refs = refs[:slots], refs[slots:]
    outs, (far, turn, spread) = refs[:n_i], refs[n_i:]
    rows = xmsgs[0].shape[1]
    quarter = rows // DILATION
    pos, chip = position(slots)
    for m in range(slots):
        far[pl.ds(chip ^ m, 1), :] = xmsgs[m][2 * slots + m : 2 * slots + m + 1, :]
        far[pl.ds(slots + (chip ^ m), 1), :] = xmsgs[m][3 * slots + m : 3 * slots + m + 1, :]
    e, d = merge_stats(
        xmsgs[0][:slots], xmsgs[0][slots : 2 * slots], far[:slots], far[slots:]
    )
    spread[...] = jnp.zeros_like(spread)
    spread[pl.ds(pos * slots, slots), :] = e
    spread[pl.ds(HEADS + pos * slots, slots), :] = d
    spread[...] = spread[...].T
    own = pick_rows(spread, rows)
    turn[...] = jnp.concatenate([own] + [join(ref) for ref in mids[1:]], axis=0).T
    owned = lax.broadcasted_iota(jnp.int32, (1, n_i * quarter), 1) < quarter
    operands = [middle_operands(slots, mids, slot) for slot in range(slots)]
    merged = [
        merge_stats(
            turn[pl.ds(pos * slots + slot, 1), :],
            turn[pl.ds(HEADS + pos * slots + slot, 1), :],
            jnp.where(owned, LOWEST, stats_ref[slot : slot + 1, :]),
            stats_ref[slots + slot : slots + slot + 1, :],
        )
        for slot in range(slots)
    ]
    for slot, parts in enumerate(level_parts(operands, merged)):
        for which, part in enumerate(parts):
            part = part.astype(BF16)
            chunks = [part[d * quarter : (d + 1) * quarter] for d in range(n_i)]
            for out, chunk in zip(outs, in_back_order(n_i, chunks)):
                out[which * slots + slot] = chunk
    chunks = [columns_ref[d * quarter : (d + 1) * quarter] for d in range(n_i)]
    for out, chunk in zip(outs, in_back_order(n_i, chunks)):
        out[4 * slots] = split(chunk)


def far_parts_kernel(slots, width, *refs):
    fulls, refs = refs[:slots], refs[slots:]
    sibs, refs = refs[: width - 1], refs[width - 1 :]
    xmsgs, refs = refs[:slots], refs[slots + 1 :]
    outs, refs = refs[:slots], refs[slots:]
    kvouts, refs = refs[: width - 1], refs[width - 1 :]
    weights, score_grads = refs
    rows = fulls[0].shape[1]
    _, chip = position(slots)
    keys, values = far_keys(fulls, sibs, 0), far_keys(fulls, sibs, 1)
    for m in range(slots):
        lse, delta = merge_stats(
            xmsgs[m][pl.ds(chip, 1), :],
            xmsgs[m][pl.ds(slots + chip, 1), :],
            xmsgs[0][2 * slots + m : 2 * slots + m + 1, :],
            xmsgs[0][3 * slots + m : 3 * slots + m + 1, :],
        )
        operands = (keys, values, fulls[m][2], fulls[m][3])
        ((p, ds),) = level_weights([operands], [(lse, delta)])
        outs[m][0] = dot_tn(p, values).astype(BF16)
        outs[m][1] = (dot_tn(ds, keys) * SCALE).astype(BF16)
        weights[:, m * rows : (m + 1) * rows] = p
        score_grads[:, m * rows : (m + 1) * rows] = ds
    queries = jnp.concatenate([ref[2] for ref in fulls], axis=0)
    ups = jnp.concatenate([ref[3] for ref in fulls], axis=0)
    key_part = (dot(score_grads[...], queries) * SCALE).astype(BF16)
    value_part = dot(weights[...], ups).astype(BF16)
    for index in range(width * slots):
        block = slice(index * rows, (index + 1) * rows)
        part, m = index // slots, index % slots
        if part == 0:
            outs[m][2], outs[m][3] = key_part[block], value_part[block]
        else:
            kvouts[part - 1][m, 0], kvouts[part - 1][m, 1] = key_part[block], value_part[block]


def far_sum_kernel(slots, *refs):
    own, refs = refs[:slots], refs[slots:]
    found, outs = refs[: -slots - 1], refs[-slots:]
    for m in range(slots):
        outs[m][:2] = own[m][:2]
        total = own[m][2:].astype(F32)
        for ref in found:
            total += ref[m].astype(F32)
        outs[m][2:] = total.astype(BF16)


def near_statistics(n_i, slots, steps, near_ref, mids, xmsgs, stats_ref, spread):
    rows = near_ref.shape[1]
    quarter = rows // DILATION
    pos, chip = position(slots)
    lane = lanes_of(quarter)
    mid = jnp.zeros((quarter, LANES), F32)
    for step, ref in zip(steps, mids):
        place = first_back(n_i, slots, step)
        found = join(ref)
        e = pltpu.roll(found, place, 1)
        de = pltpu.roll(found, place + HEADS - slots, 1)
        mid = jnp.where((lane >= place) & (lane < place + slots), e, mid)
        mid = jnp.where((lane >= HEADS + place) & (lane < HEADS + place + slots), de, mid)
    blank = jnp.where(lane < HEADS, LOWEST, 0.0)
    for residue in range(DILATION):
        spread[pl.ds(residue, quarter, stride=DILATION), :] = jnp.where(
            lane % DILATION == residue, mid, blank
        )
    across = spread[...].T
    e, d = merge_stats(
        near_ref[:HEADS], near_ref[HEADS:], across[:HEADS], across[HEADS : 2 * HEADS]
    )
    if xmsgs:
        stats_ref[:HEADS] = jnp.full((HEADS, rows), LOWEST, F32)
        stats_ref[HEADS:] = jnp.zeros((HEADS, rows), F32)
        for m in range(slots):
            head = pos * slots + (chip ^ m)
            stats_ref[pl.ds(head, 1), :] = xmsgs[m][2 * slots + m : 2 * slots + m + 1, :]
            stats_ref[pl.ds(HEADS + head, 1), :] = xmsgs[m][3 * slots + m : 3 * slots + m + 1, :]
        e, d = merge_stats(e, d, stats_ref[:HEADS], stats_ref[HEADS:])
    stats_ref[:HEADS] = e
    stats_ref[HEADS:] = d


def near_place(n_i, slots, step, sources, stats_ref):
    heads = [first_back(n_i, slots, step) + slot for slot in range(slots)]
    operands = [[ref[:, head_columns(head)] for ref in sources] for head in heads]
    stats = [(stats_ref[pl.ds(head, 1), :], stats_ref[pl.ds(HEADS + head, 1), :]) for head in heads]
    return level_parts(operands, stats)


def near_early_kernel(n_i, slots, *refs):
    sources, near_ref, refs = refs[:4], refs[4], refs[5:]
    mids, refs = refs[: n_i - 1], refs[n_i - 1 :]
    xmsgs, (out_ref, stats_ref, spread) = refs[:slots], refs[slots:]
    near_statistics(n_i, slots, range(n_i - 1), near_ref, mids, xmsgs, stats_ref, spread)
    for step in range(n_i - 1):
        for slot, parts in enumerate(near_place(n_i, slots, step, sources, stats_ref)):
            for which, part in enumerate(parts):
                out_ref[which, step * slots + slot] = part


def far_sum_kernel(slots, *refs):
    own, refs = refs[:slots], refs[slots:]
    found, outs = refs[: -slots - 1], refs[-slots:]
    for m in range(slots):
        outs[m][:2] = own[m][:2]
        total = own[m][2:].astype(F32)
        for ref in found:
            total += ref[m].astype(F32)
        outs[m][2:] = total.astype(BF16)


def near_parts_kernel(n_i, slots, *refs):
    sources, near_ref, refs = refs[:4], refs[4], refs[5:]
    mids, refs = (refs[0], *refs[n_i - 1 : 0 : -1]), refs[n_i:]
    xmsgs, (out_ref, stats_ref, spread) = refs[:slots], refs[slots:]
    rows = near_ref.shape[1]
    quarter = rows // DILATION
    pos, chip = position(slots)
    lane = lanes_of(quarter)
    mid = jnp.zeros((quarter, LANES), F32)
    for d in range(n_i):
        place = (pos ^ d) * slots
        found = join(mids[d])
        e = pltpu.roll(found, place, 1)
        de = pltpu.roll(found, place + HEADS - slots, 1)
        mid = jnp.where((lane >= place) & (lane < place + slots), e, mid)
        mid = jnp.where((lane >= HEADS + place) & (lane < HEADS + place + slots), de, mid)
    blank = jnp.where(lane < HEADS, LOWEST, 0.0)
    for residue in range(DILATION):
        spread[pl.ds(residue, quarter, stride=DILATION), :] = jnp.where(
            lane % DILATION == residue, mid, blank
        )
    across = spread[...].T
    stats_ref[:HEADS] = jnp.full((HEADS, rows), LOWEST, F32)
    stats_ref[HEADS:] = jnp.zeros((HEADS, rows), F32)
    for m in range(slots):
        head = pos * slots + (chip ^ m)
        stats_ref[pl.ds(head, 1), :] = xmsgs[m][2 * slots + m : 2 * slots + m + 1, :]
        stats_ref[pl.ds(HEADS + head, 1), :] = xmsgs[m][3 * slots + m : 3 * slots + m + 1, :]
    e, d = merge_stats(
        near_ref[:HEADS], near_ref[HEADS:], across[:HEADS], across[HEADS : 2 * HEADS]
    )
    e, d = merge_stats(e, d, stats_ref[:HEADS], stats_ref[HEADS:])
    stats_ref[:HEADS] = e
    stats_ref[HEADS:] = d
    for group in range(HEADS // DILATION):
        heads = range(group * DILATION, (group + 1) * DILATION)
        operands = [
            [ref[:, static_columns(head)] for ref in sources] for head in heads
        ]
        stats = [
            (stats_ref[head : head + 1, :], stats_ref[HEADS + head : HEADS + head + 1, :])
            for head in heads
        ]
        for head, parts in zip(heads, level_parts(operands, stats)):
            for which, part in enumerate(parts):
                out_ref[which, head] = part


def spread_rows(slots, head, slot, ref):
    quarter = ref.shape[1]
    rows = quarter * DILATION
    row = lax.broadcasted_iota(jnp.int32, (rows, quarter), 0)
    taken = lax.broadcasted_iota(jnp.int32, (rows, quarter), 1) * DILATION
    place = jnp.where(row == taken + head % DILATION, 1.0, 0.0).astype(BF16)
    return dot(place, jnp.concatenate([ref[which * slots + slot] for which in range(4)], axis=1))


def send_place(slots, first, ready, outs, sems):
    width = slots * HEAD_DIM
    cols = pl.ds(pl.multiple_of(first * HEAD_DIM, width), width)
    copies = [
        pltpu.make_async_copy(ready.at[which], out.at[:, cols], sems.at[which])
        for which, out in enumerate(outs)
    ]
    for copy in copies:
        copy.start()
    return copies


def final_others_kernel(n_i, slots, *refs):
    sources, near_ref, early_ref, refs = refs[:4], refs[4], refs[5], refs[6:]
    mids, refs = refs[: n_i - 1], refs[n_i - 1 :]
    outs, (ready, sems, stats_ref, spread) = refs[:4], refs[4:]
    last = n_i - 1
    near_statistics(n_i, slots, [last], near_ref, mids[-1:], (), stats_ref, spread)
    late = near_place(n_i, slots, last, sources, stats_ref)
    copies = []
    for step in range(1, n_i):
        first = first_back(n_i, slots, step)
        found = [spread_rows(slots, first + slot, slot, mids[step - 1]) for slot in range(slots)]
        for slot, parts in enumerate(found):
            for which in range(4):
                near = late[slot][which] if step == last else early_ref[which, step * slots + slot]
                total = near + parts[:, static_columns(which)]
                ready[step - 1, which, :, static_columns(slot)] = total.astype(BF16)
        copies += send_place(slots, first, ready.at[step - 1], outs, sems.at[step - 1])
    for copy in copies:
        copy.wait()


def final_own_kernel(slots, early_ref, mid_ref, *refs):
    fulls, refs = in_back(refs[:slots]), refs[slots:]
    outs, (ready, sems) = refs[4:8], refs[8:]
    pos, chip = position(slots)
    first = pos * slots
    found = [spread_rows(slots, first + (chip ^ m), chip ^ m, mid_ref) for m in range(slots)]
    for m, parts in enumerate(found):
        slot = chip ^ m
        for which in range(4):
            total = early_ref[which, slot] + parts[:, static_columns(which)]
            total += fulls[m][which].astype(F32)
            ready[which, :, head_columns(slot)] = total.astype(BF16)
    for copy in send_place(slots, first, ready, outs, sems):
        copy.wait()


def settle_kernel(*refs):
    refs[-1][...] = jnp.zeros_like(refs[-1])


def call(kernel, name, outs, scratch, flops, operands, hbm_in=(), hbm_out=False, cheap=False, limit=VMEM_LIMIT, aliases=None):
    moved = sum(x.size * x.dtype.itemsize for x in tuple(operands) + tuple(outs))
    if cheap:
        flops, moved = 1, 1
    spaces = [pltpu.HBM if i in hbm_in else pltpu.VMEM for i in range(len(operands))]
    return pl.pallas_call(
        kernel,
        out_shape=tuple(outs),
        in_specs=[pl.BlockSpec(memory_space=space) for space in spaces],
        out_specs=tuple(
            pl.BlockSpec(memory_space=pltpu.HBM if hbm_out else pltpu.VMEM) for _ in outs
        ),
        scratch_shapes=scratch,
        input_output_aliases=aliases or {},
        compiler_params=pltpu.CompilerParams(vmem_limit_bytes=limit),
        cost_estimate=pl.CostEstimate(flops=flops, bytes_accessed=moved, transcendentals=0),
        name=name,
    )(*operands)


def in_back(pieces):
    return [pieces[0], *pieces[:0:-1]]


def swap(x, axis, n, mask):
    return lax.ppermute(x, axis, [(i, i ^ mask) for i in range(n)])


def local(query_rows, key_rows, value_rows, upstream):
    rows, features = query_rows.shape
    n_i, n_o = lax.axis_size("seqi"), lax.axis_size("seqo")
    slots = HEADS // n_i
    width = n_o // slots
    others = (width - 1) * slots
    quarter = rows // DILATION
    sources = (key_rows, value_rows, query_rows, upstream)
    unit = 2 * rows * rows * HEAD_DIM
    bind = functools.partial

    mid = SHAPE((4 * slots + 1, quarter, HEAD_DIM), BF16)
    full = SHAPE((4, rows, HEAD_DIM), BF16)
    half = SHAPE((slots, 2, rows, HEAD_DIM), BF16)
    square = pltpu.VMEM((LANES, rows), F32)

    def stats(count, lanes=rows):
        return SHAPE((count, lanes), F32)

    def swap_mids(pieces):
        found = [pieces[0]]
        for step in range(1, n_i):
            pairs = [
                (o * n_i + i, o * n_i + (i ^ distance(n_i, step, o % 2 == 1)))
                for o in range(n_o)
                for i in range(n_i)
            ]
            found.append(lax.ppermute(pieces[step], ("seqo", "seqi"), pairs))
        return found

    def swap_back(pieces):
        return [pieces[0]] + [
            swap(pieces[step], "seqi", n_i, distance_back(n_i, step)) for step in range(1, n_i)
        ]

    def swap_fulls(pieces):
        return [pieces[0]] + [swap(pieces[m], "seqo", n_o, m * width) for m in range(1, slots)]

    pieces = call(
        bind(pick_kernel, n_i, slots),
        "pick",
        [mid] * n_i + [full] * slots + [stats(2 * HEADS)],
        [
            pltpu.VMEM((4, rows, features), BF16),
            pltpu.SemaphoreType.DMA((4, HEADS // DILATION)),
            pltpu.VMEM((4, HEADS, rows, HEAD_DIM), F32),
            pltpu.VMEM((n_i, 4 * slots, quarter, HEAD_DIM), BF16),
            square,
        ],
        unit * HEADS * 2,
        sources,
        hbm_in=range(4),
        limit=PICK_LIMIT,
    )
    mids = swap_mids(pieces[:n_i])
    fulls = swap_fulls(pieces[n_i : n_i + slots])
    near = pieces[-1]

    (settled,) = call(settle_kernel, "far_in", [stats(8)], [], SHORT, [mids[1]])
    (settled,) = call(settle_kernel, "chips_back", [stats(8)], [], LONG, [settled])
    (packed,) = call(bind(pack_kernel, slots), "pack", [half], [], 1, fulls + [settled])
    sibs = [swap(packed, "seqo", n_o, part) for part in range(1, width)]
    (settled,) = call(settle_kernel, "packed_back", [stats(8)], [], LONG, [near])
    (far,) = call(
        bind(far_stats_kernel, slots),
        "far_stats",
        [stats(2 * slots)],
        [],
        1,
        fulls + sibs + [settled],
    )
    xmsg, middle, columns = call(
        bind(middle_stats_kernel, n_i, slots),
        "middle_stats",
        [stats(4 * slots), stats(2 * slots, n_i * quarter), stats(n_i * quarter, LANES)],
        [pltpu.VMEM((LANES, n_i * quarter), F32), square],
        unit * slots * 2,
        mids + [near, far],
    )
    xmsgs = swap_fulls([xmsg] * slots)

    midparts = call(
        bind(middle_parts_kernel, n_i, slots),
        "middle_parts",
        [mid] * n_i,
        [pltpu.VMEM((2 * slots, rows), F32), pltpu.VMEM((LANES, n_i * quarter), F32), square],
        unit * slots * 6,
        mids + [middle, columns] + xmsgs,
    )
    midparts = swap_back(midparts)
    farparts = call(
        bind(far_parts_kernel, slots, width),
        "far_parts",
        [full] * slots + [half] * (width - 1),
        [pltpu.VMEM((n_o * rows, slots * rows), BF16)] * 2,
        unit * n_o * slots * 6,
        fulls + sibs + xmsgs + [midparts[0]],
        cheap=True,
    )
    sibparts = [swap(x, "seqo", n_o, part + 1) for part, x in enumerate(farparts[slots:])]
    (settled,) = call(settle_kernel, "far_back", [stats(8)], [], SHORT, [midparts[1]])
    (settled,) = call(settle_kernel, "sib_back", [stats(8)], [], 1, sibparts + [settled])
    (settled,) = call(settle_kernel, "settle", [stats(8)], [], LONG, [settled])
    fullparts = call(
        bind(far_sum_kernel, slots),
        "far_sum",
        [full] * slots,
        [],
        unit,
        list(farparts[:slots]) + sibparts + [settled],
        cheap=True,
    )
    fullparts = swap_fulls(fullparts)

    back = midparts
    kept = [pltpu.VMEM((2 * HEADS, rows), F32), square]
    (early,) = call(
        bind(near_early_kernel, n_i, slots),
        "near_early",
        [SHAPE((4, (n_i - 1) * slots, rows, HEAD_DIM), F32)],
        kept,
        SHORT,
        [*sources, near, *back[:-1], *xmsgs],
    )
    whole = [SHAPE((rows, features), BF16)] * 4
    outs = call(
        bind(final_others_kernel, n_i, slots),
        "final_others",
        whole,
        [
            pltpu.VMEM((n_i - 1, 4, rows, slots * HEAD_DIM), BF16),
            pltpu.SemaphoreType.DMA((n_i - 1, 4)),
            *kept,
        ],
        SHORT // 2,
        [*sources, near, early, *back[1:]],
        hbm_out=True,
    )
    return call(
        bind(final_own_kernel, slots),
        "final_own",
        whole,
        [pltpu.VMEM((4, rows, slots * HEAD_DIM), BF16), pltpu.SemaphoreType.DMA((4,))],
        unit * slots,
        [early, midparts[0], *in_back(fullparts), *outs],
        hbm_in=range(2 + slots, 6 + slots),
        hbm_out=True,
        aliases={2 + slots + which: which for which in range(4)},
    )


def solution(mesh):
    rows = P(("seqo", "seqi"), None)
    return jax.shard_map(
        local,
        mesh=mesh,
        in_specs=(rows,) * 4,
        out_specs=(rows,) * 4,
        check_vma=False,
    )
```

```python
import functools

import jax
import jax.numpy as jnp
from jax import lax
from jax.experimental import pallas as pl
from jax.experimental.pallas import tpu as pltpu
from jax.sharding import PartitionSpec as P

HEADS = 16
HEAD_DIM = 128
DILATION = 4
LANES = 128
SCALE = HEAD_DIM**-0.5
LOWEST = -1e30
LONG = 4 * 10**10
SHORT = 2 * 10**9
VMEM_LIMIT = 32 * 1024 * 1024
PICK_LIMIT = 53 * 1024 * 1024
NEAR_LIMIT = 54784 * 1024
F32, BF16 = jnp.float32, jnp.bfloat16
SHAPE = jax.ShapeDtypeStruct

NT = (((1,), (1,)), ((), ()))
TN = (((0,), (0,)), ((), ()))


def dot(a, b):
    return jnp.dot(a, b, preferred_element_type=F32)


def dot_nt(a, b):
    return lax.dot_general(a, b, NT, preferred_element_type=F32)


def dot_tn(a, b):
    return lax.dot_general(a, b, TN, preferred_element_type=F32)


def head_columns(head):
    return pl.ds(pl.multiple_of(head * HEAD_DIM, HEAD_DIM), HEAD_DIM)


def static_columns(index):
    return slice(index * HEAD_DIM, (index + 1) * HEAD_DIM)


def position(slots):
    width = lax.axis_size("seqo") // slots
    return lax.axis_index("seqi"), lax.axis_index("seqo") // width


def distance(n_i, step, odd):
    order = [1, *range(n_i - 1, 1, -1)] if odd else list(range(n_i - 1, 0, -1))
    return order[step - 1]


def distance_back(n_i, step):
    return n_i - 1 if step == 1 else step - 1


def is_odd():
    return lax.axis_index("seqo") % 2 == 1


def place_in(n_i, slots, step):
    pos, _ = position(slots)
    if step == 0:
        return pos
    return pos ^ jnp.where(is_odd(), distance(n_i, step, True), distance(n_i, step, False))


def first_back(n_i, slots, step):
    pos, _ = position(slots)
    return (pos if step == 0 else pos ^ distance_back(n_i, step)) * slots


def in_back_order(n_i, chunks):
    found = [chunks[0]]
    for step in range(1, n_i):
        even, odd = [
            [distance(n_i, k, parity) for k in range(1, n_i)].index(distance_back(n_i, step)) + 1
            for parity in (False, True)
        ]
        found.append(jnp.where(is_odd(), chunks[odd], chunks[even]))
    return found


def lanes_of(rows):
    return lax.broadcasted_iota(jnp.int32, (rows, LANES), 1)


def level_stats(operands):
    products = [(dot_nt(k, q) * SCALE, dot_nt(v, u)) for k, v, q, u in operands]
    tops = [jnp.max(s, axis=0, keepdims=True) for s, _ in products]
    weights = [jnp.exp(s - top) for (s, _), top in zip(products, tops)]
    totals = [jnp.sum(p, axis=0, keepdims=True) for p in weights]
    return [
        (top + jnp.log(total), jnp.sum(p * dp, axis=0, keepdims=True) / total)
        for (_, dp), top, p, total in zip(products, tops, weights, totals)
    ]


def merge_stats(ea, da, eb, db):
    top = jnp.maximum(ea, eb)
    wa, wb = jnp.exp(ea - top), jnp.exp(eb - top)
    total = wa + wb
    return top + jnp.log(total), (wa * da + wb * db) / total


def level_weights(operands, stats):
    products = [(dot_nt(k, q) * SCALE, dot_nt(v, u)) for k, v, q, u in operands]
    found = []
    for (s, dp), (lse, delta) in zip(products, stats):
        g = jnp.exp(s - lse)
        found.append((g.astype(BF16), (g * (dp - delta)).astype(BF16)))
    return found


def level_parts(operands, stats):
    found = level_weights(operands, stats)
    keyed = [
        (dot(ds, q) * SCALE, dot(p, u)) for (p, ds), (k, v, q, u) in zip(found, operands)
    ]
    queried = [
        (dot_tn(p, v), dot_tn(ds, k) * SCALE) for (p, ds), (k, v, q, u) in zip(found, operands)
    ]
    return [a + b for a, b in zip(queried, keyed)]


def pick_rows(ref, rows):
    quarter = rows // DILATION
    lane = lanes_of(quarter)
    picked = jnp.zeros((quarter, LANES), F32)
    for residue in range(DILATION):
        part = ref[pl.ds(residue, quarter, stride=DILATION), :]
        picked = jnp.where(lane % DILATION == residue, part, picked)
    return picked


def fetch(sources, buffers, sems):
    width = DILATION * HEAD_DIM
    groups = []
    for group in range(HEADS // DILATION):
        cols = pl.ds(group * width, width)
        groups.append(
            [
                pltpu.make_async_copy(
                    source.at[:, cols], buffers.at[which, :, cols], sems.at[which, group]
                )
                for which, source in enumerate(sources)
            ]
        )
        for copy in groups[-1]:
            copy.start()
    return groups


def split(x):
    high = x.astype(BF16).astype(F32)
    rest = x - high
    middle = rest.astype(BF16).astype(F32)
    low = rest - middle
    return (high + pltpu.roll(middle, 2 * HEADS, 1) + pltpu.roll(low, 4 * HEADS, 1)).astype(BF16)


def join(ref):
    x = ref[ref.shape[0] - 1].astype(F32)
    x = x + (pltpu.roll(x, LANES - 2 * HEADS, 1) + pltpu.roll(x, LANES - 4 * HEADS, 1))
    return jnp.where(lanes_of(x.shape[0]) < 2 * HEADS, x, 0.0)


def pick_kernel(n_i, slots, *refs):
    sources, refs = refs[:4], refs[4:]
    mids, refs = refs[:n_i], refs[n_i:]
    fulls, refs = refs[:slots], refs[slots:]
    stats_ref, buffers, sems, wide, picked, turn = refs
    rows = sources[0].shape[0]
    quarter = rows // DILATION
    pos, chip = position(slots)
    turn[...] = jnp.zeros_like(turn)
    for group, copies in enumerate(fetch(sources, buffers, sems)):
        for which, copy in enumerate(copies):
            copy.wait()
            for residue in range(DILATION):
                head = group * DILATION + residue
                wide[which, head] = buffers[which, :, static_columns(head)].astype(F32)
                rowset = wide[which, head, pl.ds(residue, quarter, stride=DILATION), :]
                picked[head // slots, which * slots + head % slots] = rowset.astype(BF16)
        heads = range(group * DILATION, (group + 1) * DILATION)
        operands = [[buffers[which, :, static_columns(head)] for which in range(4)] for head in heads]
        for head, (e, d) in zip(heads, level_stats(operands)):
            turn[head : head + 1, :] = e
            turn[HEADS + head : HEADS + head + 1, :] = d
    stats_ref[...] = turn[: 2 * HEADS, :]
    turn[...] = turn[...].T
    near = split(pick_rows(turn, rows))
    for d in range(n_i):
        mids[d][: 4 * slots] = picked[place_in(n_i, slots, d)]
        mids[d][4 * slots] = near
    for m in range(slots):
        fulls[m][...] = buffers[:, :, head_columns(pos * slots + (chip ^ m))]


def pack_kernel(slots, *refs):
    packed_ref = refs[-1]
    for m, ref in enumerate(refs[:slots]):
        packed_ref[m] = ref[:2]


def far_keys(fulls, sibs, which):
    blocks = [ref[which] for ref in fulls]
    return jnp.concatenate(blocks + [ref[m, which] for ref in sibs for m in range(len(fulls))], axis=0)


def far_stats_kernel(slots, *refs):
    fulls, sibs, stats_ref = refs[:slots], refs[slots:-2], refs[-1]
    keys, values = far_keys(fulls, sibs, 0), far_keys(fulls, sibs, 1)
    for m in range(slots):
        ((e, d),) = level_stats([(keys, values, fulls[m][2], fulls[m][3])])
        stats_ref[m : m + 1, :] = e
        stats_ref[slots + m : slots + m + 1, :] = d


def middle_operands(slots, mids, slot):
    return [
        jnp.concatenate([ref[which * slots + slot] for ref in mids], axis=0) for which in range(4)
    ]


def middle_stats_kernel(n_i, slots, *refs):
    mids, refs = refs[:n_i], refs[n_i:]
    near_ref, far_ref, xmsg_ref, stats_ref, columns_ref, turn, spread = refs
    rows = near_ref.shape[1]
    quarter = rows // DILATION
    pos, _ = position(slots)
    turn[...] = jnp.zeros_like(turn)
    operands = [middle_operands(slots, mids, slot) for slot in range(slots)]
    for slot, (e, d) in enumerate(level_stats(operands)):
        turn[slot : slot + 1, :] = e
        turn[slots + slot : slots + slot + 1, :] = d
    stats_ref[...] = turn[: 2 * slots, :]
    columns_ref[...] = turn[...].T
    lane = lanes_of(quarter)
    lane_residue = (pos * slots + lane % slots) % DILATION
    blank = jnp.where(lane < slots, LOWEST, 0.0)
    for residue in range(DILATION):
        spread[pl.ds(residue, quarter, stride=DILATION), :] = jnp.where(
            lane_residue == residue, columns_ref[:quarter], blank
        )
    across = spread[...].T
    e, d = merge_stats(
        near_ref[pl.ds(pos * slots, slots), :],
        near_ref[pl.ds(HEADS + pos * slots, slots), :],
        across[:slots],
        across[slots : 2 * slots],
    )
    xmsg_ref[:slots] = e
    xmsg_ref[slots : 2 * slots] = d
    xmsg_ref[2 * slots :] = far_ref[...]


def middle_parts_kernel(n_i, slots, *refs):
    mids, refs = refs[:n_i], refs[n_i:]
    stats_ref, columns_ref = refs[:2]
    refs = refs[2:]
    xmsgs, refs = refs[:slots], refs[slots:]
    outs, (far, turn, spread) = refs[:n_i], refs[n_i:]
    rows = xmsgs[0].shape[1]
    quarter = rows // DILATION
    pos, chip = position(slots)
    for m in range(slots):
        far[pl.ds(chip ^ m, 1), :] = xmsgs[m][2 * slots + m : 2 * slots + m + 1, :]
        far[pl.ds(slots + (chip ^ m), 1), :] = xmsgs[m][3 * slots + m : 3 * slots + m + 1, :]
    e, d = merge_stats(
        xmsgs[0][:slots], xmsgs[0][slots : 2 * slots], far[:slots], far[slots:]
    )
    spread[...] = jnp.zeros_like(spread)
    spread[pl.ds(pos * slots, slots), :] = e
    spread[pl.ds(HEADS + pos * slots, slots), :] = d
    spread[...] = spread[...].T
    own = pick_rows(spread, rows)
    turn[...] = jnp.concatenate([own] + [join(ref) for ref in mids[1:]], axis=0).T
    owned = lax.broadcasted_iota(jnp.int32, (1, n_i * quarter), 1) < quarter
    operands = [middle_operands(slots, mids, slot) for slot in range(slots)]
    merged = [
        merge_stats(
            turn[pl.ds(pos * slots + slot, 1), :],
            turn[pl.ds(HEADS + pos * slots + slot, 1), :],
            jnp.where(owned, LOWEST, stats_ref[slot : slot + 1, :]),
            stats_ref[slots + slot : slots + slot + 1, :],
        )
        for slot in range(slots)
    ]
    for slot, parts in enumerate(level_parts(operands, merged)):
        for which, part in enumerate(parts):
            part = part.astype(BF16)
            chunks = [part[d * quarter : (d + 1) * quarter] for d in range(n_i)]
            for out, chunk in zip(outs, in_back_order(n_i, chunks)):
                out[which * slots + slot] = chunk
    chunks = [columns_ref[d * quarter : (d + 1) * quarter] for d in range(n_i)]
    for out, chunk in zip(outs, in_back_order(n_i, chunks)):
        out[4 * slots] = split(chunk)


def far_parts_kernel(slots, width, *refs):
    fulls, refs = refs[:slots], refs[slots:]
    sibs, refs = refs[: width - 1], refs[width - 1 :]
    xmsgs, refs = refs[:slots], refs[slots + 1 :]
    outs, refs = refs[:slots], refs[slots:]
    kvouts, refs = refs[: width - 1], refs[width - 1 :]
    weights, score_grads = refs
    rows = fulls[0].shape[1]
    _, chip = position(slots)
    keys, values = far_keys(fulls, sibs, 0), far_keys(fulls, sibs, 1)
    for m in range(slots):
        lse, delta = merge_stats(
            xmsgs[m][pl.ds(chip, 1), :],
            xmsgs[m][pl.ds(slots + chip, 1), :],
            xmsgs[0][2 * slots + m : 2 * slots + m + 1, :],
            xmsgs[0][3 * slots + m : 3 * slots + m + 1, :],
        )
        operands = (keys, values, fulls[m][2], fulls[m][3])
        ((p, ds),) = level_weights([operands], [(lse, delta)])
        outs[m][0] = dot_tn(p, values).astype(BF16)
        outs[m][1] = (dot_tn(ds, keys) * SCALE).astype(BF16)
        weights[:, m * rows : (m + 1) * rows] = p
        score_grads[:, m * rows : (m + 1) * rows] = ds
    queries = jnp.concatenate([ref[2] for ref in fulls], axis=0)
    ups = jnp.concatenate([ref[3] for ref in fulls], axis=0)
    key_part = (dot(score_grads[...], queries) * SCALE).astype(BF16)
    value_part = dot(weights[...], ups).astype(BF16)
    for index in range(width * slots):
        block = slice(index * rows, (index + 1) * rows)
        part, m = index // slots, index % slots
        if part == 0:
            outs[m][2], outs[m][3] = key_part[block], value_part[block]
        else:
            kvouts[part - 1][m, 0], kvouts[part - 1][m, 1] = key_part[block], value_part[block]


def far_sum_kernel(slots, *refs):
    own, refs = refs[:slots], refs[slots:]
    found, outs = refs[: -slots - 1], refs[-slots:]
    for m in range(slots):
        outs[m][:2] = own[m][:2]
        total = own[m][2:].astype(F32)
        for ref in found:
            total += ref[m].astype(F32)
        outs[m][2:] = total.astype(BF16)


def near_statistics(n_i, slots, steps, near_ref, mids, xmsgs, stats_ref, spread):
    rows = near_ref.shape[1]
    quarter = rows // DILATION
    pos, chip = position(slots)
    lane = lanes_of(quarter)
    mid = jnp.zeros((quarter, LANES), F32)
    for step, ref in zip(steps, mids):
        place = first_back(n_i, slots, step)
        found = join(ref)
        e = pltpu.roll(found, place, 1)
        de = pltpu.roll(found, place + HEADS - slots, 1)
        mid = jnp.where((lane >= place) & (lane < place + slots), e, mid)
        mid = jnp.where((lane >= HEADS + place) & (lane < HEADS + place + slots), de, mid)
    blank = jnp.where(lane < HEADS, LOWEST, 0.0)
    for residue in range(DILATION):
        spread[pl.ds(residue, quarter, stride=DILATION), :] = jnp.where(
            lane % DILATION == residue, mid, blank
        )
    across = spread[...].T
    e, d = merge_stats(
        near_ref[:HEADS], near_ref[HEADS:], across[:HEADS], across[HEADS : 2 * HEADS]
    )
    if xmsgs:
        stats_ref[:HEADS] = jnp.full((HEADS, rows), LOWEST, F32)
        stats_ref[HEADS:] = jnp.zeros((HEADS, rows), F32)
        for m in range(slots):
            head = pos * slots + (chip ^ m)
            stats_ref[pl.ds(head, 1), :] = xmsgs[m][2 * slots + m : 2 * slots + m + 1, :]
            stats_ref[pl.ds(HEADS + head, 1), :] = xmsgs[m][3 * slots + m : 3 * slots + m + 1, :]
        e, d = merge_stats(e, d, stats_ref[:HEADS], stats_ref[HEADS:])
    stats_ref[:HEADS] = e
    stats_ref[HEADS:] = d


def near_place(n_i, slots, step, sources, stats_ref):
    heads = [first_back(n_i, slots, step) + slot for slot in range(slots)]
    operands = [[ref[:, head_columns(head)] for ref in sources] for head in heads]
    stats = [(stats_ref[pl.ds(head, 1), :], stats_ref[pl.ds(HEADS + head, 1), :]) for head in heads]
    return level_parts(operands, stats)


def near_early_kernel(n_i, slots, *refs):
    sources, near_ref, refs = refs[:4], refs[4], refs[5:]
    mids, refs = refs[: n_i - 1], refs[n_i - 1 :]
    xmsgs, (out_ref, stats_ref, spread) = refs[:slots], refs[slots:]
    near_statistics(n_i, slots, range(n_i - 1), near_ref, mids, xmsgs, stats_ref, spread)
    for step in range(n_i - 1):
        for slot, parts in enumerate(near_place(n_i, slots, step, sources, stats_ref)):
            for which, part in enumerate(parts):
                out_ref[which, step * slots + slot] = part


def far_sum_kernel(slots, *refs):
    own, refs = refs[:slots], refs[slots:]
    found, outs = refs[: -slots - 1], refs[-slots:]
    for m in range(slots):
        outs[m][:2] = own[m][:2]
        total = own[m][2:].astype(F32)
        for ref in found:
            total += ref[m].astype(F32)
        outs[m][2:] = total.astype(BF16)


def near_parts_kernel(n_i, slots, *refs):
    sources, near_ref, refs = refs[:4], refs[4], refs[5:]
    mids, refs = (refs[0], *refs[n_i - 1 : 0 : -1]), refs[n_i:]
    xmsgs, (out_ref, stats_ref, spread) = refs[:slots], refs[slots:]
    rows = near_ref.shape[1]
    quarter = rows // DILATION
    pos, chip = position(slots)
    lane = lanes_of(quarter)
    mid = jnp.zeros((quarter, LANES), F32)
    for d in range(n_i):
        place = (pos ^ d) * slots
        found = join(mids[d])
        e = pltpu.roll(found, place, 1)
        de = pltpu.roll(found, place + HEADS - slots, 1)
        mid = jnp.where((lane >= place) & (lane < place + slots), e, mid)
        mid = jnp.where((lane >= HEADS + place) & (lane < HEADS + place + slots), de, mid)
    blank = jnp.where(lane < HEADS, LOWEST, 0.0)
    for residue in range(DILATION):
        spread[pl.ds(residue, quarter, stride=DILATION), :] = jnp.where(
            lane % DILATION == residue, mid, blank
        )
    across = spread[...].T
    stats_ref[:HEADS] = jnp.full((HEADS, rows), LOWEST, F32)
    stats_ref[HEADS:] = jnp.zeros((HEADS, rows), F32)
    for m in range(slots):
        head = pos * slots + (chip ^ m)
        stats_ref[pl.ds(head, 1), :] = xmsgs[m][2 * slots + m : 2 * slots + m + 1, :]
        stats_ref[pl.ds(HEADS + head, 1), :] = xmsgs[m][3 * slots + m : 3 * slots + m + 1, :]
    e, d = merge_stats(
        near_ref[:HEADS], near_ref[HEADS:], across[:HEADS], across[HEADS : 2 * HEADS]
    )
    e, d = merge_stats(e, d, stats_ref[:HEADS], stats_ref[HEADS:])
    stats_ref[:HEADS] = e
    stats_ref[HEADS:] = d
    for group in range(HEADS // DILATION):
        heads = range(group * DILATION, (group + 1) * DILATION)
        operands = [
            [ref[:, static_columns(head)] for ref in sources] for head in heads
        ]
        stats = [
            (stats_ref[head : head + 1, :], stats_ref[HEADS + head : HEADS + head + 1, :])
            for head in heads
        ]
        for head, parts in zip(heads, level_parts(operands, stats)):
            for which, part in enumerate(parts):
                out_ref[which, head] = part


def spread_rows(slots, head, slot, ref):
    quarter = ref.shape[1]
    rows = quarter * DILATION
    row = lax.broadcasted_iota(jnp.int32, (rows, quarter), 0)
    taken = lax.broadcasted_iota(jnp.int32, (rows, quarter), 1) * DILATION
    place = jnp.where(row == taken + head % DILATION, 1.0, 0.0).astype(BF16)
    return dot(place, jnp.concatenate([ref[which * slots + slot] for which in range(4)], axis=1))


def send_place(slots, first, ready, outs, sems):
    width = slots * HEAD_DIM
    cols = pl.ds(pl.multiple_of(first * HEAD_DIM, width), width)
    copies = [
        pltpu.make_async_copy(ready.at[which], out.at[:, cols], sems.at[which])
        for which, out in enumerate(outs)
    ]
    for copy in copies:
        copy.start()
    return copies


def final_others_kernel(n_i, slots, *refs):
    sources, near_ref, early_ref, refs = refs[:4], refs[4], refs[5], refs[6:]
    mids, refs = refs[: n_i - 1], refs[n_i - 1 :]
    outs, (ready, sems, stats_ref, spread) = refs[:4], refs[4:]
    last = n_i - 1
    near_statistics(n_i, slots, [last], near_ref, mids[-1:], (), stats_ref, spread)
    late = near_place(n_i, slots, last, sources, stats_ref)
    copies = []
    for step in range(1, n_i):
        first = first_back(n_i, slots, step)
        found = [spread_rows(slots, first + slot, slot, mids[step - 1]) for slot in range(slots)]
        for slot, parts in enumerate(found):
            for which in range(4):
                near = late[slot][which] if step == last else early_ref[which, step * slots + slot]
                total = near + parts[:, static_columns(which)]
                ready[step - 1, which, :, static_columns(slot)] = total.astype(BF16)
        copies += send_place(slots, first, ready.at[step - 1], outs, sems.at[step - 1])
    for copy in copies:
        copy.wait()


def final_own_kernel(slots, early_ref, mid_ref, *refs):
    fulls, refs = in_back(refs[:slots]), refs[slots:]
    outs, (ready, sems) = refs[4:8], refs[8:]
    pos, chip = position(slots)
    first = pos * slots
    found = [spread_rows(slots, first + (chip ^ m), chip ^ m, mid_ref) for m in range(slots)]
    for m, parts in enumerate(found):
        slot = chip ^ m
        for which in range(4):
            total = early_ref[which, slot] + parts[:, static_columns(which)]
            total += fulls[m][which].astype(F32)
            ready[which, :, head_columns(slot)] = total.astype(BF16)
    for copy in send_place(slots, first, ready, outs, sems):
        copy.wait()


def settle_kernel(*refs):
    refs[-1][...] = jnp.zeros_like(refs[-1])


def call(kernel, name, outs, scratch, flops, operands, hbm_in=(), hbm_out=False, cheap=False, limit=VMEM_LIMIT, aliases=None):
    moved = sum(x.size * x.dtype.itemsize for x in tuple(operands) + tuple(outs))
    if cheap:
        flops, moved = 1, 1
    spaces = [pltpu.HBM if i in hbm_in else pltpu.VMEM for i in range(len(operands))]
    return pl.pallas_call(
        kernel,
        out_shape=tuple(outs),
        in_specs=[pl.BlockSpec(memory_space=space) for space in spaces],
        out_specs=tuple(
            pl.BlockSpec(memory_space=pltpu.HBM if hbm_out else pltpu.VMEM) for _ in outs
        ),
        scratch_shapes=scratch,
        input_output_aliases=aliases or {},
        compiler_params=pltpu.CompilerParams(vmem_limit_bytes=limit),
        cost_estimate=pl.CostEstimate(flops=flops, bytes_accessed=moved, transcendentals=0),
        name=name,
    )(*operands)


def in_back(pieces):
    return [pieces[0], *pieces[:0:-1]]


def swap(x, axis, n, mask):
    return lax.ppermute(x, axis, [(i, i ^ mask) for i in range(n)])


def local(query_rows, key_rows, value_rows, upstream):
    rows, features = query_rows.shape
    n_i, n_o = lax.axis_size("seqi"), lax.axis_size("seqo")
    slots = HEADS // n_i
    width = n_o // slots
    others = (width - 1) * slots
    quarter = rows // DILATION
    sources = (key_rows, value_rows, query_rows, upstream)
    unit = 2 * rows * rows * HEAD_DIM
    bind = functools.partial

    mid = SHAPE((4 * slots + 1, quarter, HEAD_DIM), BF16)
    full = SHAPE((4, rows, HEAD_DIM), BF16)
    half = SHAPE((slots, 2, rows, HEAD_DIM), BF16)
    square = pltpu.VMEM((LANES, rows), F32)

    def stats(count, lanes=rows):
        return SHAPE((count, lanes), F32)

    def swap_mids(pieces):
        found = [pieces[0]]
        for step in range(1, n_i):
            pairs = [
                (o * n_i + i, o * n_i + (i ^ distance(n_i, step, o % 2 == 1)))
                for o in range(n_o)
                for i in range(n_i)
            ]
            found.append(lax.ppermute(pieces[step], ("seqo", "seqi"), pairs))
        return found

    def swap_back(pieces):
        return [pieces[0]] + [
            swap(pieces[step], "seqi", n_i, distance_back(n_i, step)) for step in range(1, n_i)
        ]

    def swap_fulls(pieces):
        return [pieces[0]] + [swap(pieces[m], "seqo", n_o, m * width) for m in range(1, slots)]

    pieces = call(
        bind(pick_kernel, n_i, slots),
        "pick",
        [mid] * n_i + [full] * slots + [stats(2 * HEADS)],
        [
            pltpu.VMEM((4, rows, features), BF16),
            pltpu.SemaphoreType.DMA((4, HEADS // DILATION)),
            pltpu.VMEM((4, HEADS, rows, HEAD_DIM), F32),
            pltpu.VMEM((n_i, 4 * slots, quarter, HEAD_DIM), BF16),
            square,
        ],
        unit * HEADS * 2,
        sources,
        hbm_in=range(4),
        limit=PICK_LIMIT,
    )
    mids = swap_mids(pieces[:n_i])
    fulls = swap_fulls(pieces[n_i : n_i + slots])
    near = pieces[-1]

    (settled,) = call(settle_kernel, "far_in", [stats(8)], [], SHORT, mids[1:3])
    (settled,) = call(settle_kernel, "chips_back", [stats(8)], [], LONG, [settled])
    (packed,) = call(bind(pack_kernel, slots), "pack", [half], [], 1, fulls + [settled])
    sibs = [swap(packed, "seqo", n_o, part) for part in range(1, width)]
    (settled,) = call(settle_kernel, "packed_back", [stats(8)], [], LONG, [near])
    (far,) = call(
        bind(far_stats_kernel, slots),
        "far_stats",
        [stats(2 * slots)],
        [],
        1,
        fulls + sibs + [settled],
    )
    xmsg, middle, columns = call(
        bind(middle_stats_kernel, n_i, slots),
        "middle_stats",
        [stats(4 * slots), stats(2 * slots, n_i * quarter), stats(n_i * quarter, LANES)],
        [pltpu.VMEM((LANES, n_i * quarter), F32), square],
        unit * slots * 2,
        mids + [near, far],
    )
    xmsgs = swap_fulls([xmsg] * slots)

    midparts = call(
        bind(middle_parts_kernel, n_i, slots),
        "middle_parts",
        [mid] * n_i,
        [pltpu.VMEM((2 * slots, rows), F32), pltpu.VMEM((LANES, n_i * quarter), F32), square],
        unit * slots * 6,
        mids + [middle, columns] + xmsgs,
    )
    midparts = swap_back(midparts)
    farparts = call(
        bind(far_parts_kernel, slots, width),
        "far_parts",
        [full] * slots + [half] * (width - 1),
        [pltpu.VMEM((n_o * rows, slots * rows), BF16)] * 2,
        unit * n_o * slots * 6,
        fulls + sibs + xmsgs + [midparts[0]],
        cheap=True,
    )
    sibparts = [swap(x, "seqo", n_o, part + 1) for part, x in enumerate(farparts[slots:])]
    (settled,) = call(settle_kernel, "far_back", [stats(8)], [], SHORT, [midparts[1]])
    (settled,) = call(settle_kernel, "sib_back", [stats(8)], [], 1, sibparts + [settled])
    (settled,) = call(settle_kernel, "settle", [stats(8)], [], LONG, [settled])
    fullparts = call(
        bind(far_sum_kernel, slots),
        "far_sum",
        [full] * slots,
        [],
        unit,
        list(farparts[:slots]) + sibparts + [settled],
        cheap=True,
    )
    fullparts = swap_fulls(fullparts)

    back = midparts
    kept = [pltpu.VMEM((2 * HEADS, rows), F32), square]
    (early,) = call(
        bind(near_early_kernel, n_i, slots),
        "near_early",
        [SHAPE((4, (n_i - 1) * slots, rows, HEAD_DIM), F32)],
        kept,
        SHORT,
        [*sources, near, *back[:-1], *xmsgs],
    )
    whole = [SHAPE((rows, features), BF16)] * 4
    outs = call(
        bind(final_others_kernel, n_i, slots),
        "final_others",
        whole,
        [
            pltpu.VMEM((n_i - 1, 4, rows, slots * HEAD_DIM), BF16),
            pltpu.SemaphoreType.DMA((n_i - 1, 4)),
            *kept,
        ],
        SHORT // 2,
        [*sources, near, early, *back[1:]],
        hbm_out=True,
    )
    return call(
        bind(final_own_kernel, slots),
        "final_own",
        whole,
        [pltpu.VMEM((4, rows, slots * HEAD_DIM), BF16), pltpu.SemaphoreType.DMA((4,))],
        unit * slots,
        [early, midparts[0], *in_back(fullparts), *outs],
        hbm_in=range(2 + slots, 6 + slots),
        hbm_out=True,
        aliases={2 + slots + which: which for which in range(4)},
    )


def solution(mesh):
    rows = P(("seqo", "seqi"), None)
    return jax.shard_map(
        local,
        mesh=mesh,
        in_specs=(rows,) * 4,
        out_specs=(rows,) * 4,
        check_vma=False,
    )
```

```python
import functools

import jax
import jax.numpy as jnp
from jax import lax
from jax.experimental import pallas as pl
from jax.experimental.pallas import tpu as pltpu
from jax.sharding import PartitionSpec as P

HEADS = 16
HEAD_DIM = 128
DILATION = 4
LANES = 128
SCALE = HEAD_DIM**-0.5
LOWEST = -1e30
LONG = 4 * 10**10
SHORT = 2 * 10**9
VMEM_LIMIT = 32 * 1024 * 1024
PICK_LIMIT = 53 * 1024 * 1024
FIRST_LIMIT = 54784 * 1024
NEAR_LIMIT = 54784 * 1024
F32, BF16 = jnp.float32, jnp.bfloat16
SHAPE = jax.ShapeDtypeStruct

NT = (((1,), (1,)), ((), ()))
TN = (((0,), (0,)), ((), ()))


def dot(a, b):
    return jnp.dot(a, b, preferred_element_type=F32)


def dot_nt(a, b):
    return lax.dot_general(a, b, NT, preferred_element_type=F32)


def dot_tn(a, b):
    return lax.dot_general(a, b, TN, preferred_element_type=F32)


def head_columns(head):
    return pl.ds(pl.multiple_of(head * HEAD_DIM, HEAD_DIM), HEAD_DIM)


def static_columns(index):
    return slice(index * HEAD_DIM, (index + 1) * HEAD_DIM)


def position(slots):
    width = lax.axis_size("seqo") // slots
    return lax.axis_index("seqi"), lax.axis_index("seqo") // width


def distance(n_i, step):
    return n_i - step


def distance_back(n_i, step):
    return n_i - 1 if step == 1 else step - 1


def place_in(n_i, slots, step):
    pos, _ = position(slots)
    return pos if step == 0 else pos ^ distance(n_i, step)


def first_back(n_i, slots, step):
    pos, _ = position(slots)
    return (pos if step == 0 else pos ^ distance_back(n_i, step)) * slots


def in_back_order(n_i, chunks):
    order = [distance(n_i, step) for step in range(1, n_i)]
    return [chunks[0]] + [
        chunks[order.index(distance_back(n_i, step)) + 1] for step in range(1, n_i)
    ]


def lanes_of(rows):
    return lax.broadcasted_iota(jnp.int32, (rows, LANES), 1)


def level_stats(operands):
    products = [(dot_nt(k, q) * SCALE, dot_nt(v, u)) for k, v, q, u in operands]
    tops = [jnp.max(s, axis=0, keepdims=True) for s, _ in products]
    weights = [jnp.exp(s - top) for (s, _), top in zip(products, tops)]
    totals = [jnp.sum(p, axis=0, keepdims=True) for p in weights]
    return [
        (top + jnp.log(total), jnp.sum(p * dp, axis=0, keepdims=True) / total)
        for (_, dp), top, p, total in zip(products, tops, weights, totals)
    ]


def merge_stats(ea, da, eb, db):
    top = jnp.maximum(ea, eb)
    wa, wb = jnp.exp(ea - top), jnp.exp(eb - top)
    total = wa + wb
    return top + jnp.log(total), (wa * da + wb * db) / total


def level_weights(operands, stats):
    products = [(dot_nt(k, q) * SCALE, dot_nt(v, u)) for k, v, q, u in operands]
    found = []
    for (s, dp), (lse, delta) in zip(products, stats):
        g = jnp.exp(s - lse)
        found.append((g.astype(BF16), (g * (dp - delta)).astype(BF16)))
    return found


def level_parts(operands, stats):
    found = level_weights(operands, stats)
    keyed = [
        (dot(ds, q) * SCALE, dot(p, u)) for (p, ds), (k, v, q, u) in zip(found, operands)
    ]
    queried = [
        (dot_tn(p, v), dot_tn(ds, k) * SCALE) for (p, ds), (k, v, q, u) in zip(found, operands)
    ]
    return [a + b for a, b in zip(queried, keyed)]


def pick_rows(ref, rows):
    quarter = rows // DILATION
    lane = lanes_of(quarter)
    picked = jnp.zeros((quarter, LANES), F32)
    for residue in range(DILATION):
        part = ref[pl.ds(residue, quarter, stride=DILATION), :]
        picked = jnp.where(lane % DILATION == residue, part, picked)
    return picked


def fetch(slots, places, sources, buffers, sems):
    width = slots * HEAD_DIM
    groups = []
    for index, place in enumerate(places):
        cols = pl.ds(pl.multiple_of(place * width, width), width)
        groups.append(
            [
                pltpu.make_async_copy(
                    source.at[:, cols], buffers.at[index, which], sems.at[index, which]
                )
                for which, source in enumerate(sources)
            ]
        )
        for copy in groups[-1]:
            copy.start()
    return groups


def split(x):
    high = x.astype(BF16).astype(F32)
    rest = x - high
    middle = rest.astype(BF16).astype(F32)
    low = rest - middle
    return (high + pltpu.roll(middle, 2 * HEADS, 1) + pltpu.roll(low, 4 * HEADS, 1)).astype(BF16)


def join(ref):
    x = ref[ref.shape[0] - 1].astype(F32)
    x = x + (pltpu.roll(x, LANES - 2 * HEADS, 1) + pltpu.roll(x, LANES - 4 * HEADS, 1))
    return jnp.where(lanes_of(x.shape[0]) < 2 * HEADS, x, 0.0)


def pick_places(n_i, slots, steps, sources, mids, buffers, sems, wide, turn):
    rows = sources[0].shape[0]
    quarter = rows // DILATION
    places = [place_in(n_i, slots, step) for step in steps]
    for index, copies in enumerate(fetch(slots, places, sources, buffers, sems)):
        first = places[index] * slots
        for which, copy in enumerate(copies):
            copy.wait()
            for slot in range(slots):
                wide[index, which, slot] = buffers[index, which, :, static_columns(slot)].astype(F32)
                residue = (first + slot) % DILATION if slots % DILATION else slot % DILATION
                rowset = wide[index, which, slot, pl.ds(residue, quarter, stride=DILATION), :]
                mids[index][which * slots + slot] = rowset.astype(BF16)
        operands = [
            [buffers[index, which, :, static_columns(slot)] for which in range(4)]
            for slot in range(slots)
        ]
        for slot, (e, d) in enumerate(level_stats(operands)):
            turn[pl.ds(first + slot, 1), :] = e
            turn[pl.ds(HEADS + first + slot, 1), :] = d


def pick_first_kernel(n_i, slots, *refs):
    sources, (mid_ref, stats_ref, buffers, sems, wide, turn) = refs[:4], refs[4:]
    rows = sources[0].shape[0]
    turn[...] = jnp.zeros_like(turn)
    pick_places(n_i, slots, [1], sources, [mid_ref], buffers, sems, wide, turn)
    stats_ref[...] = turn[: 2 * HEADS, :]
    turn[...] = turn[...].T
    mid_ref[4 * slots] = split(pick_rows(turn, rows))


def pick_rest_kernel(n_i, slots, *refs):
    sources, first_ref, refs = refs[:4], refs[4], refs[5:]
    mids, refs = refs[: n_i - 1], refs[n_i - 1 :]
    fulls, refs = refs[:slots], refs[slots:]
    stats_ref, buffers, sems, wide, turn = refs
    rows = sources[0].shape[0]
    _, chip = position(slots)
    turn[...] = jnp.zeros_like(turn)
    turn[: 2 * HEADS, :] = first_ref[...]
    steps = [0, *range(2, n_i)]
    pick_places(n_i, slots, steps, sources, mids, buffers, sems, wide, turn)
    for m in range(slots):
        fulls[m][...] = buffers[0, :, :, head_columns(chip ^ m)]
    stats_ref[...] = turn[: 2 * HEADS, :]
    turn[...] = turn[...].T
    near = split(pick_rows(turn, rows))
    for ref in mids:
        ref[4 * slots] = near


def pack_kernel(slots, *refs):
    packed_ref = refs[-1]
    for m, ref in enumerate(in_back(refs[:slots])):
        packed_ref[m] = ref[:2]


def far_keys(fulls, sibs, which):
    blocks = [ref[which] for ref in fulls]
    return jnp.concatenate(blocks + [ref[m, which] for ref in sibs for m in range(len(fulls))], axis=0)


def far_stats_kernel(slots, *refs):
    fulls, sibs, stats_ref = refs[:slots], refs[slots:-2], refs[-1]
    keys, values = far_keys(fulls, sibs, 0), far_keys(fulls, sibs, 1)
    for m in range(slots):
        ((e, d),) = level_stats([(keys, values, fulls[m][2], fulls[m][3])])
        stats_ref[m : m + 1, :] = e
        stats_ref[slots + m : slots + m + 1, :] = d


def middle_operands(slots, mids, slot):
    return [
        jnp.concatenate([ref[which * slots + slot] for ref in mids], axis=0) for which in range(4)
    ]


def middle_stats_kernel(n_i, slots, *refs):
    mids, refs = refs[:n_i], refs[n_i:]
    near_ref, far_ref, xmsg_ref, stats_ref, columns_ref, turn, spread = refs
    rows = near_ref.shape[1]
    quarter = rows // DILATION
    pos, _ = position(slots)
    turn[...] = jnp.zeros_like(turn)
    operands = [middle_operands(slots, mids, slot) for slot in range(slots)]
    for slot, (e, d) in enumerate(level_stats(operands)):
        turn[slot : slot + 1, :] = e
        turn[slots + slot : slots + slot + 1, :] = d
    stats_ref[...] = turn[: 2 * slots, :]
    columns_ref[...] = turn[...].T
    lane = lanes_of(quarter)
    lane_residue = (pos * slots + lane % slots) % DILATION
    blank = jnp.where(lane < slots, LOWEST, 0.0)
    for residue in range(DILATION):
        spread[pl.ds(residue, quarter, stride=DILATION), :] = jnp.where(
            lane_residue == residue, columns_ref[:quarter], blank
        )
    across = spread[...].T
    e, d = merge_stats(
        near_ref[pl.ds(pos * slots, slots), :],
        near_ref[pl.ds(HEADS + pos * slots, slots), :],
        across[:slots],
        across[slots : 2 * slots],
    )
    xmsg_ref[:slots] = e
    xmsg_ref[slots : 2 * slots] = d
    xmsg_ref[2 * slots :] = far_ref[...]


def middle_parts_kernel(n_i, slots, *refs):
    mids, refs = refs[:n_i], refs[n_i:]
    stats_ref, columns_ref = refs[:2]
    refs = refs[2:]
    xmsgs, refs = refs[:slots], refs[slots:]
    outs, (far, turn, spread) = refs[:n_i], refs[n_i:]
    rows = xmsgs[0].shape[1]
    quarter = rows // DILATION
    pos, chip = position(slots)
    for m in range(slots):
        far[pl.ds(chip ^ m, 1), :] = xmsgs[m][2 * slots + m : 2 * slots + m + 1, :]
        far[pl.ds(slots + (chip ^ m), 1), :] = xmsgs[m][3 * slots + m : 3 * slots + m + 1, :]
    e, d = merge_stats(
        xmsgs[0][:slots], xmsgs[0][slots : 2 * slots], far[:slots], far[slots:]
    )
    spread[...] = jnp.zeros_like(spread)
    spread[pl.ds(pos * slots, slots), :] = e
    spread[pl.ds(HEADS + pos * slots, slots), :] = d
    spread[...] = spread[...].T
    own = pick_rows(spread, rows)
    turn[...] = jnp.concatenate([own] + [join(ref) for ref in mids[1:]], axis=0).T
    owned = lax.broadcasted_iota(jnp.int32, (1, n_i * quarter), 1) < quarter
    operands = [middle_operands(slots, mids, slot) for slot in range(slots)]
    merged = [
        merge_stats(
            turn[pl.ds(pos * slots + slot, 1), :],
            turn[pl.ds(HEADS + pos * slots + slot, 1), :],
            jnp.where(owned, LOWEST, stats_ref[slot : slot + 1, :]),
            stats_ref[slots + slot : slots + slot + 1, :],
        )
        for slot in range(slots)
    ]
    for slot, parts in enumerate(level_parts(operands, merged)):
        for which, part in enumerate(parts):
            part = part.astype(BF16)
            chunks = [part[d * quarter : (d + 1) * quarter] for d in range(n_i)]
            for out, chunk in zip(outs, in_back_order(n_i, chunks)):
                out[which * slots + slot] = chunk
    chunks = [columns_ref[d * quarter : (d + 1) * quarter] for d in range(n_i)]
    for out, chunk in zip(outs, in_back_order(n_i, chunks)):
        out[4 * slots] = split(chunk)


def far_parts_kernel(slots, width, *refs):
    fulls, refs = refs[:slots], refs[slots:]
    sibs, refs = refs[: width - 1], refs[width - 1 :]
    xmsgs, refs = refs[:slots], refs[slots + 1 :]
    outs, refs = refs[:slots], refs[slots:]
    kvouts, refs = refs[: width - 1], refs[width - 1 :]
    weights, score_grads = refs
    rows = fulls[0].shape[1]
    _, chip = position(slots)
    keys, values = far_keys(fulls, sibs, 0), far_keys(fulls, sibs, 1)
    for m in range(slots):
        lse, delta = merge_stats(
            xmsgs[m][pl.ds(chip, 1), :],
            xmsgs[m][pl.ds(slots + chip, 1), :],
            xmsgs[0][2 * slots + m : 2 * slots + m + 1, :],
            xmsgs[0][3 * slots + m : 3 * slots + m + 1, :],
        )
        operands = (keys, values, fulls[m][2], fulls[m][3])
        ((p, ds),) = level_weights([operands], [(lse, delta)])
        outs[m][0] = dot_tn(p, values).astype(BF16)
        outs[m][1] = (dot_tn(ds, keys) * SCALE).astype(BF16)
        weights[:, m * rows : (m + 1) * rows] = p
        score_grads[:, m * rows : (m + 1) * rows] = ds
    queries = jnp.concatenate([ref[2] for ref in fulls], axis=0)
    ups = jnp.concatenate([ref[3] for ref in fulls], axis=0)
    key_part = (dot(score_grads[...], queries) * SCALE).astype(BF16)
    value_part = dot(weights[...], ups).astype(BF16)
    for index in range(width * slots):
        block = slice(index * rows, (index + 1) * rows)
        part, m = index // slots, index % slots
        if part == 0:
            outs[m][2], outs[m][3] = key_part[block], value_part[block]
        else:
            kvouts[part - 1][m, 0], kvouts[part - 1][m, 1] = key_part[block], value_part[block]


def far_sum_kernel(slots, *refs):
    own, refs = refs[:slots], refs[slots:]
    found, outs = refs[: -slots - 1], refs[-slots:]
    for m in range(slots):
        outs[m][:2] = own[m][:2]
        total = own[m][2:].astype(F32)
        for ref in found:
            total += ref[m].astype(F32)
        outs[m][2:] = total.astype(BF16)


def near_statistics(n_i, slots, steps, near_ref, mids, xmsgs, stats_ref, spread):
    rows = near_ref.shape[1]
    quarter = rows // DILATION
    pos, chip = position(slots)
    lane = lanes_of(quarter)
    mid = jnp.zeros((quarter, LANES), F32)
    for step, ref in zip(steps, mids):
        place = first_back(n_i, slots, step)
        found = join(ref)
        e = pltpu.roll(found, place, 1)
        de = pltpu.roll(found, place + HEADS - slots, 1)
        mid = jnp.where((lane >= place) & (lane < place + slots), e, mid)
        mid = jnp.where((lane >= HEADS + place) & (lane < HEADS + place + slots), de, mid)
    blank = jnp.where(lane < HEADS, LOWEST, 0.0)
    for residue in range(DILATION):
        spread[pl.ds(residue, quarter, stride=DILATION), :] = jnp.where(
            lane % DILATION == residue, mid, blank
        )
    across = spread[...].T
    e, d = merge_stats(
        near_ref[:HEADS], near_ref[HEADS:], across[:HEADS], across[HEADS : 2 * HEADS]
    )
    if xmsgs:
        stats_ref[:HEADS] = jnp.full((HEADS, rows), LOWEST, F32)
        stats_ref[HEADS:] = jnp.zeros((HEADS, rows), F32)
        for m in range(slots):
            head = pos * slots + (chip ^ m)
            stats_ref[pl.ds(head, 1), :] = xmsgs[m][2 * slots + m : 2 * slots + m + 1, :]
            stats_ref[pl.ds(HEADS + head, 1), :] = xmsgs[m][3 * slots + m : 3 * slots + m + 1, :]
        e, d = merge_stats(e, d, stats_ref[:HEADS], stats_ref[HEADS:])
    stats_ref[:HEADS] = e
    stats_ref[HEADS:] = d


def near_place(n_i, slots, step, sources, stats_ref):
    heads = [first_back(n_i, slots, step) + slot for slot in range(slots)]
    operands = [[ref[:, head_columns(head)] for ref in sources] for head in heads]
    stats = [(stats_ref[pl.ds(head, 1), :], stats_ref[pl.ds(HEADS + head, 1), :]) for head in heads]
    return level_parts(operands, stats)


def near_early_kernel(n_i, slots, *refs):
    sources, near_ref, refs = refs[:4], refs[4], refs[5:]
    mids, refs = refs[: n_i - 1], refs[n_i - 1 :]
    xmsgs, (out_ref, stats_ref, spread) = refs[:slots], refs[slots:]
    near_statistics(n_i, slots, range(n_i - 1), near_ref, mids, xmsgs, stats_ref, spread)
    for step in range(n_i - 1):
        for slot, parts in enumerate(near_place(n_i, slots, step, sources, stats_ref)):
            for which, part in enumerate(parts):
                out_ref[which, step * slots + slot] = part


def far_sum_kernel(slots, *refs):
    own, refs = refs[:slots], refs[slots:]
    found, outs = refs[: -slots - 1], refs[-slots:]
    for m in range(slots):
        outs[m][:2] = own[m][:2]
        total = own[m][2:].astype(F32)
        for ref in found:
            total += ref[m].astype(F32)
        outs[m][2:] = total.astype(BF16)


def near_parts_kernel(n_i, slots, *refs):
    sources, near_ref, refs = refs[:4], refs[4], refs[5:]
    mids, refs = (refs[0], *refs[n_i - 1 : 0 : -1]), refs[n_i:]
    xmsgs, (out_ref, stats_ref, spread) = refs[:slots], refs[slots:]
    rows = near_ref.shape[1]
    quarter = rows // DILATION
    pos, chip = position(slots)
    lane = lanes_of(quarter)
    mid = jnp.zeros((quarter, LANES), F32)
    for d in range(n_i):
        place = (pos ^ d) * slots
        found = join(mids[d])
        e = pltpu.roll(found, place, 1)
        de = pltpu.roll(found, place + HEADS - slots, 1)
        mid = jnp.where((lane >= place) & (lane < place + slots), e, mid)
        mid = jnp.where((lane >= HEADS + place) & (lane < HEADS + place + slots), de, mid)
    blank = jnp.where(lane < HEADS, LOWEST, 0.0)
    for residue in range(DILATION):
        spread[pl.ds(residue, quarter, stride=DILATION), :] = jnp.where(
            lane % DILATION == residue, mid, blank
        )
    across = spread[...].T
    stats_ref[:HEADS] = jnp.full((HEADS, rows), LOWEST, F32)
    stats_ref[HEADS:] = jnp.zeros((HEADS, rows), F32)
    for m in range(slots):
        head = pos * slots + (chip ^ m)
        stats_ref[pl.ds(head, 1), :] = xmsgs[m][2 * slots + m : 2 * slots + m + 1, :]
        stats_ref[pl.ds(HEADS + head, 1), :] = xmsgs[m][3 * slots + m : 3 * slots + m + 1, :]
    e, d = merge_stats(
        near_ref[:HEADS], near_ref[HEADS:], across[:HEADS], across[HEADS : 2 * HEADS]
    )
    e, d = merge_stats(e, d, stats_ref[:HEADS], stats_ref[HEADS:])
    stats_ref[:HEADS] = e
    stats_ref[HEADS:] = d
    for group in range(HEADS // DILATION):
        heads = range(group * DILATION, (group + 1) * DILATION)
        operands = [
            [ref[:, static_columns(head)] for ref in sources] for head in heads
        ]
        stats = [
            (stats_ref[head : head + 1, :], stats_ref[HEADS + head : HEADS + head + 1, :])
            for head in heads
        ]
        for head, parts in zip(heads, level_parts(operands, stats)):
            for which, part in enumerate(parts):
                out_ref[which, head] = part


def spread_rows(slots, head, slot, ref):
    quarter = ref.shape[1]
    rows = quarter * DILATION
    row = lax.broadcasted_iota(jnp.int32, (rows, quarter), 0)
    taken = lax.broadcasted_iota(jnp.int32, (rows, quarter), 1) * DILATION
    place = jnp.where(row == taken + head % DILATION, 1.0, 0.0).astype(BF16)
    return dot(place, jnp.concatenate([ref[which * slots + slot] for which in range(4)], axis=1))


def send_place(slots, first, ready, outs, sems):
    width = slots * HEAD_DIM
    cols = pl.ds(pl.multiple_of(first * HEAD_DIM, width), width)
    copies = [
        pltpu.make_async_copy(ready.at[which], out.at[:, cols], sems.at[which])
        for which, out in enumerate(outs)
    ]
    for copy in copies:
        copy.start()
    return copies


def final_others_kernel(n_i, slots, *refs):
    sources, near_ref, early_ref, refs = refs[:4], refs[4], refs[5], refs[6:]
    mids, refs = refs[: n_i - 1], refs[n_i - 1 :]
    outs, (ready, sems, stats_ref, spread) = refs[:4], refs[4:]
    last = n_i - 1
    near_statistics(n_i, slots, [last], near_ref, mids[-1:], (), stats_ref, spread)
    late = near_place(n_i, slots, last, sources, stats_ref)
    copies = []
    for step in range(1, n_i):
        first = first_back(n_i, slots, step)
        found = [spread_rows(slots, first + slot, slot, mids[step - 1]) for slot in range(slots)]
        for slot, parts in enumerate(found):
            for which in range(4):
                near = late[slot][which] if step == last else early_ref[which, step * slots + slot]
                total = near + parts[:, static_columns(which)]
                ready[step - 1, which, :, static_columns(slot)] = total.astype(BF16)
        copies += send_place(slots, first, ready.at[step - 1], outs, sems.at[step - 1])
    for copy in copies:
        copy.wait()


def final_own_kernel(slots, early_ref, mid_ref, *refs):
    fulls, refs = in_back(refs[:slots]), refs[slots:]
    outs, (ready, sems) = refs[4:8], refs[8:]
    pos, chip = position(slots)
    first = pos * slots
    found = [spread_rows(slots, first + (chip ^ m), chip ^ m, mid_ref) for m in range(slots)]
    for m, parts in enumerate(found):
        slot = chip ^ m
        for which in range(4):
            total = early_ref[which, slot] + parts[:, static_columns(which)]
            total += fulls[m][which].astype(F32)
            ready[which, :, head_columns(slot)] = total.astype(BF16)
    for copy in send_place(slots, first, ready, outs, sems):
        copy.wait()


def settle_kernel(*refs):
    refs[-1][...] = jnp.zeros_like(refs[-1])


def call(kernel, name, outs, scratch, flops, operands, hbm_in=(), hbm_out=False, cheap=False, limit=VMEM_LIMIT, aliases=None):
    moved = sum(x.size * x.dtype.itemsize for x in tuple(operands) + tuple(outs))
    if cheap:
        flops, moved = 1, 1
    spaces = [pltpu.HBM if i in hbm_in else pltpu.VMEM for i in range(len(operands))]
    return pl.pallas_call(
        kernel,
        out_shape=tuple(outs),
        in_specs=[pl.BlockSpec(memory_space=space) for space in spaces],
        out_specs=tuple(
            pl.BlockSpec(memory_space=pltpu.HBM if hbm_out else pltpu.VMEM) for _ in outs
        ),
        scratch_shapes=scratch,
        input_output_aliases=aliases or {},
        compiler_params=pltpu.CompilerParams(vmem_limit_bytes=limit),
        cost_estimate=pl.CostEstimate(flops=flops, bytes_accessed=moved, transcendentals=0),
        name=name,
    )(*operands)


def in_back(pieces):
    return [pieces[0], *pieces[:0:-1]]


def swap(x, axis, n, mask):
    return lax.ppermute(x, axis, [(i, i ^ mask) for i in range(n)])


def local(query_rows, key_rows, value_rows, upstream):
    rows, features = query_rows.shape
    n_i, n_o = lax.axis_size("seqi"), lax.axis_size("seqo")
    slots = HEADS // n_i
    width = n_o // slots
    others = (width - 1) * slots
    quarter = rows // DILATION
    sources = (key_rows, value_rows, query_rows, upstream)
    unit = 2 * rows * rows * HEAD_DIM
    bind = functools.partial

    mid = SHAPE((4 * slots + 1, quarter, HEAD_DIM), BF16)
    full = SHAPE((4, rows, HEAD_DIM), BF16)
    half = SHAPE((slots, 2, rows, HEAD_DIM), BF16)
    square = pltpu.VMEM((LANES, rows), F32)

    def stats(count, lanes=rows):
        return SHAPE((count, lanes), F32)

    def swap_mids(pieces):
        return [pieces[0]] + [
            swap(pieces[step], "seqi", n_i, distance(n_i, step)) for step in range(1, n_i)
        ]

    def swap_back(pieces):
        return [pieces[0]] + [
            swap(pieces[step], "seqi", n_i, distance_back(n_i, step)) for step in range(1, n_i)
        ]

    def swap_fulls(pieces):
        return [pieces[0]] + [swap(pieces[m], "seqo", n_o, m * width) for m in range(1, slots)]

    def pick_scratch(count):
        return [
            pltpu.VMEM((count, 4, rows, slots * HEAD_DIM), BF16),
            pltpu.SemaphoreType.DMA((count, 4)),
            pltpu.VMEM((count, 4, slots, rows, HEAD_DIM), F32),
            square,
        ]

    first, firststats = call(
        bind(pick_first_kernel, n_i, slots),
        "pick_first",
        [mid, stats(2 * HEADS)],
        pick_scratch(1),
        unit * slots * 2,
        sources,
        hbm_in=range(4),
        limit=FIRST_LIMIT,
    )
    pieces = call(
        bind(pick_rest_kernel, n_i, slots),
        "pick_rest",
        [mid] * (n_i - 1) + [full] * slots + [stats(2 * HEADS)],
        pick_scratch(n_i - 1),
        unit * HEADS * 2,
        [*sources, firststats],
        hbm_in=range(4),
        limit=PICK_LIMIT,
    )
    mids = swap_mids([pieces[0], first, *pieces[1 : n_i - 1]])
    fulls = swap_fulls(pieces[n_i - 1 : n_i - 1 + slots])
    near = pieces[-1]

    (settled,) = call(settle_kernel, "far_in", [stats(8)], [], SHORT, [mids[1]])
    (settled,) = call(settle_kernel, "chips_back", [stats(8)], [], LONG, [settled])
    (packed,) = call(bind(pack_kernel, slots), "pack", [half], [], 1, [*in_back(fulls), settled])
    sibs = [swap(packed, "seqo", n_o, part) for part in range(1, width)]
    (settled,) = call(settle_kernel, "packed_back", [stats(8)], [], LONG, [near])
    (far,) = call(
        bind(far_stats_kernel, slots),
        "far_stats",
        [stats(2 * slots)],
        [],
        1,
        fulls + sibs + [settled],
    )
    xmsg, middle, columns = call(
        bind(middle_stats_kernel, n_i, slots),
        "middle_stats",
        [stats(4 * slots), stats(2 * slots, n_i * quarter), stats(n_i * quarter, LANES)],
        [pltpu.VMEM((LANES, n_i * quarter), F32), square],
        unit * slots * 2,
        mids + [near, far],
    )
    xmsgs = swap_fulls([xmsg] * slots)

    midparts = call(
        bind(middle_parts_kernel, n_i, slots),
        "middle_parts",
        [mid] * n_i,
        [pltpu.VMEM((2 * slots, rows), F32), pltpu.VMEM((LANES, n_i * quarter), F32), square],
        unit * slots * 6,
        mids + [middle, columns] + xmsgs,
    )
    midparts = swap_back(midparts)
    farparts = call(
        bind(far_parts_kernel, slots, width),
        "far_parts",
        [full] * slots + [half] * (width - 1),
        [pltpu.VMEM((n_o * rows, slots * rows), BF16)] * 2,
        unit * n_o * slots * 6,
        fulls + sibs + xmsgs + [midparts[0]],
        cheap=True,
    )
    sibparts = [swap(x, "seqo", n_o, part + 1) for part, x in enumerate(farparts[slots:])]
    (settled,) = call(settle_kernel, "far_back", [stats(8)], [], SHORT, [midparts[1]])
    (settled,) = call(settle_kernel, "sib_back", [stats(8)], [], 1, sibparts + [settled])
    (settled,) = call(settle_kernel, "settle", [stats(8)], [], LONG, [settled])
    fullparts = call(
        bind(far_sum_kernel, slots),
        "far_sum",
        [full] * slots,
        [],
        unit,
        list(farparts[:slots]) + sibparts + [settled],
        cheap=True,
    )
    fullparts = swap_fulls(fullparts)

    back = midparts
    kept = [pltpu.VMEM((2 * HEADS, rows), F32), square]
    (early,) = call(
        bind(near_early_kernel, n_i, slots),
        "near_early",
        [SHAPE((4, (n_i - 1) * slots, rows, HEAD_DIM), F32)],
        kept,
        SHORT,
        [*sources, near, *back[:-1], *xmsgs],
    )
    whole = [SHAPE((rows, features), BF16)] * 4
    outs = call(
        bind(final_others_kernel, n_i, slots),
        "final_others",
        whole,
        [
            pltpu.VMEM((n_i - 1, 4, rows, slots * HEAD_DIM), BF16),
            pltpu.SemaphoreType.DMA((n_i - 1, 4)),
            *kept,
        ],
        SHORT // 2,
        [*sources, near, early, *back[1:]],
        hbm_out=True,
    )
    return call(
        bind(final_own_kernel, slots),
        "final_own",
        whole,
        [pltpu.VMEM((4, rows, slots * HEAD_DIM), BF16), pltpu.SemaphoreType.DMA((4,))],
        unit * slots,
        [early, midparts[0], *in_back(fullparts), *outs],
        hbm_in=range(2 + slots, 6 + slots),
        hbm_out=True,
        aliases={2 + slots + which: which for which in range(4)},
    )


def solution(mesh):
    rows = P(("seqo", "seqi"), None)
    return jax.shard_map(
        local,
        mesh=mesh,
        in_specs=(rows,) * 4,
        out_specs=(rows,) * 4,
        check_vma=False,
    )
```

```python
import functools

import jax
import jax.numpy as jnp
from jax import lax
from jax.experimental import pallas as pl
from jax.experimental.pallas import tpu as pltpu
from jax.sharding import PartitionSpec as P

HEADS = 16
HEAD_DIM = 128
DILATION = 4
LANES = 128
SCALE = HEAD_DIM**-0.5
LOWEST = -1e30
LONG = 4 * 10**10
SHORT = 2 * 10**9
VMEM_LIMIT = 32 * 1024 * 1024
PICK_LIMIT = 53 * 1024 * 1024
FIRST_LIMIT = 54784 * 1024
NEAR_LIMIT = 54784 * 1024
F32, BF16 = jnp.float32, jnp.bfloat16
SHAPE = jax.ShapeDtypeStruct

NT = (((1,), (1,)), ((), ()))
TN = (((0,), (0,)), ((), ()))


def dot(a, b):
    return jnp.dot(a, b, preferred_element_type=F32)


def dot_nt(a, b):
    return lax.dot_general(a, b, NT, preferred_element_type=F32)


def dot_tn(a, b):
    return lax.dot_general(a, b, TN, preferred_element_type=F32)


def head_columns(head):
    return pl.ds(pl.multiple_of(head * HEAD_DIM, HEAD_DIM), HEAD_DIM)


def static_columns(index):
    return slice(index * HEAD_DIM, (index + 1) * HEAD_DIM)


def position(slots):
    width = lax.axis_size("seqo") // slots
    return lax.axis_index("seqi"), lax.axis_index("seqo") // width


def distance(n_i, step):
    return n_i - step


def distance_back(n_i, step):
    return n_i - 1 if step == 1 else step - 1


def place_in(n_i, slots, step):
    pos, _ = position(slots)
    return pos if step == 0 else pos ^ distance(n_i, step)


def first_back(n_i, slots, step):
    pos, _ = position(slots)
    return (pos if step == 0 else pos ^ distance_back(n_i, step)) * slots


def in_back_order(n_i, chunks):
    order = [distance(n_i, step) for step in range(1, n_i)]
    return [chunks[0]] + [
        chunks[order.index(distance_back(n_i, step)) + 1] for step in range(1, n_i)
    ]


def lanes_of(rows):
    return lax.broadcasted_iota(jnp.int32, (rows, LANES), 1)


def level_stats(operands):
    products = [(dot_nt(k, q) * SCALE, dot_nt(v, u)) for k, v, q, u in operands]
    tops = [jnp.max(s, axis=0, keepdims=True) for s, _ in products]
    weights = [jnp.exp(s - top) for (s, _), top in zip(products, tops)]
    totals = [jnp.sum(p, axis=0, keepdims=True) for p in weights]
    return [
        (top + jnp.log(total), jnp.sum(p * dp, axis=0, keepdims=True) / total)
        for (_, dp), top, p, total in zip(products, tops, weights, totals)
    ]


def merge_stats(ea, da, eb, db):
    top = jnp.maximum(ea, eb)
    wa, wb = jnp.exp(ea - top), jnp.exp(eb - top)
    total = wa + wb
    return top + jnp.log(total), (wa * da + wb * db) / total


def level_weights(operands, stats):
    products = [(dot_nt(k, q) * SCALE, dot_nt(v, u)) for k, v, q, u in operands]
    found = []
    for (s, dp), (lse, delta) in zip(products, stats):
        g = jnp.exp(s - lse)
        found.append((g.astype(BF16), (g * (dp - delta)).astype(BF16)))
    return found


def level_parts(operands, stats):
    found = level_weights(operands, stats)
    keyed = [
        (dot(ds, q) * SCALE, dot(p, u)) for (p, ds), (k, v, q, u) in zip(found, operands)
    ]
    queried = [
        (dot_tn(p, v), dot_tn(ds, k) * SCALE) for (p, ds), (k, v, q, u) in zip(found, operands)
    ]
    return [a + b for a, b in zip(queried, keyed)]


def pick_rows(ref, rows):
    quarter = rows // DILATION
    lane = lanes_of(quarter)
    picked = jnp.zeros((quarter, LANES), F32)
    for residue in range(DILATION):
        part = ref[pl.ds(residue, quarter, stride=DILATION), :]
        picked = jnp.where(lane % DILATION == residue, part, picked)
    return picked


def fetch(slots, places, sources, buffers, sems):
    width = slots * HEAD_DIM
    groups = []
    for index, place in enumerate(places):
        cols = pl.ds(pl.multiple_of(place * width, width), width)
        groups.append(
            [
                pltpu.make_async_copy(
                    source.at[:, cols], buffers.at[index, which], sems.at[index, which]
                )
                for which, source in enumerate(sources)
            ]
        )
        for copy in groups[-1]:
            copy.start()
    return groups


def split(x):
    high = x.astype(BF16).astype(F32)
    rest = x - high
    middle = rest.astype(BF16).astype(F32)
    low = rest - middle
    return (high + pltpu.roll(middle, 2 * HEADS, 1) + pltpu.roll(low, 4 * HEADS, 1)).astype(BF16)


def join(ref):
    x = ref[ref.shape[0] - 1].astype(F32)
    x = x + (pltpu.roll(x, LANES - 2 * HEADS, 1) + pltpu.roll(x, LANES - 4 * HEADS, 1))
    return jnp.where(lanes_of(x.shape[0]) < 2 * HEADS, x, 0.0)


def pick_places(n_i, slots, steps, sources, mids, buffers, sems, wide, turn):
    rows = sources[0].shape[0]
    quarter = rows // DILATION
    places = [place_in(n_i, slots, step) for step in steps]
    for index, copies in enumerate(fetch(slots, places, sources, buffers, sems)):
        first = places[index] * slots
        for which, copy in enumerate(copies):
            copy.wait()
            for slot in range(slots):
                wide[index, which, slot] = buffers[index, which, :, static_columns(slot)].astype(F32)
                residue = (first + slot) % DILATION if slots % DILATION else slot % DILATION
                rowset = wide[index, which, slot, pl.ds(residue, quarter, stride=DILATION), :]
                mids[index][which * slots + slot] = rowset.astype(BF16)
        operands = [
            [buffers[index, which, :, static_columns(slot)] for which in range(4)]
            for slot in range(slots)
        ]
        for slot, (e, d) in enumerate(level_stats(operands)):
            turn[pl.ds(first + slot, 1), :] = e
            turn[pl.ds(HEADS + first + slot, 1), :] = d


def pick_first_kernel(n_i, slots, *refs):
    sources, (mid_ref, stats_ref, buffers, sems, wide, turn) = refs[:4], refs[4:]
    rows = sources[0].shape[0]
    turn[...] = jnp.zeros_like(turn)
    pick_places(n_i, slots, [1], sources, [mid_ref], buffers, sems, wide, turn)
    stats_ref[...] = turn[: 2 * HEADS, :]
    turn[...] = turn[...].T
    mid_ref[4 * slots] = split(pick_rows(turn, rows))


def pick_rest_kernel(n_i, slots, *refs):
    sources, first_ref, refs = refs[:4], refs[4], refs[5:]
    mids, refs = refs[: n_i - 1], refs[n_i - 1 :]
    fulls, refs = refs[:slots], refs[slots:]
    stats_ref, buffers, sems, wide, turn = refs
    rows = sources[0].shape[0]
    _, chip = position(slots)
    turn[...] = jnp.zeros_like(turn)
    turn[: 2 * HEADS, :] = first_ref[...]
    steps = [0, *range(2, n_i)]
    pick_places(n_i, slots, steps, sources, mids, buffers, sems, wide, turn)
    for m in range(slots):
        fulls[m][...] = buffers[0, :, :, head_columns(chip ^ m)]
    stats_ref[...] = turn[: 2 * HEADS, :]
    turn[...] = turn[...].T
    near = split(pick_rows(turn, rows))
    for ref in mids:
        ref[4 * slots] = near


def pack_kernel(slots, *refs):
    packed_ref = refs[-1]
    for m, ref in enumerate(in_back(refs[:slots])):
        packed_ref[m] = ref[:2]


def far_keys(fulls, sibs, which):
    blocks = [ref[which] for ref in fulls]
    return jnp.concatenate(blocks + [ref[m, which] for ref in sibs for m in range(len(fulls))], axis=0)


def far_stats_kernel(slots, *refs):
    fulls, sibs, stats_ref = in_back(refs[:slots]), refs[slots:-2], refs[-1]
    keys, values = far_keys(fulls, sibs, 0), far_keys(fulls, sibs, 1)
    for m in range(slots):
        ((e, d),) = level_stats([(keys, values, fulls[m][2], fulls[m][3])])
        stats_ref[m : m + 1, :] = e
        stats_ref[slots + m : slots + m + 1, :] = d


def middle_operands(slots, mids, slot):
    return [
        jnp.concatenate([ref[which * slots + slot] for ref in mids], axis=0) for which in range(4)
    ]


def middle_stats_kernel(n_i, slots, *refs):
    mids, refs = refs[:n_i], refs[n_i:]
    near_ref, far_ref, xmsg_ref, stats_ref, columns_ref, turn, spread = refs
    rows = near_ref.shape[1]
    quarter = rows // DILATION
    pos, _ = position(slots)
    turn[...] = jnp.zeros_like(turn)
    operands = [middle_operands(slots, mids, slot) for slot in range(slots)]
    for slot, (e, d) in enumerate(level_stats(operands)):
        turn[slot : slot + 1, :] = e
        turn[slots + slot : slots + slot + 1, :] = d
    stats_ref[...] = turn[: 2 * slots, :]
    columns_ref[...] = turn[...].T
    lane = lanes_of(quarter)
    lane_residue = (pos * slots + lane % slots) % DILATION
    blank = jnp.where(lane < slots, LOWEST, 0.0)
    for residue in range(DILATION):
        spread[pl.ds(residue, quarter, stride=DILATION), :] = jnp.where(
            lane_residue == residue, columns_ref[:quarter], blank
        )
    across = spread[...].T
    e, d = merge_stats(
        near_ref[pl.ds(pos * slots, slots), :],
        near_ref[pl.ds(HEADS + pos * slots, slots), :],
        across[:slots],
        across[slots : 2 * slots],
    )
    xmsg_ref[:slots] = e
    xmsg_ref[slots : 2 * slots] = d
    xmsg_ref[2 * slots :] = far_ref[...]


def middle_parts_kernel(n_i, slots, *refs):
    mids, refs = refs[:n_i], refs[n_i:]
    stats_ref, columns_ref = refs[:2]
    refs = refs[2:]
    xmsgs, refs = refs[:slots], refs[slots:]
    outs, (far, turn, spread) = refs[:n_i], refs[n_i:]
    rows = xmsgs[0].shape[1]
    quarter = rows // DILATION
    pos, chip = position(slots)
    for m in range(slots):
        far[pl.ds(chip ^ m, 1), :] = xmsgs[m][2 * slots + m : 2 * slots + m + 1, :]
        far[pl.ds(slots + (chip ^ m), 1), :] = xmsgs[m][3 * slots + m : 3 * slots + m + 1, :]
    e, d = merge_stats(
        xmsgs[0][:slots], xmsgs[0][slots : 2 * slots], far[:slots], far[slots:]
    )
    spread[...] = jnp.zeros_like(spread)
    spread[pl.ds(pos * slots, slots), :] = e
    spread[pl.ds(HEADS + pos * slots, slots), :] = d
    spread[...] = spread[...].T
    own = pick_rows(spread, rows)
    turn[...] = jnp.concatenate([own] + [join(ref) for ref in mids[1:]], axis=0).T
    owned = lax.broadcasted_iota(jnp.int32, (1, n_i * quarter), 1) < quarter
    operands = [middle_operands(slots, mids, slot) for slot in range(slots)]
    merged = [
        merge_stats(
            turn[pl.ds(pos * slots + slot, 1), :],
            turn[pl.ds(HEADS + pos * slots + slot, 1), :],
            jnp.where(owned, LOWEST, stats_ref[slot : slot + 1, :]),
            stats_ref[slots + slot : slots + slot + 1, :],
        )
        for slot in range(slots)
    ]
    for slot, parts in enumerate(level_parts(operands, merged)):
        for which, part in enumerate(parts):
            part = part.astype(BF16)
            chunks = [part[d * quarter : (d + 1) * quarter] for d in range(n_i)]
            for out, chunk in zip(outs, in_back_order(n_i, chunks)):
                out[which * slots + slot] = chunk
    chunks = [columns_ref[d * quarter : (d + 1) * quarter] for d in range(n_i)]
    for out, chunk in zip(outs, in_back_order(n_i, chunks)):
        out[4 * slots] = split(chunk)


def far_parts_kernel(slots, width, *refs):
    fulls, refs = in_back(refs[:slots]), refs[slots:]
    sibs, refs = refs[: width - 1], refs[width - 1 :]
    xmsgs, refs = refs[:slots], refs[slots + 1 :]
    outs, refs = refs[:slots], refs[slots:]
    kvouts, refs = refs[: width - 1], refs[width - 1 :]
    weights, score_grads = refs
    rows = fulls[0].shape[1]
    _, chip = position(slots)
    keys, values = far_keys(fulls, sibs, 0), far_keys(fulls, sibs, 1)
    for m in range(slots):
        lse, delta = merge_stats(
            xmsgs[m][pl.ds(chip, 1), :],
            xmsgs[m][pl.ds(slots + chip, 1), :],
            xmsgs[0][2 * slots + m : 2 * slots + m + 1, :],
            xmsgs[0][3 * slots + m : 3 * slots + m + 1, :],
        )
        operands = (keys, values, fulls[m][2], fulls[m][3])
        ((p, ds),) = level_weights([operands], [(lse, delta)])
        outs[m][0] = dot_tn(p, values).astype(BF16)
        outs[m][1] = (dot_tn(ds, keys) * SCALE).astype(BF16)
        weights[:, m * rows : (m + 1) * rows] = p
        score_grads[:, m * rows : (m + 1) * rows] = ds
    queries = jnp.concatenate([ref[2] for ref in fulls], axis=0)
    ups = jnp.concatenate([ref[3] for ref in fulls], axis=0)
    key_part = (dot(score_grads[...], queries) * SCALE).astype(BF16)
    value_part = dot(weights[...], ups).astype(BF16)
    for index in range(width * slots):
        block = slice(index * rows, (index + 1) * rows)
        part, m = index // slots, index % slots
        if part == 0:
            outs[m][2], outs[m][3] = key_part[block], value_part[block]
        else:
            kvouts[part - 1][m, 0], kvouts[part - 1][m, 1] = key_part[block], value_part[block]


def far_sum_kernel(slots, *refs):
    own, refs = refs[:slots], refs[slots:]
    found, outs = refs[: -slots - 1], refs[-slots:]
    for m in range(slots):
        outs[m][:2] = own[m][:2]
        total = own[m][2:].astype(F32)
        for ref in found:
            total += ref[m].astype(F32)
        outs[m][2:] = total.astype(BF16)


def near_statistics(n_i, slots, steps, near_ref, mids, xmsgs, stats_ref, spread):
    rows = near_ref.shape[1]
    quarter = rows // DILATION
    pos, chip = position(slots)
    lane = lanes_of(quarter)
    mid = jnp.zeros((quarter, LANES), F32)
    for step, ref in zip(steps, mids):
        place = first_back(n_i, slots, step)
        found = join(ref)
        e = pltpu.roll(found, place, 1)
        de = pltpu.roll(found, place + HEADS - slots, 1)
        mid = jnp.where((lane >= place) & (lane < place + slots), e, mid)
        mid = jnp.where((lane >= HEADS + place) & (lane < HEADS + place + slots), de, mid)
    blank = jnp.where(lane < HEADS, LOWEST, 0.0)
    for residue in range(DILATION):
        spread[pl.ds(residue, quarter, stride=DILATION), :] = jnp.where(
            lane % DILATION == residue, mid, blank
        )
    across = spread[...].T
    e, d = merge_stats(
        near_ref[:HEADS], near_ref[HEADS:], across[:HEADS], across[HEADS : 2 * HEADS]
    )
    if xmsgs:
        stats_ref[:HEADS] = jnp.full((HEADS, rows), LOWEST, F32)
        stats_ref[HEADS:] = jnp.zeros((HEADS, rows), F32)
        for m in range(slots):
            head = pos * slots + (chip ^ m)
            stats_ref[pl.ds(head, 1), :] = xmsgs[m][2 * slots + m : 2 * slots + m + 1, :]
            stats_ref[pl.ds(HEADS + head, 1), :] = xmsgs[m][3 * slots + m : 3 * slots + m + 1, :]
        e, d = merge_stats(e, d, stats_ref[:HEADS], stats_ref[HEADS:])
    stats_ref[:HEADS] = e
    stats_ref[HEADS:] = d


def near_place(n_i, slots, step, sources, stats_ref):
    heads = [first_back(n_i, slots, step) + slot for slot in range(slots)]
    operands = [[ref[:, head_columns(head)] for ref in sources] for head in heads]
    stats = [(stats_ref[pl.ds(head, 1), :], stats_ref[pl.ds(HEADS + head, 1), :]) for head in heads]
    return level_parts(operands, stats)


def near_early_kernel(n_i, slots, *refs):
    sources, near_ref, refs = refs[:4], refs[4], refs[5:]
    mids, refs = refs[: n_i - 1], refs[n_i - 1 :]
    xmsgs, (out_ref, stats_ref, spread) = refs[:slots], refs[slots:]
    near_statistics(n_i, slots, range(n_i - 1), near_ref, mids, xmsgs, stats_ref, spread)
    for step in range(n_i - 1):
        for slot, parts in enumerate(near_place(n_i, slots, step, sources, stats_ref)):
            for which, part in enumerate(parts):
                out_ref[which, step * slots + slot] = part


def far_sum_kernel(slots, *refs):
    own, refs = refs[:slots], refs[slots:]
    found, outs = refs[: -slots - 1], refs[-slots:]
    for m in range(slots):
        outs[m][:2] = own[m][:2]
        total = own[m][2:].astype(F32)
        for ref in found:
            total += ref[m].astype(F32)
        outs[m][2:] = total.astype(BF16)


def near_parts_kernel(n_i, slots, *refs):
    sources, near_ref, refs = refs[:4], refs[4], refs[5:]
    mids, refs = (refs[0], *refs[n_i - 1 : 0 : -1]), refs[n_i:]
    xmsgs, (out_ref, stats_ref, spread) = refs[:slots], refs[slots:]
    rows = near_ref.shape[1]
    quarter = rows // DILATION
    pos, chip = position(slots)
    lane = lanes_of(quarter)
    mid = jnp.zeros((quarter, LANES), F32)
    for d in range(n_i):
        place = (pos ^ d) * slots
        found = join(mids[d])
        e = pltpu.roll(found, place, 1)
        de = pltpu.roll(found, place + HEADS - slots, 1)
        mid = jnp.where((lane >= place) & (lane < place + slots), e, mid)
        mid = jnp.where((lane >= HEADS + place) & (lane < HEADS + place + slots), de, mid)
    blank = jnp.where(lane < HEADS, LOWEST, 0.0)
    for residue in range(DILATION):
        spread[pl.ds(residue, quarter, stride=DILATION), :] = jnp.where(
            lane % DILATION == residue, mid, blank
        )
    across = spread[...].T
    stats_ref[:HEADS] = jnp.full((HEADS, rows), LOWEST, F32)
    stats_ref[HEADS:] = jnp.zeros((HEADS, rows), F32)
    for m in range(slots):
        head = pos * slots + (chip ^ m)
        stats_ref[pl.ds(head, 1), :] = xmsgs[m][2 * slots + m : 2 * slots + m + 1, :]
        stats_ref[pl.ds(HEADS + head, 1), :] = xmsgs[m][3 * slots + m : 3 * slots + m + 1, :]
    e, d = merge_stats(
        near_ref[:HEADS], near_ref[HEADS:], across[:HEADS], across[HEADS : 2 * HEADS]
    )
    e, d = merge_stats(e, d, stats_ref[:HEADS], stats_ref[HEADS:])
    stats_ref[:HEADS] = e
    stats_ref[HEADS:] = d
    for group in range(HEADS // DILATION):
        heads = range(group * DILATION, (group + 1) * DILATION)
        operands = [
            [ref[:, static_columns(head)] for ref in sources] for head in heads
        ]
        stats = [
            (stats_ref[head : head + 1, :], stats_ref[HEADS + head : HEADS + head + 1, :])
            for head in heads
        ]
        for head, parts in zip(heads, level_parts(operands, stats)):
            for which, part in enumerate(parts):
                out_ref[which, head] = part


def spread_rows(slots, head, slot, ref):
    quarter = ref.shape[1]
    rows = quarter * DILATION
    row = lax.broadcasted_iota(jnp.int32, (rows, quarter), 0)
    taken = lax.broadcasted_iota(jnp.int32, (rows, quarter), 1) * DILATION
    place = jnp.where(row == taken + head % DILATION, 1.0, 0.0).astype(BF16)
    return dot(place, jnp.concatenate([ref[which * slots + slot] for which in range(4)], axis=1))


def send_place(slots, first, ready, outs, sems):
    width = slots * HEAD_DIM
    cols = pl.ds(pl.multiple_of(first * HEAD_DIM, width), width)
    copies = [
        pltpu.make_async_copy(ready.at[which], out.at[:, cols], sems.at[which])
        for which, out in enumerate(outs)
    ]
    for copy in copies:
        copy.start()
    return copies


def final_others_kernel(n_i, slots, *refs):
    sources, near_ref, early_ref, refs = refs[:4], refs[4], refs[5], refs[6:]
    mids, refs = refs[: n_i - 1], refs[n_i - 1 :]
    outs, (ready, sems, stats_ref, spread) = refs[:4], refs[4:]
    last = n_i - 1
    near_statistics(n_i, slots, [last], near_ref, mids[-1:], (), stats_ref, spread)
    late = near_place(n_i, slots, last, sources, stats_ref)
    copies = []
    for step in range(1, n_i):
        first = first_back(n_i, slots, step)
        found = [spread_rows(slots, first + slot, slot, mids[step - 1]) for slot in range(slots)]
        for slot, parts in enumerate(found):
            for which in range(4):
                near = late[slot][which] if step == last else early_ref[which, step * slots + slot]
                total = near + parts[:, static_columns(which)]
                ready[step - 1, which, :, static_columns(slot)] = total.astype(BF16)
        copies += send_place(slots, first, ready.at[step - 1], outs, sems.at[step - 1])
    for copy in copies:
        copy.wait()


def final_own_kernel(slots, early_ref, mid_ref, *refs):
    fulls, refs = in_back(refs[:slots]), refs[slots:]
    outs, (ready, sems) = refs[4:8], refs[8:]
    pos, chip = position(slots)
    first = pos * slots
    found = [spread_rows(slots, first + (chip ^ m), chip ^ m, mid_ref) for m in range(slots)]
    for m, parts in enumerate(found):
        slot = chip ^ m
        for which in range(4):
            total = early_ref[which, slot] + parts[:, static_columns(which)]
            total += fulls[m][which].astype(F32)
            ready[which, :, head_columns(slot)] = total.astype(BF16)
    for copy in send_place(slots, first, ready, outs, sems):
        copy.wait()


def settle_kernel(*refs):
    refs[-1][...] = jnp.zeros_like(refs[-1])


def call(kernel, name, outs, scratch, flops, operands, hbm_in=(), hbm_out=False, cheap=False, limit=VMEM_LIMIT, aliases=None):
    moved = sum(x.size * x.dtype.itemsize for x in tuple(operands) + tuple(outs))
    if cheap:
        flops, moved = 1, 1
    spaces = [pltpu.HBM if i in hbm_in else pltpu.VMEM for i in range(len(operands))]
    return pl.pallas_call(
        kernel,
        out_shape=tuple(outs),
        in_specs=[pl.BlockSpec(memory_space=space) for space in spaces],
        out_specs=tuple(
            pl.BlockSpec(memory_space=pltpu.HBM if hbm_out else pltpu.VMEM) for _ in outs
        ),
        scratch_shapes=scratch,
        input_output_aliases=aliases or {},
        compiler_params=pltpu.CompilerParams(vmem_limit_bytes=limit),
        cost_estimate=pl.CostEstimate(flops=flops, bytes_accessed=moved, transcendentals=0),
        name=name,
    )(*operands)


def in_back(pieces):
    return [pieces[0], *pieces[:0:-1]]


def swap(x, axis, n, mask):
    return lax.ppermute(x, axis, [(i, i ^ mask) for i in range(n)])


def local(query_rows, key_rows, value_rows, upstream):
    rows, features = query_rows.shape
    n_i, n_o = lax.axis_size("seqi"), lax.axis_size("seqo")
    slots = HEADS // n_i
    width = n_o // slots
    others = (width - 1) * slots
    quarter = rows // DILATION
    sources = (key_rows, value_rows, query_rows, upstream)
    unit = 2 * rows * rows * HEAD_DIM
    bind = functools.partial

    mid = SHAPE((4 * slots + 1, quarter, HEAD_DIM), BF16)
    full = SHAPE((4, rows, HEAD_DIM), BF16)
    half = SHAPE((slots, 2, rows, HEAD_DIM), BF16)
    square = pltpu.VMEM((LANES, rows), F32)

    def stats(count, lanes=rows):
        return SHAPE((count, lanes), F32)

    def swap_mids(pieces):
        return [pieces[0]] + [
            swap(pieces[step], "seqi", n_i, distance(n_i, step)) for step in range(1, n_i)
        ]

    def swap_back(pieces):
        return [pieces[0]] + [
            swap(pieces[step], "seqi", n_i, distance_back(n_i, step)) for step in range(1, n_i)
        ]

    def swap_fulls(pieces):
        return [pieces[0]] + [swap(pieces[m], "seqo", n_o, m * width) for m in range(1, slots)]

    def pick_scratch(count):
        return [
            pltpu.VMEM((count, 4, rows, slots * HEAD_DIM), BF16),
            pltpu.SemaphoreType.DMA((count, 4)),
            pltpu.VMEM((count, 4, slots, rows, HEAD_DIM), F32),
            square,
        ]

    first, firststats = call(
        bind(pick_first_kernel, n_i, slots),
        "pick_first",
        [mid, stats(2 * HEADS)],
        pick_scratch(1),
        unit * slots * 2,
        sources,
        hbm_in=range(4),
        limit=FIRST_LIMIT,
    )
    pieces = call(
        bind(pick_rest_kernel, n_i, slots),
        "pick_rest",
        [mid] * (n_i - 1) + [full] * slots + [stats(2 * HEADS)],
        pick_scratch(n_i - 1),
        unit * HEADS * 2,
        [*sources, firststats],
        hbm_in=range(4),
        limit=PICK_LIMIT,
    )
    mids = swap_mids([pieces[0], first, *pieces[1 : n_i - 1]])
    fulls = swap_fulls(pieces[n_i - 1 : n_i - 1 + slots])
    near = pieces[-1]

    (settled,) = call(settle_kernel, "far_in", [stats(8)], [], SHORT, [mids[1]])
    (settled,) = call(settle_kernel, "chips_back", [stats(8)], [], LONG, [settled])
    (packed,) = call(bind(pack_kernel, slots), "pack", [half], [], 1, [*in_back(fulls), settled])
    sibs = [swap(packed, "seqo", n_o, part) for part in range(1, width)]
    (settled,) = call(settle_kernel, "packed_back", [stats(8)], [], LONG, [near])
    (far,) = call(
        bind(far_stats_kernel, slots),
        "far_stats",
        [stats(2 * slots)],
        [],
        1,
        [*in_back(fulls), *sibs, settled],
    )
    xmsg, middle, columns = call(
        bind(middle_stats_kernel, n_i, slots),
        "middle_stats",
        [stats(4 * slots), stats(2 * slots, n_i * quarter), stats(n_i * quarter, LANES)],
        [pltpu.VMEM((LANES, n_i * quarter), F32), square],
        unit * slots * 2,
        mids + [near, far],
    )
    xmsgs = swap_fulls([xmsg] * slots)

    midparts = call(
        bind(middle_parts_kernel, n_i, slots),
        "middle_parts",
        [mid] * n_i,
        [pltpu.VMEM((2 * slots, rows), F32), pltpu.VMEM((LANES, n_i * quarter), F32), square],
        unit * slots * 6,
        mids + [middle, columns] + xmsgs,
    )
    midparts = swap_back(midparts)
    farparts = call(
        bind(far_parts_kernel, slots, width),
        "far_parts",
        [full] * slots + [half] * (width - 1),
        [pltpu.VMEM((n_o * rows, slots * rows), BF16)] * 2,
        unit * n_o * slots * 6,
        [*in_back(fulls), *sibs, *xmsgs, midparts[0]],
        cheap=True,
    )
    sibparts = [swap(x, "seqo", n_o, part + 1) for part, x in enumerate(farparts[slots:])]
    (settled,) = call(settle_kernel, "far_back", [stats(8)], [], SHORT, [midparts[1]])
    (settled,) = call(settle_kernel, "sib_back", [stats(8)], [], 1, sibparts + [settled])
    (settled,) = call(settle_kernel, "settle", [stats(8)], [], LONG, [settled])
    fullparts = call(
        bind(far_sum_kernel, slots),
        "far_sum",
        [full] * slots,
        [],
        unit,
        list(farparts[:slots]) + sibparts + [settled],
        cheap=True,
    )
    fullparts = swap_fulls(fullparts)

    back = midparts
    kept = [pltpu.VMEM((2 * HEADS, rows), F32), square]
    (early,) = call(
        bind(near_early_kernel, n_i, slots),
        "near_early",
        [SHAPE((4, (n_i - 1) * slots, rows, HEAD_DIM), F32)],
        kept,
        SHORT,
        [*sources, near, *back[:-1], *xmsgs],
    )
    whole = [SHAPE((rows, features), BF16)] * 4
    outs = call(
        bind(final_others_kernel, n_i, slots),
        "final_others",
        whole,
        [
            pltpu.VMEM((n_i - 1, 4, rows, slots * HEAD_DIM), BF16),
            pltpu.SemaphoreType.DMA((n_i - 1, 4)),
            *kept,
        ],
        SHORT // 2,
        [*sources, near, early, *back[1:]],
        hbm_out=True,
    )
    return call(
        bind(final_own_kernel, slots),
        "final_own",
        whole,
        [pltpu.VMEM((4, rows, slots * HEAD_DIM), BF16), pltpu.SemaphoreType.DMA((4,))],
        unit * slots,
        [early, midparts[0], *in_back(fullparts), *outs],
        hbm_in=range(2 + slots, 6 + slots),
        hbm_out=True,
        aliases={2 + slots + which: which for which in range(4)},
    )


def solution(mesh):
    rows = P(("seqo", "seqi"), None)
    return jax.shard_map(
        local,
        mesh=mesh,
        in_specs=(rows,) * 4,
        out_specs=(rows,) * 4,
        check_vma=False,
    )
```

```python
import functools

import jax
import jax.numpy as jnp
from jax import lax
from jax.experimental import pallas as pl
from jax.experimental.pallas import tpu as pltpu
from jax.sharding import PartitionSpec as P

HEADS = 16
HEAD_DIM = 128
DILATION = 4
LANES = 128
SCALE = HEAD_DIM**-0.5
LOWEST = -1e30
LONG = 4 * 10**10
SHORT = 2 * 10**9
VMEM_LIMIT = 32 * 1024 * 1024
PICK_LIMIT = 54784 * 1024
FIRST_LIMIT = 54272 * 1024
NEAR_LIMIT = 54784 * 1024
F32, BF16 = jnp.float32, jnp.bfloat16
SHAPE = jax.ShapeDtypeStruct

NT = (((1,), (1,)), ((), ()))
TN = (((0,), (0,)), ((), ()))


def dot(a, b):
    return jnp.dot(a, b, preferred_element_type=F32)


def dot_nt(a, b):
    return lax.dot_general(a, b, NT, preferred_element_type=F32)


def dot_tn(a, b):
    return lax.dot_general(a, b, TN, preferred_element_type=F32)


def head_columns(head):
    return pl.ds(pl.multiple_of(head * HEAD_DIM, HEAD_DIM), HEAD_DIM)


def static_columns(index):
    return slice(index * HEAD_DIM, (index + 1) * HEAD_DIM)


def position(slots):
    width = lax.axis_size("seqo") // slots
    return lax.axis_index("seqi"), lax.axis_index("seqo") // width


def distance(n_i, step):
    return n_i - step


def distance_back(n_i, step):
    return n_i - 1 if step == 1 else step - 1


def place_in(n_i, slots, step):
    pos, _ = position(slots)
    return pos if step == 0 else pos ^ distance(n_i, step)


def first_back(n_i, slots, step):
    pos, _ = position(slots)
    return (pos if step == 0 else pos ^ distance_back(n_i, step)) * slots


def in_back_order(n_i, chunks):
    order = [distance(n_i, step) for step in range(1, n_i)]
    return [chunks[0]] + [
        chunks[order.index(distance_back(n_i, step)) + 1] for step in range(1, n_i)
    ]


def lanes_of(rows):
    return lax.broadcasted_iota(jnp.int32, (rows, LANES), 1)


def level_stats(operands):
    products = [(dot_nt(k, q) * SCALE, dot_nt(v, u)) for k, v, q, u in operands]
    tops = [jnp.max(s, axis=0, keepdims=True) for s, _ in products]
    weights = [jnp.exp(s - top) for (s, _), top in zip(products, tops)]
    totals = [jnp.sum(p, axis=0, keepdims=True) for p in weights]
    return [
        (top + jnp.log(total), jnp.sum(p * dp, axis=0, keepdims=True) / total)
        for (_, dp), top, p, total in zip(products, tops, weights, totals)
    ]


def merge_stats(ea, da, eb, db):
    top = jnp.maximum(ea, eb)
    wa, wb = jnp.exp(ea - top), jnp.exp(eb - top)
    total = wa + wb
    return top + jnp.log(total), (wa * da + wb * db) / total


def level_weights(operands, stats):
    products = [(dot_nt(k, q) * SCALE, dot_nt(v, u)) for k, v, q, u in operands]
    found = []
    for (s, dp), (lse, delta) in zip(products, stats):
        g = jnp.exp(s - lse)
        found.append((g.astype(BF16), (g * (dp - delta)).astype(BF16)))
    return found


def level_parts(operands, stats):
    found = level_weights(operands, stats)
    keyed = [
        (dot(ds, q) * SCALE, dot(p, u)) for (p, ds), (k, v, q, u) in zip(found, operands)
    ]
    queried = [
        (dot_tn(p, v), dot_tn(ds, k) * SCALE) for (p, ds), (k, v, q, u) in zip(found, operands)
    ]
    return [a + b for a, b in zip(queried, keyed)]


def pick_rows(ref, rows):
    quarter = rows // DILATION
    lane = lanes_of(quarter)
    picked = jnp.zeros((quarter, LANES), F32)
    for residue in range(DILATION):
        part = ref[pl.ds(residue, quarter, stride=DILATION), :]
        picked = jnp.where(lane % DILATION == residue, part, picked)
    return picked


def fetch(slots, places, sources, buffers, sems):
    width = slots * HEAD_DIM
    groups = []
    for index, place in enumerate(places):
        cols = pl.ds(pl.multiple_of(place * width, width), width)
        groups.append(
            [
                pltpu.make_async_copy(
                    source.at[:, cols], buffers.at[index, which], sems.at[index, which]
                )
                for which, source in enumerate(sources)
            ]
        )
        for copy in groups[-1]:
            copy.start()
    return groups


def split(x):
    high = x.astype(BF16).astype(F32)
    rest = x - high
    middle = rest.astype(BF16).astype(F32)
    low = rest - middle
    return (high + pltpu.roll(middle, 2 * HEADS, 1) + pltpu.roll(low, 4 * HEADS, 1)).astype(BF16)


def join(ref):
    x = ref[ref.shape[0] - 1].astype(F32)
    x = x + (pltpu.roll(x, LANES - 2 * HEADS, 1) + pltpu.roll(x, LANES - 4 * HEADS, 1))
    return jnp.where(lanes_of(x.shape[0]) < 2 * HEADS, x, 0.0)


def pick_places(n_i, slots, steps, sources, mids, buffers, sems, wide, turn):
    rows = sources[0].shape[0]
    quarter = rows // DILATION
    places = [place_in(n_i, slots, step) for step in steps]
    for index, copies in enumerate(fetch(slots, places, sources, buffers, sems)):
        first = places[index] * slots
        for which, copy in enumerate(copies):
            copy.wait()
            for slot in range(slots):
                wide[index, which, slot] = buffers[index, which, :, static_columns(slot)].astype(F32)
                residue = (first + slot) % DILATION if slots % DILATION else slot % DILATION
                rowset = wide[index, which, slot, pl.ds(residue, quarter, stride=DILATION), :]
                mids[index][which * slots + slot] = rowset.astype(BF16)
        operands = [
            [buffers[index, which, :, static_columns(slot)] for which in range(4)]
            for slot in range(slots)
        ]
        for slot, (e, d) in enumerate(level_stats(operands)):
            turn[pl.ds(first + slot, 1), :] = e
            turn[pl.ds(HEADS + first + slot, 1), :] = d


def pick_first_kernel(n_i, slots, *refs):
    sources, (mid_ref, own_ref, *refs) = refs[:4], refs[4:]
    fulls, (stats_ref, buffers, sems, wide, turn) = refs[:slots], refs[slots:]
    rows = sources[0].shape[0]
    _, chip = position(slots)
    turn[...] = jnp.zeros_like(turn)
    pick_places(n_i, slots, [1, 0], sources, [mid_ref, own_ref], buffers, sems, wide, turn)
    for m in range(slots):
        fulls[m][...] = buffers[1, :, :, head_columns(chip ^ m)]
    stats_ref[...] = turn[: 2 * HEADS, :]
    turn[...] = turn[...].T
    near = split(pick_rows(turn, rows))
    mid_ref[4 * slots] = near
    own_ref[4 * slots] = near


def pick_rest_kernel(n_i, slots, *refs):
    sources, first_ref, refs = refs[:4], refs[4], refs[5:]
    mids, refs = refs[: n_i - 2], refs[n_i - 2 :]
    stats_ref, buffers, sems, wide, turn = refs
    rows = sources[0].shape[0]
    turn[...] = jnp.zeros_like(turn)
    turn[: 2 * HEADS, :] = first_ref[...]
    pick_places(n_i, slots, range(2, n_i), sources, mids, buffers, sems, wide, turn)
    stats_ref[...] = turn[: 2 * HEADS, :]
    turn[...] = turn[...].T
    near = split(pick_rows(turn, rows))
    for ref in mids:
        ref[4 * slots] = near


def pack_kernel(slots, *refs):
    packed_ref = refs[-1]
    for m, ref in enumerate(in_back(refs[:slots])):
        packed_ref[m] = ref[:2]


def far_keys(fulls, sibs, which):
    blocks = [ref[which] for ref in fulls]
    return jnp.concatenate(blocks + [ref[m, which] for ref in sibs for m in range(len(fulls))], axis=0)


def far_stats_kernel(slots, *refs):
    fulls, sibs, stats_ref = in_back(refs[:slots]), refs[slots:-2], refs[-1]
    keys, values = far_keys(fulls, sibs, 0), far_keys(fulls, sibs, 1)
    for m in range(slots):
        ((e, d),) = level_stats([(keys, values, fulls[m][2], fulls[m][3])])
        stats_ref[m : m + 1, :] = e
        stats_ref[slots + m : slots + m + 1, :] = d


def middle_operands(slots, mids, slot):
    return [
        jnp.concatenate([ref[which * slots + slot] for ref in mids], axis=0) for which in range(4)
    ]


def middle_stats_kernel(n_i, slots, *refs):
    mids, refs = refs[:n_i], refs[n_i:]
    near_ref, far_ref, xmsg_ref, stats_ref, columns_ref, turn, spread = refs
    rows = near_ref.shape[1]
    quarter = rows // DILATION
    pos, _ = position(slots)
    turn[...] = jnp.zeros_like(turn)
    operands = [middle_operands(slots, mids, slot) for slot in range(slots)]
    for slot, (e, d) in enumerate(level_stats(operands)):
        turn[slot : slot + 1, :] = e
        turn[slots + slot : slots + slot + 1, :] = d
    stats_ref[...] = turn[: 2 * slots, :]
    columns_ref[...] = turn[...].T
    lane = lanes_of(quarter)
    lane_residue = (pos * slots + lane % slots) % DILATION
    blank = jnp.where(lane < slots, LOWEST, 0.0)
    for residue in range(DILATION):
        spread[pl.ds(residue, quarter, stride=DILATION), :] = jnp.where(
            lane_residue == residue, columns_ref[:quarter], blank
        )
    across = spread[...].T
    e, d = merge_stats(
        near_ref[pl.ds(pos * slots, slots), :],
        near_ref[pl.ds(HEADS + pos * slots, slots), :],
        across[:slots],
        across[slots : 2 * slots],
    )
    xmsg_ref[:slots] = e
    xmsg_ref[slots : 2 * slots] = d
    xmsg_ref[2 * slots :] = far_ref[...]


def middle_parts_kernel(n_i, slots, *refs):
    mids, refs = refs[:n_i], refs[n_i:]
    stats_ref, columns_ref = refs[:2]
    refs = refs[2:]
    xmsgs, refs = refs[:slots], refs[slots:]
    outs, (far, turn, spread) = refs[:n_i], refs[n_i:]
    rows = xmsgs[0].shape[1]
    quarter = rows // DILATION
    pos, chip = position(slots)
    for m in range(slots):
        far[pl.ds(chip ^ m, 1), :] = xmsgs[m][2 * slots + m : 2 * slots + m + 1, :]
        far[pl.ds(slots + (chip ^ m), 1), :] = xmsgs[m][3 * slots + m : 3 * slots + m + 1, :]
    e, d = merge_stats(
        xmsgs[0][:slots], xmsgs[0][slots : 2 * slots], far[:slots], far[slots:]
    )
    spread[...] = jnp.zeros_like(spread)
    spread[pl.ds(pos * slots, slots), :] = e
    spread[pl.ds(HEADS + pos * slots, slots), :] = d
    spread[...] = spread[...].T
    own = pick_rows(spread, rows)
    turn[...] = jnp.concatenate([own] + [join(ref) for ref in mids[1:]], axis=0).T
    owned = lax.broadcasted_iota(jnp.int32, (1, n_i * quarter), 1) < quarter
    operands = [middle_operands(slots, mids, slot) for slot in range(slots)]
    merged = [
        merge_stats(
            turn[pl.ds(pos * slots + slot, 1), :],
            turn[pl.ds(HEADS + pos * slots + slot, 1), :],
            jnp.where(owned, LOWEST, stats_ref[slot : slot + 1, :]),
            stats_ref[slots + slot : slots + slot + 1, :],
        )
        for slot in range(slots)
    ]
    for slot, parts in enumerate(level_parts(operands, merged)):
        for which, part in enumerate(parts):
            part = part.astype(BF16)
            chunks = [part[d * quarter : (d + 1) * quarter] for d in range(n_i)]
            for out, chunk in zip(outs, in_back_order(n_i, chunks)):
                out[which * slots + slot] = chunk
    chunks = [columns_ref[d * quarter : (d + 1) * quarter] for d in range(n_i)]
    for out, chunk in zip(outs, in_back_order(n_i, chunks)):
        out[4 * slots] = split(chunk)


def far_parts_kernel(slots, width, *refs):
    fulls, refs = in_back(refs[:slots]), refs[slots:]
    sibs, refs = refs[: width - 1], refs[width - 1 :]
    xmsgs, refs = refs[:slots], refs[slots + 1 :]
    outs, refs = refs[:slots], refs[slots:]
    kvouts, refs = refs[: width - 1], refs[width - 1 :]
    weights, score_grads = refs
    rows = fulls[0].shape[1]
    _, chip = position(slots)
    keys, values = far_keys(fulls, sibs, 0), far_keys(fulls, sibs, 1)
    for m in range(slots):
        lse, delta = merge_stats(
            xmsgs[m][pl.ds(chip, 1), :],
            xmsgs[m][pl.ds(slots + chip, 1), :],
            xmsgs[0][2 * slots + m : 2 * slots + m + 1, :],
            xmsgs[0][3 * slots + m : 3 * slots + m + 1, :],
        )
        operands = (keys, values, fulls[m][2], fulls[m][3])
        ((p, ds),) = level_weights([operands], [(lse, delta)])
        outs[m][0] = dot_tn(p, values).astype(BF16)
        outs[m][1] = (dot_tn(ds, keys) * SCALE).astype(BF16)
        weights[:, m * rows : (m + 1) * rows] = p
        score_grads[:, m * rows : (m + 1) * rows] = ds
    queries = jnp.concatenate([ref[2] for ref in fulls], axis=0)
    ups = jnp.concatenate([ref[3] for ref in fulls], axis=0)
    key_part = (dot(score_grads[...], queries) * SCALE).astype(BF16)
    value_part = dot(weights[...], ups).astype(BF16)
    for index in range(width * slots):
        block = slice(index * rows, (index + 1) * rows)
        part, m = index // slots, index % slots
        if part == 0:
            outs[m][2], outs[m][3] = key_part[block], value_part[block]
        else:
            kvouts[part - 1][m, 0], kvouts[part - 1][m, 1] = key_part[block], value_part[block]


def far_sum_kernel(slots, *refs):
    own, refs = refs[:slots], refs[slots:]
    found, outs = refs[: -slots - 1], refs[-slots:]
    for m in range(slots):
        outs[m][:2] = own[m][:2]
        total = own[m][2:].astype(F32)
        for ref in found:
            total += ref[m].astype(F32)
        outs[m][2:] = total.astype(BF16)


def near_statistics(n_i, slots, steps, near_ref, mids, xmsgs, stats_ref, spread):
    rows = near_ref.shape[1]
    quarter = rows // DILATION
    pos, chip = position(slots)
    lane = lanes_of(quarter)
    mid = jnp.zeros((quarter, LANES), F32)
    for step, ref in zip(steps, mids):
        place = first_back(n_i, slots, step)
        found = join(ref)
        e = pltpu.roll(found, place, 1)
        de = pltpu.roll(found, place + HEADS - slots, 1)
        mid = jnp.where((lane >= place) & (lane < place + slots), e, mid)
        mid = jnp.where((lane >= HEADS + place) & (lane < HEADS + place + slots), de, mid)
    blank = jnp.where(lane < HEADS, LOWEST, 0.0)
    for residue in range(DILATION):
        spread[pl.ds(residue, quarter, stride=DILATION), :] = jnp.where(
            lane % DILATION == residue, mid, blank
        )
    across = spread[...].T
    e, d = merge_stats(
        near_ref[:HEADS], near_ref[HEADS:], across[:HEADS], across[HEADS : 2 * HEADS]
    )
    if xmsgs:
        stats_ref[:HEADS] = jnp.full((HEADS, rows), LOWEST, F32)
        stats_ref[HEADS:] = jnp.zeros((HEADS, rows), F32)
        for m in range(slots):
            head = pos * slots + (chip ^ m)
            stats_ref[pl.ds(head, 1), :] = xmsgs[m][2 * slots + m : 2 * slots + m + 1, :]
            stats_ref[pl.ds(HEADS + head, 1), :] = xmsgs[m][3 * slots + m : 3 * slots + m + 1, :]
        e, d = merge_stats(e, d, stats_ref[:HEADS], stats_ref[HEADS:])
    stats_ref[:HEADS] = e
    stats_ref[HEADS:] = d


def near_place(n_i, slots, step, sources, stats_ref):
    heads = [first_back(n_i, slots, step) + slot for slot in range(slots)]
    operands = [[ref[:, head_columns(head)] for ref in sources] for head in heads]
    stats = [(stats_ref[pl.ds(head, 1), :], stats_ref[pl.ds(HEADS + head, 1), :]) for head in heads]
    return level_parts(operands, stats)


def near_early_kernel(n_i, slots, *refs):
    sources, near_ref, refs = refs[:4], refs[4], refs[5:]
    mids, refs = refs[: n_i - 1], refs[n_i - 1 :]
    xmsgs, (out_ref, stats_ref, spread) = refs[:slots], refs[slots:]
    near_statistics(n_i, slots, range(n_i - 1), near_ref, mids, xmsgs, stats_ref, spread)
    for step in range(n_i - 1):
        for slot, parts in enumerate(near_place(n_i, slots, step, sources, stats_ref)):
            for which, part in enumerate(parts):
                out_ref[which, step * slots + slot] = part


def far_sum_kernel(slots, *refs):
    own, refs = refs[:slots], refs[slots:]
    found, outs = refs[: -slots - 1], refs[-slots:]
    for m in range(slots):
        outs[m][:2] = own[m][:2]
        total = own[m][2:].astype(F32)
        for ref in found:
            total += ref[m].astype(F32)
        outs[m][2:] = total.astype(BF16)


def near_parts_kernel(n_i, slots, *refs):
    sources, near_ref, refs = refs[:4], refs[4], refs[5:]
    mids, refs = (refs[0], *refs[n_i - 1 : 0 : -1]), refs[n_i:]
    xmsgs, (out_ref, stats_ref, spread) = refs[:slots], refs[slots:]
    rows = near_ref.shape[1]
    quarter = rows // DILATION
    pos, chip = position(slots)
    lane = lanes_of(quarter)
    mid = jnp.zeros((quarter, LANES), F32)
    for d in range(n_i):
        place = (pos ^ d) * slots
        found = join(mids[d])
        e = pltpu.roll(found, place, 1)
        de = pltpu.roll(found, place + HEADS - slots, 1)
        mid = jnp.where((lane >= place) & (lane < place + slots), e, mid)
        mid = jnp.where((lane >= HEADS + place) & (lane < HEADS + place + slots), de, mid)
    blank = jnp.where(lane < HEADS, LOWEST, 0.0)
    for residue in range(DILATION):
        spread[pl.ds(residue, quarter, stride=DILATION), :] = jnp.where(
            lane % DILATION == residue, mid, blank
        )
    across = spread[...].T
    stats_ref[:HEADS] = jnp.full((HEADS, rows), LOWEST, F32)
    stats_ref[HEADS:] = jnp.zeros((HEADS, rows), F32)
    for m in range(slots):
        head = pos * slots + (chip ^ m)
        stats_ref[pl.ds(head, 1), :] = xmsgs[m][2 * slots + m : 2 * slots + m + 1, :]
        stats_ref[pl.ds(HEADS + head, 1), :] = xmsgs[m][3 * slots + m : 3 * slots + m + 1, :]
    e, d = merge_stats(
        near_ref[:HEADS], near_ref[HEADS:], across[:HEADS], across[HEADS : 2 * HEADS]
    )
    e, d = merge_stats(e, d, stats_ref[:HEADS], stats_ref[HEADS:])
    stats_ref[:HEADS] = e
    stats_ref[HEADS:] = d
    for group in range(HEADS // DILATION):
        heads = range(group * DILATION, (group + 1) * DILATION)
        operands = [
            [ref[:, static_columns(head)] for ref in sources] for head in heads
        ]
        stats = [
            (stats_ref[head : head + 1, :], stats_ref[HEADS + head : HEADS + head + 1, :])
            for head in heads
        ]
        for head, parts in zip(heads, level_parts(operands, stats)):
            for which, part in enumerate(parts):
                out_ref[which, head] = part


def spread_rows(slots, head, slot, ref):
    quarter = ref.shape[1]
    rows = quarter * DILATION
    row = lax.broadcasted_iota(jnp.int32, (rows, quarter), 0)
    taken = lax.broadcasted_iota(jnp.int32, (rows, quarter), 1) * DILATION
    place = jnp.where(row == taken + head % DILATION, 1.0, 0.0).astype(BF16)
    return dot(place, jnp.concatenate([ref[which * slots + slot] for which in range(4)], axis=1))


def send_place(slots, first, ready, outs, sems):
    width = slots * HEAD_DIM
    cols = pl.ds(pl.multiple_of(first * HEAD_DIM, width), width)
    copies = [
        pltpu.make_async_copy(ready.at[which], out.at[:, cols], sems.at[which])
        for which, out in enumerate(outs)
    ]
    for copy in copies:
        copy.start()
    return copies


def final_others_kernel(n_i, slots, *refs):
    sources, near_ref, early_ref, refs = refs[:4], refs[4], refs[5], refs[6:]
    mids, refs = refs[: n_i - 1], refs[n_i - 1 :]
    outs, (ready, sems, stats_ref, spread) = refs[:4], refs[4:]
    last = n_i - 1
    near_statistics(n_i, slots, [last], near_ref, mids[-1:], (), stats_ref, spread)
    late = near_place(n_i, slots, last, sources, stats_ref)
    copies = []
    for step in range(1, n_i):
        first = first_back(n_i, slots, step)
        found = [spread_rows(slots, first + slot, slot, mids[step - 1]) for slot in range(slots)]
        for slot, parts in enumerate(found):
            for which in range(4):
                near = late[slot][which] if step == last else early_ref[which, step * slots + slot]
                total = near + parts[:, static_columns(which)]
                ready[step - 1, which, :, static_columns(slot)] = total.astype(BF16)
        copies += send_place(slots, first, ready.at[step - 1], outs, sems.at[step - 1])
    for copy in copies:
        copy.wait()


def final_own_kernel(slots, early_ref, mid_ref, *refs):
    fulls, refs = in_back(refs[:slots]), refs[slots:]
    outs, (ready, sems) = refs[4:8], refs[8:]
    pos, chip = position(slots)
    first = pos * slots
    found = [spread_rows(slots, first + (chip ^ m), chip ^ m, mid_ref) for m in range(slots)]
    for m, parts in enumerate(found):
        slot = chip ^ m
        for which in range(4):
            total = early_ref[which, slot] + parts[:, static_columns(which)]
            total += fulls[m][which].astype(F32)
            ready[which, :, head_columns(slot)] = total.astype(BF16)
    for copy in send_place(slots, first, ready, outs, sems):
        copy.wait()


def settle_kernel(*refs):
    refs[-1][...] = jnp.zeros_like(refs[-1])


def call(kernel, name, outs, scratch, flops, operands, hbm_in=(), hbm_out=False, cheap=False, limit=VMEM_LIMIT, aliases=None):
    moved = sum(x.size * x.dtype.itemsize for x in tuple(operands) + tuple(outs))
    if cheap:
        flops, moved = 1, 1
    spaces = [pltpu.HBM if i in hbm_in else pltpu.VMEM for i in range(len(operands))]
    return pl.pallas_call(
        kernel,
        out_shape=tuple(outs),
        in_specs=[pl.BlockSpec(memory_space=space) for space in spaces],
        out_specs=tuple(
            pl.BlockSpec(memory_space=pltpu.HBM if hbm_out else pltpu.VMEM) for _ in outs
        ),
        scratch_shapes=scratch,
        input_output_aliases=aliases or {},
        compiler_params=pltpu.CompilerParams(vmem_limit_bytes=limit),
        cost_estimate=pl.CostEstimate(flops=flops, bytes_accessed=moved, transcendentals=0),
        name=name,
    )(*operands)


def in_back(pieces):
    return [pieces[0], *pieces[:0:-1]]


def swap(x, axis, n, mask):
    return lax.ppermute(x, axis, [(i, i ^ mask) for i in range(n)])


def local(query_rows, key_rows, value_rows, upstream):
    rows, features = query_rows.shape
    n_i, n_o = lax.axis_size("seqi"), lax.axis_size("seqo")
    slots = HEADS // n_i
    width = n_o // slots
    others = (width - 1) * slots
    quarter = rows // DILATION
    sources = (key_rows, value_rows, query_rows, upstream)
    unit = 2 * rows * rows * HEAD_DIM
    bind = functools.partial

    mid = SHAPE((4 * slots + 1, quarter, HEAD_DIM), BF16)
    full = SHAPE((4, rows, HEAD_DIM), BF16)
    half = SHAPE((slots, 2, rows, HEAD_DIM), BF16)
    square = pltpu.VMEM((LANES, rows), F32)

    def stats(count, lanes=rows):
        return SHAPE((count, lanes), F32)

    def swap_mids(pieces):
        return [pieces[0]] + [
            swap(pieces[step], "seqi", n_i, distance(n_i, step)) for step in range(1, n_i)
        ]

    def swap_back(pieces):
        return [pieces[0]] + [
            swap(pieces[step], "seqi", n_i, distance_back(n_i, step)) for step in range(1, n_i)
        ]

    def swap_fulls(pieces):
        return [pieces[0]] + [swap(pieces[m], "seqo", n_o, m * width) for m in range(1, slots)]

    def pick_scratch(count):
        return [
            pltpu.VMEM((count, 4, rows, slots * HEAD_DIM), BF16),
            pltpu.SemaphoreType.DMA((count, 4)),
            pltpu.VMEM((count, 4, slots, rows, HEAD_DIM), F32),
            square,
        ]

    first, own, *fulls, firststats = call(
        bind(pick_first_kernel, n_i, slots),
        "pick_first",
        [mid, mid] + [full] * slots + [stats(2 * HEADS)],
        pick_scratch(2),
        unit * slots * 4,
        sources,
        hbm_in=range(4),
        limit=FIRST_LIMIT,
    )
    *pieces, near = call(
        bind(pick_rest_kernel, n_i, slots),
        "pick_rest",
        [mid] * (n_i - 2) + [stats(2 * HEADS)],
        pick_scratch(n_i - 2),
        unit * HEADS * 2,
        [*sources, firststats],
        hbm_in=range(4),
        limit=PICK_LIMIT,
    )
    mids = swap_mids([own, first, *pieces])
    fulls = swap_fulls(fulls)

    (settled,) = call(settle_kernel, "far_in", [stats(8)], [], SHORT, [mids[1]])
    (settled,) = call(settle_kernel, "chips_back", [stats(8)], [], LONG, [settled])
    (packed,) = call(bind(pack_kernel, slots), "pack", [half], [], 1, [*in_back(fulls), settled])
    sibs = [swap(packed, "seqo", n_o, part) for part in range(1, width)]
    (settled,) = call(settle_kernel, "packed_back", [stats(8)], [], LONG, [near])
    (far,) = call(
        bind(far_stats_kernel, slots),
        "far_stats",
        [stats(2 * slots)],
        [],
        1,
        [*in_back(fulls), *sibs, settled],
    )
    xmsg, middle, columns = call(
        bind(middle_stats_kernel, n_i, slots),
        "middle_stats",
        [stats(4 * slots), stats(2 * slots, n_i * quarter), stats(n_i * quarter, LANES)],
        [pltpu.VMEM((LANES, n_i * quarter), F32), square],
        unit * slots * 2,
        mids + [near, far],
    )
    xmsgs = swap_fulls([xmsg] * slots)

    midparts = call(
        bind(middle_parts_kernel, n_i, slots),
        "middle_parts",
        [mid] * n_i,
        [pltpu.VMEM((2 * slots, rows), F32), pltpu.VMEM((LANES, n_i * quarter), F32), square],
        unit * slots * 6,
        mids + [middle, columns] + xmsgs,
    )
    midparts = swap_back(midparts)
    farparts = call(
        bind(far_parts_kernel, slots, width),
        "far_parts",
        [full] * slots + [half] * (width - 1),
        [pltpu.VMEM((n_o * rows, slots * rows), BF16)] * 2,
        unit * n_o * slots * 6,
        [*in_back(fulls), *sibs, *xmsgs, midparts[0]],
        cheap=True,
    )
    sibparts = [swap(x, "seqo", n_o, part + 1) for part, x in enumerate(farparts[slots:])]
    (settled,) = call(settle_kernel, "far_back", [stats(8)], [], SHORT, [midparts[1]])
    (settled,) = call(settle_kernel, "sib_back", [stats(8)], [], 1, sibparts + [settled])
    (settled,) = call(settle_kernel, "settle", [stats(8)], [], LONG, [settled])
    fullparts = call(
        bind(far_sum_kernel, slots),
        "far_sum",
        [full] * slots,
        [],
        unit,
        list(farparts[:slots]) + sibparts + [settled],
        cheap=True,
    )
    fullparts = swap_fulls(fullparts)

    back = midparts
    kept = [pltpu.VMEM((2 * HEADS, rows), F32), square]
    (early,) = call(
        bind(near_early_kernel, n_i, slots),
        "near_early",
        [SHAPE((4, (n_i - 1) * slots, rows, HEAD_DIM), F32)],
        kept,
        SHORT,
        [*sources, near, *back[:-1], *xmsgs],
    )
    whole = [SHAPE((rows, features), BF16)] * 4
    outs = call(
        bind(final_others_kernel, n_i, slots),
        "final_others",
        whole,
        [
            pltpu.VMEM((n_i - 1, 4, rows, slots * HEAD_DIM), BF16),
            pltpu.SemaphoreType.DMA((n_i - 1, 4)),
            *kept,
        ],
        SHORT // 2,
        [*sources, near, early, *back[1:]],
        hbm_out=True,
    )
    return call(
        bind(final_own_kernel, slots),
        "final_own",
        whole,
        [pltpu.VMEM((4, rows, slots * HEAD_DIM), BF16), pltpu.SemaphoreType.DMA((4,))],
        unit * slots,
        [early, midparts[0], *in_back(fullparts), *outs],
        hbm_in=range(2 + slots, 6 + slots),
        hbm_out=True,
        aliases={2 + slots + which: which for which in range(4)},
    )


def solution(mesh):
    rows = P(("seqo", "seqi"), None)
    return jax.shard_map(
        local,
        mesh=mesh,
        in_specs=(rows,) * 4,
        out_specs=(rows,) * 4,
        check_vma=False,
    )
```

```python
import functools

import jax
import jax.numpy as jnp
from jax import lax
from jax.experimental import pallas as pl
from jax.experimental.pallas import tpu as pltpu
from jax.sharding import PartitionSpec as P

HEADS = 16
HEAD_DIM = 128
DILATION = 4
LANES = 128
SCALE = HEAD_DIM**-0.5
LOWEST = -1e30
LONG = 4 * 10**10
SHORT = 2 * 10**9
VMEM_LIMIT = 32 * 1024 * 1024
PICK_LIMIT = 54784 * 1024
FIRST_LIMIT = 54272 * 1024
NEAR_LIMIT = 54784 * 1024
F32, BF16 = jnp.float32, jnp.bfloat16
SHAPE = jax.ShapeDtypeStruct

NT = (((1,), (1,)), ((), ()))
TN = (((0,), (0,)), ((), ()))


def dot(a, b):
    return jnp.dot(a, b, preferred_element_type=F32)


def dot_nt(a, b):
    return lax.dot_general(a, b, NT, preferred_element_type=F32)


def dot_tn(a, b):
    return lax.dot_general(a, b, TN, preferred_element_type=F32)


def head_columns(head):
    return pl.ds(pl.multiple_of(head * HEAD_DIM, HEAD_DIM), HEAD_DIM)


def static_columns(index):
    return slice(index * HEAD_DIM, (index + 1) * HEAD_DIM)


def position(slots):
    width = lax.axis_size("seqo") // slots
    return lax.axis_index("seqi"), lax.axis_index("seqo") // width


def distance(n_i, step, odd):
    if odd and step > 1:
        return step - 1
    return n_i - step


def distance_back(n_i, step):
    return n_i - 1 if step == 1 else step - 1


def is_odd():
    return lax.axis_index("seqo") % 2 == 1


def place_in(n_i, slots, step):
    pos, _ = position(slots)
    if step == 0:
        return pos
    if distance(n_i, step, False) == distance(n_i, step, True):
        return pos ^ distance(n_i, step, False)
    return pos ^ jnp.where(is_odd(), distance(n_i, step, True), distance(n_i, step, False))


def first_back(n_i, slots, step):
    pos, _ = position(slots)
    return (pos if step == 0 else pos ^ distance_back(n_i, step)) * slots


def in_back_order(n_i, chunks):
    found = [chunks[0]]
    for step in range(1, n_i):
        even, odd = [
            [distance(n_i, k, parity) for k in range(1, n_i)].index(distance_back(n_i, step)) + 1
            for parity in (False, True)
        ]
        if even == odd:
            found.append(chunks[even])
        else:
            found.append(jnp.where(is_odd(), chunks[odd], chunks[even]))
    return found


def lanes_of(rows):
    return lax.broadcasted_iota(jnp.int32, (rows, LANES), 1)


def level_stats(operands):
    products = [(dot_nt(k, q) * SCALE, dot_nt(v, u)) for k, v, q, u in operands]
    tops = [jnp.max(s, axis=0, keepdims=True) for s, _ in products]
    weights = [jnp.exp(s - top) for (s, _), top in zip(products, tops)]
    totals = [jnp.sum(p, axis=0, keepdims=True) for p in weights]
    return [
        (top + jnp.log(total), jnp.sum(p * dp, axis=0, keepdims=True) / total)
        for (_, dp), top, p, total in zip(products, tops, weights, totals)
    ]


def merge_stats(ea, da, eb, db):
    top = jnp.maximum(ea, eb)
    wa, wb = jnp.exp(ea - top), jnp.exp(eb - top)
    total = wa + wb
    return top + jnp.log(total), (wa * da + wb * db) / total


def level_weights(operands, stats):
    products = [(dot_nt(k, q) * SCALE, dot_nt(v, u)) for k, v, q, u in operands]
    found = []
    for (s, dp), (lse, delta) in zip(products, stats):
        g = jnp.exp(s - lse)
        found.append((g.astype(BF16), (g * (dp - delta)).astype(BF16)))
    return found


def level_parts(operands, stats):
    found = level_weights(operands, stats)
    keyed = [
        (dot(ds, q) * SCALE, dot(p, u)) for (p, ds), (k, v, q, u) in zip(found, operands)
    ]
    queried = [
        (dot_tn(p, v), dot_tn(ds, k) * SCALE) for (p, ds), (k, v, q, u) in zip(found, operands)
    ]
    return [a + b for a, b in zip(queried, keyed)]


def pick_rows(ref, rows):
    quarter = rows // DILATION
    lane = lanes_of(quarter)
    picked = jnp.zeros((quarter, LANES), F32)
    for residue in range(DILATION):
        part = ref[pl.ds(residue, quarter, stride=DILATION), :]
        picked = jnp.where(lane % DILATION == residue, part, picked)
    return picked


def fetch(slots, places, sources, buffers, sems):
    width = slots * HEAD_DIM
    groups = []
    for index, place in enumerate(places):
        cols = pl.ds(pl.multiple_of(place * width, width), width)
        groups.append(
            [
                pltpu.make_async_copy(
                    source.at[:, cols], buffers.at[index, which], sems.at[index, which]
                )
                for which, source in enumerate(sources)
            ]
        )
        for copy in groups[-1]:
            copy.start()
    return groups


def split(x):
    high = x.astype(BF16).astype(F32)
    rest = x - high
    middle = rest.astype(BF16).astype(F32)
    low = rest - middle
    return (high + pltpu.roll(middle, 2 * HEADS, 1) + pltpu.roll(low, 4 * HEADS, 1)).astype(BF16)


def join(ref):
    x = ref[ref.shape[0] - 1].astype(F32)
    x = x + (pltpu.roll(x, LANES - 2 * HEADS, 1) + pltpu.roll(x, LANES - 4 * HEADS, 1))
    return jnp.where(lanes_of(x.shape[0]) < 2 * HEADS, x, 0.0)


def pick_places(n_i, slots, steps, sources, mids, buffers, sems, wide, turn):
    rows = sources[0].shape[0]
    quarter = rows // DILATION
    places = [place_in(n_i, slots, step) for step in steps]
    for index, copies in enumerate(fetch(slots, places, sources, buffers, sems)):
        first = places[index] * slots
        for which, copy in enumerate(copies):
            copy.wait()
            for slot in range(slots):
                wide[index, which, slot] = buffers[index, which, :, static_columns(slot)].astype(F32)
                residue = (first + slot) % DILATION if slots % DILATION else slot % DILATION
                rowset = wide[index, which, slot, pl.ds(residue, quarter, stride=DILATION), :]
                mids[index][which * slots + slot] = rowset.astype(BF16)
        operands = [
            [buffers[index, which, :, static_columns(slot)] for which in range(4)]
            for slot in range(slots)
        ]
        for slot, (e, d) in enumerate(level_stats(operands)):
            turn[pl.ds(first + slot, 1), :] = e
            turn[pl.ds(HEADS + first + slot, 1), :] = d


def pick_first_kernel(n_i, slots, *refs):
    sources, (mid_ref, own_ref, *refs) = refs[:4], refs[4:]
    fulls, (stats_ref, buffers, sems, wide, turn) = refs[:slots], refs[slots:]
    rows = sources[0].shape[0]
    _, chip = position(slots)
    turn[...] = jnp.zeros_like(turn)
    pick_places(n_i, slots, [1, 0], sources, [mid_ref, own_ref], buffers, sems, wide, turn)
    for m in range(slots):
        fulls[m][...] = buffers[1, :, :, head_columns(chip ^ m)]
    stats_ref[...] = turn[: 2 * HEADS, :]
    turn[...] = turn[...].T
    near = split(pick_rows(turn, rows))
    mid_ref[4 * slots] = near
    own_ref[4 * slots] = near


def pick_rest_kernel(n_i, slots, *refs):
    sources, first_ref, refs = refs[:4], refs[4], refs[5:]
    mids, refs = refs[: n_i - 2], refs[n_i - 2 :]
    stats_ref, buffers, sems, wide, turn = refs
    rows = sources[0].shape[0]
    turn[...] = jnp.zeros_like(turn)
    turn[: 2 * HEADS, :] = first_ref[...]
    pick_places(n_i, slots, range(2, n_i), sources, mids, buffers, sems, wide, turn)
    stats_ref[...] = turn[: 2 * HEADS, :]
    turn[...] = turn[...].T
    near = split(pick_rows(turn, rows))
    for ref in mids:
        ref[4 * slots] = near


def pack_kernel(slots, *refs):
    packed_ref = refs[-1]
    for m, ref in enumerate(in_back(refs[:slots])):
        packed_ref[m] = ref[:2]


def far_keys(fulls, sibs, which):
    blocks = [ref[which] for ref in fulls]
    return jnp.concatenate(blocks + [ref[m, which] for ref in sibs for m in range(len(fulls))], axis=0)


def far_stats_kernel(slots, *refs):
    fulls, sibs, stats_ref = in_back(refs[:slots]), refs[slots:-2], refs[-1]
    keys, values = far_keys(fulls, sibs, 0), far_keys(fulls, sibs, 1)
    for m in range(slots):
        ((e, d),) = level_stats([(keys, values, fulls[m][2], fulls[m][3])])
        stats_ref[m : m + 1, :] = e
        stats_ref[slots + m : slots + m + 1, :] = d


def middle_operands(slots, mids, slot):
    return [
        jnp.concatenate([ref[which * slots + slot] for ref in mids], axis=0) for which in range(4)
    ]


def middle_stats_kernel(n_i, slots, *refs):
    mids, refs = refs[:n_i], refs[n_i:]
    near_ref, far_ref, xmsg_ref, stats_ref, columns_ref, turn, spread = refs
    rows = near_ref.shape[1]
    quarter = rows // DILATION
    pos, _ = position(slots)
    turn[...] = jnp.zeros_like(turn)
    operands = [middle_operands(slots, mids, slot) for slot in range(slots)]
    for slot, (e, d) in enumerate(level_stats(operands)):
        turn[slot : slot + 1, :] = e
        turn[slots + slot : slots + slot + 1, :] = d
    stats_ref[...] = turn[: 2 * slots, :]
    columns_ref[...] = turn[...].T
    lane = lanes_of(quarter)
    lane_residue = (pos * slots + lane % slots) % DILATION
    blank = jnp.where(lane < slots, LOWEST, 0.0)
    for residue in range(DILATION):
        spread[pl.ds(residue, quarter, stride=DILATION), :] = jnp.where(
            lane_residue == residue, columns_ref[:quarter], blank
        )
    across = spread[...].T
    e, d = merge_stats(
        near_ref[pl.ds(pos * slots, slots), :],
        near_ref[pl.ds(HEADS + pos * slots, slots), :],
        across[:slots],
        across[slots : 2 * slots],
    )
    xmsg_ref[:slots] = e
    xmsg_ref[slots : 2 * slots] = d
    xmsg_ref[2 * slots :] = far_ref[...]


def middle_parts_kernel(n_i, slots, *refs):
    mids, refs = refs[:n_i], refs[n_i:]
    stats_ref, columns_ref = refs[:2]
    refs = refs[2:]
    xmsgs, refs = refs[:slots], refs[slots:]
    outs, (far, turn, spread) = refs[:n_i], refs[n_i:]
    rows = xmsgs[0].shape[1]
    quarter = rows // DILATION
    pos, chip = position(slots)
    for m in range(slots):
        far[pl.ds(chip ^ m, 1), :] = xmsgs[m][2 * slots + m : 2 * slots + m + 1, :]
        far[pl.ds(slots + (chip ^ m), 1), :] = xmsgs[m][3 * slots + m : 3 * slots + m + 1, :]
    e, d = merge_stats(
        xmsgs[0][:slots], xmsgs[0][slots : 2 * slots], far[:slots], far[slots:]
    )
    spread[...] = jnp.zeros_like(spread)
    spread[pl.ds(pos * slots, slots), :] = e
    spread[pl.ds(HEADS + pos * slots, slots), :] = d
    spread[...] = spread[...].T
    own = pick_rows(spread, rows)
    turn[...] = jnp.concatenate([own] + [join(ref) for ref in mids[1:]], axis=0).T
    owned = lax.broadcasted_iota(jnp.int32, (1, n_i * quarter), 1) < quarter
    operands = [middle_operands(slots, mids, slot) for slot in range(slots)]
    merged = [
        merge_stats(
            turn[pl.ds(pos * slots + slot, 1), :],
            turn[pl.ds(HEADS + pos * slots + slot, 1), :],
            jnp.where(owned, LOWEST, stats_ref[slot : slot + 1, :]),
            stats_ref[slots + slot : slots + slot + 1, :],
        )
        for slot in range(slots)
    ]
    for slot, parts in enumerate(level_parts(operands, merged)):
        for which, part in enumerate(parts):
            part = part.astype(BF16)
            chunks = [part[d * quarter : (d + 1) * quarter] for d in range(n_i)]
            for out, chunk in zip(outs, in_back_order(n_i, chunks)):
                out[which * slots + slot] = chunk
    chunks = [columns_ref[d * quarter : (d + 1) * quarter] for d in range(n_i)]
    for out, chunk in zip(outs, in_back_order(n_i, chunks)):
        out[4 * slots] = split(chunk)


def far_parts_kernel(slots, width, *refs):
    fulls, refs = in_back(refs[:slots]), refs[slots:]
    sibs, refs = refs[: width - 1], refs[width - 1 :]
    xmsgs, refs = refs[:slots], refs[slots + 1 :]
    outs, refs = refs[:slots], refs[slots:]
    kvouts, refs = refs[: width - 1], refs[width - 1 :]
    weights, score_grads = refs
    rows = fulls[0].shape[1]
    _, chip = position(slots)
    keys, values = far_keys(fulls, sibs, 0), far_keys(fulls, sibs, 1)
    for m in range(slots):
        lse, delta = merge_stats(
            xmsgs[m][pl.ds(chip, 1), :],
            xmsgs[m][pl.ds(slots + chip, 1), :],
            xmsgs[0][2 * slots + m : 2 * slots + m + 1, :],
            xmsgs[0][3 * slots + m : 3 * slots + m + 1, :],
        )
        operands = (keys, values, fulls[m][2], fulls[m][3])
        ((p, ds),) = level_weights([operands], [(lse, delta)])
        outs[m][0] = dot_tn(p, values).astype(BF16)
        outs[m][1] = (dot_tn(ds, keys) * SCALE).astype(BF16)
        weights[:, m * rows : (m + 1) * rows] = p
        score_grads[:, m * rows : (m + 1) * rows] = ds
    queries = jnp.concatenate([ref[2] for ref in fulls], axis=0)
    ups = jnp.concatenate([ref[3] for ref in fulls], axis=0)
    key_part = (dot(score_grads[...], queries) * SCALE).astype(BF16)
    value_part = dot(weights[...], ups).astype(BF16)
    for index in range(width * slots):
        block = slice(index * rows, (index + 1) * rows)
        part, m = index // slots, index % slots
        if part == 0:
            outs[m][2], outs[m][3] = key_part[block], value_part[block]
        else:
            kvouts[part - 1][m, 0], kvouts[part - 1][m, 1] = key_part[block], value_part[block]


def far_sum_kernel(slots, *refs):
    own, refs = refs[:slots], refs[slots:]
    found, outs = refs[: -slots - 1], refs[-slots:]
    for m in range(slots):
        outs[m][:2] = own[m][:2]
        total = own[m][2:].astype(F32)
        for ref in found:
            total += ref[m].astype(F32)
        outs[m][2:] = total.astype(BF16)


def near_statistics(n_i, slots, steps, near_ref, mids, xmsgs, stats_ref, spread):
    rows = near_ref.shape[1]
    quarter = rows // DILATION
    pos, chip = position(slots)
    lane = lanes_of(quarter)
    mid = jnp.zeros((quarter, LANES), F32)
    for step, ref in zip(steps, mids):
        place = first_back(n_i, slots, step)
        found = join(ref)
        e = pltpu.roll(found, place, 1)
        de = pltpu.roll(found, place + HEADS - slots, 1)
        mid = jnp.where((lane >= place) & (lane < place + slots), e, mid)
        mid = jnp.where((lane >= HEADS + place) & (lane < HEADS + place + slots), de, mid)
    blank = jnp.where(lane < HEADS, LOWEST, 0.0)
    for residue in range(DILATION):
        spread[pl.ds(residue, quarter, stride=DILATION), :] = jnp.where(
            lane % DILATION == residue, mid, blank
        )
    across = spread[...].T
    e, d = merge_stats(
        near_ref[:HEADS], near_ref[HEADS:], across[:HEADS], across[HEADS : 2 * HEADS]
    )
    if xmsgs:
        stats_ref[:HEADS] = jnp.full((HEADS, rows), LOWEST, F32)
        stats_ref[HEADS:] = jnp.zeros((HEADS, rows), F32)
        for m in range(slots):
            head = pos * slots + (chip ^ m)
            stats_ref[pl.ds(head, 1), :] = xmsgs[m][2 * slots + m : 2 * slots + m + 1, :]
            stats_ref[pl.ds(HEADS + head, 1), :] = xmsgs[m][3 * slots + m : 3 * slots + m + 1, :]
        e, d = merge_stats(e, d, stats_ref[:HEADS], stats_ref[HEADS:])
    stats_ref[:HEADS] = e
    stats_ref[HEADS:] = d


def near_place(n_i, slots, step, sources, stats_ref):
    heads = [first_back(n_i, slots, step) + slot for slot in range(slots)]
    operands = [[ref[:, head_columns(head)] for ref in sources] for head in heads]
    stats = [(stats_ref[pl.ds(head, 1), :], stats_ref[pl.ds(HEADS + head, 1), :]) for head in heads]
    return level_parts(operands, stats)


def near_early_kernel(n_i, slots, *refs):
    sources, near_ref, refs = refs[:4], refs[4], refs[5:]
    mids, refs = refs[: n_i - 1], refs[n_i - 1 :]
    xmsgs, (out_ref, stats_ref, spread) = refs[:slots], refs[slots:]
    near_statistics(n_i, slots, range(n_i - 1), near_ref, mids, xmsgs, stats_ref, spread)
    for step in range(n_i - 1):
        for slot, parts in enumerate(near_place(n_i, slots, step, sources, stats_ref)):
            for which, part in enumerate(parts):
                out_ref[which, step * slots + slot] = part


def far_sum_kernel(slots, *refs):
    own, refs = refs[:slots], refs[slots:]
    found, outs = refs[: -slots - 1], refs[-slots:]
    for m in range(slots):
        outs[m][:2] = own[m][:2]
        total = own[m][2:].astype(F32)
        for ref in found:
            total += ref[m].astype(F32)
        outs[m][2:] = total.astype(BF16)


def near_parts_kernel(n_i, slots, *refs):
    sources, near_ref, refs = refs[:4], refs[4], refs[5:]
    mids, refs = (refs[0], *refs[n_i - 1 : 0 : -1]), refs[n_i:]
    xmsgs, (out_ref, stats_ref, spread) = refs[:slots], refs[slots:]
    rows = near_ref.shape[1]
    quarter = rows // DILATION
    pos, chip = position(slots)
    lane = lanes_of(quarter)
    mid = jnp.zeros((quarter, LANES), F32)
    for d in range(n_i):
        place = (pos ^ d) * slots
        found = join(mids[d])
        e = pltpu.roll(found, place, 1)
        de = pltpu.roll(found, place + HEADS - slots, 1)
        mid = jnp.where((lane >= place) & (lane < place + slots), e, mid)
        mid = jnp.where((lane >= HEADS + place) & (lane < HEADS + place + slots), de, mid)
    blank = jnp.where(lane < HEADS, LOWEST, 0.0)
    for residue in range(DILATION):
        spread[pl.ds(residue, quarter, stride=DILATION), :] = jnp.where(
            lane % DILATION == residue, mid, blank
        )
    across = spread[...].T
    stats_ref[:HEADS] = jnp.full((HEADS, rows), LOWEST, F32)
    stats_ref[HEADS:] = jnp.zeros((HEADS, rows), F32)
    for m in range(slots):
        head = pos * slots + (chip ^ m)
        stats_ref[pl.ds(head, 1), :] = xmsgs[m][2 * slots + m : 2 * slots + m + 1, :]
        stats_ref[pl.ds(HEADS + head, 1), :] = xmsgs[m][3 * slots + m : 3 * slots + m + 1, :]
    e, d = merge_stats(
        near_ref[:HEADS], near_ref[HEADS:], across[:HEADS], across[HEADS : 2 * HEADS]
    )
    e, d = merge_stats(e, d, stats_ref[:HEADS], stats_ref[HEADS:])
    stats_ref[:HEADS] = e
    stats_ref[HEADS:] = d
    for group in range(HEADS // DILATION):
        heads = range(group * DILATION, (group + 1) * DILATION)
        operands = [
            [ref[:, static_columns(head)] for ref in sources] for head in heads
        ]
        stats = [
            (stats_ref[head : head + 1, :], stats_ref[HEADS + head : HEADS + head + 1, :])
            for head in heads
        ]
        for head, parts in zip(heads, level_parts(operands, stats)):
            for which, part in enumerate(parts):
                out_ref[which, head] = part


def spread_rows(slots, head, slot, ref):
    quarter = ref.shape[1]
    rows = quarter * DILATION
    row = lax.broadcasted_iota(jnp.int32, (rows, quarter), 0)
    taken = lax.broadcasted_iota(jnp.int32, (rows, quarter), 1) * DILATION
    place = jnp.where(row == taken + head % DILATION, 1.0, 0.0).astype(BF16)
    return dot(place, jnp.concatenate([ref[which * slots + slot] for which in range(4)], axis=1))


def send_place(slots, first, ready, outs, sems):
    width = slots * HEAD_DIM
    cols = pl.ds(pl.multiple_of(first * HEAD_DIM, width), width)
    copies = [
        pltpu.make_async_copy(ready.at[which], out.at[:, cols], sems.at[which])
        for which, out in enumerate(outs)
    ]
    for copy in copies:
        copy.start()
    return copies


def final_others_kernel(n_i, slots, *refs):
    sources, near_ref, early_ref, refs = refs[:4], refs[4], refs[5], refs[6:]
    mids, refs = refs[: n_i - 1], refs[n_i - 1 :]
    outs, (ready, sems, stats_ref, spread) = refs[:4], refs[4:]
    last = n_i - 1
    copies = []
    for step in range(1, n_i):
        first = first_back(n_i, slots, step)
        found = [spread_rows(slots, first + slot, slot, mids[step - 1]) for slot in range(slots)]
        if step == last:
            near_statistics(n_i, slots, [last], near_ref, mids[-1:], (), stats_ref, spread)
            late = near_place(n_i, slots, last, sources, stats_ref)
        for slot, parts in enumerate(found):
            for which in range(4):
                near = late[slot][which] if step == last else early_ref[which, step * slots + slot]
                total = near + parts[:, static_columns(which)]
                ready[step - 1, which, :, static_columns(slot)] = total.astype(BF16)
        copies += send_place(slots, first, ready.at[step - 1], outs, sems.at[step - 1])
    for copy in copies:
        copy.wait()


def final_own_kernel(slots, early_ref, mid_ref, *refs):
    fulls, refs = in_back(refs[:slots]), refs[slots:]
    outs, (ready, sems) = refs[4:8], refs[8:]
    pos, chip = position(slots)
    first = pos * slots
    found = [spread_rows(slots, first + (chip ^ m), chip ^ m, mid_ref) for m in range(slots)]
    for m, parts in enumerate(found):
        slot = chip ^ m
        for which in range(4):
            total = early_ref[which, slot] + parts[:, static_columns(which)]
            total += fulls[m][which].astype(F32)
            ready[which, :, head_columns(slot)] = total.astype(BF16)
    for copy in send_place(slots, first, ready, outs, sems):
        copy.wait()


def settle_kernel(*refs):
    refs[-1][...] = jnp.zeros_like(refs[-1])


def call(kernel, name, outs, scratch, flops, operands, hbm_in=(), hbm_out=False, cheap=False, limit=VMEM_LIMIT, aliases=None):
    moved = sum(x.size * x.dtype.itemsize for x in tuple(operands) + tuple(outs))
    if cheap:
        flops, moved = 1, 1
    spaces = [pltpu.HBM if i in hbm_in else pltpu.VMEM for i in range(len(operands))]
    return pl.pallas_call(
        kernel,
        out_shape=tuple(outs),
        in_specs=[pl.BlockSpec(memory_space=space) for space in spaces],
        out_specs=tuple(
            pl.BlockSpec(memory_space=pltpu.HBM if hbm_out else pltpu.VMEM) for _ in outs
        ),
        scratch_shapes=scratch,
        input_output_aliases=aliases or {},
        compiler_params=pltpu.CompilerParams(vmem_limit_bytes=limit),
        cost_estimate=pl.CostEstimate(flops=flops, bytes_accessed=moved, transcendentals=0),
        name=name,
    )(*operands)


def in_back(pieces):
    return [pieces[0], *pieces[:0:-1]]


def swap(x, axis, n, mask):
    return lax.ppermute(x, axis, [(i, i ^ mask) for i in range(n)])


def local(query_rows, key_rows, value_rows, upstream):
    rows, features = query_rows.shape
    n_i, n_o = lax.axis_size("seqi"), lax.axis_size("seqo")
    slots = HEADS // n_i
    width = n_o // slots
    others = (width - 1) * slots
    quarter = rows // DILATION
    sources = (key_rows, value_rows, query_rows, upstream)
    unit = 2 * rows * rows * HEAD_DIM
    bind = functools.partial

    mid = SHAPE((4 * slots + 1, quarter, HEAD_DIM), BF16)
    full = SHAPE((4, rows, HEAD_DIM), BF16)
    half = SHAPE((slots, 2, rows, HEAD_DIM), BF16)
    square = pltpu.VMEM((LANES, rows), F32)

    def stats(count, lanes=rows):
        return SHAPE((count, lanes), F32)

    def swap_mids(pieces):
        found = [pieces[0]]
        for step in range(1, n_i):
            pairs = [
                (o * n_i + i, o * n_i + (i ^ distance(n_i, step, o % 2 == 1)))
                for o in range(n_o)
                for i in range(n_i)
            ]
            found.append(lax.ppermute(pieces[step], ("seqo", "seqi"), pairs))
        return found

    def swap_back(pieces):
        return [pieces[0]] + [
            swap(pieces[step], "seqi", n_i, distance_back(n_i, step)) for step in range(1, n_i)
        ]

    def swap_fulls(pieces):
        return [pieces[0]] + [swap(pieces[m], "seqo", n_o, m * width) for m in range(1, slots)]

    def pick_scratch(count):
        return [
            pltpu.VMEM((count, 4, rows, slots * HEAD_DIM), BF16),
            pltpu.SemaphoreType.DMA((count, 4)),
            pltpu.VMEM((count, 4, slots, rows, HEAD_DIM), F32),
            square,
        ]

    first, own, *fulls, firststats = call(
        bind(pick_first_kernel, n_i, slots),
        "pick_first",
        [mid, mid] + [full] * slots + [stats(2 * HEADS)],
        pick_scratch(2),
        unit * slots * 4,
        sources,
        hbm_in=range(4),
        limit=FIRST_LIMIT,
    )
    *pieces, near = call(
        bind(pick_rest_kernel, n_i, slots),
        "pick_rest",
        [mid] * (n_i - 2) + [stats(2 * HEADS)],
        pick_scratch(n_i - 2),
        unit * HEADS * 2,
        [*sources, firststats],
        hbm_in=range(4),
        limit=PICK_LIMIT,
    )
    mids = swap_mids([own, first, *pieces])
    fulls = swap_fulls(fulls)

    (settled,) = call(settle_kernel, "far_in", [stats(8)], [], SHORT, [mids[1]])
    (settled,) = call(settle_kernel, "chips_back", [stats(8)], [], LONG, [settled])
    (packed,) = call(bind(pack_kernel, slots), "pack", [half], [], 1, [*in_back(fulls), settled])
    sibs = [swap(packed, "seqo", n_o, part) for part in range(1, width)]
    (settled,) = call(settle_kernel, "packed_back", [stats(8)], [], LONG, [near])
    (far,) = call(
        bind(far_stats_kernel, slots),
        "far_stats",
        [stats(2 * slots)],
        [],
        1,
        [*in_back(fulls), *sibs, settled],
    )
    xmsg, middle, columns = call(
        bind(middle_stats_kernel, n_i, slots),
        "middle_stats",
        [stats(4 * slots), stats(2 * slots, n_i * quarter), stats(n_i * quarter, LANES)],
        [pltpu.VMEM((LANES, n_i * quarter), F32), square],
        unit * slots * 2,
        mids + [near, far],
    )
    xmsgs = swap_fulls([xmsg] * slots)

    midparts = call(
        bind(middle_parts_kernel, n_i, slots),
        "middle_parts",
        [mid] * n_i,
        [pltpu.VMEM((2 * slots, rows), F32), pltpu.VMEM((LANES, n_i * quarter), F32), square],
        unit * slots * 6,
        mids + [middle, columns] + xmsgs,
    )
    midparts = swap_back(midparts)
    farparts = call(
        bind(far_parts_kernel, slots, width),
        "far_parts",
        [full] * slots + [half] * (width - 1),
        [pltpu.VMEM((n_o * rows, slots * rows), BF16)] * 2,
        unit * n_o * slots * 6,
        [*in_back(fulls), *sibs, *xmsgs, midparts[0]],
        cheap=True,
    )
    sibparts = [swap(x, "seqo", n_o, part + 1) for part, x in enumerate(farparts[slots:])]
    (settled,) = call(settle_kernel, "far_back", [stats(8)], [], SHORT, [midparts[1]])
    (settled,) = call(settle_kernel, "sib_back", [stats(8)], [], 1, sibparts + [settled])
    (settled,) = call(settle_kernel, "settle", [stats(8)], [], LONG, [settled])
    fullparts = call(
        bind(far_sum_kernel, slots),
        "far_sum",
        [full] * slots,
        [],
        unit,
        list(farparts[:slots]) + sibparts + [settled],
        cheap=True,
    )
    fullparts = swap_fulls(fullparts)

    back = midparts
    kept = [pltpu.VMEM((2 * HEADS, rows), F32), square]
    (early,) = call(
        bind(near_early_kernel, n_i, slots),
        "near_early",
        [SHAPE((4, (n_i - 1) * slots, rows, HEAD_DIM), F32)],
        kept,
        SHORT,
        [*sources, near, *back[:-1], *xmsgs],
    )
    whole = [SHAPE((rows, features), BF16)] * 4
    outs = call(
        bind(final_others_kernel, n_i, slots),
        "final_others",
        whole,
        [
            pltpu.VMEM((n_i - 1, 4, rows, slots * HEAD_DIM), BF16),
            pltpu.SemaphoreType.DMA((n_i - 1, 4)),
            *kept,
        ],
        SHORT // 2,
        [*sources, near, early, *back[1:]],
        hbm_out=True,
    )
    return call(
        bind(final_own_kernel, slots),
        "final_own",
        whole,
        [pltpu.VMEM((4, rows, slots * HEAD_DIM), BF16), pltpu.SemaphoreType.DMA((4,))],
        unit * slots,
        [early, midparts[0], *in_back(fullparts), *outs],
        hbm_in=range(2 + slots, 6 + slots),
        hbm_out=True,
        aliases={2 + slots + which: which for which in range(4)},
    )


def solution(mesh):
    rows = P(("seqo", "seqi"), None)
    return jax.shard_map(
        local,
        mesh=mesh,
        in_specs=(rows,) * 4,
        out_specs=(rows,) * 4,
        check_vma=False,
    )
```

```python
import functools

import jax
import jax.numpy as jnp
from jax import lax
from jax.experimental import pallas as pl
from jax.experimental.pallas import tpu as pltpu
from jax.sharding import PartitionSpec as P

HEADS = 16
HEAD_DIM = 128
DILATION = 4
LANES = 128
SCALE = HEAD_DIM**-0.5
LOWEST = -1e30
LONG = 4 * 10**10
SHORT = 2 * 10**9
VMEM_LIMIT = 32 * 1024 * 1024
PICK_LIMIT = 54784 * 1024
FIRST_LIMIT = 54272 * 1024
NEAR_LIMIT = 54784 * 1024
F32, BF16 = jnp.float32, jnp.bfloat16
SHAPE = jax.ShapeDtypeStruct

NT = (((1,), (1,)), ((), ()))
TN = (((0,), (0,)), ((), ()))


def dot(a, b):
    return jnp.dot(a, b, preferred_element_type=F32)


def dot_nt(a, b):
    return lax.dot_general(a, b, NT, preferred_element_type=F32)


def dot_tn(a, b):
    return lax.dot_general(a, b, TN, preferred_element_type=F32)


def head_columns(head):
    return pl.ds(pl.multiple_of(head * HEAD_DIM, HEAD_DIM), HEAD_DIM)


def static_columns(index):
    return slice(index * HEAD_DIM, (index + 1) * HEAD_DIM)


def position(slots):
    width = lax.axis_size("seqo") // slots
    return lax.axis_index("seqi"), lax.axis_index("seqo") // width


def distance(n_i, step):
    return n_i - step


def distance_back(n_i, step):
    return n_i - 1 if step == 1 else step - 1


def place_in(n_i, slots, step):
    pos, _ = position(slots)
    return pos if step == 0 else pos ^ distance(n_i, step)


def first_back(n_i, slots, step):
    pos, _ = position(slots)
    return (pos if step == 0 else pos ^ distance_back(n_i, step)) * slots


def in_back_order(n_i, chunks):
    order = [distance(n_i, step) for step in range(1, n_i)]
    return [chunks[0]] + [
        chunks[order.index(distance_back(n_i, step)) + 1] for step in range(1, n_i)
    ]


def lanes_of(rows):
    return lax.broadcasted_iota(jnp.int32, (rows, LANES), 1)


def level_stats(operands):
    products = [(dot_nt(k, q) * SCALE, dot_nt(v, u)) for k, v, q, u in operands]
    tops = [jnp.max(s, axis=0, keepdims=True) for s, _ in products]
    weights = [jnp.exp(s - top) for (s, _), top in zip(products, tops)]
    totals = [jnp.sum(p, axis=0, keepdims=True) for p in weights]
    return [
        (top + jnp.log(total), jnp.sum(p * dp, axis=0, keepdims=True) / total)
        for (_, dp), top, p, total in zip(products, tops, weights, totals)
    ]


def merge_stats(ea, da, eb, db):
    top = jnp.maximum(ea, eb)
    wa, wb = jnp.exp(ea - top), jnp.exp(eb - top)
    total = wa + wb
    return top + jnp.log(total), (wa * da + wb * db) / total


def level_weights(operands, stats):
    products = [(dot_nt(k, q) * SCALE, dot_nt(v, u)) for k, v, q, u in operands]
    found = []
    for (s, dp), (lse, delta) in zip(products, stats):
        g = jnp.exp(s - lse)
        found.append((g.astype(BF16), (g * (dp - delta)).astype(BF16)))
    return found


def level_parts(operands, stats):
    found = level_weights(operands, stats)
    keyed = [
        (dot(ds, q) * SCALE, dot(p, u)) for (p, ds), (k, v, q, u) in zip(found, operands)
    ]
    queried = [
        (dot_tn(p, v), dot_tn(ds, k) * SCALE) for (p, ds), (k, v, q, u) in zip(found, operands)
    ]
    return [a + b for a, b in zip(queried, keyed)]


def pick_rows(ref, rows):
    quarter = rows // DILATION
    lane = lanes_of(quarter)
    picked = jnp.zeros((quarter, LANES), F32)
    for residue in range(DILATION):
        part = ref[pl.ds(residue, quarter, stride=DILATION), :]
        picked = jnp.where(lane % DILATION == residue, part, picked)
    return picked


def fetch(slots, places, sources, buffers, sems):
    width = slots * HEAD_DIM
    groups = []
    for index, place in enumerate(places):
        cols = pl.ds(pl.multiple_of(place * width, width), width)
        groups.append(
            [
                pltpu.make_async_copy(
                    source.at[:, cols], buffers.at[index, which], sems.at[index, which]
                )
                for which, source in enumerate(sources)
            ]
        )
        for copy in groups[-1]:
            copy.start()
    return groups


def split(x):
    high = x.astype(BF16).astype(F32)
    rest = x - high
    middle = rest.astype(BF16).astype(F32)
    low = rest - middle
    return (high + pltpu.roll(middle, 2 * HEADS, 1) + pltpu.roll(low, 4 * HEADS, 1)).astype(BF16)


def join(ref):
    x = ref[ref.shape[0] - 1].astype(F32)
    x = x + (pltpu.roll(x, LANES - 2 * HEADS, 1) + pltpu.roll(x, LANES - 4 * HEADS, 1))
    return jnp.where(lanes_of(x.shape[0]) < 2 * HEADS, x, 0.0)


def pick_places(n_i, slots, steps, sources, mids, buffers, sems, wide, turn):
    rows = sources[0].shape[0]
    quarter = rows // DILATION
    places = [place_in(n_i, slots, step) for step in steps]
    for index, copies in enumerate(fetch(slots, places, sources, buffers, sems)):
        first = places[index] * slots
        for which, copy in enumerate(copies):
            copy.wait()
            for slot in range(slots):
                wide[index, which, slot] = buffers[index, which, :, static_columns(slot)].astype(F32)
                residue = (first + slot) % DILATION if slots % DILATION else slot % DILATION
                rowset = wide[index, which, slot, pl.ds(residue, quarter, stride=DILATION), :]
                mids[index][which * slots + slot] = rowset.astype(BF16)
        operands = [
            [buffers[index, which, :, static_columns(slot)] for which in range(4)]
            for slot in range(slots)
        ]
        for slot, (e, d) in enumerate(level_stats(operands)):
            turn[pl.ds(first + slot, 1), :] = e
            turn[pl.ds(HEADS + first + slot, 1), :] = d


def pick_first_kernel(n_i, slots, *refs):
    sources, (mid_ref, own_ref, *refs) = refs[:4], refs[4:]
    fulls, (stats_ref, buffers, sems, wide, turn) = refs[:slots], refs[slots:]
    rows = sources[0].shape[0]
    _, chip = position(slots)
    turn[...] = jnp.zeros_like(turn)
    pick_places(n_i, slots, [1, 0], sources, [mid_ref, own_ref], buffers, sems, wide, turn)
    for m in range(slots):
        fulls[m][...] = buffers[1, :, :, head_columns(chip ^ m)]
    stats_ref[...] = turn[: 2 * HEADS, :]
    turn[...] = turn[...].T
    near = split(pick_rows(turn, rows))
    mid_ref[4 * slots] = near
    own_ref[4 * slots] = near


def pick_rest_kernel(n_i, slots, steps, *refs):
    sources, first_ref, refs = refs[:4], refs[4], refs[6:]
    mids, refs = refs[: len(steps)], refs[len(steps) :]
    stats_ref, buffers, sems, wide, turn = refs
    rows = sources[0].shape[0]
    turn[...] = jnp.zeros_like(turn)
    turn[: 2 * HEADS, :] = first_ref[...]
    pick_places(n_i, slots, steps, sources, mids, buffers, sems, wide, turn)
    stats_ref[...] = turn[: 2 * HEADS, :]
    turn[...] = turn[...].T
    near = split(pick_rows(turn, rows))
    for ref in mids:
        ref[4 * slots] = near


def pack_kernel(slots, *refs):
    packed_ref = refs[-1]
    for m, ref in enumerate(in_back(refs[:slots])):
        packed_ref[m] = ref[:2]


def far_keys(fulls, sibs, which):
    blocks = [ref[which] for ref in fulls]
    return jnp.concatenate(blocks + [ref[m, which] for ref in sibs for m in range(len(fulls))], axis=0)


def far_stats_kernel(slots, *refs):
    fulls, sibs, stats_ref = in_back(refs[:slots]), refs[slots:-2], refs[-1]
    keys, values = far_keys(fulls, sibs, 0), far_keys(fulls, sibs, 1)
    for m in range(slots):
        ((e, d),) = level_stats([(keys, values, fulls[m][2], fulls[m][3])])
        stats_ref[m : m + 1, :] = e
        stats_ref[slots + m : slots + m + 1, :] = d


def middle_operands(slots, mids, slot):
    return [
        jnp.concatenate([ref[which * slots + slot] for ref in mids], axis=0) for which in range(4)
    ]


def middle_stats_kernel(n_i, slots, *refs):
    mids, refs = refs[:n_i], refs[n_i:]
    near_ref, far_ref, xmsg_ref, stats_ref, columns_ref, turn, spread = refs
    rows = near_ref.shape[1]
    quarter = rows // DILATION
    pos, _ = position(slots)
    turn[...] = jnp.zeros_like(turn)
    operands = [middle_operands(slots, mids, slot) for slot in range(slots)]
    for slot, (e, d) in enumerate(level_stats(operands)):
        turn[slot : slot + 1, :] = e
        turn[slots + slot : slots + slot + 1, :] = d
    stats_ref[...] = turn[: 2 * slots, :]
    columns_ref[...] = turn[...].T
    lane = lanes_of(quarter)
    lane_residue = (pos * slots + lane % slots) % DILATION
    blank = jnp.where(lane < slots, LOWEST, 0.0)
    for residue in range(DILATION):
        spread[pl.ds(residue, quarter, stride=DILATION), :] = jnp.where(
            lane_residue == residue, columns_ref[:quarter], blank
        )
    across = spread[...].T
    e, d = merge_stats(
        near_ref[pl.ds(pos * slots, slots), :],
        near_ref[pl.ds(HEADS + pos * slots, slots), :],
        across[:slots],
        across[slots : 2 * slots],
    )
    xmsg_ref[:slots] = e
    xmsg_ref[slots : 2 * slots] = d
    xmsg_ref[2 * slots :] = far_ref[...]


def middle_parts_kernel(n_i, slots, *refs):
    mids, refs = refs[:n_i], refs[n_i:]
    stats_ref, columns_ref = refs[:2]
    refs = refs[2:]
    xmsgs, refs = refs[:slots], refs[slots:]
    outs, (far, turn, spread) = refs[:n_i], refs[n_i:]
    rows = xmsgs[0].shape[1]
    quarter = rows // DILATION
    pos, chip = position(slots)
    for m in range(slots):
        far[pl.ds(chip ^ m, 1), :] = xmsgs[m][2 * slots + m : 2 * slots + m + 1, :]
        far[pl.ds(slots + (chip ^ m), 1), :] = xmsgs[m][3 * slots + m : 3 * slots + m + 1, :]
    e, d = merge_stats(
        xmsgs[0][:slots], xmsgs[0][slots : 2 * slots], far[:slots], far[slots:]
    )
    spread[...] = jnp.zeros_like(spread)
    spread[pl.ds(pos * slots, slots), :] = e
    spread[pl.ds(HEADS + pos * slots, slots), :] = d
    spread[...] = spread[...].T
    own = pick_rows(spread, rows)
    turn[...] = jnp.concatenate([own] + [join(ref) for ref in mids[1:]], axis=0).T
    owned = lax.broadcasted_iota(jnp.int32, (1, n_i * quarter), 1) < quarter
    operands = [middle_operands(slots, mids, slot) for slot in range(slots)]
    merged = [
        merge_stats(
            turn[pl.ds(pos * slots + slot, 1), :],
            turn[pl.ds(HEADS + pos * slots + slot, 1), :],
            jnp.where(owned, LOWEST, stats_ref[slot : slot + 1, :]),
            stats_ref[slots + slot : slots + slot + 1, :],
        )
        for slot in range(slots)
    ]
    for slot, parts in enumerate(level_parts(operands, merged)):
        for which, part in enumerate(parts):
            part = part.astype(BF16)
            chunks = [part[d * quarter : (d + 1) * quarter] for d in range(n_i)]
            for out, chunk in zip(outs, in_back_order(n_i, chunks)):
                out[which * slots + slot] = chunk
    chunks = [columns_ref[d * quarter : (d + 1) * quarter] for d in range(n_i)]
    for out, chunk in zip(outs, in_back_order(n_i, chunks)):
        out[4 * slots] = split(chunk)


def far_parts_kernel(slots, width, *refs):
    fulls, refs = in_back(refs[:slots]), refs[slots:]
    sibs, refs = refs[: width - 1], refs[width - 1 :]
    xmsgs, refs = refs[:slots], refs[slots + 1 :]
    outs, refs = refs[:slots], refs[slots:]
    kvouts, refs = refs[: width - 1], refs[width - 1 :]
    weights, score_grads = refs
    rows = fulls[0].shape[1]
    _, chip = position(slots)
    keys, values = far_keys(fulls, sibs, 0), far_keys(fulls, sibs, 1)
    for m in range(slots):
        lse, delta = merge_stats(
            xmsgs[m][pl.ds(chip, 1), :],
            xmsgs[m][pl.ds(slots + chip, 1), :],
            xmsgs[0][2 * slots + m : 2 * slots + m + 1, :],
            xmsgs[0][3 * slots + m : 3 * slots + m + 1, :],
        )
        operands = (keys, values, fulls[m][2], fulls[m][3])
        ((p, ds),) = level_weights([operands], [(lse, delta)])
        outs[m][0] = dot_tn(p, values).astype(BF16)
        outs[m][1] = (dot_tn(ds, keys) * SCALE).astype(BF16)
        weights[:, m * rows : (m + 1) * rows] = p
        score_grads[:, m * rows : (m + 1) * rows] = ds
    queries = jnp.concatenate([ref[2] for ref in fulls], axis=0)
    ups = jnp.concatenate([ref[3] for ref in fulls], axis=0)
    key_part = (dot(score_grads[...], queries) * SCALE).astype(BF16)
    value_part = dot(weights[...], ups).astype(BF16)
    for index in range(width * slots):
        block = slice(index * rows, (index + 1) * rows)
        part, m = index // slots, index % slots
        if part == 0:
            outs[m][2], outs[m][3] = key_part[block], value_part[block]
        else:
            kvouts[part - 1][m, 0], kvouts[part - 1][m, 1] = key_part[block], value_part[block]


def far_sum_kernel(slots, *refs):
    own, refs = refs[:slots], refs[slots:]
    found, outs = refs[: -slots - 1], refs[-slots:]
    for m in range(slots):
        outs[m][:2] = own[m][:2]
        total = own[m][2:].astype(F32)
        for ref in found:
            total += ref[m].astype(F32)
        outs[m][2:] = total.astype(BF16)


def near_statistics(n_i, slots, steps, near_ref, mids, xmsgs, stats_ref, spread):
    rows = near_ref.shape[1]
    quarter = rows // DILATION
    pos, chip = position(slots)
    lane = lanes_of(quarter)
    mid = jnp.zeros((quarter, LANES), F32)
    for step, ref in zip(steps, mids):
        place = first_back(n_i, slots, step)
        found = join(ref)
        e = pltpu.roll(found, place, 1)
        de = pltpu.roll(found, place + HEADS - slots, 1)
        mid = jnp.where((lane >= place) & (lane < place + slots), e, mid)
        mid = jnp.where((lane >= HEADS + place) & (lane < HEADS + place + slots), de, mid)
    blank = jnp.where(lane < HEADS, LOWEST, 0.0)
    for residue in range(DILATION):
        spread[pl.ds(residue, quarter, stride=DILATION), :] = jnp.where(
            lane % DILATION == residue, mid, blank
        )
    across = spread[...].T
    e, d = merge_stats(
        near_ref[:HEADS], near_ref[HEADS:], across[:HEADS], across[HEADS : 2 * HEADS]
    )
    if xmsgs:
        stats_ref[:HEADS] = jnp.full((HEADS, rows), LOWEST, F32)
        stats_ref[HEADS:] = jnp.zeros((HEADS, rows), F32)
        for m in range(slots):
            head = pos * slots + (chip ^ m)
            stats_ref[pl.ds(head, 1), :] = xmsgs[m][2 * slots + m : 2 * slots + m + 1, :]
            stats_ref[pl.ds(HEADS + head, 1), :] = xmsgs[m][3 * slots + m : 3 * slots + m + 1, :]
        e, d = merge_stats(e, d, stats_ref[:HEADS], stats_ref[HEADS:])
    stats_ref[:HEADS] = e
    stats_ref[HEADS:] = d


def near_place(n_i, slots, step, sources, stats_ref):
    heads = [first_back(n_i, slots, step) + slot for slot in range(slots)]
    operands = [[ref[:, head_columns(head)] for ref in sources] for head in heads]
    stats = [(stats_ref[pl.ds(head, 1), :], stats_ref[pl.ds(HEADS + head, 1), :]) for head in heads]
    return level_parts(operands, stats)


def near_early_kernel(n_i, slots, *refs):
    sources, near_ref, refs = refs[:4], refs[4], refs[5:]
    mids, refs = refs[: n_i - 1], refs[n_i - 1 :]
    xmsgs, (out_ref, stats_ref, spread) = refs[:slots], refs[slots:]
    near_statistics(n_i, slots, range(n_i - 1), near_ref, mids, xmsgs, stats_ref, spread)
    for step in range(n_i - 1):
        for slot, parts in enumerate(near_place(n_i, slots, step, sources, stats_ref)):
            for which, part in enumerate(parts):
                out_ref[which, step * slots + slot] = part


def far_sum_kernel(slots, *refs):
    own, refs = refs[:slots], refs[slots:]
    found, outs = refs[: -slots - 1], refs[-slots:]
    for m in range(slots):
        outs[m][:2] = own[m][:2]
        total = own[m][2:].astype(F32)
        for ref in found:
            total += ref[m].astype(F32)
        outs[m][2:] = total.astype(BF16)


def near_parts_kernel(n_i, slots, *refs):
    sources, near_ref, refs = refs[:4], refs[4], refs[5:]
    mids, refs = (refs[0], *refs[n_i - 1 : 0 : -1]), refs[n_i:]
    xmsgs, (out_ref, stats_ref, spread) = refs[:slots], refs[slots:]
    rows = near_ref.shape[1]
    quarter = rows // DILATION
    pos, chip = position(slots)
    lane = lanes_of(quarter)
    mid = jnp.zeros((quarter, LANES), F32)
    for d in range(n_i):
        place = (pos ^ d) * slots
        found = join(mids[d])
        e = pltpu.roll(found, place, 1)
        de = pltpu.roll(found, place + HEADS - slots, 1)
        mid = jnp.where((lane >= place) & (lane < place + slots), e, mid)
        mid = jnp.where((lane >= HEADS + place) & (lane < HEADS + place + slots), de, mid)
    blank = jnp.where(lane < HEADS, LOWEST, 0.0)
    for residue in range(DILATION):
        spread[pl.ds(residue, quarter, stride=DILATION), :] = jnp.where(
            lane % DILATION == residue, mid, blank
        )
    across = spread[...].T
    stats_ref[:HEADS] = jnp.full((HEADS, rows), LOWEST, F32)
    stats_ref[HEADS:] = jnp.zeros((HEADS, rows), F32)
    for m in range(slots):
        head = pos * slots + (chip ^ m)
        stats_ref[pl.ds(head, 1), :] = xmsgs[m][2 * slots + m : 2 * slots + m + 1, :]
        stats_ref[pl.ds(HEADS + head, 1), :] = xmsgs[m][3 * slots + m : 3 * slots + m + 1, :]
    e, d = merge_stats(
        near_ref[:HEADS], near_ref[HEADS:], across[:HEADS], across[HEADS : 2 * HEADS]
    )
    e, d = merge_stats(e, d, stats_ref[:HEADS], stats_ref[HEADS:])
    stats_ref[:HEADS] = e
    stats_ref[HEADS:] = d
    for group in range(HEADS // DILATION):
        heads = range(group * DILATION, (group + 1) * DILATION)
        operands = [
            [ref[:, static_columns(head)] for ref in sources] for head in heads
        ]
        stats = [
            (stats_ref[head : head + 1, :], stats_ref[HEADS + head : HEADS + head + 1, :])
            for head in heads
        ]
        for head, parts in zip(heads, level_parts(operands, stats)):
            for which, part in enumerate(parts):
                out_ref[which, head] = part


def spread_rows(slots, head, slot, ref):
    quarter = ref.shape[1]
    rows = quarter * DILATION
    row = lax.broadcasted_iota(jnp.int32, (rows, quarter), 0)
    taken = lax.broadcasted_iota(jnp.int32, (rows, quarter), 1) * DILATION
    place = jnp.where(row == taken + head % DILATION, 1.0, 0.0).astype(BF16)
    return dot(place, jnp.concatenate([ref[which * slots + slot] for which in range(4)], axis=1))


def send_place(slots, first, ready, outs, sems):
    width = slots * HEAD_DIM
    cols = pl.ds(pl.multiple_of(first * HEAD_DIM, width), width)
    copies = [
        pltpu.make_async_copy(ready.at[which], out.at[:, cols], sems.at[which])
        for which, out in enumerate(outs)
    ]
    for copy in copies:
        copy.start()
    return copies


def final_others_kernel(n_i, slots, *refs):
    sources, near_ref, early_ref, refs = refs[:4], refs[4], refs[5], refs[6:]
    mids, refs = refs[: n_i - 1], refs[n_i - 1 :]
    outs, (ready, sems, stats_ref, spread) = refs[:4], refs[4:]
    last = n_i - 1
    copies = []
    for step in range(1, n_i):
        first = first_back(n_i, slots, step)
        found = [spread_rows(slots, first + slot, slot, mids[step - 1]) for slot in range(slots)]
        if step == last:
            near_statistics(n_i, slots, [last], near_ref, mids[-1:], (), stats_ref, spread)
            late = near_place(n_i, slots, last, sources, stats_ref)
        for slot, parts in enumerate(found):
            for which in range(4):
                near = late[slot][which] if step == last else early_ref[which, step * slots + slot]
                total = near + parts[:, static_columns(which)]
                ready[step - 1, which, :, static_columns(slot)] = total.astype(BF16)
        copies += send_place(slots, first, ready.at[step - 1], outs, sems.at[step - 1])
    for copy in copies:
        copy.wait()


def final_own_kernel(slots, early_ref, mid_ref, *refs):
    fulls, refs = in_back(refs[:slots]), refs[slots:]
    outs, (ready, sems) = refs[4:8], refs[8:]
    pos, chip = position(slots)
    first = pos * slots
    found = [spread_rows(slots, first + (chip ^ m), chip ^ m, mid_ref) for m in range(slots)]
    for m, parts in enumerate(found):
        slot = chip ^ m
        for which in range(4):
            total = early_ref[which, slot] + parts[:, static_columns(which)]
            total += fulls[m][which].astype(F32)
            ready[which, :, head_columns(slot)] = total.astype(BF16)
    for copy in send_place(slots, first, ready, outs, sems):
        copy.wait()


def settle_kernel(*refs):
    refs[-1][...] = jnp.zeros_like(refs[-1])


def call(kernel, name, outs, scratch, flops, operands, hbm_in=(), hbm_out=False, cheap=False, limit=VMEM_LIMIT, aliases=None):
    moved = sum(x.size * x.dtype.itemsize for x in tuple(operands) + tuple(outs))
    if cheap:
        flops, moved = 1, 1
    spaces = [pltpu.HBM if i in hbm_in else pltpu.VMEM for i in range(len(operands))]
    return pl.pallas_call(
        kernel,
        out_shape=tuple(outs),
        in_specs=[pl.BlockSpec(memory_space=space) for space in spaces],
        out_specs=tuple(
            pl.BlockSpec(memory_space=pltpu.HBM if hbm_out else pltpu.VMEM) for _ in outs
        ),
        scratch_shapes=scratch,
        input_output_aliases=aliases or {},
        compiler_params=pltpu.CompilerParams(vmem_limit_bytes=limit),
        cost_estimate=pl.CostEstimate(flops=flops, bytes_accessed=moved, transcendentals=0),
        name=name,
    )(*operands)


def in_back(pieces):
    return [pieces[0], *pieces[:0:-1]]


def swap(x, axis, n, mask):
    return lax.ppermute(x, axis, [(i, i ^ mask) for i in range(n)])


def local(query_rows, key_rows, value_rows, upstream):
    rows, features = query_rows.shape
    n_i, n_o = lax.axis_size("seqi"), lax.axis_size("seqo")
    slots = HEADS // n_i
    width = n_o // slots
    others = (width - 1) * slots
    quarter = rows // DILATION
    sources = (key_rows, value_rows, query_rows, upstream)
    unit = 2 * rows * rows * HEAD_DIM
    bind = functools.partial

    mid = SHAPE((4 * slots + 1, quarter, HEAD_DIM), BF16)
    full = SHAPE((4, rows, HEAD_DIM), BF16)
    half = SHAPE((slots, 2, rows, HEAD_DIM), BF16)
    square = pltpu.VMEM((LANES, rows), F32)

    def stats(count, lanes=rows):
        return SHAPE((count, lanes), F32)

    def swap_mids(pieces, begin):
        return [
            swap(pieces[step], "seqi", n_i, distance(n_i, step)) for step in range(begin, len(pieces))
        ]

    def swap_back(pieces):
        return [pieces[0]] + [
            swap(pieces[step], "seqi", n_i, distance_back(n_i, step)) for step in range(1, n_i)
        ]

    def swap_fulls(pieces):
        return [pieces[0]] + [swap(pieces[m], "seqo", n_o, m * width) for m in range(1, slots)]

    def pick_scratch(count):
        return [
            pltpu.VMEM((count, 4, rows, slots * HEAD_DIM), BF16),
            pltpu.SemaphoreType.DMA((count, 4)),
            pltpu.VMEM((count, 4, slots, rows, HEAD_DIM), F32),
            square,
        ]

    first, own, *fulls, firststats = call(
        bind(pick_first_kernel, n_i, slots),
        "pick_first",
        [mid, mid] + [full] * slots + [stats(2 * HEADS)],
        pick_scratch(2),
        unit * slots * 4,
        sources,
        hbm_in=range(4),
        limit=FIRST_LIMIT,
    )
    mids = [own, *swap_mids([own, first], 1)]
    near, pieces, after = firststats, [], own
    for name, steps in (("pick_second", [2]), ("pick_rest", list(range(3, n_i)))):
        *picked, near = call(
            bind(pick_rest_kernel, n_i, slots, steps),
            name,
            [mid] * len(steps) + [stats(2 * HEADS)],
            pick_scratch(len(steps)),
            unit * HEADS,
            [*sources, near, after],
            hbm_in=range(4),
            limit=PICK_LIMIT,
        )
        pieces += picked
        after = mids[1]

    mids += swap_mids([own, first, *pieces], 2)
    fulls = swap_fulls(fulls)

    (settled,) = call(settle_kernel, "far_in", [stats(8)], [], SHORT, [mids[1]])
    (settled,) = call(settle_kernel, "chips_back", [stats(8)], [], LONG, [settled])
    (packed,) = call(bind(pack_kernel, slots), "pack", [half], [], 1, [*in_back(fulls), settled])
    sibs = [swap(packed, "seqo", n_o, part) for part in range(1, width)]
    (settled,) = call(settle_kernel, "packed_back", [stats(8)], [], LONG, [near])
    (far,) = call(
        bind(far_stats_kernel, slots),
        "far_stats",
        [stats(2 * slots)],
        [],
        1,
        [*in_back(fulls), *sibs, settled],
    )
    xmsg, middle, columns = call(
        bind(middle_stats_kernel, n_i, slots),
        "middle_stats",
        [stats(4 * slots), stats(2 * slots, n_i * quarter), stats(n_i * quarter, LANES)],
        [pltpu.VMEM((LANES, n_i * quarter), F32), square],
        unit * slots * 2,
        mids + [near, far],
    )
    xmsgs = swap_fulls([xmsg] * slots)

    midparts = call(
        bind(middle_parts_kernel, n_i, slots),
        "middle_parts",
        [mid] * n_i,
        [pltpu.VMEM((2 * slots, rows), F32), pltpu.VMEM((LANES, n_i * quarter), F32), square],
        unit * slots * 6,
        mids + [middle, columns] + xmsgs,
    )
    midparts = swap_back(midparts)
    farparts = call(
        bind(far_parts_kernel, slots, width),
        "far_parts",
        [full] * slots + [half] * (width - 1),
        [pltpu.VMEM((n_o * rows, slots * rows), BF16)] * 2,
        unit * n_o * slots * 6,
        [*in_back(fulls), *sibs, *xmsgs, midparts[0]],
        cheap=True,
    )
    sibparts = [swap(x, "seqo", n_o, part + 1) for part, x in enumerate(farparts[slots:])]
    (settled,) = call(settle_kernel, "far_back", [stats(8)], [], SHORT, [midparts[1]])
    (settled,) = call(settle_kernel, "sib_back", [stats(8)], [], 1, sibparts + [settled])
    (settled,) = call(settle_kernel, "settle", [stats(8)], [], LONG, [settled])
    fullparts = call(
        bind(far_sum_kernel, slots),
        "far_sum",
        [full] * slots,
        [],
        unit,
        list(farparts[:slots]) + sibparts + [settled],
        cheap=True,
    )
    fullparts = swap_fulls(fullparts)

    back = midparts
    kept = [pltpu.VMEM((2 * HEADS, rows), F32), square]
    (early,) = call(
        bind(near_early_kernel, n_i, slots),
        "near_early",
        [SHAPE((4, (n_i - 1) * slots, rows, HEAD_DIM), F32)],
        kept,
        SHORT,
        [*sources, near, *back[:-1], *xmsgs],
    )
    whole = [SHAPE((rows, features), BF16)] * 4
    outs = call(
        bind(final_others_kernel, n_i, slots),
        "final_others",
        whole,
        [
            pltpu.VMEM((n_i - 1, 4, rows, slots * HEAD_DIM), BF16),
            pltpu.SemaphoreType.DMA((n_i - 1, 4)),
            *kept,
        ],
        SHORT // 2,
        [*sources, near, early, *back[1:]],
        hbm_out=True,
    )
    return call(
        bind(final_own_kernel, slots),
        "final_own",
        whole,
        [pltpu.VMEM((4, rows, slots * HEAD_DIM), BF16), pltpu.SemaphoreType.DMA((4,))],
        unit * slots,
        [early, midparts[0], *in_back(fullparts), *outs],
        hbm_in=range(2 + slots, 6 + slots),
        hbm_out=True,
        aliases={2 + slots + which: which for which in range(4)},
    )


def solution(mesh):
    rows = P(("seqo", "seqi"), None)
    return jax.shard_map(
        local,
        mesh=mesh,
        in_specs=(rows,) * 4,
        out_specs=(rows,) * 4,
        check_vma=False,
    )
```

```python
import functools

import jax
import jax.numpy as jnp
from jax import lax
from jax.experimental import pallas as pl
from jax.experimental.pallas import tpu as pltpu
from jax.sharding import PartitionSpec as P

HEADS = 16
HEAD_DIM = 128
DILATION = 4
LANES = 128
SCALE = HEAD_DIM**-0.5
LOWEST = -1e30
LONG = 4 * 10**10
SHORT = 2 * 10**9
VMEM_LIMIT = 32 * 1024 * 1024
PICK_LIMIT = 54784 * 1024
FIRST_LIMIT = 54272 * 1024
NEAR_LIMIT = 54784 * 1024
F32, BF16 = jnp.float32, jnp.bfloat16
SHAPE = jax.ShapeDtypeStruct

NT = (((1,), (1,)), ((), ()))
TN = (((0,), (0,)), ((), ()))


def dot(a, b):
    return jnp.dot(a, b, preferred_element_type=F32)


def dot_nt(a, b):
    return lax.dot_general(a, b, NT, preferred_element_type=F32)


def dot_tn(a, b):
    return lax.dot_general(a, b, TN, preferred_element_type=F32)


def head_columns(head):
    return pl.ds(pl.multiple_of(head * HEAD_DIM, HEAD_DIM), HEAD_DIM)


def static_columns(index):
    return slice(index * HEAD_DIM, (index + 1) * HEAD_DIM)


def position(slots):
    width = lax.axis_size("seqo") // slots
    return lax.axis_index("seqi"), lax.axis_index("seqo") // width


def distance(n_i, step):
    return n_i - step


def distance_back(n_i, step):
    return n_i - 1 if step == 1 else step - 1


def place_in(n_i, slots, step):
    pos, _ = position(slots)
    return pos if step == 0 else pos ^ distance(n_i, step)


def first_back(n_i, slots, step):
    pos, _ = position(slots)
    return (pos if step == 0 else pos ^ distance_back(n_i, step)) * slots


def in_back_order(n_i, chunks):
    order = [distance(n_i, step) for step in range(1, n_i)]
    return [chunks[0]] + [
        chunks[order.index(distance_back(n_i, step)) + 1] for step in range(1, n_i)
    ]


def lanes_of(rows):
    return lax.broadcasted_iota(jnp.int32, (rows, LANES), 1)


def level_stats(operands):
    products = [(dot_nt(k, q) * SCALE, dot_nt(v, u)) for k, v, q, u in operands]
    tops = [jnp.max(s, axis=0, keepdims=True) for s, _ in products]
    weights = [jnp.exp(s - top) for (s, _), top in zip(products, tops)]
    totals = [jnp.sum(p, axis=0, keepdims=True) for p in weights]
    return [
        (top + jnp.log(total), jnp.sum(p * dp, axis=0, keepdims=True) / total)
        for (_, dp), top, p, total in zip(products, tops, weights, totals)
    ]


def merge_stats(ea, da, eb, db):
    top = jnp.maximum(ea, eb)
    wa, wb = jnp.exp(ea - top), jnp.exp(eb - top)
    total = wa + wb
    return top + jnp.log(total), (wa * da + wb * db) / total


def level_weights(operands, stats):
    products = [(dot_nt(k, q) * SCALE, dot_nt(v, u)) for k, v, q, u in operands]
    found = []
    for (s, dp), (lse, delta) in zip(products, stats):
        g = jnp.exp(s - lse)
        found.append((g.astype(BF16), (g * (dp - delta)).astype(BF16)))
    return found


def level_parts(operands, stats):
    found = level_weights(operands, stats)
    keyed = [
        (dot(ds, q) * SCALE, dot(p, u)) for (p, ds), (k, v, q, u) in zip(found, operands)
    ]
    queried = [
        (dot_tn(p, v), dot_tn(ds, k) * SCALE) for (p, ds), (k, v, q, u) in zip(found, operands)
    ]
    return [a + b for a, b in zip(queried, keyed)]


def pick_rows(ref, rows):
    quarter = rows // DILATION
    lane = lanes_of(quarter)
    picked = jnp.zeros((quarter, LANES), F32)
    for residue in range(DILATION):
        part = ref[pl.ds(residue, quarter, stride=DILATION), :]
        picked = jnp.where(lane % DILATION == residue, part, picked)
    return picked


def fetch(slots, places, sources, buffers, sems):
    width = slots * HEAD_DIM
    groups = []
    for index, place in enumerate(places):
        cols = pl.ds(pl.multiple_of(place * width, width), width)
        groups.append(
            [
                pltpu.make_async_copy(
                    source.at[:, cols], buffers.at[index, which], sems.at[index, which]
                )
                for which, source in enumerate(sources)
            ]
        )
        for copy in groups[-1]:
            copy.start()
    return groups


def split(x):
    high = x.astype(BF16).astype(F32)
    rest = x - high
    middle = rest.astype(BF16).astype(F32)
    low = rest - middle
    return (high + pltpu.roll(middle, 2 * HEADS, 1) + pltpu.roll(low, 4 * HEADS, 1)).astype(BF16)


def join(ref):
    x = ref[ref.shape[0] - 1].astype(F32)
    x = x + (pltpu.roll(x, LANES - 2 * HEADS, 1) + pltpu.roll(x, LANES - 4 * HEADS, 1))
    return jnp.where(lanes_of(x.shape[0]) < 2 * HEADS, x, 0.0)


def pick_places(n_i, slots, steps, sources, mids, buffers, sems, wide, turn):
    rows = sources[0].shape[0]
    quarter = rows // DILATION
    places = [place_in(n_i, slots, step) for step in steps]
    for index, copies in enumerate(fetch(slots, places, sources, buffers, sems)):
        first = places[index] * slots
        for which, copy in enumerate(copies):
            copy.wait()
            for slot in range(slots):
                wide[index, which, slot] = buffers[index, which, :, static_columns(slot)].astype(F32)
                residue = (first + slot) % DILATION if slots % DILATION else slot % DILATION
                rowset = wide[index, which, slot, pl.ds(residue, quarter, stride=DILATION), :]
                mids[index][which * slots + slot] = rowset.astype(BF16)
        operands = [
            [buffers[index, which, :, static_columns(slot)] for which in range(4)]
            for slot in range(slots)
        ]
        for slot, (e, d) in enumerate(level_stats(operands)):
            turn[pl.ds(first + slot, 1), :] = e
            turn[pl.ds(HEADS + first + slot, 1), :] = d


def pick_first_kernel(n_i, slots, *refs):
    sources, (mid_ref, own_ref, *refs) = refs[:4], refs[4:]
    fulls, (stats_ref, buffers, sems, wide, turn) = refs[:slots], refs[slots:]
    rows = sources[0].shape[0]
    _, chip = position(slots)
    turn[...] = jnp.zeros_like(turn)
    pick_places(n_i, slots, [1, 0], sources, [mid_ref, own_ref], buffers, sems, wide, turn)
    for m in range(slots):
        fulls[m][...] = buffers[1, :, :, head_columns(chip ^ m)]
    stats_ref[...] = turn[: 2 * HEADS, :]
    turn[...] = turn[...].T
    near = split(pick_rows(turn, rows))
    mid_ref[4 * slots] = near
    own_ref[4 * slots] = near


def pick_rest_kernel(n_i, slots, *refs):
    sources, first_ref, refs = refs[:4], refs[4], refs[5:]
    mids, refs = refs[: n_i - 2], refs[n_i - 2 :]
    stats_ref, buffers, sems, wide, turn = refs
    rows = sources[0].shape[0]
    turn[...] = jnp.zeros_like(turn)
    turn[: 2 * HEADS, :] = first_ref[...]
    pick_places(n_i, slots, range(2, n_i), sources, mids, buffers, sems, wide, turn)
    stats_ref[...] = turn[: 2 * HEADS, :]
    turn[...] = turn[...].T
    near = split(pick_rows(turn, rows))
    for ref in mids:
        ref[4 * slots] = near


def pack_kernel(slots, *refs):
    packed_ref = refs[-1]
    for m, ref in enumerate(in_back(refs[:slots])):
        packed_ref[m] = ref[:2]


def far_keys(fulls, sibs, which):
    blocks = [ref[which] for ref in fulls]
    return jnp.concatenate(blocks + [ref[m, which] for ref in sibs for m in range(len(fulls))], axis=0)


def far_stats_kernel(slots, *refs):
    fulls, sibs, stats_ref = in_back(refs[:slots]), refs[slots:-2], refs[-1]
    keys, values = far_keys(fulls, sibs, 0), far_keys(fulls, sibs, 1)
    operands = [(keys, values, ref[2], ref[3]) for ref in fulls]
    for m, (e, d) in enumerate(level_stats(operands)):
        stats_ref[m : m + 1, :] = e
        stats_ref[slots + m : slots + m + 1, :] = d


def middle_operands(slots, mids, slot):
    return [
        jnp.concatenate([ref[which * slots + slot] for ref in mids], axis=0) for which in range(4)
    ]


def middle_stats_kernel(n_i, slots, *refs):
    mids, refs = refs[:n_i], refs[n_i:]
    near_ref, far_ref, xmsg_ref, stats_ref, columns_ref, turn, spread = refs
    rows = near_ref.shape[1]
    quarter = rows // DILATION
    pos, _ = position(slots)
    turn[...] = jnp.zeros_like(turn)
    operands = [middle_operands(slots, mids, slot) for slot in range(slots)]
    for slot, (e, d) in enumerate(level_stats(operands)):
        turn[slot : slot + 1, :] = e
        turn[slots + slot : slots + slot + 1, :] = d
    stats_ref[...] = turn[: 2 * slots, :]
    columns_ref[...] = turn[...].T
    lane = lanes_of(quarter)
    lane_residue = (pos * slots + lane % slots) % DILATION
    blank = jnp.where(lane < slots, LOWEST, 0.0)
    for residue in range(DILATION):
        spread[pl.ds(residue, quarter, stride=DILATION), :] = jnp.where(
            lane_residue == residue, columns_ref[:quarter], blank
        )
    across = spread[...].T
    e, d = merge_stats(
        near_ref[pl.ds(pos * slots, slots), :],
        near_ref[pl.ds(HEADS + pos * slots, slots), :],
        across[:slots],
        across[slots : 2 * slots],
    )
    xmsg_ref[:slots] = e
    xmsg_ref[slots : 2 * slots] = d
    xmsg_ref[2 * slots :] = far_ref[...]


def middle_parts_kernel(n_i, slots, *refs):
    mids, refs = refs[:n_i], refs[n_i:]
    stats_ref, columns_ref = refs[:2]
    refs = refs[2:]
    xmsgs, refs = refs[:slots], refs[slots:]
    outs, (far, turn, spread) = refs[:n_i], refs[n_i:]
    rows = xmsgs[0].shape[1]
    quarter = rows // DILATION
    pos, chip = position(slots)
    for m in range(slots):
        far[pl.ds(chip ^ m, 1), :] = xmsgs[m][2 * slots + m : 2 * slots + m + 1, :]
        far[pl.ds(slots + (chip ^ m), 1), :] = xmsgs[m][3 * slots + m : 3 * slots + m + 1, :]
    e, d = merge_stats(
        xmsgs[0][:slots], xmsgs[0][slots : 2 * slots], far[:slots], far[slots:]
    )
    spread[...] = jnp.zeros_like(spread)
    spread[pl.ds(pos * slots, slots), :] = e
    spread[pl.ds(HEADS + pos * slots, slots), :] = d
    spread[...] = spread[...].T
    own = pick_rows(spread, rows)
    turn[...] = jnp.concatenate([own] + [join(ref) for ref in mids[1:]], axis=0).T
    owned = lax.broadcasted_iota(jnp.int32, (1, n_i * quarter), 1) < quarter
    operands = [middle_operands(slots, mids, slot) for slot in range(slots)]
    merged = [
        merge_stats(
            turn[pl.ds(pos * slots + slot, 1), :],
            turn[pl.ds(HEADS + pos * slots + slot, 1), :],
            jnp.where(owned, LOWEST, stats_ref[slot : slot + 1, :]),
            stats_ref[slots + slot : slots + slot + 1, :],
        )
        for slot in range(slots)
    ]
    for slot, parts in enumerate(level_parts(operands, merged)):
        for which, part in enumerate(parts):
            part = part.astype(BF16)
            chunks = [part[d * quarter : (d + 1) * quarter] for d in range(n_i)]
            for out, chunk in zip(outs, in_back_order(n_i, chunks)):
                out[which * slots + slot] = chunk
    chunks = [columns_ref[d * quarter : (d + 1) * quarter] for d in range(n_i)]
    for out, chunk in zip(outs, in_back_order(n_i, chunks)):
        out[4 * slots] = split(chunk)


def far_parts_kernel(slots, width, *refs):
    fulls, refs = in_back(refs[:slots]), refs[slots:]
    sibs, refs = refs[: width - 1], refs[width - 1 :]
    xmsgs, refs = refs[:slots], refs[slots + 1 :]
    outs, refs = refs[:slots], refs[slots:]
    kvouts, refs = refs[: width - 1], refs[width - 1 :]
    weights, score_grads = refs
    rows = fulls[0].shape[1]
    _, chip = position(slots)
    keys, values = far_keys(fulls, sibs, 0), far_keys(fulls, sibs, 1)
    merged = [
        merge_stats(
            xmsgs[m][pl.ds(chip, 1), :],
            xmsgs[m][pl.ds(slots + chip, 1), :],
            xmsgs[0][2 * slots + m : 2 * slots + m + 1, :],
            xmsgs[0][3 * slots + m : 3 * slots + m + 1, :],
        )
        for m in range(slots)
    ]
    operands = [(keys, values, ref[2], ref[3]) for ref in fulls]
    found = level_weights(operands, merged)
    for m, (p, ds) in enumerate(found):
        weights[:, m * rows : (m + 1) * rows] = p
        score_grads[:, m * rows : (m + 1) * rows] = ds
    for m, (p, ds) in enumerate(found):
        outs[m][0] = dot_tn(p, values).astype(BF16)
        outs[m][1] = (dot_tn(ds, keys) * SCALE).astype(BF16)
    queries = jnp.concatenate([ref[2] for ref in fulls], axis=0)
    ups = jnp.concatenate([ref[3] for ref in fulls], axis=0)
    key_part = (dot(score_grads[...], queries) * SCALE).astype(BF16)
    value_part = dot(weights[...], ups).astype(BF16)
    for index in range(width * slots):
        block = slice(index * rows, (index + 1) * rows)
        part, m = index // slots, index % slots
        if part == 0:
            outs[m][2], outs[m][3] = key_part[block], value_part[block]
        else:
            kvouts[part - 1][m, 0], kvouts[part - 1][m, 1] = key_part[block], value_part[block]


def far_sum_kernel(slots, *refs):
    own, refs = refs[:slots], refs[slots:]
    found, outs = refs[: -slots - 1], refs[-slots:]
    for m in range(slots):
        outs[m][:2] = own[m][:2]
        total = own[m][2:].astype(F32)
        for ref in found:
            total += ref[m].astype(F32)
        outs[m][2:] = total.astype(BF16)


def near_statistics(n_i, slots, steps, near_ref, mids, xmsgs, stats_ref, spread):
    rows = near_ref.shape[1]
    quarter = rows // DILATION
    pos, chip = position(slots)
    lane = lanes_of(quarter)
    mid = jnp.zeros((quarter, LANES), F32)
    for step, ref in zip(steps, mids):
        place = first_back(n_i, slots, step)
        found = join(ref)
        e = pltpu.roll(found, place, 1)
        de = pltpu.roll(found, place + HEADS - slots, 1)
        mid = jnp.where((lane >= place) & (lane < place + slots), e, mid)
        mid = jnp.where((lane >= HEADS + place) & (lane < HEADS + place + slots), de, mid)
    blank = jnp.where(lane < HEADS, LOWEST, 0.0)
    for residue in range(DILATION):
        spread[pl.ds(residue, quarter, stride=DILATION), :] = jnp.where(
            lane % DILATION == residue, mid, blank
        )
    across = spread[...].T
    e, d = merge_stats(
        near_ref[:HEADS], near_ref[HEADS:], across[:HEADS], across[HEADS : 2 * HEADS]
    )
    if xmsgs:
        stats_ref[:HEADS] = jnp.full((HEADS, rows), LOWEST, F32)
        stats_ref[HEADS:] = jnp.zeros((HEADS, rows), F32)
        for m in range(slots):
            head = pos * slots + (chip ^ m)
            stats_ref[pl.ds(head, 1), :] = xmsgs[m][2 * slots + m : 2 * slots + m + 1, :]
            stats_ref[pl.ds(HEADS + head, 1), :] = xmsgs[m][3 * slots + m : 3 * slots + m + 1, :]
        e, d = merge_stats(e, d, stats_ref[:HEADS], stats_ref[HEADS:])
    stats_ref[:HEADS] = e
    stats_ref[HEADS:] = d


def near_place(n_i, slots, step, sources, stats_ref):
    heads = [first_back(n_i, slots, step) + slot for slot in range(slots)]
    operands = [[ref[:, head_columns(head)] for ref in sources] for head in heads]
    stats = [(stats_ref[pl.ds(head, 1), :], stats_ref[pl.ds(HEADS + head, 1), :]) for head in heads]
    return level_parts(operands, stats)


def near_early_kernel(n_i, slots, *refs):
    sources, near_ref, refs = refs[:4], refs[4], refs[5:]
    mids, refs = refs[: n_i - 1], refs[n_i - 1 :]
    xmsgs, (out_ref, stats_ref, spread) = refs[:slots], refs[slots:]
    near_statistics(n_i, slots, range(n_i - 1), near_ref, mids, xmsgs, stats_ref, spread)
    for step in range(n_i - 1):
        for slot, parts in enumerate(near_place(n_i, slots, step, sources, stats_ref)):
            for which, part in enumerate(parts):
                out_ref[which, step * slots + slot] = part


def far_sum_kernel(slots, *refs):
    own, refs = refs[:slots], refs[slots:]
    found, outs = refs[: -slots - 1], refs[-slots:]
    for m in range(slots):
        outs[m][:2] = own[m][:2]
        total = own[m][2:].astype(F32)
        for ref in found:
            total += ref[m].astype(F32)
        outs[m][2:] = total.astype(BF16)


def near_parts_kernel(n_i, slots, *refs):
    sources, near_ref, refs = refs[:4], refs[4], refs[5:]
    mids, refs = (refs[0], *refs[n_i - 1 : 0 : -1]), refs[n_i:]
    xmsgs, (out_ref, stats_ref, spread) = refs[:slots], refs[slots:]
    rows = near_ref.shape[1]
    quarter = rows // DILATION
    pos, chip = position(slots)
    lane = lanes_of(quarter)
    mid = jnp.zeros((quarter, LANES), F32)
    for d in range(n_i):
        place = (pos ^ d) * slots
        found = join(mids[d])
        e = pltpu.roll(found, place, 1)
        de = pltpu.roll(found, place + HEADS - slots, 1)
        mid = jnp.where((lane >= place) & (lane < place + slots), e, mid)
        mid = jnp.where((lane >= HEADS + place) & (lane < HEADS + place + slots), de, mid)
    blank = jnp.where(lane < HEADS, LOWEST, 0.0)
    for residue in range(DILATION):
        spread[pl.ds(residue, quarter, stride=DILATION), :] = jnp.where(
            lane % DILATION == residue, mid, blank
        )
    across = spread[...].T
    stats_ref[:HEADS] = jnp.full((HEADS, rows), LOWEST, F32)
    stats_ref[HEADS:] = jnp.zeros((HEADS, rows), F32)
    for m in range(slots):
        head = pos * slots + (chip ^ m)
        stats_ref[pl.ds(head, 1), :] = xmsgs[m][2 * slots + m : 2 * slots + m + 1, :]
        stats_ref[pl.ds(HEADS + head, 1), :] = xmsgs[m][3 * slots + m : 3 * slots + m + 1, :]
    e, d = merge_stats(
        near_ref[:HEADS], near_ref[HEADS:], across[:HEADS], across[HEADS : 2 * HEADS]
    )
    e, d = merge_stats(e, d, stats_ref[:HEADS], stats_ref[HEADS:])
    stats_ref[:HEADS] = e
    stats_ref[HEADS:] = d
    for group in range(HEADS // DILATION):
        heads = range(group * DILATION, (group + 1) * DILATION)
        operands = [
            [ref[:, static_columns(head)] for ref in sources] for head in heads
        ]
        stats = [
            (stats_ref[head : head + 1, :], stats_ref[HEADS + head : HEADS + head + 1, :])
            for head in heads
        ]
        for head, parts in zip(heads, level_parts(operands, stats)):
            for which, part in enumerate(parts):
                out_ref[which, head] = part


def spread_rows(slots, head, slot, ref):
    quarter = ref.shape[1]
    rows = quarter * DILATION
    row = lax.broadcasted_iota(jnp.int32, (rows, quarter), 0)
    taken = lax.broadcasted_iota(jnp.int32, (rows, quarter), 1) * DILATION
    place = jnp.where(row == taken + head % DILATION, 1.0, 0.0).astype(BF16)
    return dot(place, jnp.concatenate([ref[which * slots + slot] for which in range(4)], axis=1))


def send_place(slots, first, ready, outs, sems):
    width = slots * HEAD_DIM
    cols = pl.ds(pl.multiple_of(first * HEAD_DIM, width), width)
    copies = [
        pltpu.make_async_copy(ready.at[which], out.at[:, cols], sems.at[which])
        for which, out in enumerate(outs)
    ]
    for copy in copies:
        copy.start()
    return copies


def final_others_kernel(n_i, slots, *refs):
    sources, near_ref, early_ref, refs = refs[:4], refs[4], refs[5], refs[6:]
    mids, refs = refs[: n_i - 1], refs[n_i - 1 :]
    outs, (ready, sems, stats_ref, spread) = refs[:4], refs[4:]
    last = n_i - 1
    copies = []
    for step in range(1, n_i):
        first = first_back(n_i, slots, step)
        found = [spread_rows(slots, first + slot, slot, mids[step - 1]) for slot in range(slots)]
        if step == last:
            near_statistics(n_i, slots, [last], near_ref, mids[-1:], (), stats_ref, spread)
            late = near_place(n_i, slots, last, sources, stats_ref)
        for slot, parts in enumerate(found):
            for which in range(4):
                near = late[slot][which] if step == last else early_ref[which, step * slots + slot]
                total = near + parts[:, static_columns(which)]
                ready[step - 1, which, :, static_columns(slot)] = total.astype(BF16)
        copies += send_place(slots, first, ready.at[step - 1], outs, sems.at[step - 1])
    for copy in copies:
        copy.wait()


def final_own_kernel(slots, early_ref, mid_ref, *refs):
    fulls, refs = in_back(refs[:slots]), refs[slots:]
    outs, (ready, sems) = refs[4:8], refs[8:]
    pos, chip = position(slots)
    first = pos * slots
    found = [spread_rows(slots, first + (chip ^ m), chip ^ m, mid_ref) for m in range(slots)]
    for m, parts in enumerate(found):
        slot = chip ^ m
        for which in range(4):
            total = early_ref[which, slot] + parts[:, static_columns(which)]
            total += fulls[m][which].astype(F32)
            ready[which, :, head_columns(slot)] = total.astype(BF16)
    for copy in send_place(slots, first, ready, outs, sems):
        copy.wait()


def settle_kernel(*refs):
    refs[-1][...] = jnp.zeros_like(refs[-1])


def call(kernel, name, outs, scratch, flops, operands, hbm_in=(), hbm_out=False, cheap=False, limit=VMEM_LIMIT, aliases=None):
    moved = sum(x.size * x.dtype.itemsize for x in tuple(operands) + tuple(outs))
    if cheap:
        flops, moved = 1, 1
    spaces = [pltpu.HBM if i in hbm_in else pltpu.VMEM for i in range(len(operands))]
    return pl.pallas_call(
        kernel,
        out_shape=tuple(outs),
        in_specs=[pl.BlockSpec(memory_space=space) for space in spaces],
        out_specs=tuple(
            pl.BlockSpec(memory_space=pltpu.HBM if hbm_out else pltpu.VMEM) for _ in outs
        ),
        scratch_shapes=scratch,
        input_output_aliases=aliases or {},
        compiler_params=pltpu.CompilerParams(vmem_limit_bytes=limit),
        cost_estimate=pl.CostEstimate(flops=flops, bytes_accessed=moved, transcendentals=0),
        name=name,
    )(*operands)


def in_back(pieces):
    return [pieces[0], *pieces[:0:-1]]


def swap(x, axis, n, mask):
    return lax.ppermute(x, axis, [(i, i ^ mask) for i in range(n)])


def local(query_rows, key_rows, value_rows, upstream):
    rows, features = query_rows.shape
    n_i, n_o = lax.axis_size("seqi"), lax.axis_size("seqo")
    slots = HEADS // n_i
    width = n_o // slots
    others = (width - 1) * slots
    quarter = rows // DILATION
    sources = (key_rows, value_rows, query_rows, upstream)
    unit = 2 * rows * rows * HEAD_DIM
    bind = functools.partial

    mid = SHAPE((4 * slots + 1, quarter, HEAD_DIM), BF16)
    full = SHAPE((4, rows, HEAD_DIM), BF16)
    half = SHAPE((slots, 2, rows, HEAD_DIM), BF16)
    square = pltpu.VMEM((LANES, rows), F32)

    def stats(count, lanes=rows):
        return SHAPE((count, lanes), F32)

    def swap_mids(pieces):
        return [pieces[0]] + [
            swap(pieces[step], "seqi", n_i, distance(n_i, step)) for step in range(1, n_i)
        ]

    def swap_back(pieces):
        return [pieces[0]] + [
            swap(pieces[step], "seqi", n_i, distance_back(n_i, step)) for step in range(1, n_i)
        ]

    def swap_fulls(pieces):
        return [pieces[0]] + [swap(pieces[m], "seqo", n_o, m * width) for m in range(1, slots)]

    def pick_scratch(count):
        return [
            pltpu.VMEM((count, 4, rows, slots * HEAD_DIM), BF16),
            pltpu.SemaphoreType.DMA((count, 4)),
            pltpu.VMEM((count, 4, slots, rows, HEAD_DIM), F32),
            square,
        ]

    first, own, *fulls, firststats = call(
        bind(pick_first_kernel, n_i, slots),
        "pick_first",
        [mid, mid] + [full] * slots + [stats(2 * HEADS)],
        pick_scratch(2),
        unit * slots * 4,
        sources,
        hbm_in=range(4),
        limit=FIRST_LIMIT,
    )
    *pieces, near = call(
        bind(pick_rest_kernel, n_i, slots),
        "pick_rest",
        [mid] * (n_i - 2) + [stats(2 * HEADS)],
        pick_scratch(n_i - 2),
        unit * HEADS * 2,
        [*sources, firststats],
        hbm_in=range(4),
        limit=PICK_LIMIT,
    )
    mids = swap_mids([own, first, *pieces])
    fulls = swap_fulls(fulls)

    (settled,) = call(settle_kernel, "far_in", [stats(8)], [], SHORT, [mids[1]])
    (settled,) = call(settle_kernel, "chips_back", [stats(8)], [], LONG, [settled])
    (packed,) = call(bind(pack_kernel, slots), "pack", [half], [], 1, [*in_back(fulls), settled])
    sibs = [swap(packed, "seqo", n_o, part) for part in range(1, width)]
    (settled,) = call(settle_kernel, "packed_back", [stats(8)], [], LONG, [near])
    (far,) = call(
        bind(far_stats_kernel, slots),
        "far_stats",
        [stats(2 * slots)],
        [],
        1,
        [*in_back(fulls), *sibs, settled],
    )
    xmsg, middle, columns = call(
        bind(middle_stats_kernel, n_i, slots),
        "middle_stats",
        [stats(4 * slots), stats(2 * slots, n_i * quarter), stats(n_i * quarter, LANES)],
        [pltpu.VMEM((LANES, n_i * quarter), F32), square],
        unit * slots * 2,
        mids + [near, far],
    )
    xmsgs = swap_fulls([xmsg] * slots)

    midparts = call(
        bind(middle_parts_kernel, n_i, slots),
        "middle_parts",
        [mid] * n_i,
        [pltpu.VMEM((2 * slots, rows), F32), pltpu.VMEM((LANES, n_i * quarter), F32), square],
        unit * slots * 6,
        mids + [middle, columns] + xmsgs,
    )
    midparts = swap_back(midparts)
    farparts = call(
        bind(far_parts_kernel, slots, width),
        "far_parts",
        [full] * slots + [half] * (width - 1),
        [pltpu.VMEM((n_o * rows, slots * rows), BF16)] * 2,
        unit * n_o * slots * 6,
        [*in_back(fulls), *sibs, *xmsgs, midparts[0]],
        cheap=True,
    )
    sibparts = [swap(x, "seqo", n_o, part + 1) for part, x in enumerate(farparts[slots:])]
    (settled,) = call(settle_kernel, "far_back", [stats(8)], [], SHORT, [midparts[1]])
    (settled,) = call(settle_kernel, "sib_back", [stats(8)], [], 1, sibparts + [settled])
    (settled,) = call(settle_kernel, "settle", [stats(8)], [], LONG, [settled])
    fullparts = call(
        bind(far_sum_kernel, slots),
        "far_sum",
        [full] * slots,
        [],
        unit,
        list(farparts[:slots]) + sibparts + [settled],
        cheap=True,
    )
    fullparts = swap_fulls(fullparts)

    back = midparts
    kept = [pltpu.VMEM((2 * HEADS, rows), F32), square]
    (early,) = call(
        bind(near_early_kernel, n_i, slots),
        "near_early",
        [SHAPE((4, (n_i - 1) * slots, rows, HEAD_DIM), F32)],
        kept,
        SHORT,
        [*sources, near, *back[:-1], *xmsgs],
    )
    whole = [SHAPE((rows, features), BF16)] * 4
    outs = call(
        bind(final_others_kernel, n_i, slots),
        "final_others",
        whole,
        [
            pltpu.VMEM((n_i - 1, 4, rows, slots * HEAD_DIM), BF16),
            pltpu.SemaphoreType.DMA((n_i - 1, 4)),
            *kept,
        ],
        SHORT // 2,
        [*sources, near, early, *back[1:]],
        hbm_out=True,
    )
    return call(
        bind(final_own_kernel, slots),
        "final_own",
        whole,
        [pltpu.VMEM((4, rows, slots * HEAD_DIM), BF16), pltpu.SemaphoreType.DMA((4,))],
        unit * slots,
        [early, midparts[0], *in_back(fullparts), *outs],
        hbm_in=range(2 + slots, 6 + slots),
        hbm_out=True,
        aliases={2 + slots + which: which for which in range(4)},
    )


def solution(mesh):
    rows = P(("seqo", "seqi"), None)
    return jax.shard_map(
        local,
        mesh=mesh,
        in_specs=(rows,) * 4,
        out_specs=(rows,) * 4,
        check_vma=False,
    )
```

```python
import functools

import jax
import jax.numpy as jnp
from jax import lax
from jax.experimental import pallas as pl
from jax.experimental.pallas import tpu as pltpu
from jax.sharding import PartitionSpec as P

HEADS = 16
HEAD_DIM = 128
DILATION = 4
LANES = 128
SCALE = HEAD_DIM**-0.5
LOWEST = -1e30
LONG = 4 * 10**10
SHORT = 2 * 10**9
VMEM_LIMIT = 32 * 1024 * 1024
PICK_LIMIT = 54784 * 1024
FIRST_LIMIT = 54272 * 1024
NEAR_LIMIT = 54784 * 1024
F32, BF16 = jnp.float32, jnp.bfloat16
SHAPE = jax.ShapeDtypeStruct

NT = (((1,), (1,)), ((), ()))
TN = (((0,), (0,)), ((), ()))


def dot(a, b):
    return jnp.dot(a, b, preferred_element_type=F32)


def dot_nt(a, b):
    return lax.dot_general(a, b, NT, preferred_element_type=F32)


def dot_tn(a, b):
    return lax.dot_general(a, b, TN, preferred_element_type=F32)


def head_columns(head):
    return pl.ds(pl.multiple_of(head * HEAD_DIM, HEAD_DIM), HEAD_DIM)


def static_columns(index):
    return slice(index * HEAD_DIM, (index + 1) * HEAD_DIM)


def position(slots):
    width = lax.axis_size("seqo") // slots
    return lax.axis_index("seqi"), lax.axis_index("seqo") // width


def distance(n_i, step):
    return n_i - step


def distance_back(n_i, step):
    return n_i - 1 if step == 1 else step - 1


def place_in(n_i, slots, step):
    pos, _ = position(slots)
    return pos if step == 0 else pos ^ distance(n_i, step)


def first_back(n_i, slots, step):
    pos, _ = position(slots)
    return (pos if step == 0 else pos ^ distance_back(n_i, step)) * slots


def in_back_order(n_i, chunks):
    order = [distance(n_i, step) for step in range(1, n_i)]
    return [chunks[0]] + [
        chunks[order.index(distance_back(n_i, step)) + 1] for step in range(1, n_i)
    ]


def lanes_of(rows):
    return lax.broadcasted_iota(jnp.int32, (rows, LANES), 1)


def level_stats(operands):
    products = [(dot_nt(k, q) * SCALE, dot_nt(v, u)) for k, v, q, u in operands]
    tops = [jnp.max(s, axis=0, keepdims=True) for s, _ in products]
    weights = [jnp.exp(s - top) for (s, _), top in zip(products, tops)]
    totals = [jnp.sum(p, axis=0, keepdims=True) for p in weights]
    return [
        (top + jnp.log(total), jnp.sum(p * dp, axis=0, keepdims=True) / total)
        for (_, dp), top, p, total in zip(products, tops, weights, totals)
    ]


def merge_stats(ea, da, eb, db):
    top = jnp.maximum(ea, eb)
    wa, wb = jnp.exp(ea - top), jnp.exp(eb - top)
    total = wa + wb
    return top + jnp.log(total), (wa * da + wb * db) / total


def level_weights(operands, stats):
    products = [(dot_nt(k, q) * SCALE, dot_nt(v, u)) for k, v, q, u in operands]
    found = []
    for (s, dp), (lse, delta) in zip(products, stats):
        g = jnp.exp(s - lse)
        found.append((g.astype(BF16), (g * (dp - delta)).astype(BF16)))
    return found


def level_parts(operands, stats):
    found = level_weights(operands, stats)
    keyed = [
        (dot(ds, q) * SCALE, dot(p, u)) for (p, ds), (k, v, q, u) in zip(found, operands)
    ]
    queried = [
        (dot_tn(p, v), dot_tn(ds, k) * SCALE) for (p, ds), (k, v, q, u) in zip(found, operands)
    ]
    return [a + b for a, b in zip(queried, keyed)]


def pick_rows(ref, rows):
    quarter = rows // DILATION
    lane = lanes_of(quarter)
    picked = jnp.zeros((quarter, LANES), F32)
    for residue in range(DILATION):
        part = ref[pl.ds(residue, quarter, stride=DILATION), :]
        picked = jnp.where(lane % DILATION == residue, part, picked)
    return picked


def fetch(slots, places, sources, buffers, sems):
    width = slots * HEAD_DIM
    groups = []
    for index, place in enumerate(places):
        cols = pl.ds(pl.multiple_of(place * width, width), width)
        groups.append(
            [
                pltpu.make_async_copy(
                    source.at[:, cols], buffers.at[index, which], sems.at[index, which]
                )
                for which, source in enumerate(sources)
            ]
        )
        for copy in groups[-1]:
            copy.start()
    return groups


def split(x):
    high = x.astype(BF16).astype(F32)
    rest = x - high
    middle = rest.astype(BF16).astype(F32)
    low = rest - middle
    return (high + pltpu.roll(middle, 2 * HEADS, 1) + pltpu.roll(low, 4 * HEADS, 1)).astype(BF16)


def join(ref):
    x = ref[ref.shape[0] - 1].astype(F32)
    x = x + (pltpu.roll(x, LANES - 2 * HEADS, 1) + pltpu.roll(x, LANES - 4 * HEADS, 1))
    return jnp.where(lanes_of(x.shape[0]) < 2 * HEADS, x, 0.0)


def pick_places(n_i, slots, steps, sources, mids, buffers, sems, wide, turn):
    rows = sources[0].shape[0]
    quarter = rows // DILATION
    places = [place_in(n_i, slots, step) for step in steps]
    for index, copies in enumerate(fetch(slots, places, sources, buffers, sems)):
        first = places[index] * slots
        for which, copy in enumerate(copies):
            copy.wait()
            for slot in range(slots):
                wide[index, which, slot] = buffers[index, which, :, static_columns(slot)].astype(F32)
                residue = (first + slot) % DILATION if slots % DILATION else slot % DILATION
                rowset = wide[index, which, slot, pl.ds(residue, quarter, stride=DILATION), :]
                mids[index][which * slots + slot] = rowset.astype(BF16)
        operands = [
            [buffers[index, which, :, static_columns(slot)] for which in range(4)]
            for slot in range(slots)
        ]
        for slot, (e, d) in enumerate(level_stats(operands)):
            turn[pl.ds(first + slot, 1), :] = e
            turn[pl.ds(HEADS + first + slot, 1), :] = d


def pick_first_kernel(n_i, slots, *refs):
    sources, (mid_ref, own_ref, *refs) = refs[:4], refs[4:]
    fulls, (stats_ref, buffers, sems, wide, turn) = refs[:slots], refs[slots:]
    rows = sources[0].shape[0]
    _, chip = position(slots)
    turn[...] = jnp.zeros_like(turn)
    pick_places(n_i, slots, [1, 0], sources, [mid_ref, own_ref], buffers, sems, wide, turn)
    for m in range(slots):
        fulls[m][...] = buffers[1, :, :, head_columns(chip ^ m)]
    stats_ref[...] = turn[: 2 * HEADS, :]
    turn[...] = turn[...].T
    near = split(pick_rows(turn, rows))
    mid_ref[4 * slots] = near
    own_ref[4 * slots] = near


def pick_rest_kernel(n_i, slots, *refs):
    sources, first_ref, refs = refs[:4], refs[4], refs[5:]
    mids, refs = refs[: n_i - 2], refs[n_i - 2 :]
    stats_ref, buffers, sems, wide, turn = refs
    rows = sources[0].shape[0]
    turn[...] = jnp.zeros_like(turn)
    turn[: 2 * HEADS, :] = first_ref[...]
    pick_places(n_i, slots, range(2, n_i), sources, mids, buffers, sems, wide, turn)
    stats_ref[...] = turn[: 2 * HEADS, :]
    turn[...] = turn[...].T
    near = split(pick_rows(turn, rows))
    for ref in mids:
        ref[4 * slots] = near


def pack_kernel(slots, *refs):
    packed_ref = refs[-1]
    for m, ref in enumerate(in_back(refs[:slots])):
        packed_ref[m] = ref[:2]


def far_keys(fulls, sibs, which):
    blocks = [ref[which] for ref in fulls]
    return jnp.concatenate(blocks + [ref[m, which] for ref in sibs for m in range(len(fulls))], axis=0)


def far_stats_kernel(slots, *refs):
    fulls, sibs, stats_ref = in_back(refs[:slots]), refs[slots:-2], refs[-1]
    keys, values = far_keys(fulls, sibs, 0), far_keys(fulls, sibs, 1)
    operands = [(keys, values, ref[2], ref[3]) for ref in fulls]
    for m, (e, d) in enumerate(level_stats(operands)):
        stats_ref[m : m + 1, :] = e
        stats_ref[slots + m : slots + m + 1, :] = d


def middle_operands(slots, mids, slot):
    return [
        jnp.concatenate([ref[which * slots + slot] for ref in mids], axis=0) for which in range(4)
    ]


def middle_stats_kernel(n_i, slots, *refs):
    mids, refs = refs[:n_i], refs[n_i:]
    near_ref, far_ref, xmsg_ref, stats_ref, columns_ref, turn, spread = refs
    rows = near_ref.shape[1]
    quarter = rows // DILATION
    pos, _ = position(slots)
    turn[...] = jnp.zeros_like(turn)
    operands = [middle_operands(slots, mids, slot) for slot in range(slots)]
    for slot, (e, d) in enumerate(level_stats(operands)):
        turn[slot : slot + 1, :] = e
        turn[slots + slot : slots + slot + 1, :] = d
    stats_ref[...] = turn[: 2 * slots, :]
    columns_ref[...] = turn[...].T
    lane = lanes_of(quarter)
    lane_residue = (pos * slots + lane % slots) % DILATION
    blank = jnp.where(lane < slots, LOWEST, 0.0)
    for residue in range(DILATION):
        spread[pl.ds(residue, quarter, stride=DILATION), :] = jnp.where(
            lane_residue == residue, columns_ref[:quarter], blank
        )
    across = spread[...].T
    e, d = merge_stats(
        near_ref[pl.ds(pos * slots, slots), :],
        near_ref[pl.ds(HEADS + pos * slots, slots), :],
        across[:slots],
        across[slots : 2 * slots],
    )
    xmsg_ref[:slots] = e
    xmsg_ref[slots : 2 * slots] = d
    xmsg_ref[2 * slots :] = far_ref[...]


def middle_parts_kernel(n_i, slots, *refs):
    mids, refs = refs[:n_i], refs[n_i:]
    stats_ref, columns_ref = refs[:2]
    refs = refs[2:]
    xmsgs, refs = in_back(refs[:slots]), refs[slots:]
    outs, (far, turn, spread) = refs[:n_i], refs[n_i:]
    rows = xmsgs[0].shape[1]
    quarter = rows // DILATION
    pos, chip = position(slots)
    for m in range(slots):
        far[pl.ds(chip ^ m, 1), :] = xmsgs[m][2 * slots + m : 2 * slots + m + 1, :]
        far[pl.ds(slots + (chip ^ m), 1), :] = xmsgs[m][3 * slots + m : 3 * slots + m + 1, :]
    e, d = merge_stats(
        xmsgs[0][:slots], xmsgs[0][slots : 2 * slots], far[:slots], far[slots:]
    )
    spread[...] = jnp.zeros_like(spread)
    spread[pl.ds(pos * slots, slots), :] = e
    spread[pl.ds(HEADS + pos * slots, slots), :] = d
    spread[...] = spread[...].T
    own = pick_rows(spread, rows)
    turn[...] = jnp.concatenate([own] + [join(ref) for ref in mids[1:]], axis=0).T
    owned = lax.broadcasted_iota(jnp.int32, (1, n_i * quarter), 1) < quarter
    operands = [middle_operands(slots, mids, slot) for slot in range(slots)]
    merged = [
        merge_stats(
            turn[pl.ds(pos * slots + slot, 1), :],
            turn[pl.ds(HEADS + pos * slots + slot, 1), :],
            jnp.where(owned, LOWEST, stats_ref[slot : slot + 1, :]),
            stats_ref[slots + slot : slots + slot + 1, :],
        )
        for slot in range(slots)
    ]
    for slot, parts in enumerate(level_parts(operands, merged)):
        for which, part in enumerate(parts):
            part = part.astype(BF16)
            chunks = [part[d * quarter : (d + 1) * quarter] for d in range(n_i)]
            for out, chunk in zip(outs, in_back_order(n_i, chunks)):
                out[which * slots + slot] = chunk
    chunks = [columns_ref[d * quarter : (d + 1) * quarter] for d in range(n_i)]
    for out, chunk in zip(outs, in_back_order(n_i, chunks)):
        out[4 * slots] = split(chunk)


def far_parts_kernel(slots, width, *refs):
    fulls, refs = in_back(refs[:slots]), refs[slots:]
    sibs, refs = refs[: width - 1], refs[width - 1 :]
    xmsgs, refs = in_back(refs[:slots]), refs[slots + 1 :]
    outs, refs = refs[:slots], refs[slots:]
    kvouts, refs = refs[: width - 1], refs[width - 1 :]
    weights, score_grads = refs
    rows = fulls[0].shape[1]
    _, chip = position(slots)
    keys, values = far_keys(fulls, sibs, 0), far_keys(fulls, sibs, 1)
    merged = [
        merge_stats(
            xmsgs[m][pl.ds(chip, 1), :],
            xmsgs[m][pl.ds(slots + chip, 1), :],
            xmsgs[0][2 * slots + m : 2 * slots + m + 1, :],
            xmsgs[0][3 * slots + m : 3 * slots + m + 1, :],
        )
        for m in range(slots)
    ]
    operands = [(keys, values, ref[2], ref[3]) for ref in fulls]
    found = level_weights(operands, merged)
    for m, (p, ds) in enumerate(found):
        weights[:, m * rows : (m + 1) * rows] = p
        score_grads[:, m * rows : (m + 1) * rows] = ds
    for m, (p, ds) in enumerate(found):
        outs[m][0] = dot_tn(p, values).astype(BF16)
        outs[m][1] = (dot_tn(ds, keys) * SCALE).astype(BF16)
    queries = jnp.concatenate([ref[2] for ref in fulls], axis=0)
    ups = jnp.concatenate([ref[3] for ref in fulls], axis=0)
    key_part = (dot(score_grads[...], queries) * SCALE).astype(BF16)
    value_part = dot(weights[...], ups).astype(BF16)
    for index in range(width * slots):
        block = slice(index * rows, (index + 1) * rows)
        part, m = index // slots, index % slots
        if part == 0:
            outs[m][2], outs[m][3] = key_part[block], value_part[block]
        else:
            kvouts[part - 1][m, 0], kvouts[part - 1][m, 1] = key_part[block], value_part[block]


def far_sum_kernel(slots, *refs):
    own, refs = refs[:slots], refs[slots:]
    found, outs = refs[: -slots - 1], refs[-slots:]
    for m in range(slots):
        outs[m][:2] = own[m][:2]
        total = own[m][2:].astype(F32)
        for ref in found:
            total += ref[m].astype(F32)
        outs[m][2:] = total.astype(BF16)


def near_statistics(n_i, slots, steps, near_ref, mids, xmsgs, stats_ref, spread):
    rows = near_ref.shape[1]
    quarter = rows // DILATION
    pos, chip = position(slots)
    lane = lanes_of(quarter)
    mid = jnp.zeros((quarter, LANES), F32)
    for step, ref in zip(steps, mids):
        place = first_back(n_i, slots, step)
        found = join(ref)
        e = pltpu.roll(found, place, 1)
        de = pltpu.roll(found, place + HEADS - slots, 1)
        mid = jnp.where((lane >= place) & (lane < place + slots), e, mid)
        mid = jnp.where((lane >= HEADS + place) & (lane < HEADS + place + slots), de, mid)
    blank = jnp.where(lane < HEADS, LOWEST, 0.0)
    for residue in range(DILATION):
        spread[pl.ds(residue, quarter, stride=DILATION), :] = jnp.where(
            lane % DILATION == residue, mid, blank
        )
    across = spread[...].T
    e, d = merge_stats(
        near_ref[:HEADS], near_ref[HEADS:], across[:HEADS], across[HEADS : 2 * HEADS]
    )
    if xmsgs:
        stats_ref[:HEADS] = jnp.full((HEADS, rows), LOWEST, F32)
        stats_ref[HEADS:] = jnp.zeros((HEADS, rows), F32)
        for m in range(slots):
            head = pos * slots + (chip ^ m)
            stats_ref[pl.ds(head, 1), :] = xmsgs[m][2 * slots + m : 2 * slots + m + 1, :]
            stats_ref[pl.ds(HEADS + head, 1), :] = xmsgs[m][3 * slots + m : 3 * slots + m + 1, :]
        e, d = merge_stats(e, d, stats_ref[:HEADS], stats_ref[HEADS:])
    stats_ref[:HEADS] = e
    stats_ref[HEADS:] = d


def near_place(n_i, slots, step, sources, stats_ref):
    heads = [first_back(n_i, slots, step) + slot for slot in range(slots)]
    operands = [[ref[:, head_columns(head)] for ref in sources] for head in heads]
    stats = [(stats_ref[pl.ds(head, 1), :], stats_ref[pl.ds(HEADS + head, 1), :]) for head in heads]
    return level_parts(operands, stats)


def near_early_kernel(n_i, slots, *refs):
    sources, near_ref, refs = refs[:4], refs[4], refs[5:]
    mids, refs = refs[: n_i - 1], refs[n_i - 1 :]
    xmsgs, (out_ref, stats_ref, spread) = in_back(refs[:slots]), refs[slots:]
    near_statistics(n_i, slots, range(n_i - 1), near_ref, mids, xmsgs, stats_ref, spread)
    for step in range(n_i - 1):
        for slot, parts in enumerate(near_place(n_i, slots, step, sources, stats_ref)):
            for which, part in enumerate(parts):
                out_ref[which, step * slots + slot] = part


def far_sum_kernel(slots, *refs):
    own, refs = refs[:slots], refs[slots:]
    found, outs = refs[: -slots - 1], refs[-slots:]
    for m in range(slots):
        outs[m][:2] = own[m][:2]
        total = own[m][2:].astype(F32)
        for ref in found:
            total += ref[m].astype(F32)
        outs[m][2:] = total.astype(BF16)


def near_parts_kernel(n_i, slots, *refs):
    sources, near_ref, refs = refs[:4], refs[4], refs[5:]
    mids, refs = (refs[0], *refs[n_i - 1 : 0 : -1]), refs[n_i:]
    xmsgs, (out_ref, stats_ref, spread) = refs[:slots], refs[slots:]
    rows = near_ref.shape[1]
    quarter = rows // DILATION
    pos, chip = position(slots)
    lane = lanes_of(quarter)
    mid = jnp.zeros((quarter, LANES), F32)
    for d in range(n_i):
        place = (pos ^ d) * slots
        found = join(mids[d])
        e = pltpu.roll(found, place, 1)
        de = pltpu.roll(found, place + HEADS - slots, 1)
        mid = jnp.where((lane >= place) & (lane < place + slots), e, mid)
        mid = jnp.where((lane >= HEADS + place) & (lane < HEADS + place + slots), de, mid)
    blank = jnp.where(lane < HEADS, LOWEST, 0.0)
    for residue in range(DILATION):
        spread[pl.ds(residue, quarter, stride=DILATION), :] = jnp.where(
            lane % DILATION == residue, mid, blank
        )
    across = spread[...].T
    stats_ref[:HEADS] = jnp.full((HEADS, rows), LOWEST, F32)
    stats_ref[HEADS:] = jnp.zeros((HEADS, rows), F32)
    for m in range(slots):
        head = pos * slots + (chip ^ m)
        stats_ref[pl.ds(head, 1), :] = xmsgs[m][2 * slots + m : 2 * slots + m + 1, :]
        stats_ref[pl.ds(HEADS + head, 1), :] = xmsgs[m][3 * slots + m : 3 * slots + m + 1, :]
    e, d = merge_stats(
        near_ref[:HEADS], near_ref[HEADS:], across[:HEADS], across[HEADS : 2 * HEADS]
    )
    e, d = merge_stats(e, d, stats_ref[:HEADS], stats_ref[HEADS:])
    stats_ref[:HEADS] = e
    stats_ref[HEADS:] = d
    for group in range(HEADS // DILATION):
        heads = range(group * DILATION, (group + 1) * DILATION)
        operands = [
            [ref[:, static_columns(head)] for ref in sources] for head in heads
        ]
        stats = [
            (stats_ref[head : head + 1, :], stats_ref[HEADS + head : HEADS + head + 1, :])
            for head in heads
        ]
        for head, parts in zip(heads, level_parts(operands, stats)):
            for which, part in enumerate(parts):
                out_ref[which, head] = part


def spread_rows(slots, head, slot, ref):
    quarter = ref.shape[1]
    rows = quarter * DILATION
    row = lax.broadcasted_iota(jnp.int32, (rows, quarter), 0)
    taken = lax.broadcasted_iota(jnp.int32, (rows, quarter), 1) * DILATION
    place = jnp.where(row == taken + head % DILATION, 1.0, 0.0).astype(BF16)
    return dot(place, jnp.concatenate([ref[which * slots + slot] for which in range(4)], axis=1))


def send_place(slots, first, ready, outs, sems):
    width = slots * HEAD_DIM
    cols = pl.ds(pl.multiple_of(first * HEAD_DIM, width), width)
    copies = [
        pltpu.make_async_copy(ready.at[which], out.at[:, cols], sems.at[which])
        for which, out in enumerate(outs)
    ]
    for copy in copies:
        copy.start()
    return copies


def final_others_kernel(n_i, slots, *refs):
    sources, near_ref, early_ref, refs = refs[:4], refs[4], refs[5], refs[6:]
    mids, refs = refs[: n_i - 1], refs[n_i - 1 :]
    outs, (ready, sems, stats_ref, spread) = refs[:4], refs[4:]
    last = n_i - 1
    copies = []
    for step in range(1, n_i):
        first = first_back(n_i, slots, step)
        found = [spread_rows(slots, first + slot, slot, mids[step - 1]) for slot in range(slots)]
        if step == last:
            near_statistics(n_i, slots, [last], near_ref, mids[-1:], (), stats_ref, spread)
            late = near_place(n_i, slots, last, sources, stats_ref)
        for slot, parts in enumerate(found):
            for which in range(4):
                near = late[slot][which] if step == last else early_ref[which, step * slots + slot]
                total = near + parts[:, static_columns(which)]
                ready[step - 1, which, :, static_columns(slot)] = total.astype(BF16)
        copies += send_place(slots, first, ready.at[step - 1], outs, sems.at[step - 1])
    for copy in copies:
        copy.wait()


def final_own_kernel(slots, early_ref, mid_ref, *refs):
    fulls, refs = in_back(refs[:slots]), refs[slots:]
    outs, (ready, sems) = refs[4:8], refs[8:]
    pos, chip = position(slots)
    first = pos * slots
    found = [spread_rows(slots, first + (chip ^ m), chip ^ m, mid_ref) for m in range(slots)]
    for m, parts in enumerate(found):
        slot = chip ^ m
        for which in range(4):
            total = early_ref[which, slot] + parts[:, static_columns(which)]
            total += fulls[m][which].astype(F32)
            ready[which, :, head_columns(slot)] = total.astype(BF16)
    for copy in send_place(slots, first, ready, outs, sems):
        copy.wait()


def settle_kernel(*refs):
    refs[-1][...] = jnp.zeros_like(refs[-1])


def call(kernel, name, outs, scratch, flops, operands, hbm_in=(), hbm_out=False, cheap=False, limit=VMEM_LIMIT, aliases=None):
    moved = sum(x.size * x.dtype.itemsize for x in tuple(operands) + tuple(outs))
    if cheap:
        flops, moved = 1, 1
    spaces = [pltpu.HBM if i in hbm_in else pltpu.VMEM for i in range(len(operands))]
    return pl.pallas_call(
        kernel,
        out_shape=tuple(outs),
        in_specs=[pl.BlockSpec(memory_space=space) for space in spaces],
        out_specs=tuple(
            pl.BlockSpec(memory_space=pltpu.HBM if hbm_out else pltpu.VMEM) for _ in outs
        ),
        scratch_shapes=scratch,
        input_output_aliases=aliases or {},
        compiler_params=pltpu.CompilerParams(vmem_limit_bytes=limit),
        cost_estimate=pl.CostEstimate(flops=flops, bytes_accessed=moved, transcendentals=0),
        name=name,
    )(*operands)


def in_back(pieces):
    return [pieces[0], *pieces[:0:-1]]


def swap(x, axis, n, mask):
    return lax.ppermute(x, axis, [(i, i ^ mask) for i in range(n)])


def local(query_rows, key_rows, value_rows, upstream):
    rows, features = query_rows.shape
    n_i, n_o = lax.axis_size("seqi"), lax.axis_size("seqo")
    slots = HEADS // n_i
    width = n_o // slots
    others = (width - 1) * slots
    quarter = rows // DILATION
    sources = (key_rows, value_rows, query_rows, upstream)
    unit = 2 * rows * rows * HEAD_DIM
    bind = functools.partial

    mid = SHAPE((4 * slots + 1, quarter, HEAD_DIM), BF16)
    full = SHAPE((4, rows, HEAD_DIM), BF16)
    half = SHAPE((slots, 2, rows, HEAD_DIM), BF16)
    square = pltpu.VMEM((LANES, rows), F32)

    def stats(count, lanes=rows):
        return SHAPE((count, lanes), F32)

    def swap_mids(pieces):
        return [pieces[0]] + [
            swap(pieces[step], "seqi", n_i, distance(n_i, step)) for step in range(1, n_i)
        ]

    def swap_back(pieces):
        return [pieces[0]] + [
            swap(pieces[step], "seqi", n_i, distance_back(n_i, step)) for step in range(1, n_i)
        ]

    def swap_fulls(pieces):
        return [pieces[0]] + [swap(pieces[m], "seqo", n_o, m * width) for m in range(1, slots)]

    def pick_scratch(count):
        return [
            pltpu.VMEM((count, 4, rows, slots * HEAD_DIM), BF16),
            pltpu.SemaphoreType.DMA((count, 4)),
            pltpu.VMEM((count, 4, slots, rows, HEAD_DIM), F32),
            square,
        ]

    first, own, *fulls, firststats = call(
        bind(pick_first_kernel, n_i, slots),
        "pick_first",
        [mid, mid] + [full] * slots + [stats(2 * HEADS)],
        pick_scratch(2),
        unit * slots * 4,
        sources,
        hbm_in=range(4),
        limit=FIRST_LIMIT,
    )
    *pieces, near = call(
        bind(pick_rest_kernel, n_i, slots),
        "pick_rest",
        [mid] * (n_i - 2) + [stats(2 * HEADS)],
        pick_scratch(n_i - 2),
        unit * HEADS * 2,
        [*sources, firststats],
        hbm_in=range(4),
        limit=PICK_LIMIT,
    )
    mids = swap_mids([own, first, *pieces])
    fulls = swap_fulls(fulls)

    (settled,) = call(settle_kernel, "far_in", [stats(8)], [], SHORT, [mids[1]])
    (settled,) = call(settle_kernel, "chips_back", [stats(8)], [], LONG, [settled])
    (packed,) = call(bind(pack_kernel, slots), "pack", [half], [], 1, [*in_back(fulls), settled])
    sibs = [swap(packed, "seqo", n_o, part) for part in range(1, width)]
    (settled,) = call(settle_kernel, "packed_back", [stats(8)], [], LONG, [near])
    (far,) = call(
        bind(far_stats_kernel, slots),
        "far_stats",
        [stats(2 * slots)],
        [],
        1,
        [*in_back(fulls), *sibs, settled],
    )
    xmsg, middle, columns = call(
        bind(middle_stats_kernel, n_i, slots),
        "middle_stats",
        [stats(4 * slots), stats(2 * slots, n_i * quarter), stats(n_i * quarter, LANES)],
        [pltpu.VMEM((LANES, n_i * quarter), F32), square],
        unit * slots * 2,
        mids + [near, far],
    )
    xmsgs = swap_fulls([xmsg] * slots)

    midparts = call(
        bind(middle_parts_kernel, n_i, slots),
        "middle_parts",
        [mid] * n_i,
        [pltpu.VMEM((2 * slots, rows), F32), pltpu.VMEM((LANES, n_i * quarter), F32), square],
        unit * slots * 6,
        mids + [middle, columns] + in_back(xmsgs),
    )
    midparts = swap_back(midparts)
    farparts = call(
        bind(far_parts_kernel, slots, width),
        "far_parts",
        [full] * slots + [half] * (width - 1),
        [pltpu.VMEM((n_o * rows, slots * rows), BF16)] * 2,
        unit * n_o * slots * 6,
        [*in_back(fulls), *sibs, *in_back(xmsgs), midparts[0]],
        cheap=True,
    )
    sibparts = [swap(x, "seqo", n_o, part + 1) for part, x in enumerate(farparts[slots:])]
    (settled,) = call(settle_kernel, "far_back", [stats(8)], [], SHORT, [midparts[1]])
    (settled,) = call(settle_kernel, "sib_back", [stats(8)], [], 1, sibparts + [settled])
    (settled,) = call(settle_kernel, "settle", [stats(8)], [], LONG, [settled])
    fullparts = call(
        bind(far_sum_kernel, slots),
        "far_sum",
        [full] * slots,
        [],
        unit,
        list(farparts[:slots]) + sibparts + [settled],
        cheap=True,
    )
    fullparts = swap_fulls(fullparts)

    back = midparts
    kept = [pltpu.VMEM((2 * HEADS, rows), F32), square]
    (early,) = call(
        bind(near_early_kernel, n_i, slots),
        "near_early",
        [SHAPE((4, (n_i - 1) * slots, rows, HEAD_DIM), F32)],
        kept,
        SHORT,
        [*sources, near, *back[:-1], *in_back(xmsgs)],
    )
    whole = [SHAPE((rows, features), BF16)] * 4
    outs = call(
        bind(final_others_kernel, n_i, slots),
        "final_others",
        whole,
        [
            pltpu.VMEM((n_i - 1, 4, rows, slots * HEAD_DIM), BF16),
            pltpu.SemaphoreType.DMA((n_i - 1, 4)),
            *kept,
        ],
        SHORT // 2,
        [*sources, near, early, *back[1:]],
        hbm_out=True,
    )
    return call(
        bind(final_own_kernel, slots),
        "final_own",
        whole,
        [pltpu.VMEM((4, rows, slots * HEAD_DIM), BF16), pltpu.SemaphoreType.DMA((4,))],
        unit * slots,
        [early, midparts[0], *in_back(fullparts), *outs],
        hbm_in=range(2 + slots, 6 + slots),
        hbm_out=True,
        aliases={2 + slots + which: which for which in range(4)},
    )


def solution(mesh):
    rows = P(("seqo", "seqi"), None)
    return jax.shard_map(
        local,
        mesh=mesh,
        in_specs=(rows,) * 4,
        out_specs=(rows,) * 4,
        check_vma=False,
    )
```

```python
import functools

import jax
import jax.numpy as jnp
from jax import lax
from jax.experimental import pallas as pl
from jax.experimental.pallas import tpu as pltpu
from jax.sharding import PartitionSpec as P

HEADS = 16
HEAD_DIM = 128
DILATION = 4
LANES = 128
SCALE = HEAD_DIM**-0.5
LOWEST = -1e30
LONG = 4 * 10**10
SHORT = 2 * 10**9
VMEM_LIMIT = 32 * 1024 * 1024
PICK_LIMIT = 54784 * 1024
FIRST_LIMIT = 54272 * 1024
NEAR_LIMIT = 54784 * 1024
F32, BF16 = jnp.float32, jnp.bfloat16
SHAPE = jax.ShapeDtypeStruct

NT = (((1,), (1,)), ((), ()))
TN = (((0,), (0,)), ((), ()))


def dot(a, b):
    return jnp.dot(a, b, preferred_element_type=F32)


def dot_nt(a, b):
    return lax.dot_general(a, b, NT, preferred_element_type=F32)


def dot_tn(a, b):
    return lax.dot_general(a, b, TN, preferred_element_type=F32)


def head_columns(head):
    return pl.ds(pl.multiple_of(head * HEAD_DIM, HEAD_DIM), HEAD_DIM)


def static_columns(index):
    return slice(index * HEAD_DIM, (index + 1) * HEAD_DIM)


def position(slots):
    width = lax.axis_size("seqo") // slots
    return lax.axis_index("seqi"), lax.axis_index("seqo") // width


def distance(n_i, step):
    return n_i - step


def distance_back(n_i, step):
    return n_i - step


def place_in(n_i, slots, step):
    pos, _ = position(slots)
    return pos if step == 0 else pos ^ distance(n_i, step)


def first_back(n_i, slots, step):
    pos, _ = position(slots)
    return (pos if step == 0 else pos ^ distance_back(n_i, step)) * slots


def in_back_order(n_i, chunks):
    order = [distance(n_i, step) for step in range(1, n_i)]
    return [chunks[0]] + [
        chunks[order.index(distance_back(n_i, step)) + 1] for step in range(1, n_i)
    ]


def lanes_of(rows):
    return lax.broadcasted_iota(jnp.int32, (rows, LANES), 1)


def level_stats(operands):
    products = [(dot_nt(k, q) * SCALE, dot_nt(v, u)) for k, v, q, u in operands]
    tops = [jnp.max(s, axis=0, keepdims=True) for s, _ in products]
    weights = [jnp.exp(s - top) for (s, _), top in zip(products, tops)]
    totals = [jnp.sum(p, axis=0, keepdims=True) for p in weights]
    return [
        (top + jnp.log(total), jnp.sum(p * dp, axis=0, keepdims=True) / total)
        for (_, dp), top, p, total in zip(products, tops, weights, totals)
    ]


def merge_stats(ea, da, eb, db):
    top = jnp.maximum(ea, eb)
    wa, wb = jnp.exp(ea - top), jnp.exp(eb - top)
    total = wa + wb
    return top + jnp.log(total), (wa * da + wb * db) / total


def level_weights(operands, stats):
    products = [(dot_nt(k, q) * SCALE, dot_nt(v, u)) for k, v, q, u in operands]
    found = []
    for (s, dp), (lse, delta) in zip(products, stats):
        g = jnp.exp(s - lse)
        found.append((g.astype(BF16), (g * (dp - delta)).astype(BF16)))
    return found


def level_parts(operands, stats):
    found = level_weights(operands, stats)
    keyed = [
        (dot(ds, q) * SCALE, dot(p, u)) for (p, ds), (k, v, q, u) in zip(found, operands)
    ]
    queried = [
        (dot_tn(p, v), dot_tn(ds, k) * SCALE) for (p, ds), (k, v, q, u) in zip(found, operands)
    ]
    return [a + b for a, b in zip(queried, keyed)]


def pick_rows(ref, rows):
    quarter = rows // DILATION
    lane = lanes_of(quarter)
    picked = jnp.zeros((quarter, LANES), F32)
    for residue in range(DILATION):
        part = ref[pl.ds(residue, quarter, stride=DILATION), :]
        picked = jnp.where(lane % DILATION == residue, part, picked)
    return picked


def fetch(slots, places, sources, buffers, sems):
    width = slots * HEAD_DIM
    groups = []
    for index, place in enumerate(places):
        cols = pl.ds(pl.multiple_of(place * width, width), width)
        groups.append(
            [
                pltpu.make_async_copy(
                    source.at[:, cols], buffers.at[index, which], sems.at[index, which]
                )
                for which, source in enumerate(sources)
            ]
        )
        for copy in groups[-1]:
            copy.start()
    return groups


def split(x):
    high = x.astype(BF16).astype(F32)
    rest = x - high
    middle = rest.astype(BF16).astype(F32)
    low = rest - middle
    return (high + pltpu.roll(middle, 2 * HEADS, 1) + pltpu.roll(low, 4 * HEADS, 1)).astype(BF16)


def join(ref):
    x = ref[ref.shape[0] - 1].astype(F32)
    x = x + (pltpu.roll(x, LANES - 2 * HEADS, 1) + pltpu.roll(x, LANES - 4 * HEADS, 1))
    return jnp.where(lanes_of(x.shape[0]) < 2 * HEADS, x, 0.0)


def pick_places(n_i, slots, steps, sources, mids, buffers, sems, wide, turn):
    rows = sources[0].shape[0]
    quarter = rows // DILATION
    places = [place_in(n_i, slots, step) for step in steps]
    for index, copies in enumerate(fetch(slots, places, sources, buffers, sems)):
        first = places[index] * slots
        for which, copy in enumerate(copies):
            copy.wait()
            for slot in range(slots):
                wide[index, which, slot] = buffers[index, which, :, static_columns(slot)].astype(F32)
                residue = (first + slot) % DILATION if slots % DILATION else slot % DILATION
                rowset = wide[index, which, slot, pl.ds(residue, quarter, stride=DILATION), :]
                mids[index][which * slots + slot] = rowset.astype(BF16)
        operands = [
            [buffers[index, which, :, static_columns(slot)] for which in range(4)]
            for slot in range(slots)
        ]
        for slot, (e, d) in enumerate(level_stats(operands)):
            turn[pl.ds(first + slot, 1), :] = e
            turn[pl.ds(HEADS + first + slot, 1), :] = d


def pick_first_kernel(n_i, slots, *refs):
    sources, (mid_ref, own_ref, *refs) = refs[:4], refs[4:]
    fulls, (stats_ref, buffers, sems, wide, turn) = refs[:slots], refs[slots:]
    rows = sources[0].shape[0]
    _, chip = position(slots)
    turn[...] = jnp.zeros_like(turn)
    pick_places(n_i, slots, [1, 0], sources, [mid_ref, own_ref], buffers, sems, wide, turn)
    for m in range(slots):
        fulls[m][...] = buffers[1, :, :, head_columns(chip ^ m)]
    stats_ref[...] = turn[: 2 * HEADS, :]
    turn[...] = turn[...].T
    near = split(pick_rows(turn, rows))
    mid_ref[4 * slots] = near
    own_ref[4 * slots] = near


def pick_rest_kernel(n_i, slots, *refs):
    sources, first_ref, refs = refs[:4], refs[4], refs[5:]
    mids, refs = refs[: n_i - 2], refs[n_i - 2 :]
    stats_ref, buffers, sems, wide, turn = refs
    rows = sources[0].shape[0]
    turn[...] = jnp.zeros_like(turn)
    turn[: 2 * HEADS, :] = first_ref[...]
    pick_places(n_i, slots, range(2, n_i), sources, mids, buffers, sems, wide, turn)
    stats_ref[...] = turn[: 2 * HEADS, :]
    turn[...] = turn[...].T
    near = split(pick_rows(turn, rows))
    for ref in mids:
        ref[4 * slots] = near


def pack_kernel(slots, *refs):
    packed_ref = refs[-1]
    for m, ref in enumerate(in_back(refs[:slots])):
        packed_ref[m] = ref[:2]


def far_keys(fulls, sibs, which):
    blocks = [ref[which] for ref in fulls]
    return jnp.concatenate(blocks + [ref[m, which] for ref in sibs for m in range(len(fulls))], axis=0)


def far_stats_kernel(slots, *refs):
    fulls, sibs, stats_ref = in_back(refs[:slots]), refs[slots:-2], refs[-1]
    keys, values = far_keys(fulls, sibs, 0), far_keys(fulls, sibs, 1)
    operands = [(keys, values, ref[2], ref[3]) for ref in fulls]
    for m, (e, d) in enumerate(level_stats(operands)):
        stats_ref[m : m + 1, :] = e
        stats_ref[slots + m : slots + m + 1, :] = d


def middle_operands(slots, mids, slot):
    return [
        jnp.concatenate([ref[which * slots + slot] for ref in mids], axis=0) for which in range(4)
    ]


def middle_stats_kernel(n_i, slots, *refs):
    mids, refs = refs[:n_i], refs[n_i:]
    near_ref, far_ref, xmsg_ref, stats_ref, columns_ref, turn, spread = refs
    rows = near_ref.shape[1]
    quarter = rows // DILATION
    pos, _ = position(slots)
    turn[...] = jnp.zeros_like(turn)
    operands = [middle_operands(slots, mids, slot) for slot in range(slots)]
    for slot, (e, d) in enumerate(level_stats(operands)):
        turn[slot : slot + 1, :] = e
        turn[slots + slot : slots + slot + 1, :] = d
    stats_ref[...] = turn[: 2 * slots, :]
    columns_ref[...] = turn[...].T
    lane = lanes_of(quarter)
    lane_residue = (pos * slots + lane % slots) % DILATION
    blank = jnp.where(lane < slots, LOWEST, 0.0)
    for residue in range(DILATION):
        spread[pl.ds(residue, quarter, stride=DILATION), :] = jnp.where(
            lane_residue == residue, columns_ref[:quarter], blank
        )
    across = spread[...].T
    e, d = merge_stats(
        near_ref[pl.ds(pos * slots, slots), :],
        near_ref[pl.ds(HEADS + pos * slots, slots), :],
        across[:slots],
        across[slots : 2 * slots],
    )
    xmsg_ref[:slots] = e
    xmsg_ref[slots : 2 * slots] = d
    xmsg_ref[2 * slots :] = far_ref[...]


def middle_parts_kernel(n_i, slots, *refs):
    mids, refs = refs[:n_i], refs[n_i:]
    stats_ref, columns_ref = refs[:2]
    refs = refs[2:]
    xmsgs, refs = refs[:slots], refs[slots:]
    outs, (far, turn, spread) = refs[:n_i], refs[n_i:]
    rows = xmsgs[0].shape[1]
    quarter = rows // DILATION
    pos, chip = position(slots)
    for m in range(slots):
        far[pl.ds(chip ^ m, 1), :] = xmsgs[m][2 * slots + m : 2 * slots + m + 1, :]
        far[pl.ds(slots + (chip ^ m), 1), :] = xmsgs[m][3 * slots + m : 3 * slots + m + 1, :]
    e, d = merge_stats(
        xmsgs[0][:slots], xmsgs[0][slots : 2 * slots], far[:slots], far[slots:]
    )
    spread[...] = jnp.zeros_like(spread)
    spread[pl.ds(pos * slots, slots), :] = e
    spread[pl.ds(HEADS + pos * slots, slots), :] = d
    spread[...] = spread[...].T
    own = pick_rows(spread, rows)
    turn[...] = jnp.concatenate([own] + [join(ref) for ref in mids[1:]], axis=0).T
    owned = lax.broadcasted_iota(jnp.int32, (1, n_i * quarter), 1) < quarter
    operands = [middle_operands(slots, mids, slot) for slot in range(slots)]
    merged = [
        merge_stats(
            turn[pl.ds(pos * slots + slot, 1), :],
            turn[pl.ds(HEADS + pos * slots + slot, 1), :],
            jnp.where(owned, LOWEST, stats_ref[slot : slot + 1, :]),
            stats_ref[slots + slot : slots + slot + 1, :],
        )
        for slot in range(slots)
    ]
    for slot, parts in enumerate(level_parts(operands, merged)):
        for which, part in enumerate(parts):
            part = part.astype(BF16)
            chunks = [part[d * quarter : (d + 1) * quarter] for d in range(n_i)]
            for out, chunk in zip(outs, in_back_order(n_i, chunks)):
                out[which * slots + slot] = chunk
    chunks = [columns_ref[d * quarter : (d + 1) * quarter] for d in range(n_i)]
    for out, chunk in zip(outs, in_back_order(n_i, chunks)):
        out[4 * slots] = split(chunk)


def far_parts_kernel(slots, width, *refs):
    fulls, refs = in_back(refs[:slots]), refs[slots:]
    sibs, refs = refs[: width - 1], refs[width - 1 :]
    xmsgs, refs = refs[:slots], refs[slots + 1 :]
    outs, refs = refs[:slots], refs[slots:]
    kvouts, refs = refs[: width - 1], refs[width - 1 :]
    weights, score_grads = refs
    rows = fulls[0].shape[1]
    _, chip = position(slots)
    keys, values = far_keys(fulls, sibs, 0), far_keys(fulls, sibs, 1)
    merged = [
        merge_stats(
            xmsgs[m][pl.ds(chip, 1), :],
            xmsgs[m][pl.ds(slots + chip, 1), :],
            xmsgs[0][2 * slots + m : 2 * slots + m + 1, :],
            xmsgs[0][3 * slots + m : 3 * slots + m + 1, :],
        )
        for m in range(slots)
    ]
    operands = [(keys, values, ref[2], ref[3]) for ref in fulls]
    found = level_weights(operands, merged)
    for m, (p, ds) in enumerate(found):
        weights[:, m * rows : (m + 1) * rows] = p
        score_grads[:, m * rows : (m + 1) * rows] = ds
    for m, (p, ds) in enumerate(found):
        outs[m][0] = dot_tn(p, values).astype(BF16)
        outs[m][1] = (dot_tn(ds, keys) * SCALE).astype(BF16)
    queries = jnp.concatenate([ref[2] for ref in fulls], axis=0)
    ups = jnp.concatenate([ref[3] for ref in fulls], axis=0)
    key_part = (dot(score_grads[...], queries) * SCALE).astype(BF16)
    value_part = dot(weights[...], ups).astype(BF16)
    for index in range(width * slots):
        block = slice(index * rows, (index + 1) * rows)
        part, m = index // slots, index % slots
        if part == 0:
            outs[m][2], outs[m][3] = key_part[block], value_part[block]
        else:
            kvouts[part - 1][m, 0], kvouts[part - 1][m, 1] = key_part[block], value_part[block]


def far_sum_kernel(slots, *refs):
    own, refs = refs[:slots], refs[slots:]
    found, outs = refs[: -slots - 1], refs[-slots:]
    for m in range(slots):
        outs[m][:2] = own[m][:2]
        total = own[m][2:].astype(F32)
        for ref in found:
            total += ref[m].astype(F32)
        outs[m][2:] = total.astype(BF16)


def near_statistics(n_i, slots, steps, near_ref, mids, xmsgs, stats_ref, spread):
    rows = near_ref.shape[1]
    quarter = rows // DILATION
    pos, chip = position(slots)
    lane = lanes_of(quarter)
    mid = jnp.zeros((quarter, LANES), F32)
    for step, ref in zip(steps, mids):
        place = first_back(n_i, slots, step)
        found = join(ref)
        e = pltpu.roll(found, place, 1)
        de = pltpu.roll(found, place + HEADS - slots, 1)
        mid = jnp.where((lane >= place) & (lane < place + slots), e, mid)
        mid = jnp.where((lane >= HEADS + place) & (lane < HEADS + place + slots), de, mid)
    blank = jnp.where(lane < HEADS, LOWEST, 0.0)
    for residue in range(DILATION):
        spread[pl.ds(residue, quarter, stride=DILATION), :] = jnp.where(
            lane % DILATION == residue, mid, blank
        )
    across = spread[...].T
    e, d = merge_stats(
        near_ref[:HEADS], near_ref[HEADS:], across[:HEADS], across[HEADS : 2 * HEADS]
    )
    if xmsgs:
        stats_ref[:HEADS] = jnp.full((HEADS, rows), LOWEST, F32)
        stats_ref[HEADS:] = jnp.zeros((HEADS, rows), F32)
        for m in range(slots):
            head = pos * slots + (chip ^ m)
            stats_ref[pl.ds(head, 1), :] = xmsgs[m][2 * slots + m : 2 * slots + m + 1, :]
            stats_ref[pl.ds(HEADS + head, 1), :] = xmsgs[m][3 * slots + m : 3 * slots + m + 1, :]
        e, d = merge_stats(e, d, stats_ref[:HEADS], stats_ref[HEADS:])
    stats_ref[:HEADS] = e
    stats_ref[HEADS:] = d


def near_place(n_i, slots, step, sources, stats_ref):
    heads = [first_back(n_i, slots, step) + slot for slot in range(slots)]
    operands = [[ref[:, head_columns(head)] for ref in sources] for head in heads]
    stats = [(stats_ref[pl.ds(head, 1), :], stats_ref[pl.ds(HEADS + head, 1), :]) for head in heads]
    return level_parts(operands, stats)


def near_early_kernel(n_i, slots, *refs):
    sources, near_ref, refs = refs[:4], refs[4], refs[5:]
    mids, refs = refs[: n_i - 1], refs[n_i - 1 :]
    xmsgs, (out_ref, stats_ref, spread) = refs[:slots], refs[slots:]
    near_statistics(n_i, slots, range(n_i - 1), near_ref, mids, xmsgs, stats_ref, spread)
    for step in range(n_i - 1):
        for slot, parts in enumerate(near_place(n_i, slots, step, sources, stats_ref)):
            for which, part in enumerate(parts):
                out_ref[which, step * slots + slot] = part


def far_sum_kernel(slots, *refs):
    own, refs = refs[:slots], refs[slots:]
    found, outs = refs[: -slots - 1], refs[-slots:]
    for m in range(slots):
        outs[m][:2] = own[m][:2]
        total = own[m][2:].astype(F32)
        for ref in found:
            total += ref[m].astype(F32)
        outs[m][2:] = total.astype(BF16)


def near_parts_kernel(n_i, slots, *refs):
    sources, near_ref, refs = refs[:4], refs[4], refs[5:]
    mids, refs = (refs[0], *refs[n_i - 1 : 0 : -1]), refs[n_i:]
    xmsgs, (out_ref, stats_ref, spread) = refs[:slots], refs[slots:]
    rows = near_ref.shape[1]
    quarter = rows // DILATION
    pos, chip = position(slots)
    lane = lanes_of(quarter)
    mid = jnp.zeros((quarter, LANES), F32)
    for d in range(n_i):
        place = (pos ^ d) * slots
        found = join(mids[d])
        e = pltpu.roll(found, place, 1)
        de = pltpu.roll(found, place + HEADS - slots, 1)
        mid = jnp.where((lane >= place) & (lane < place + slots), e, mid)
        mid = jnp.where((lane >= HEADS + place) & (lane < HEADS + place + slots), de, mid)
    blank = jnp.where(lane < HEADS, LOWEST, 0.0)
    for residue in range(DILATION):
        spread[pl.ds(residue, quarter, stride=DILATION), :] = jnp.where(
            lane % DILATION == residue, mid, blank
        )
    across = spread[...].T
    stats_ref[:HEADS] = jnp.full((HEADS, rows), LOWEST, F32)
    stats_ref[HEADS:] = jnp.zeros((HEADS, rows), F32)
    for m in range(slots):
        head = pos * slots + (chip ^ m)
        stats_ref[pl.ds(head, 1), :] = xmsgs[m][2 * slots + m : 2 * slots + m + 1, :]
        stats_ref[pl.ds(HEADS + head, 1), :] = xmsgs[m][3 * slots + m : 3 * slots + m + 1, :]
    e, d = merge_stats(
        near_ref[:HEADS], near_ref[HEADS:], across[:HEADS], across[HEADS : 2 * HEADS]
    )
    e, d = merge_stats(e, d, stats_ref[:HEADS], stats_ref[HEADS:])
    stats_ref[:HEADS] = e
    stats_ref[HEADS:] = d
    for group in range(HEADS // DILATION):
        heads = range(group * DILATION, (group + 1) * DILATION)
        operands = [
            [ref[:, static_columns(head)] for ref in sources] for head in heads
        ]
        stats = [
            (stats_ref[head : head + 1, :], stats_ref[HEADS + head : HEADS + head + 1, :])
            for head in heads
        ]
        for head, parts in zip(heads, level_parts(operands, stats)):
            for which, part in enumerate(parts):
                out_ref[which, head] = part


def spread_rows(slots, head, slot, ref):
    quarter = ref.shape[1]
    rows = quarter * DILATION
    row = lax.broadcasted_iota(jnp.int32, (rows, quarter), 0)
    taken = lax.broadcasted_iota(jnp.int32, (rows, quarter), 1) * DILATION
    place = jnp.where(row == taken + head % DILATION, 1.0, 0.0).astype(BF16)
    return dot(place, jnp.concatenate([ref[which * slots + slot] for which in range(4)], axis=1))


def send_place(slots, first, ready, outs, sems):
    width = slots * HEAD_DIM
    cols = pl.ds(pl.multiple_of(first * HEAD_DIM, width), width)
    copies = [
        pltpu.make_async_copy(ready.at[which], out.at[:, cols], sems.at[which])
        for which, out in enumerate(outs)
    ]
    for copy in copies:
        copy.start()
    return copies


def final_others_kernel(n_i, slots, *refs):
    sources, near_ref, early_ref, refs = refs[:4], refs[4], refs[5], refs[6:]
    mids, refs = refs[: n_i - 1], refs[n_i - 1 :]
    outs, (ready, sems, stats_ref, spread) = refs[:4], refs[4:]
    last = n_i - 1
    copies = []
    for step in range(1, n_i):
        first = first_back(n_i, slots, step)
        found = [spread_rows(slots, first + slot, slot, mids[step - 1]) for slot in range(slots)]
        if step == last:
            near_statistics(n_i, slots, [last], near_ref, mids[-1:], (), stats_ref, spread)
            late = near_place(n_i, slots, last, sources, stats_ref)
        for slot, parts in enumerate(found):
            for which in range(4):
                near = late[slot][which] if step == last else early_ref[which, step * slots + slot]
                total = near + parts[:, static_columns(which)]
                ready[step - 1, which, :, static_columns(slot)] = total.astype(BF16)
        copies += send_place(slots, first, ready.at[step - 1], outs, sems.at[step - 1])
    for copy in copies:
        copy.wait()


def final_own_kernel(slots, early_ref, mid_ref, *refs):
    fulls, refs = in_back(refs[:slots]), refs[slots:]
    outs, (ready, sems) = refs[4:8], refs[8:]
    pos, chip = position(slots)
    first = pos * slots
    found = [spread_rows(slots, first + (chip ^ m), chip ^ m, mid_ref) for m in range(slots)]
    for m, parts in enumerate(found):
        slot = chip ^ m
        for which in range(4):
            total = early_ref[which, slot] + parts[:, static_columns(which)]
            total += fulls[m][which].astype(F32)
            ready[which, :, head_columns(slot)] = total.astype(BF16)
    for copy in send_place(slots, first, ready, outs, sems):
        copy.wait()


def settle_kernel(*refs):
    refs[-1][...] = jnp.zeros_like(refs[-1])


def call(kernel, name, outs, scratch, flops, operands, hbm_in=(), hbm_out=False, cheap=False, limit=VMEM_LIMIT, aliases=None):
    moved = sum(x.size * x.dtype.itemsize for x in tuple(operands) + tuple(outs))
    if cheap:
        flops, moved = 1, 1
    spaces = [pltpu.HBM if i in hbm_in else pltpu.VMEM for i in range(len(operands))]
    return pl.pallas_call(
        kernel,
        out_shape=tuple(outs),
        in_specs=[pl.BlockSpec(memory_space=space) for space in spaces],
        out_specs=tuple(
            pl.BlockSpec(memory_space=pltpu.HBM if hbm_out else pltpu.VMEM) for _ in outs
        ),
        scratch_shapes=scratch,
        input_output_aliases=aliases or {},
        compiler_params=pltpu.CompilerParams(vmem_limit_bytes=limit),
        cost_estimate=pl.CostEstimate(flops=flops, bytes_accessed=moved, transcendentals=0),
        name=name,
    )(*operands)


def in_back(pieces):
    return [pieces[0], *pieces[:0:-1]]


def swap(x, axis, n, mask):
    return lax.ppermute(x, axis, [(i, i ^ mask) for i in range(n)])


def local(query_rows, key_rows, value_rows, upstream):
    rows, features = query_rows.shape
    n_i, n_o = lax.axis_size("seqi"), lax.axis_size("seqo")
    slots = HEADS // n_i
    width = n_o // slots
    others = (width - 1) * slots
    quarter = rows // DILATION
    sources = (key_rows, value_rows, query_rows, upstream)
    unit = 2 * rows * rows * HEAD_DIM
    bind = functools.partial

    mid = SHAPE((4 * slots + 1, quarter, HEAD_DIM), BF16)
    full = SHAPE((4, rows, HEAD_DIM), BF16)
    half = SHAPE((slots, 2, rows, HEAD_DIM), BF16)
    square = pltpu.VMEM((LANES, rows), F32)

    def stats(count, lanes=rows):
        return SHAPE((count, lanes), F32)

    def swap_mids(pieces):
        return [pieces[0]] + [
            swap(pieces[step], "seqi", n_i, distance(n_i, step)) for step in range(1, n_i)
        ]

    def swap_back(pieces):
        return [pieces[0]] + [
            swap(pieces[step], "seqi", n_i, distance_back(n_i, step)) for step in range(1, n_i)
        ]

    def swap_fulls(pieces):
        return [pieces[0]] + [swap(pieces[m], "seqo", n_o, m * width) for m in range(1, slots)]

    def pick_scratch(count):
        return [
            pltpu.VMEM((count, 4, rows, slots * HEAD_DIM), BF16),
            pltpu.SemaphoreType.DMA((count, 4)),
            pltpu.VMEM((count, 4, slots, rows, HEAD_DIM), F32),
            square,
        ]

    first, own, *fulls, firststats = call(
        bind(pick_first_kernel, n_i, slots),
        "pick_first",
        [mid, mid] + [full] * slots + [stats(2 * HEADS)],
        pick_scratch(2),
        unit * slots * 4,
        sources,
        hbm_in=range(4),
        limit=FIRST_LIMIT,
    )
    *pieces, near = call(
        bind(pick_rest_kernel, n_i, slots),
        "pick_rest",
        [mid] * (n_i - 2) + [stats(2 * HEADS)],
        pick_scratch(n_i - 2),
        unit * HEADS * 2,
        [*sources, firststats],
        hbm_in=range(4),
        limit=PICK_LIMIT,
    )
    mids = swap_mids([own, first, *pieces])
    fulls = swap_fulls(fulls)

    (settled,) = call(settle_kernel, "far_in", [stats(8)], [], SHORT, [mids[1]])
    (settled,) = call(settle_kernel, "chips_back", [stats(8)], [], LONG, [settled])
    (packed,) = call(bind(pack_kernel, slots), "pack", [half], [], 1, [*in_back(fulls), settled])
    sibs = [swap(packed, "seqo", n_o, part) for part in range(1, width)]
    (settled,) = call(settle_kernel, "packed_back", [stats(8)], [], LONG, [near])
    (far,) = call(
        bind(far_stats_kernel, slots),
        "far_stats",
        [stats(2 * slots)],
        [],
        1,
        [*in_back(fulls), *sibs, settled],
    )
    xmsg, middle, columns = call(
        bind(middle_stats_kernel, n_i, slots),
        "middle_stats",
        [stats(4 * slots), stats(2 * slots, n_i * quarter), stats(n_i * quarter, LANES)],
        [pltpu.VMEM((LANES, n_i * quarter), F32), square],
        unit * slots * 2,
        mids + [near, far],
    )
    xmsgs = swap_fulls([xmsg] * slots)

    midparts = call(
        bind(middle_parts_kernel, n_i, slots),
        "middle_parts",
        [mid] * n_i,
        [pltpu.VMEM((2 * slots, rows), F32), pltpu.VMEM((LANES, n_i * quarter), F32), square],
        unit * slots * 6,
        mids + [middle, columns] + xmsgs,
    )
    midparts = swap_back(midparts)
    farparts = call(
        bind(far_parts_kernel, slots, width),
        "far_parts",
        [full] * slots + [half] * (width - 1),
        [pltpu.VMEM((n_o * rows, slots * rows), BF16)] * 2,
        unit * n_o * slots * 6,
        [*in_back(fulls), *sibs, *xmsgs, midparts[0]],
        cheap=True,
    )
    sibparts = [swap(x, "seqo", n_o, part + 1) for part, x in enumerate(farparts[slots:])]
    (settled,) = call(settle_kernel, "far_back", [stats(8)], [], SHORT, [midparts[1]])
    (settled,) = call(settle_kernel, "sib_back", [stats(8)], [], 1, sibparts + [settled])
    (settled,) = call(settle_kernel, "settle", [stats(8)], [], LONG, [settled])
    fullparts = call(
        bind(far_sum_kernel, slots),
        "far_sum",
        [full] * slots,
        [],
        unit,
        list(farparts[:slots]) + sibparts + [settled],
        cheap=True,
    )
    fullparts = swap_fulls(fullparts)

    back = midparts
    kept = [pltpu.VMEM((2 * HEADS, rows), F32), square]
    (early,) = call(
        bind(near_early_kernel, n_i, slots),
        "near_early",
        [SHAPE((4, (n_i - 1) * slots, rows, HEAD_DIM), F32)],
        kept,
        SHORT,
        [*sources, near, *back[:-1], *xmsgs],
    )
    whole = [SHAPE((rows, features), BF16)] * 4
    outs = call(
        bind(final_others_kernel, n_i, slots),
        "final_others",
        whole,
        [
            pltpu.VMEM((n_i - 1, 4, rows, slots * HEAD_DIM), BF16),
            pltpu.SemaphoreType.DMA((n_i - 1, 4)),
            *kept,
        ],
        SHORT // 2,
        [*sources, near, early, *back[1:]],
        hbm_out=True,
    )
    return call(
        bind(final_own_kernel, slots),
        "final_own",
        whole,
        [pltpu.VMEM((4, rows, slots * HEAD_DIM), BF16), pltpu.SemaphoreType.DMA((4,))],
        unit * slots,
        [early, midparts[0], *in_back(fullparts), *outs],
        hbm_in=range(2 + slots, 6 + slots),
        hbm_out=True,
        aliases={2 + slots + which: which for which in range(4)},
    )


def solution(mesh):
    rows = P(("seqo", "seqi"), None)
    return jax.shard_map(
        local,
        mesh=mesh,
        in_specs=(rows,) * 4,
        out_specs=(rows,) * 4,
        check_vma=False,
    )
```

```python
import functools

import jax
import jax.numpy as jnp
from jax import lax
from jax.experimental import pallas as pl
from jax.experimental.pallas import tpu as pltpu
from jax.sharding import PartitionSpec as P

HEADS = 16
HEAD_DIM = 128
DILATION = 4
LANES = 128
SCALE = HEAD_DIM**-0.5
LOWEST = -1e30
LONG = 4 * 10**10
SHORT = 2 * 10**9
VMEM_LIMIT = 32 * 1024 * 1024
PICK_LIMIT = 54784 * 1024
FIRST_LIMIT = 54272 * 1024
NEAR_LIMIT = 54784 * 1024
F32, BF16 = jnp.float32, jnp.bfloat16
SHAPE = jax.ShapeDtypeStruct

NT = (((1,), (1,)), ((), ()))
TN = (((0,), (0,)), ((), ()))


def dot(a, b):
    return jnp.dot(a, b, preferred_element_type=F32)


def dot_nt(a, b):
    return lax.dot_general(a, b, NT, preferred_element_type=F32)


def dot_tn(a, b):
    return lax.dot_general(a, b, TN, preferred_element_type=F32)


def head_columns(head):
    return pl.ds(pl.multiple_of(head * HEAD_DIM, HEAD_DIM), HEAD_DIM)


def static_columns(index):
    return slice(index * HEAD_DIM, (index + 1) * HEAD_DIM)


def position(slots):
    width = lax.axis_size("seqo") // slots
    return lax.axis_index("seqi"), lax.axis_index("seqo") // width


def distance(n_i, step):
    return n_i - step


def distance_back(n_i, step):
    return n_i - 1 if step == 1 else step - 1


def place_in(n_i, slots, step):
    pos, _ = position(slots)
    return pos if step == 0 else pos ^ distance(n_i, step)


def first_back(n_i, slots, step):
    pos, _ = position(slots)
    return (pos if step == 0 else pos ^ distance_back(n_i, step)) * slots


def in_back_order(n_i, chunks):
    order = [distance(n_i, step) for step in range(1, n_i)]
    return [chunks[0]] + [
        chunks[order.index(distance_back(n_i, step)) + 1] for step in range(1, n_i)
    ]


def lanes_of(rows):
    return lax.broadcasted_iota(jnp.int32, (rows, LANES), 1)


def level_stats(operands):
    products = [(dot_nt(k, q) * SCALE, dot_nt(v, u)) for k, v, q, u in operands]
    tops = [jnp.max(s, axis=0, keepdims=True) for s, _ in products]
    weights = [jnp.exp(s - top) for (s, _), top in zip(products, tops)]
    totals = [jnp.sum(p, axis=0, keepdims=True) for p in weights]
    return [
        (top + jnp.log(total), jnp.sum(p * dp, axis=0, keepdims=True) / total)
        for (_, dp), top, p, total in zip(products, tops, weights, totals)
    ]


def merge_stats(ea, da, eb, db):
    top = jnp.maximum(ea, eb)
    wa, wb = jnp.exp(ea - top), jnp.exp(eb - top)
    total = wa + wb
    return top + jnp.log(total), (wa * da + wb * db) / total


def level_weights(operands, stats):
    products = [(dot_nt(k, q) * SCALE, dot_nt(v, u)) for k, v, q, u in operands]
    found = []
    for (s, dp), (lse, delta) in zip(products, stats):
        g = jnp.exp(s - lse)
        found.append((g.astype(BF16), (g * (dp - delta)).astype(BF16)))
    return found


def level_parts(operands, stats):
    found = level_weights(operands, stats)
    keyed = [
        (dot(ds, q) * SCALE, dot(p, u)) for (p, ds), (k, v, q, u) in zip(found, operands)
    ]
    queried = [
        (dot_tn(p, v), dot_tn(ds, k) * SCALE) for (p, ds), (k, v, q, u) in zip(found, operands)
    ]
    return [a + b for a, b in zip(queried, keyed)]


def pick_rows(ref, rows):
    quarter = rows // DILATION
    lane = lanes_of(quarter)
    picked = jnp.zeros((quarter, LANES), F32)
    for residue in range(DILATION):
        part = ref[pl.ds(residue, quarter, stride=DILATION), :]
        picked = jnp.where(lane % DILATION == residue, part, picked)
    return picked


def fetch(slots, places, sources, buffers, sems):
    width = slots * HEAD_DIM
    groups = []
    for index, place in enumerate(places):
        cols = pl.ds(pl.multiple_of(place * width, width), width)
        groups.append(
            [
                pltpu.make_async_copy(
                    source.at[:, cols], buffers.at[index, which], sems.at[index, which]
                )
                for which, source in enumerate(sources)
            ]
        )
        for copy in groups[-1]:
            copy.start()
    return groups


def split(x):
    high = x.astype(BF16).astype(F32)
    rest = x - high
    middle = rest.astype(BF16).astype(F32)
    low = rest - middle
    return (high + pltpu.roll(middle, 2 * HEADS, 1) + pltpu.roll(low, 4 * HEADS, 1)).astype(BF16)


def join(ref):
    x = ref[ref.shape[0] - 1].astype(F32)
    x = x + (pltpu.roll(x, LANES - 2 * HEADS, 1) + pltpu.roll(x, LANES - 4 * HEADS, 1))
    return jnp.where(lanes_of(x.shape[0]) < 2 * HEADS, x, 0.0)


def pick_places(n_i, slots, steps, sources, mids, buffers, sems, wide, turn):
    rows = sources[0].shape[0]
    quarter = rows // DILATION
    places = [place_in(n_i, slots, step) for step in steps]
    for index, copies in enumerate(fetch(slots, places, sources, buffers, sems)):
        first = places[index] * slots
        for which, copy in enumerate(copies):
            copy.wait()
            for slot in range(slots):
                wide[index, which, slot] = buffers[index, which, :, static_columns(slot)].astype(F32)
                residue = (first + slot) % DILATION if slots % DILATION else slot % DILATION
                rowset = wide[index, which, slot, pl.ds(residue, quarter, stride=DILATION), :]
                mids[index][which * slots + slot] = rowset.astype(BF16)
    heads = [(index, slot) for index in range(len(places)) for slot in range(slots)]
    operands = [
        [buffers[index, which, :, static_columns(slot)] for which in range(4)]
        for index, slot in heads
    ]
    for (index, slot), (e, d) in zip(heads, level_stats(operands)):
        turn[pl.ds(places[index] * slots + slot, 1), :] = e
        turn[pl.ds(HEADS + places[index] * slots + slot, 1), :] = d


def pick_first_kernel(n_i, slots, *refs):
    sources, (mid_ref, own_ref, *refs) = refs[:4], refs[4:]
    fulls, (stats_ref, buffers, sems, wide, turn) = refs[:slots], refs[slots:]
    rows = sources[0].shape[0]
    _, chip = position(slots)
    turn[...] = jnp.zeros_like(turn)
    pick_places(n_i, slots, [1, 0], sources, [mid_ref, own_ref], buffers, sems, wide, turn)
    for m in range(slots):
        fulls[m][...] = buffers[1, :, :, head_columns(chip ^ m)]
    stats_ref[...] = turn[: 2 * HEADS, :]
    turn[...] = turn[...].T
    near = split(pick_rows(turn, rows))
    mid_ref[4 * slots] = near
    own_ref[4 * slots] = near


def pick_rest_kernel(n_i, slots, *refs):
    sources, first_ref, refs = refs[:4], refs[4], refs[5:]
    mids, refs = refs[: n_i - 2], refs[n_i - 2 :]
    stats_ref, buffers, sems, wide, turn = refs
    rows = sources[0].shape[0]
    turn[...] = jnp.zeros_like(turn)
    turn[: 2 * HEADS, :] = first_ref[...]
    pick_places(n_i, slots, range(2, n_i), sources, mids, buffers, sems, wide, turn)
    stats_ref[...] = turn[: 2 * HEADS, :]
    turn[...] = turn[...].T
    near = split(pick_rows(turn, rows))
    for ref in mids:
        ref[4 * slots] = near


def pack_kernel(slots, *refs):
    packed_ref = refs[-1]
    for m, ref in enumerate(in_back(refs[:slots])):
        packed_ref[m] = ref[:2]


def far_keys(fulls, sibs, which):
    blocks = [ref[which] for ref in fulls]
    return jnp.concatenate(blocks + [ref[m, which] for ref in sibs for m in range(len(fulls))], axis=0)


def far_stats_kernel(slots, *refs):
    fulls, sibs, stats_ref = in_back(refs[:slots]), refs[slots:-2], refs[-1]
    keys, values = far_keys(fulls, sibs, 0), far_keys(fulls, sibs, 1)
    operands = [(keys, values, ref[2], ref[3]) for ref in fulls]
    for m, (e, d) in enumerate(level_stats(operands)):
        stats_ref[m : m + 1, :] = e
        stats_ref[slots + m : slots + m + 1, :] = d


def middle_operands(slots, mids, slot):
    return [
        jnp.concatenate([ref[which * slots + slot] for ref in mids], axis=0) for which in range(4)
    ]


def middle_stats_kernel(n_i, slots, *refs):
    mids, refs = refs[:n_i], refs[n_i:]
    near_ref, far_ref, xmsg_ref, stats_ref, columns_ref, turn, spread = refs
    rows = near_ref.shape[1]
    quarter = rows // DILATION
    pos, _ = position(slots)
    turn[...] = jnp.zeros_like(turn)
    operands = [middle_operands(slots, mids, slot) for slot in range(slots)]
    for slot, (e, d) in enumerate(level_stats(operands)):
        turn[slot : slot + 1, :] = e
        turn[slots + slot : slots + slot + 1, :] = d
    stats_ref[...] = turn[: 2 * slots, :]
    columns_ref[...] = turn[...].T
    lane = lanes_of(quarter)
    lane_residue = (pos * slots + lane % slots) % DILATION
    blank = jnp.where(lane < slots, LOWEST, 0.0)
    for residue in range(DILATION):
        spread[pl.ds(residue, quarter, stride=DILATION), :] = jnp.where(
            lane_residue == residue, columns_ref[:quarter], blank
        )
    across = spread[...].T
    e, d = merge_stats(
        near_ref[pl.ds(pos * slots, slots), :],
        near_ref[pl.ds(HEADS + pos * slots, slots), :],
        across[:slots],
        across[slots : 2 * slots],
    )
    xmsg_ref[:slots] = e
    xmsg_ref[slots : 2 * slots] = d
    xmsg_ref[2 * slots :] = far_ref[...]


def middle_parts_kernel(n_i, slots, *refs):
    mids, refs = refs[:n_i], refs[n_i:]
    stats_ref, columns_ref = refs[:2]
    refs = refs[2:]
    xmsgs, refs = refs[:slots], refs[slots:]
    outs, (far, turn, spread) = refs[:n_i], refs[n_i:]
    rows = xmsgs[0].shape[1]
    quarter = rows // DILATION
    pos, chip = position(slots)
    for m in range(slots):
        far[pl.ds(chip ^ m, 1), :] = xmsgs[m][2 * slots + m : 2 * slots + m + 1, :]
        far[pl.ds(slots + (chip ^ m), 1), :] = xmsgs[m][3 * slots + m : 3 * slots + m + 1, :]
    e, d = merge_stats(
        xmsgs[0][:slots], xmsgs[0][slots : 2 * slots], far[:slots], far[slots:]
    )
    spread[...] = jnp.zeros_like(spread)
    spread[pl.ds(pos * slots, slots), :] = e
    spread[pl.ds(HEADS + pos * slots, slots), :] = d
    spread[...] = spread[...].T
    own = pick_rows(spread, rows)
    turn[...] = jnp.concatenate([own] + [join(ref) for ref in mids[1:]], axis=0).T
    owned = lax.broadcasted_iota(jnp.int32, (1, n_i * quarter), 1) < quarter
    operands = [middle_operands(slots, mids, slot) for slot in range(slots)]
    merged = [
        merge_stats(
            turn[pl.ds(pos * slots + slot, 1), :],
            turn[pl.ds(HEADS + pos * slots + slot, 1), :],
            jnp.where(owned, LOWEST, stats_ref[slot : slot + 1, :]),
            stats_ref[slots + slot : slots + slot + 1, :],
        )
        for slot in range(slots)
    ]
    for slot, parts in enumerate(level_parts(operands, merged)):
        for which, part in enumerate(parts):
            part = part.astype(BF16)
            chunks = [part[d * quarter : (d + 1) * quarter] for d in range(n_i)]
            for out, chunk in zip(outs, in_back_order(n_i, chunks)):
                out[which * slots + slot] = chunk
    chunks = [columns_ref[d * quarter : (d + 1) * quarter] for d in range(n_i)]
    for out, chunk in zip(outs, in_back_order(n_i, chunks)):
        out[4 * slots] = split(chunk)


def far_parts_kernel(slots, width, *refs):
    fulls, refs = in_back(refs[:slots]), refs[slots:]
    sibs, refs = refs[: width - 1], refs[width - 1 :]
    xmsgs, refs = refs[:slots], refs[slots + 1 :]
    outs, refs = refs[:slots], refs[slots:]
    kvouts, refs = refs[: width - 1], refs[width - 1 :]
    weights, score_grads = refs
    rows = fulls[0].shape[1]
    _, chip = position(slots)
    keys, values = far_keys(fulls, sibs, 0), far_keys(fulls, sibs, 1)
    merged = [
        merge_stats(
            xmsgs[m][pl.ds(chip, 1), :],
            xmsgs[m][pl.ds(slots + chip, 1), :],
            xmsgs[0][2 * slots + m : 2 * slots + m + 1, :],
            xmsgs[0][3 * slots + m : 3 * slots + m + 1, :],
        )
        for m in range(slots)
    ]
    operands = [(keys, values, ref[2], ref[3]) for ref in fulls]
    found = level_weights(operands, merged)
    for m, (p, ds) in enumerate(found):
        weights[:, m * rows : (m + 1) * rows] = p
        score_grads[:, m * rows : (m + 1) * rows] = ds
    for m, (p, ds) in enumerate(found):
        outs[m][0] = dot_tn(p, values).astype(BF16)
        outs[m][1] = (dot_tn(ds, keys) * SCALE).astype(BF16)
    queries = jnp.concatenate([ref[2] for ref in fulls], axis=0)
    ups = jnp.concatenate([ref[3] for ref in fulls], axis=0)
    key_part = (dot(score_grads[...], queries) * SCALE).astype(BF16)
    value_part = dot(weights[...], ups).astype(BF16)
    for index in range(width * slots):
        block = slice(index * rows, (index + 1) * rows)
        part, m = index // slots, index % slots
        if part == 0:
            outs[m][2], outs[m][3] = key_part[block], value_part[block]
        else:
            kvouts[part - 1][m, 0], kvouts[part - 1][m, 1] = key_part[block], value_part[block]


def far_sum_kernel(slots, *refs):
    own, refs = refs[:slots], refs[slots:]
    found, outs = refs[: -slots - 1], refs[-slots:]
    for m in range(slots):
        outs[m][:2] = own[m][:2]
        total = own[m][2:].astype(F32)
        for ref in found:
            total += ref[m].astype(F32)
        outs[m][2:] = total.astype(BF16)


def near_statistics(n_i, slots, steps, near_ref, mids, xmsgs, stats_ref, spread):
    rows = near_ref.shape[1]
    quarter = rows // DILATION
    pos, chip = position(slots)
    lane = lanes_of(quarter)
    mid = jnp.zeros((quarter, LANES), F32)
    for step, ref in zip(steps, mids):
        place = first_back(n_i, slots, step)
        found = join(ref)
        e = pltpu.roll(found, place, 1)
        de = pltpu.roll(found, place + HEADS - slots, 1)
        mid = jnp.where((lane >= place) & (lane < place + slots), e, mid)
        mid = jnp.where((lane >= HEADS + place) & (lane < HEADS + place + slots), de, mid)
    blank = jnp.where(lane < HEADS, LOWEST, 0.0)
    for residue in range(DILATION):
        spread[pl.ds(residue, quarter, stride=DILATION), :] = jnp.where(
            lane % DILATION == residue, mid, blank
        )
    across = spread[...].T
    e, d = merge_stats(
        near_ref[:HEADS], near_ref[HEADS:], across[:HEADS], across[HEADS : 2 * HEADS]
    )
    if xmsgs:
        stats_ref[:HEADS] = jnp.full((HEADS, rows), LOWEST, F32)
        stats_ref[HEADS:] = jnp.zeros((HEADS, rows), F32)
        for m in range(slots):
            head = pos * slots + (chip ^ m)
            stats_ref[pl.ds(head, 1), :] = xmsgs[m][2 * slots + m : 2 * slots + m + 1, :]
            stats_ref[pl.ds(HEADS + head, 1), :] = xmsgs[m][3 * slots + m : 3 * slots + m + 1, :]
        e, d = merge_stats(e, d, stats_ref[:HEADS], stats_ref[HEADS:])
    stats_ref[:HEADS] = e
    stats_ref[HEADS:] = d


def near_place(n_i, slots, step, sources, stats_ref):
    heads = [first_back(n_i, slots, step) + slot for slot in range(slots)]
    operands = [[ref[:, head_columns(head)] for ref in sources] for head in heads]
    stats = [(stats_ref[pl.ds(head, 1), :], stats_ref[pl.ds(HEADS + head, 1), :]) for head in heads]
    return level_parts(operands, stats)


def near_early_kernel(n_i, slots, *refs):
    sources, near_ref, refs = refs[:4], refs[4], refs[5:]
    mids, refs = refs[: n_i - 1], refs[n_i - 1 :]
    xmsgs, (out_ref, stats_ref, spread) = refs[:slots], refs[slots:]
    near_statistics(n_i, slots, range(n_i - 1), near_ref, mids, xmsgs, stats_ref, spread)
    for step in range(n_i - 1):
        for slot, parts in enumerate(near_place(n_i, slots, step, sources, stats_ref)):
            for which, part in enumerate(parts):
                out_ref[which, step * slots + slot] = part


def far_sum_kernel(slots, *refs):
    own, refs = refs[:slots], refs[slots:]
    found, outs = refs[: -slots - 1], refs[-slots:]
    for m in range(slots):
        outs[m][:2] = own[m][:2]
        total = own[m][2:].astype(F32)
        for ref in found:
            total += ref[m].astype(F32)
        outs[m][2:] = total.astype(BF16)


def near_parts_kernel(n_i, slots, *refs):
    sources, near_ref, refs = refs[:4], refs[4], refs[5:]
    mids, refs = (refs[0], *refs[n_i - 1 : 0 : -1]), refs[n_i:]
    xmsgs, (out_ref, stats_ref, spread) = refs[:slots], refs[slots:]
    rows = near_ref.shape[1]
    quarter = rows // DILATION
    pos, chip = position(slots)
    lane = lanes_of(quarter)
    mid = jnp.zeros((quarter, LANES), F32)
    for d in range(n_i):
        place = (pos ^ d) * slots
        found = join(mids[d])
        e = pltpu.roll(found, place, 1)
        de = pltpu.roll(found, place + HEADS - slots, 1)
        mid = jnp.where((lane >= place) & (lane < place + slots), e, mid)
        mid = jnp.where((lane >= HEADS + place) & (lane < HEADS + place + slots), de, mid)
    blank = jnp.where(lane < HEADS, LOWEST, 0.0)
    for residue in range(DILATION):
        spread[pl.ds(residue, quarter, stride=DILATION), :] = jnp.where(
            lane % DILATION == residue, mid, blank
        )
    across = spread[...].T
    stats_ref[:HEADS] = jnp.full((HEADS, rows), LOWEST, F32)
    stats_ref[HEADS:] = jnp.zeros((HEADS, rows), F32)
    for m in range(slots):
        head = pos * slots + (chip ^ m)
        stats_ref[pl.ds(head, 1), :] = xmsgs[m][2 * slots + m : 2 * slots + m + 1, :]
        stats_ref[pl.ds(HEADS + head, 1), :] = xmsgs[m][3 * slots + m : 3 * slots + m + 1, :]
    e, d = merge_stats(
        near_ref[:HEADS], near_ref[HEADS:], across[:HEADS], across[HEADS : 2 * HEADS]
    )
    e, d = merge_stats(e, d, stats_ref[:HEADS], stats_ref[HEADS:])
    stats_ref[:HEADS] = e
    stats_ref[HEADS:] = d
    for group in range(HEADS // DILATION):
        heads = range(group * DILATION, (group + 1) * DILATION)
        operands = [
            [ref[:, static_columns(head)] for ref in sources] for head in heads
        ]
        stats = [
            (stats_ref[head : head + 1, :], stats_ref[HEADS + head : HEADS + head + 1, :])
            for head in heads
        ]
        for head, parts in zip(heads, level_parts(operands, stats)):
            for which, part in enumerate(parts):
                out_ref[which, head] = part


def spread_rows(slots, head, slot, ref):
    quarter = ref.shape[1]
    rows = quarter * DILATION
    row = lax.broadcasted_iota(jnp.int32, (rows, quarter), 0)
    taken = lax.broadcasted_iota(jnp.int32, (rows, quarter), 1) * DILATION
    place = jnp.where(row == taken + head % DILATION, 1.0, 0.0).astype(BF16)
    return dot(place, jnp.concatenate([ref[which * slots + slot] for which in range(4)], axis=1))


def send_place(slots, first, ready, outs, sems):
    width = slots * HEAD_DIM
    cols = pl.ds(pl.multiple_of(first * HEAD_DIM, width), width)
    copies = [
        pltpu.make_async_copy(ready.at[which], out.at[:, cols], sems.at[which])
        for which, out in enumerate(outs)
    ]
    for copy in copies:
        copy.start()
    return copies


def final_others_kernel(n_i, slots, *refs):
    sources, near_ref, early_ref, refs = refs[:4], refs[4], refs[5], refs[6:]
    mids, refs = refs[: n_i - 1], refs[n_i - 1 :]
    outs, (ready, sems, stats_ref, spread) = refs[:4], refs[4:]
    last = n_i - 1
    copies = []
    for step in range(1, n_i):
        first = first_back(n_i, slots, step)
        found = [spread_rows(slots, first + slot, slot, mids[step - 1]) for slot in range(slots)]
        if step == last:
            near_statistics(n_i, slots, [last], near_ref, mids[-1:], (), stats_ref, spread)
            late = near_place(n_i, slots, last, sources, stats_ref)
        for slot, parts in enumerate(found):
            for which in range(4):
                near = late[slot][which] if step == last else early_ref[which, step * slots + slot]
                total = near + parts[:, static_columns(which)]
                ready[step - 1, which, :, static_columns(slot)] = total.astype(BF16)
        copies += send_place(slots, first, ready.at[step - 1], outs, sems.at[step - 1])
    for copy in copies:
        copy.wait()


def final_own_kernel(slots, early_ref, mid_ref, *refs):
    fulls, refs = in_back(refs[:slots]), refs[slots:]
    outs, (ready, sems) = refs[4:8], refs[8:]
    pos, chip = position(slots)
    first = pos * slots
    found = [spread_rows(slots, first + (chip ^ m), chip ^ m, mid_ref) for m in range(slots)]
    for m, parts in enumerate(found):
        slot = chip ^ m
        for which in range(4):
            total = early_ref[which, slot] + parts[:, static_columns(which)]
            total += fulls[m][which].astype(F32)
            ready[which, :, head_columns(slot)] = total.astype(BF16)
    for copy in send_place(slots, first, ready, outs, sems):
        copy.wait()


def settle_kernel(*refs):
    refs[-1][...] = jnp.zeros_like(refs[-1])


def call(kernel, name, outs, scratch, flops, operands, hbm_in=(), hbm_out=False, cheap=False, limit=VMEM_LIMIT, aliases=None):
    moved = sum(x.size * x.dtype.itemsize for x in tuple(operands) + tuple(outs))
    if cheap:
        flops, moved = 1, 1
    spaces = [pltpu.HBM if i in hbm_in else pltpu.VMEM for i in range(len(operands))]
    return pl.pallas_call(
        kernel,
        out_shape=tuple(outs),
        in_specs=[pl.BlockSpec(memory_space=space) for space in spaces],
        out_specs=tuple(
            pl.BlockSpec(memory_space=pltpu.HBM if hbm_out else pltpu.VMEM) for _ in outs
        ),
        scratch_shapes=scratch,
        input_output_aliases=aliases or {},
        compiler_params=pltpu.CompilerParams(vmem_limit_bytes=limit),
        cost_estimate=pl.CostEstimate(flops=flops, bytes_accessed=moved, transcendentals=0),
        name=name,
    )(*operands)


def in_back(pieces):
    return [pieces[0], *pieces[:0:-1]]


def swap(x, axis, n, mask):
    return lax.ppermute(x, axis, [(i, i ^ mask) for i in range(n)])


def local(query_rows, key_rows, value_rows, upstream):
    rows, features = query_rows.shape
    n_i, n_o = lax.axis_size("seqi"), lax.axis_size("seqo")
    slots = HEADS // n_i
    width = n_o // slots
    others = (width - 1) * slots
    quarter = rows // DILATION
    sources = (key_rows, value_rows, query_rows, upstream)
    unit = 2 * rows * rows * HEAD_DIM
    bind = functools.partial

    mid = SHAPE((4 * slots + 1, quarter, HEAD_DIM), BF16)
    full = SHAPE((4, rows, HEAD_DIM), BF16)
    half = SHAPE((slots, 2, rows, HEAD_DIM), BF16)
    square = pltpu.VMEM((LANES, rows), F32)

    def stats(count, lanes=rows):
        return SHAPE((count, lanes), F32)

    def swap_mids(pieces):
        return [pieces[0]] + [
            swap(pieces[step], "seqi", n_i, distance(n_i, step)) for step in range(1, n_i)
        ]

    def swap_back(pieces):
        return [pieces[0]] + [
            swap(pieces[step], "seqi", n_i, distance_back(n_i, step)) for step in range(1, n_i)
        ]

    def swap_fulls(pieces):
        return [pieces[0]] + [swap(pieces[m], "seqo", n_o, m * width) for m in range(1, slots)]

    def pick_scratch(count):
        return [
            pltpu.VMEM((count, 4, rows, slots * HEAD_DIM), BF16),
            pltpu.SemaphoreType.DMA((count, 4)),
            pltpu.VMEM((count, 4, slots, rows, HEAD_DIM), F32),
            square,
        ]

    first, own, *fulls, firststats = call(
        bind(pick_first_kernel, n_i, slots),
        "pick_first",
        [mid, mid] + [full] * slots + [stats(2 * HEADS)],
        pick_scratch(2),
        unit * slots * 4,
        sources,
        hbm_in=range(4),
        limit=FIRST_LIMIT,
    )
    *pieces, near = call(
        bind(pick_rest_kernel, n_i, slots),
        "pick_rest",
        [mid] * (n_i - 2) + [stats(2 * HEADS)],
        pick_scratch(n_i - 2),
        unit * HEADS * 2,
        [*sources, firststats],
        hbm_in=range(4),
        limit=PICK_LIMIT,
    )
    mids = swap_mids([own, first, *pieces])
    fulls = swap_fulls(fulls)

    (settled,) = call(settle_kernel, "far_in", [stats(8)], [], SHORT, [mids[1]])
    (settled,) = call(settle_kernel, "chips_back", [stats(8)], [], LONG, [settled])
    (packed,) = call(bind(pack_kernel, slots), "pack", [half], [], 1, [*in_back(fulls), settled])
    sibs = [swap(packed, "seqo", n_o, part) for part in range(1, width)]
    (settled,) = call(settle_kernel, "packed_back", [stats(8)], [], LONG, [near])
    (far,) = call(
        bind(far_stats_kernel, slots),
        "far_stats",
        [stats(2 * slots)],
        [],
        1,
        [*in_back(fulls), *sibs, settled],
    )
    xmsg, middle, columns = call(
        bind(middle_stats_kernel, n_i, slots),
        "middle_stats",
        [stats(4 * slots), stats(2 * slots, n_i * quarter), stats(n_i * quarter, LANES)],
        [pltpu.VMEM((LANES, n_i * quarter), F32), square],
        unit * slots * 2,
        mids + [near, far],
    )
    xmsgs = swap_fulls([xmsg] * slots)

    midparts = call(
        bind(middle_parts_kernel, n_i, slots),
        "middle_parts",
        [mid] * n_i,
        [pltpu.VMEM((2 * slots, rows), F32), pltpu.VMEM((LANES, n_i * quarter), F32), square],
        unit * slots * 6,
        mids + [middle, columns] + xmsgs,
    )
    midparts = swap_back(midparts)
    farparts = call(
        bind(far_parts_kernel, slots, width),
        "far_parts",
        [full] * slots + [half] * (width - 1),
        [pltpu.VMEM((n_o * rows, slots * rows), BF16)] * 2,
        unit * n_o * slots * 6,
        [*in_back(fulls), *sibs, *xmsgs, midparts[0]],
        cheap=True,
    )
    sibparts = [swap(x, "seqo", n_o, part + 1) for part, x in enumerate(farparts[slots:])]
    (settled,) = call(settle_kernel, "far_back", [stats(8)], [], SHORT, [midparts[1]])
    (settled,) = call(settle_kernel, "sib_back", [stats(8)], [], 1, sibparts + [settled])
    (settled,) = call(settle_kernel, "settle", [stats(8)], [], LONG, [settled])
    fullparts = call(
        bind(far_sum_kernel, slots),
        "far_sum",
        [full] * slots,
        [],
        unit,
        list(farparts[:slots]) + sibparts + [settled],
        cheap=True,
    )
    fullparts = swap_fulls(fullparts)

    back = midparts
    kept = [pltpu.VMEM((2 * HEADS, rows), F32), square]
    (early,) = call(
        bind(near_early_kernel, n_i, slots),
        "near_early",
        [SHAPE((4, (n_i - 1) * slots, rows, HEAD_DIM), F32)],
        kept,
        SHORT,
        [*sources, near, *back[:-1], *xmsgs],
    )
    whole = [SHAPE((rows, features), BF16)] * 4
    outs = call(
        bind(final_others_kernel, n_i, slots),
        "final_others",
        whole,
        [
            pltpu.VMEM((n_i - 1, 4, rows, slots * HEAD_DIM), BF16),
            pltpu.SemaphoreType.DMA((n_i - 1, 4)),
            *kept,
        ],
        SHORT // 2,
        [*sources, near, early, *back[1:]],
        hbm_out=True,
    )
    return call(
        bind(final_own_kernel, slots),
        "final_own",
        whole,
        [pltpu.VMEM((4, rows, slots * HEAD_DIM), BF16), pltpu.SemaphoreType.DMA((4,))],
        unit * slots,
        [early, midparts[0], *in_back(fullparts), *outs],
        hbm_in=range(2 + slots, 6 + slots),
        hbm_out=True,
        aliases={2 + slots + which: which for which in range(4)},
    )


def solution(mesh):
    rows = P(("seqo", "seqi"), None)
    return jax.shard_map(
        local,
        mesh=mesh,
        in_specs=(rows,) * 4,
        out_specs=(rows,) * 4,
        check_vma=False,
    )
```
